32 devices in a mesh: section: 2 (over core), expert: 8 (over z, x), shard: 2 (over y).
Axes of the slice: x: 2, y: 2, z: 4, core: 2. Of those that a mesh axis runs over, the one named last changes fastest.
Arguments:
- edge_inputs: bfloat16 [2, 2, 2048, 1536], P('section', None, ('expert', 'shard')), may hold values from -6 to 6
- seq_lengths: int32 [2, 8, 3], P(None, 'expert'), may hold values from 1 to 128, as said below
- routes: int32 [2, 2, 2048, 8], P('section', None, ('expert', 'shard')), may hold values from 0 to 15, all different within a row; in each aligned block of 128 rows (0 to 127, 128 to 255, ..., all dimensions but the last counted through in order) at most 80 rows name the same one
- w_qkv: bfloat16 [2, 1536, 2560], P('section', 'shard'), may hold values from -0.15625 to 0.15625
- w_out: bfloat16 [2, 1536, 1536], P('section', 'shard'), may hold values from -0.625 to 0.625
- w_router: bfloat16 [2, 1536, 16], P('section', 'shard'), may hold values from -0.078125 to 0.078125
- gain_attn: bfloat16 [2, 1536], P('section', 'shard'), may hold values from 0.25 to 1.75
- gain_moe: bfloat16 [2, 1536], P('section', 'shard'), may hold values from 0.25 to 1.75
- w_gate_up: bfloat16 [2, 16, 1536, 1024], P('section', 'expert'), may hold values from -0.15625 to 0.15625
- w_down: bfloat16 [2, 16, 512, 1536], P('section', 'expert'), may hold values from -0.75 to 0.75
Outputs:
- edge_outputs: float32 [2, 2, 2048, 1536], P('section', None, ('expert', 'shard'))
- grad_w_qkv: float32 [2, 1536, 2560], P('section', 'shard')
- grad_w_out: float32 [2, 1536, 1536], P('section', 'shard')
- grad_w_router: float32 [2, 1536, 16], P('section', 'shard')
- grad_gain_attn: float32 [2, 1536], P('section', 'shard')
- grad_gain_moe: float32 [2, 1536], P('section', 'shard')
- grad_w_gate_up: float32 [2, 16, 1536, 1024], P('section', 'expert')
- grad_w_down: float32 [2, 16, 512, 1536], P('section', 'expert')
The draws below stay inside these ranges and needn't reach their ends.
Inputs may be any that keep to these rules, and one draw needn't show every extreme that they name: `seq_lengths`: each group's 3 sequences come in order: the first has 1 to 127 tokens, the second exactly 128, the third the rest of the group's 256 tokens. `routes`: every row names 8 different experts; in the rows of one device for one micro-batch and layer (aligned blocks of 128 rows) no expert is named more than 80 times.
All inputs are finite; a program needn't handle non-finite values.
Results may differ from the reference program's by a relative error of at most 0.025.
Values may be sent and summed in bfloat16 or wider, within the bound.
A program may use at most 256 MiB of HBM per device.

```python
import math
import jax
import jax.numpy as jnp
import numpy as np
from jax import lax

D = 1536
QUERY_HEADS = 24
KEY_VALUE_HEADS = 8
HEAD_SIZE = 64
FF = 512
TOP = 8
SEQS = 3
TOK_MB = 128
MB = 2
EXPERTS = 16
GROUPS = 8
GROUP = 256
TOKENS = 2048
LONGEST = 128
CAP = 80
QKV = 2560


def draw_seq_lengths(key, part):
    key = jax.random.fold_in(key, 7)
    first_len = jax.random.randint(key, (MB, GROUPS), 1, TOK_MB, dtype=jnp.int32)
    middle = jnp.full((MB, GROUPS), LONGEST, jnp.int32)
    return jnp.stack([first_len, middle, TOK_MB - first_len], axis=2)


def block_levels(rng, dims, split, low, high):
    loudness = 1.0
    for axis_at, blocks in split:
        steps = jax.random.uniform(jax.random.fold_in(jax.random.fold_in(rng, 6), axis_at), (blocks,), jnp.float32, low / len(split), high / len(split))
        loudness = loudness * jnp.repeat(jnp.exp(steps), dims[axis_at] // blocks).reshape((-1,) + (1,) * (len(dims) - 1 - axis_at))
    return loudness


def deal_out(own_key, own, number, rows, count, top, most, lean):
    ranking = jax.random.permutation(own_key, count)
    crowded, common = load_shares(count, rows * top, most, lean, True), load_shares(count, rows * top, most, lean, False)
    places = jnp.arange(count)

    def named(sizes, turn):
        used = int((sizes > 0).sum())
        fixed = max(1, used // 4)
        moved = fixed + (places - fixed + turn * (used - fixed)) % max(1, count - fixed)
        return jnp.zeros((count,), jnp.int32).at[ranking[jnp.where(places < fixed, places, moved)]].set(jnp.asarray(sizes, jnp.int32))

    sizes = jnp.where(number % 4 == 0, named(crowded, number // 4), named(common, number - number // 4 - 1))
    mixed = jax.random.permutation(jax.random.fold_in(own, 3), count)
    giver, sink = mixed[0:count // 2 * 2:2], mixed[1:count // 2 * 2:2]
    slack = jnp.minimum(sizes[giver] - 1, most - sizes[sink]) // 2
    slack = jnp.where((giver == ranking[0]) | (sink == ranking[0]) | (sizes[sink] == 0), 0, jnp.maximum(slack, 0))
    moved = jax.random.randint(jax.random.fold_in(own, 4), (count // 2,), 0, 1 << 20) % (slack + 1)
    sizes = sizes.at[giver].add(-moved).at[sink].add(moved)
    items = jnp.searchsorted(jnp.cumsum(sizes), jnp.arange(rows * top), side="right").astype(jnp.int32)
    table = items.reshape(top, rows).T
    table = table[jax.random.permutation(jax.random.fold_in(own, 1), rows)]
    turn = jax.random.randint(jax.random.fold_in(own, 2), (rows, 1), 0, top)
    return jnp.take_along_axis(table, (jnp.arange(top)[None, :] + turn) % top, axis=1)


def load_shares(count, total, bound, slope, full):
    weights = [(1 << 20) // math.isqrt(rank ** slope) + 1 for rank in range(1, count + 1)]
    largest = bound if full else min(bound, max(-(-total // count), total * weights[0] // sum(weights)))
    least = 1 if total - largest >= count - 1 else 0
    holding, rest = [largest] + [least] * (count - 1), total - largest - least * (count - 1)
    while rest > 0:
        free = [i for i in range(1, count) if holding[i] < largest] or [i for i in range(1, count) if holding[i] < bound]
        pool, budget = sum([weights[i] for i in free]), rest
        for i in free:
            extra = min(bound - holding[i], max(1, budget * weights[i] // pool), rest)
            holding[i] = holding[i] + extra
            rest = rest - extra
    return np.array(holding)


def normal_values(rng, dims, scale, most, shards=(), held_as=jnp.bfloat16):
    drawn = scale * jax.random.normal(rng, dims, jnp.float32)
    if shards:
        drawn = drawn * block_levels(rng, dims, shards, -0.22, 0.18)
    return jnp.clip(drawn, -most, most).astype(held_as)


def setup_inputs(seed: int = 0) -> dict:
    arg_keys = jax.random.split(jax.random.key(seed), 11)
    edge_inputs = normal_values(arg_keys[0], (2, MB, TOKENS, D), 1.0, 6.0, ((0, 2), (2, 16)))
    seq_lengths = draw_seq_lengths(jax.random.fold_in(arg_keys[10], 71), 0)
    routes_keys = jax.random.split(jax.random.fold_in(arg_keys[2], 1), 2 * MB * TOKENS // TOK_MB)
    routes_turns = jax.random.permutation(jax.random.fold_in(arg_keys[2], 3), 2 * MB * TOKENS // TOK_MB)
    routes = jax.vmap(lambda own, number: deal_out(jax.random.fold_in(arg_keys[2], 2), own, number, TOK_MB, EXPERTS, TOP, CAP, 1))(routes_keys, routes_turns).reshape((2, MB, TOKENS, TOP))
    w_qkv = normal_values(arg_keys[3], (2, D, QKV), D ** -0.5, 0.15625, ((0, 2), (1, 2)))
    w_out = normal_values(arg_keys[4], (2, QUERY_HEADS * HEAD_SIZE, D), (QUERY_HEADS * HEAD_SIZE // 16) ** -0.5, 0.625, ((0, 2), (1, 2)))
    w_router = normal_values(arg_keys[5], (2, D, EXPERTS), (4 * D) ** -0.5, 0.078125, ((0, 2), (1, 2)))
    gain_attn = jnp.clip(1.0 + 0.15 * jax.random.normal(arg_keys[6], (2, D), jnp.float32), 0.25, 1.75).astype(jnp.bfloat16)
    gain_moe = jnp.clip(1.0 + 0.15 * jax.random.normal(arg_keys[7], (2, D), jnp.float32), 0.25, 1.75).astype(jnp.bfloat16)
    w_gate_up = normal_values(arg_keys[8], (2, EXPERTS, D, 2 * FF), D ** -0.5, 0.15625, ((0, 2), (1, 8)))
    w_down = normal_values(arg_keys[9], (2, EXPERTS, FF, D), (FF // 8) ** -0.5, 0.75, ((0, 2), (1, 8)))
    return dict(edge_inputs=edge_inputs, seq_lengths=seq_lengths, routes=routes, w_qkv=w_qkv, w_out=w_out, w_router=w_router, gain_attn=gain_attn, gain_moe=gain_moe, w_gate_up=w_gate_up, w_down=w_down)


@jax.custom_vjp
def lower_precision(v):
    return lax.optimization_barrier(v.astype(jnp.bfloat16)).astype(jnp.float32)

@jax.custom_vjp
def lower_precision_backward(v):
    return v

def low_keep(v):
    return (lower_precision(v), None)

def low_pass(kept, grad):
    return (grad,)

def back_keep(v):
    return (v, None)

def back_low(kept, grad):
    return (lower_precision(grad),)
lower_precision.defvjp(low_keep, low_pass)
lower_precision_backward.defvjp(back_keep, back_low)
EPS = 1e-05
MASKED_SCORE = -1e+30
HIGHEST_PRECISION = lax.Precision.HIGHEST

def matmul(left_side, right_side):
    return jnp.dot(left_side, right_side, precision=HIGHEST_PRECISION, preferred_element_type=jnp.float32)

def rms_scale(values):
    return lax.rsqrt(lax.optimization_barrier(jnp.mean(values * values, axis=-1, keepdims=True)) + EPS)

def block_layer(layer_in, sequence_lengths, token_routes, weights):
    w_qkv, w_out, w_router, gain_attn, gain_moe, w_gate_up, w_down = weights
    count_of_rows = layer_in.shape[0]
    query_width = QUERY_HEADS * HEAD_SIZE
    key_value_width = KEY_VALUE_HEADS * HEAD_SIZE
    scale_one = rms_scale(layer_in)
    attn_in = lower_precision(layer_in * scale_one * gain_attn)
    projected_rows = matmul(attn_in, w_qkv)
    query_rows = lower_precision(lower_precision_backward(projected_rows[:, :query_width])).reshape(count_of_rows, KEY_VALUE_HEADS, QUERY_HEADS // KEY_VALUE_HEADS, HEAD_SIZE)
    heads_of_keys = lower_precision(lower_precision_backward(projected_rows[:, query_width:query_width + key_value_width])).reshape(count_of_rows, KEY_VALUE_HEADS, HEAD_SIZE)
    heads_of_values = lower_precision(lower_precision_backward(projected_rows[:, query_width + key_value_width:])).reshape(count_of_rows, KEY_VALUE_HEADS, HEAD_SIZE)
    positions = jnp.arange(count_of_rows, dtype=jnp.int32)
    seq_ends = jnp.cumsum(sequence_lengths)
    doc_ids = lax.optimization_barrier(jnp.sum((positions[:, None] >= seq_ends[None, :]).astype(jnp.int32), axis=1))
    allowed = (doc_ids[:, None] == doc_ids[None, :]) & (positions[None, :] <= positions[:, None])
    scores = jnp.einsum('qhgd,khd->hgqk', query_rows, heads_of_keys, precision=HIGHEST_PRECISION) * HEAD_SIZE ** (-0.5)
    scores = lower_precision_backward(jnp.where(allowed[None, None], scores, MASKED_SCORE))
    row_max = lax.optimization_barrier(jnp.max(scores, axis=-1, keepdims=True))
    exponent = jnp.exp(scores - row_max)
    prob_full = exponent / lax.optimization_barrier(jnp.sum(exponent, axis=-1, keepdims=True))
    attended = jnp.einsum('hgqk,khd->qhgd', lower_precision(prob_full), heads_of_values, precision=HIGHEST_PRECISION)
    attended = lower_precision(lower_precision_backward(attended.reshape(count_of_rows, query_width)))
    hidden_one = layer_in + lower_precision_backward(matmul(attended, w_out))
    scale_two = rms_scale(hidden_one)
    mixed_in = lower_precision(hidden_one * scale_two * gain_moe)
    logits = matmul(mixed_in, w_router)
    route_hot = (token_routes[:, :, None] == jnp.arange(logits.shape[1], dtype=jnp.int32)[None, None, :]).astype(jnp.float32)
    chosen = lax.optimization_barrier(jnp.sum(route_hot * logits[:, None, :], axis=2))
    shifted = jnp.exp(chosen - lax.optimization_barrier(jnp.max(chosen, axis=1, keepdims=True)))
    gate_weights = shifted / lax.optimization_barrier(jnp.sum(shifted, axis=1, keepdims=True))
    per_expert = lax.optimization_barrier(jnp.sum(gate_weights[:, :, None] * route_hot, axis=1))

    def expert_step(running, pieces):
        gate_up_w, down_w, column = pieces
        gate_up = lower_precision_backward(matmul(lower_precision_backward(mixed_in), gate_up_w))
        gate_part = gate_up[:, :FF]
        up_part = gate_up[:, FF:]
        hidden = lower_precision(gate_part * jax.nn.sigmoid(gate_part) * up_part)
        expert_out = lower_precision(lower_precision_backward(matmul(hidden, down_w)))
        return (running + column[:, None] * expert_out, None)
    moe_out, unused = lax.scan(expert_step, jnp.zeros_like(layer_in), (w_gate_up, w_down, per_expert.T))
    return hidden_one + moe_out

def stack_layer(layer_in, layer_pos, seq_lengths, routes, params):
    weights = tuple((array_in[layer_pos] for array_in in params))
    grouped = layer_in.reshape(MB * GROUPS, GROUP, D)
    sequence_lengths = seq_lengths.reshape(MB * GROUPS, SEQS)
    token_routes = routes[layer_pos].reshape(MB * GROUPS, GROUP, TOP)
    outputs = lax.map(lambda packed: block_layer(packed[0], packed[1], packed[2], weights), (grouped, sequence_lengths, token_routes))
    return outputs.reshape(MB, TOKENS, D)

def reference(edge_inputs, seq_lengths, routes, w_qkv, w_out, w_router, gain_attn, gain_moe, w_gate_up, w_down):
    given_rows = edge_inputs.astype(jnp.float32)
    params = tuple((array_in.astype(jnp.float32) for array_in in (w_qkv, w_out, w_router, gain_attn, gain_moe, w_gate_up, w_down)))

    def two_layers(first_in, weights):
        middle = lower_precision(lower_precision_backward(stack_layer(first_in, 0, seq_lengths, routes, weights)))
        return stack_layer(middle, 1, seq_lengths, routes, weights)
    result, pullback = jax.vjp(two_layers, given_rows[0], params)
    grad_first, grad_list = pullback(given_rows[1])
    return (jnp.stack([grad_first, result]), grad_list[0], grad_list[1], grad_list[2], grad_list[3], grad_list[4], grad_list[5], grad_list[6])
```

```python
import jax
import jax.numpy as jnp
from jax import lax
from jax.sharding import PartitionSpec as P

QUERY_HEADS = 24
KEY_VALUE_HEADS = 8
HEAD_SIZE = 64
FF = 512
TOP = 8
EXP_DEV = 2
EPS = 1e-05
MASKED_SCORE = -1e30
QUERY_WIDTH = QUERY_HEADS * HEAD_SIZE
KV_WIDTH = KEY_VALUE_HEADS * HEAD_SIZE
F32 = jnp.float32
BF16 = jnp.bfloat16


def dot(a, b, dims):
    return lax.dot_general(a, b, (dims, ((), ())), preferred_element_type=F32)


def rms_scale(values):
    return lax.rsqrt(jnp.mean(values * values, axis=-1, keepdims=True) + EPS)


def swap_cores(value):
    return lax.ppermute(value, "section", [(0, 1), (1, 0)])


def both_layers(own):
    return lax.all_gather(own, "section", axis=0, tiled=False)


def document_mask(sequence_lengths, rows):
    pos = jnp.arange(rows, dtype=jnp.int32)
    ends = jnp.cumsum(sequence_lengths)
    doc = jnp.sum((pos[:, None] >= ends[None, :]).astype(jnp.int32), axis=1)
    return (doc[:, None] == doc[None, :]) & (pos[None, :] <= pos[:, None])


def attention_forward(qkv, allowed, heads, kv_heads):
    rows = qkv.shape[0]
    group = heads // kv_heads
    q = qkv[:, : heads * HEAD_SIZE].reshape(rows, kv_heads, group, HEAD_SIZE)
    k = qkv[:, heads * HEAD_SIZE : (heads + kv_heads) * HEAD_SIZE].reshape(rows, kv_heads, HEAD_SIZE)
    v = qkv[:, (heads + kv_heads) * HEAD_SIZE :].reshape(rows, kv_heads, HEAD_SIZE)
    s = jnp.einsum("qhgd,khd->hgqk", q, k, preferred_element_type=F32) * HEAD_SIZE ** (-0.5)
    s = jnp.where(allowed[None, None], s, MASKED_SCORE)
    ex = jnp.exp(s - jnp.max(s, axis=-1, keepdims=True))
    p = ex / jnp.sum(ex, axis=-1, keepdims=True)
    o = jnp.einsum("hgqk,khd->qhgd", p.astype(BF16), v, preferred_element_type=F32)
    return o.reshape(rows, heads * HEAD_SIZE).astype(BF16), p, (q, k, v)


def attention_backward(do, p, heads_in):
    q, k, v = heads_in
    rows = q.shape[0]
    dh = do.reshape(q.shape)
    dv = jnp.einsum("hgqk,qhgd->khd", p.astype(BF16), dh, preferred_element_type=F32)
    dp = jnp.einsum("qhgd,khd->hgqk", dh, v, preferred_element_type=F32)
    ds = (p * (dp - jnp.sum(p * dp, axis=-1, keepdims=True))).astype(BF16)
    dq = jnp.einsum("hgqk,khd->qhgd", ds, k, preferred_element_type=F32) * HEAD_SIZE ** (-0.5)
    dk = jnp.einsum("hgqk,qhgd->khd", ds, q, preferred_element_type=F32) * HEAD_SIZE ** (-0.5)
    return jnp.concatenate(
        [dq.reshape(rows, -1), dk.reshape(rows, -1), dv.reshape(rows, -1)], axis=1
    ).astype(BF16)


def column_parts(n, j):
    qw, kw = QUERY_WIDTH // n, KV_WIDTH // n
    return (
        (j * qw, qw),
        (QUERY_WIDTH + j * kw, kw),
        (QUERY_WIDTH + KV_WIDTH + j * kw, kw),
    )


def shards(
    edge_inputs, seq_lengths, routes, w_qkv, w_out, w_router, gain_attn, gain_moe, w_gate_up, w_down
):
    sec = lax.axis_index("section")
    owner = lax.axis_index("expert")
    shard_pos = lax.axis_index("shard")
    n_shard = lax.axis_size("shard")
    n_owner = lax.axis_size("expert")
    rows, width = edge_inputs.shape[2], edge_inputs.shape[3]
    experts = w_router.shape[2]
    group_rows = rows * n_shard
    half = width // n_shard
    heads, kv_heads = QUERY_HEADS // n_shard, KEY_VALUE_HEADS // n_shard

    def pick(array, index):
        return lax.dynamic_index_in_dim(array, index, 0, keepdims=False)

    own_edge, other_edge = pick(edge_inputs[0], sec), swap_cores(pick(edge_inputs[0], 1 - sec))
    x_in = jnp.where(sec == 0, own_edge, other_edge)
    dy = jnp.where(sec == 0, other_edge, own_edge)
    own_routes, other_routes = pick(routes[0], sec), swap_cores(pick(routes[0], 1 - sec))
    layer_routes = (
        jnp.where(sec == 0, own_routes, other_routes),
        jnp.where(sec == 0, other_routes, own_routes),
    )
    allowed = document_mask(pick(seq_lengths, sec)[0], group_rows)
    wq = both_layers(w_qkv[0])
    wo = both_layers(w_out[0])
    small = jnp.concatenate([w_router[0], gain_attn[0][:, None], gain_moe[0][:, None]], axis=1)
    small = lax.all_gather(both_layers(small), "shard", axis=1, tiled=True)
    wgu = both_layers(w_gate_up[0])
    wd = both_layers(w_down[0])
    columns = jnp.arange(experts, dtype=jnp.int32)
    route_masks = [
        jnp.any(r[:, :, None] == columns[None, None, :], axis=1).astype(BF16) for r in layer_routes
    ]
    plane_masks = [lax.all_gather(m, "expert", axis=0, tiled=True) for m in route_masks]

    def forward(layer, h):
        gain_a = small[layer, :, experts].astype(F32)[None, :]
        gain_m = small[layer, :, experts + 1].astype(F32)[None, :]
        router = small[layer, :, :experts]
        r1 = rms_scale(h)
        a = (h * r1 * gain_a).astype(BF16)
        a_half = lax.all_to_all(
            a.reshape(rows, n_shard, half), "shard", split_axis=1, concat_axis=0, tiled=True
        ).reshape(group_rows, half)
        blocks = []
        for j in range(n_shard):
            blocks.append(
                jnp.concatenate(
                    [
                        dot(a_half, wq[layer, :, at : at + size], ((1,), (0,)))
                        for at, size in column_parts(n_shard, j)
                    ],
                    axis=1,
                ).astype(BF16)
            )
        qkv = lax.psum_scatter(jnp.stack(blocks), "shard", scatter_dimension=0, tiled=False)
        o, p, heads_in = attention_forward(qkv, allowed, heads, kv_heads)
        part = dot(o, wo[layer], ((1,), (0,))).astype(BF16)
        h1 = h + lax.psum_scatter(part, "shard", scatter_dimension=0, tiled=True).astype(F32)
        r2 = rms_scale(h1)
        b = (h1 * r2 * gain_m).astype(BF16)
        b_all = lax.all_gather(b, "expert", axis=0, tiled=True)
        mask = plane_masks[layer].astype(F32) > 0
        logits = jnp.where(mask, dot(b_all, router, ((1,), (0,))), MASKED_SCORE)
        ex = jnp.where(mask, jnp.exp(logits - jnp.max(logits, axis=1, keepdims=True)), 0.0)
        gates = ex / jnp.sum(ex, axis=1, keepdims=True)
        own_gates = lax.dynamic_slice_in_dim(gates, owner * EXP_DEV, EXP_DEV, 1)
        kept, scaled = [], []
        for j in range(EXP_DEV):
            gu = dot(b_all, wgu[layer, j], ((1,), (0,)))
            g, u = gu[:, :FF], gu[:, FF:]
            scaled.append((g * jax.nn.sigmoid(g) * u * own_gates[:, j : j + 1]).astype(BF16))
            kept.append(gu.astype(BF16))
        scaled = jnp.concatenate(scaled, axis=1)
        moe_part = dot(scaled, wd[layer].reshape(EXP_DEV * FF, width), ((1,), (0,))).astype(BF16)
        moe = lax.psum_scatter(moe_part, "expert", scatter_dimension=0, tiled=True).astype(F32)
        state = (h, r1, a_half, p, heads_in, o, h1, r2, b_all, own_gates, kept, scaled, moe)
        return h1 + moe, state

    def backward(layer, dout, dout_low, state):
        h, r1, a_half, p, heads_in, o, h1, r2, b_all, own_gates, kept, scaled, moe = state
        gain_a = small[layer, :, experts].astype(F32)[None, :]
        gain_m = small[layer, :, experts + 1].astype(F32)[None, :]
        router = small[layer, :, :experts]
        own_router = lax.dynamic_slice_in_dim(router, owner * EXP_DEV, EXP_DEV, 1)
        total = lax.all_gather(jnp.sum(dout * moe, axis=1), "expert", axis=0, tiled=True)
        dout_all = lax.all_gather(dout_low, "expert", axis=0, tiled=True)
        dgus, dcs = [], []
        for j in range(EXP_DEV):
            gate = own_gates[:, j : j + 1]
            g, u = kept[j][:, :FF].astype(F32), kept[j][:, FF:].astype(F32)
            sig = jax.nn.sigmoid(g)
            silu = g * sig
            dz = dot(dout_all, wd[layer, j], ((1,), (1,)))
            dgate = jnp.sum(dz * silu * u, axis=1, keepdims=True)
            dcs.append(gate * (dgate - total[:, None]))
            dz = dz * gate
            dgus.append(
                jnp.concatenate(
                    [dz * u * sig * (1.0 + g * (1.0 - sig)), dz * silu], axis=1
                ).astype(BF16)
            )
        dc = jnp.concatenate(dcs, axis=1)
        db_part = sum(dot(dgus[j], wgu[layer, j], ((1,), (1,))) for j in range(EXP_DEV))
        for j in range(EXP_DEV):
            db_part = db_part + dc[:, j : j + 1] * own_router[:, j].astype(F32)[None, :]
        db = lax.psum_scatter(
            db_part.astype(BF16), "expert", scatter_dimension=0, tiled=True
        ).astype(F32)
        grad_down = dot(scaled, dout_all, ((0,), (0,))).reshape(EXP_DEV, FF, width)
        grad_gu = jnp.stack([dot(b_all, dgus[j], ((0,), (0,))) for j in range(EXP_DEV)])
        grad_router = lax.dot_general(
            dc, b_all.astype(F32), (((0,), (0,)), ((), ())), precision=lax.Precision.HIGHEST
        )
        normed = h1 * r2
        grad_gain_m = jnp.sum(db * normed, axis=0)
        scaled_db = db * gain_m
        dh1 = dout + r2 * (scaled_db - normed * jnp.mean(scaled_db * normed, axis=1, keepdims=True))
        dattn = lax.all_gather(dh1.astype(BF16), "shard", axis=0, tiled=True)
        do = dot(dattn, wo[layer], ((1,), (1,))).astype(BF16)
        grad_out = dot(o, dattn, ((0,), (0,)))
        dqkv = lax.all_gather(attention_backward(do, p, heads_in), "shard", axis=0, tiled=False)
        da = 0.0
        grad_qkv = []
        for part in range(3):
            grad_qkv.append([])
        for j in range(n_shard):
            at_local = 0
            for part, (at, size) in enumerate(column_parts(n_shard, j)):
                piece = dqkv[j, :, at_local : at_local + size]
                at_local += size
                da = da + dot(piece, wq[layer, :, at : at + size], ((1,), (1,)))
                grad_qkv[part].append(dot(a_half, piece, ((0,), (0,))))
        grad_qkv = jnp.concatenate([x for part in grad_qkv for x in part], axis=1)
        da = lax.all_to_all(
            da.astype(BF16), "shard", split_axis=0, concat_axis=1, tiled=True
        ).astype(F32)
        normed = h * r1
        grad_gain_a = jnp.sum(da * normed, axis=0)
        scaled_da = da * gain_a
        dh = dh1 + r1 * (scaled_da - normed * jnp.mean(scaled_da * normed, axis=1, keepdims=True))
        return dh, (grad_qkv, grad_out, grad_router, grad_gain_a, grad_gain_m, grad_gu, grad_down)

    out0, state0 = forward(0, x_in.astype(F32))
    mid = out0.astype(BF16).astype(F32)
    final, state1 = forward(1, mid)
    dh_one, grads1 = backward(1, dy.astype(F32), dy, state1)
    low = dh_one.astype(BF16)
    dh_zero, grads0 = backward(0, low.astype(F32), low, state0)

    def half_sum(grad):
        low_grad = grad.astype(BF16)
        halves = low_grad.reshape((2, -1) + low_grad.shape[1:])
        got = swap_cores(pick(halves, 1 - sec))
        return (pick(halves, sec).astype(F32) + got.astype(F32)).astype(BF16)

    def to_owner(half0, half1):
        keep = jnp.where(sec == 0, half0, half1)
        got = swap_cores(jnp.where(sec == 0, half1, half0))
        first = jnp.where(sec == 0, keep, got)
        second = jnp.where(sec == 0, got, keep)
        return jnp.concatenate([first, second], axis=0).astype(F32)

    attn_halves, exp_halves = [], []
    for grads in (grads0, grads1):
        attn = half_sum(jnp.concatenate([grads[0], grads[1]], axis=1))
        attn_halves.append(lax.psum(attn, "expert"))
        exp_halves.append(tuple(lax.psum(half_sum(g), "shard") for g in (grads[5], grads[6])))
    attn = to_owner(*attn_halves)
    grad_qkv, grad_out = attn[:, : w_qkv.shape[2]], attn[:, w_qkv.shape[2] :]
    grad_gu = to_owner(exp_halves[0][0], exp_halves[1][0])
    grad_down = to_owner(exp_halves[0][1], exp_halves[1][1])

    tiny = []
    for grads in (grads0, grads1):
        hot = jnp.arange(experts)[:, None] == owner * EXP_DEV + jnp.arange(EXP_DEV)[None, :]
        router = sum(
            jnp.where(hot[:, j : j + 1], grads[2][j][None, :], 0.0) for j in range(EXP_DEV)
        )
        tiny.append(jnp.concatenate([router, grads[3][None, :], grads[4][None, :]], axis=0))
    tiny = lax.psum(jnp.stack(tiny), ("section", "expert", "shard"))
    tiny = lax.dynamic_slice_in_dim(pick(tiny, sec), shard_pos * half, half, 1)

    send = jnp.where(sec == 0, final, dh_zero)
    keep = jnp.where(sec == 0, dh_zero, final)
    got = swap_cores(send)
    edge = jnp.where(sec == 0, jnp.stack([keep, got]), jnp.stack([got, keep]))
    return (
        edge[None],
        grad_qkv[None],
        grad_out[None],
        tiny[:experts].T[None],
        tiny[experts][None],
        tiny[experts + 1][None],
        grad_gu[None],
        grad_down[None],
    )


def solution(mesh):
    in_specs = (
        P("section", None, ("expert", "shard"), None),
        P(None, "expert", None),
        P("section", None, ("expert", "shard"), None),
        P("section", "shard", None),
        P("section", "shard", None),
        P("section", "shard", None),
        P("section", "shard"),
        P("section", "shard"),
        P("section", "expert", None, None),
        P("section", "expert", None, None),
    )
    out_specs = (
        P("section", None, ("expert", "shard"), None),
        P("section", "shard", None),
        P("section", "shard", None),
        P("section", "shard", None),
        P("section", "shard"),
        P("section", "shard"),
        P("section", "expert", None, None),
        P("section", "expert", None, None),
    )
    return jax.shard_map(shards, mesh=mesh, in_specs=in_specs, out_specs=out_specs, check_vma=False)
```

```python
import functools

import jax
import jax.numpy as jnp
from jax import lax
from jax.experimental import pallas as pl
from jax.experimental.pallas import tpu as pltpu
from jax.sharding import PartitionSpec as P

QUERY_HEADS = 24
KEY_VALUE_HEADS = 8
HEAD_SIZE = 64
FF = 512
TOP = 8
EXP_DEV = 2
EPS = 1e-05
MASKED_SCORE = -1e30
QUERY_WIDTH = QUERY_HEADS * HEAD_SIZE
KV_WIDTH = KEY_VALUE_HEADS * HEAD_SIZE
F32 = jnp.float32
BF16 = jnp.bfloat16
MESH = pl.DeviceIdType.MESH
LINE = 4
SIDE = 2
LANES = 128
TILE = 256
VMEM_BYTES = 60 * 2**20


def chunk_order(z, t):
    near = z + 1 - 2 * lax.rem(z, 2)
    third = jnp.where(z < 2, 2, 1)
    last = jnp.where(z < 2, 3, 0)
    return jnp.where(t == 0, z, jnp.where(t == 1, near, jnp.where(t == 2, third, last)))


class Plane:
    def __init__(self, rows, gathered, parts, from_side, from_low, from_high, sums, sems):
        (self.line_send, self.gather_recv, self.side_send, self.side_recv,
         self.sum_send, self.low_recv, self.high_recv) = sems
        self.rows = rows
        self.gathered, self.parts, self.from_side = gathered, parts, from_side
        self.from_low, self.from_high, self.sums = from_low, from_high, sums
        self.sec, self.owner, self.shard = (lax.axis_index(n) for n in ("section", "expert", "shard"))
        self.z, self.x = lax.div(self.owner, SIDE), lax.rem(self.owner, SIDE)

    def device(self, z, x):
        return (self.sec, z * SIDE + x, self.shard)

    def mine(self, x):
        return pl.ds(pl.multiple_of(x * self.rows, self.rows), self.rows)

    def barrier(self):
        z, x = self.z, self.x
        sem = pltpu.get_barrier_semaphore()

        def greet(device):
            pl.semaphore_signal(sem, inc=1, device_id=device, device_id_type=MESH)

        greet(self.device(z, 1 - x))
        pl.when(z > 0)(lambda: greet(self.device(z - 1, x)))
        pl.when(z < LINE - 1)(lambda: greet(self.device(z + 1, x)))
        pl.semaphore_wait(sem, 1 + (z > 0).astype(jnp.int32) + (z < LINE - 1).astype(jnp.int32))

    def gather_copy(self, way, c, x, device):
        ref = self.gathered.at[c, self.mine(x)]
        return pltpu.make_async_remote_copy(
            src_ref=ref, dst_ref=ref, send_sem=self.line_send.at[way, c],
            recv_sem=self.gather_recv.at[c, x], device_id=device, device_id_type=MESH)

    def forward_up(self, c):
        return self.gather_copy(0, c, self.x, self.device(self.z + 1, self.x))

    def forward_down(self, c):
        return self.gather_copy(1, c, self.x, self.device(self.z - 1, self.x))

    def forward_side(self, c):
        return self.gather_copy(2, c, self.x, self.device(self.z, 1 - self.x))

    def start_gather(self):
        z = self.z
        pl.when(z < LINE - 1)(lambda: self.forward_up(z).start())
        pl.when(z > 0)(lambda: self.forward_down(z).start())
        self.forward_side(z).start()

    def relay(self, t):
        z = self.z

        @pl.when((t > 0) & (z - t >= 0))
        def _():
            c = z - t
            self.forward_side(c).wait_recv()
            pl.when(z < LINE - 1)(lambda: self.forward_up(c).start())
            self.forward_side(c).start()

        @pl.when((t > 0) & (z + t <= LINE - 1))
        def _():
            c = z + t
            self.forward_side(c).wait_recv()
            pl.when(z > 0)(lambda: self.forward_down(c).start())
            self.forward_side(c).start()

    def wait_side_block(self, c):
        self.gather_copy(2, c, 1 - self.x, self.device(self.z, 1 - self.x)).wait_recv()

    def side_copy(self, c):
        return pltpu.make_async_remote_copy(
            src_ref=self.parts.at[c, self.mine(1 - self.x)], dst_ref=self.from_side.at[c],
            send_sem=self.side_send.at[c], recv_sem=self.side_recv.at[c],
            device_id=self.device(self.z, 1 - self.x), device_id_type=MESH)

    def up_copy(self, c):
        return pltpu.make_async_remote_copy(
            src_ref=self.sums.at[c], dst_ref=self.from_low.at[c], send_sem=self.sum_send.at[c],
            recv_sem=self.low_recv.at[c], device_id=self.device(self.z + 1, self.x), device_id_type=MESH)

    def down_copy(self, c):
        return pltpu.make_async_remote_copy(
            src_ref=self.sums.at[c], dst_ref=self.from_high.at[c], send_sem=self.sum_send.at[c],
            recv_sem=self.high_recv.at[c], device_id=self.device(self.z - 1, self.x), device_id_type=MESH)

    def own_part(self, c):
        return self.parts[c, self.mine(self.x)].astype(F32) + self.from_side[c].astype(F32)

    def pass_sum(self, c):
        z = self.z
        self.side_copy(c).wait_recv()

        @pl.when(c > z)
        def _():
            @pl.when(z > 0)
            def _():
                self.up_copy(c).wait_recv()
                self.sums[c] = (self.own_part(c) + self.from_low[c].astype(F32)).astype(BF16)

            @pl.when(z == 0)
            def _():
                self.sums[c] = self.own_part(c).astype(BF16)

            self.up_copy(c).start()

        @pl.when(c < z)
        def _():
            @pl.when(z < LINE - 1)
            def _():
                self.down_copy(c).wait_recv()
                self.sums[c] = (self.own_part(c) + self.from_high[c].astype(F32)).astype(BF16)

            @pl.when(z == LINE - 1)
            def _():
                self.sums[c] = self.own_part(c).astype(BF16)

            self.down_copy(c).start()

    def finish_sum(self, out_ref):
        z = self.z
        self.side_copy(z).wait_recv()
        out_ref[...] = self.own_part(z)

        @pl.when(z > 0)
        def _():
            self.up_copy(z).wait_recv()
            out_ref[...] += self.from_low[z].astype(F32)

        @pl.when(z < LINE - 1)
        def _():
            self.down_copy(z).wait_recv()
            out_ref[...] += self.from_high[z].astype(F32)

    def drain(self):
        z = self.z
        for c in range(LINE):
            pl.when((z < LINE - 1) & (c <= z))(lambda c=c: self.forward_up(c).wait_send())
            pl.when((z > 0) & (c >= z))(lambda c=c: self.forward_down(c).wait_send())
            self.forward_side(c).wait_send()
            self.side_copy(c).wait_send()
            pl.when(c > z)(lambda c=c: self.up_copy(c).wait_send())
            pl.when(c < z)(lambda c=c: self.down_copy(c).wait_send())


def plane_scratch(rows, width, wide):
    block = pltpu.VMEM((LINE, rows, width), BF16)
    return [
        pltpu.VMEM((LINE, SIDE * rows, wide), BF16),
        pltpu.VMEM((LINE, SIDE * rows, width), BF16),
        block, block, block, block,
        pltpu.SemaphoreType.DMA((3, LINE)),
        pltpu.SemaphoreType.DMA((LINE, SIDE)),
        pltpu.SemaphoreType.DMA((LINE,)),
        pltpu.SemaphoreType.DMA((LINE,)),
        pltpu.SemaphoreType.DMA((LINE,)),
        pltpu.SemaphoreType.DMA((LINE,)),
        pltpu.SemaphoreType.DMA((LINE,)),
    ]


PLANE_REFS = 13


def lane_tile(at, size=TILE):
    return pl.ds(pl.multiple_of(at * size, size), size)


def nn(a, b):
    return jnp.dot(a, b, preferred_element_type=F32)


def nt(a, b):
    return lax.dot_general(a, b, (((1,), (1,)), ((), ())), preferred_element_type=F32)


def tn(a, b):
    return lax.dot_general(a, b, (((0,), (0,)), ((), ())), preferred_element_type=F32)


def pick_lane(block, wanted):
    lane = lax.broadcasted_iota(jnp.int32, block.shape, 1)
    hot = lane == wanted[0]
    for other in wanted[1:]:
        hot = hot | (lane == other)
    return jnp.sum(jnp.where(hot, block, 0.0), axis=1, keepdims=True)


def own_gates(block, owner, experts):
    block = block.astype(F32)
    return [
        pick_lane(block, (owner * EXP_DEV + j, experts + owner * EXP_DEV + j)) for j in range(EXP_DEV)
    ]


def moe_forward_kernel(layer, experts, rows, width, block_ref, gu_hbm, down_hbm,
                       moe_ref, rows_hbm, kept_hbm, scaled_hbm,
                       gu_v, down_v, kept, scaled, load_sem, store_sem, *plane_refs):
    plane = Plane(rows, *plane_refs[:6], plane_refs[6:])
    gathered, parts = plane.gathered, plane.parts
    loads = [pltpu.make_async_copy(gu_hbm.at[layer], gu_v, load_sem.at[0])]
    for j in range(EXP_DEV):
        loads.append(pltpu.make_async_copy(
            down_hbm.at[layer, j], down_v.at[pl.ds(j * FF, FF)], load_sem.at[1 + j]))
    for load in loads:
        load.start()
    gathered[plane.z, plane.mine(plane.x)] = block_ref[...]
    plane.barrier()
    plane.start_gather()
    for load in loads:
        load.wait()

    def stores(c):
        return [
            pltpu.make_async_copy(gathered.at[c], rows_hbm.at[c], store_sem.at[0, c]),
            pltpu.make_async_copy(kept.at[c], kept_hbm.at[c], store_sem.at[1, c]),
            pltpu.make_async_copy(scaled.at[c], scaled_hbm.at[c], store_sem.at[2, c]),
        ]

    def step(t, carry):
        plane.relay(t)
        c = chunk_order(plane.z, t)
        plane.wait_side_block(c)
        gates = own_gates(gathered[c, :, pl.ds(width, LANES)], plane.owner, experts)
        for j in range(EXP_DEV):
            @pl.loop(0, FF // TILE)
            def _(f, j=j):
                data = gathered[c, :, pl.ds(0, width)]
                g = nn(data, gu_v[j, :, lane_tile(f)])
                u = nn(data, gu_v[j, :, lane_tile(f + FF // TILE)])
                z = g * jax.nn.sigmoid(g) * u * gates[j]
                scaled[c, :, lane_tile(f + j * (FF // TILE))] = z.astype(BF16)
                kept[c, :, lane_tile(f + j * (2 * FF // TILE))] = g.astype(BF16)
                kept[c, :, lane_tile(f + j * (2 * FF // TILE) + FF // TILE)] = u.astype(BF16)

        @pl.loop(0, width // TILE)
        def _(n):
            parts[c, :, lane_tile(n)] = nn(scaled[c], down_v[:, lane_tile(n)]).astype(BF16)

        plane.side_copy(c).start()
        for store in stores(c):
            store.start()
        return carry

    lax.fori_loop(0, LINE, step, 0)

    def sum_step(t, carry):
        plane.pass_sum(chunk_order(plane.z, LINE - 1 - t))
        return carry

    lax.fori_loop(0, LINE - 1, sum_step, 0)
    plane.finish_sum(moe_ref)
    plane.drain()
    for c in range(LINE):
        for store in stores(c):
            store.wait()


def moe_forward(layer, block, gu, down, experts, collective_id):
    rows, wide = block.shape
    width = wide - LANES
    total = SIDE * rows
    any_spec = pl.BlockSpec(memory_space=pl.ANY)
    vmem = pl.BlockSpec(memory_space=pltpu.VMEM)
    return pl.pallas_call(
        functools.partial(moe_forward_kernel, layer, experts, rows, width),
        name="moe_forward",
        out_shape=(
            jax.ShapeDtypeStruct((rows, width), F32),
            jax.ShapeDtypeStruct((LINE, total, wide), BF16),
            jax.ShapeDtypeStruct((LINE, total, EXP_DEV * 2 * FF), BF16),
            jax.ShapeDtypeStruct((LINE, total, EXP_DEV * FF), BF16),
        ),
        in_specs=[vmem, any_spec, any_spec],
        out_specs=(vmem, any_spec, any_spec, any_spec),
        scratch_shapes=[
            pltpu.VMEM((EXP_DEV, width, 2 * FF), BF16),
            pltpu.VMEM((EXP_DEV * FF, width), BF16),
            pltpu.VMEM((LINE, total, EXP_DEV * 2 * FF), BF16),
            pltpu.VMEM((LINE, total, EXP_DEV * FF), BF16),
            pltpu.SemaphoreType.DMA((1 + EXP_DEV,)),
            pltpu.SemaphoreType.DMA((3, LINE)),
        ] + plane_scratch(rows, width, wide),
        compiler_params=pltpu.CompilerParams(
            collective_id=collective_id, has_side_effects=True, vmem_limit_bytes=VMEM_BYTES),
    )(block, gu, down)


def moe_backward_kernel(layer, experts, rows, width, block_ref, router_ref, gu_hbm, down_hbm, rows_hbm, kept_hbm,
                        scaled_hbm, db_ref, grad_gu_hbm, grad_down_hbm, grad_router_ref,
                        gu_v, down_v, fwd_rows, kept, scaled, dgu, grad_gu, grad_down, load_sem, chunk_sem,
                        store_sem, *plane_refs):
    plane = Plane(rows, *plane_refs[:6], plane_refs[6:])
    gathered, parts = plane.gathered, plane.parts
    loads = []
    for j in range(EXP_DEV):
        loads.append(pltpu.make_async_copy(
            down_hbm.at[layer, j], down_v.at[pl.ds(j * FF, FF)], load_sem.at[1 + j]))
    loads.append(pltpu.make_async_copy(gu_hbm.at[layer], gu_v, load_sem.at[0]))
    loads.append(pltpu.make_async_copy(rows_hbm, fwd_rows, load_sem.at[3]))
    loads.append(pltpu.make_async_copy(kept_hbm, kept, load_sem.at[4]))
    loads.append(pltpu.make_async_copy(scaled_hbm, scaled, load_sem.at[5]))
    for load in loads:
        load.start()
    gathered[plane.z, plane.mine(plane.x)] = block_ref[...]
    plane.barrier()
    plane.start_gather()
    for load in loads:
        load.wait()
    total = SIDE * rows
    up_at = EXP_DEV * 2 * FF

    def step(t, carry):
        plane.relay(t)
        c = chunk_order(plane.z, t)
        plane.wait_side_block(c)
        gates = own_gates(fwd_rows[c, :, pl.ds(width, LANES)], plane.owner, experts)
        outer = jnp.sum(gathered[c, :, pl.ds(width, LANES)].astype(F32), axis=1, keepdims=True)
        dcs = []
        for j in range(EXP_DEV):
            def tile_step(f, dgate, j=j):
                data = gathered[c, :, pl.ds(0, width)]
                at = pl.multiple_of(j * FF + f * TILE, TILE)
                dz = nt(data, down_v[pl.ds(at, TILE), :])
                g = kept[c, :, lane_tile(f + j * (2 * FF // TILE))].astype(F32)
                u = kept[c, :, lane_tile(f + j * (2 * FF // TILE) + FF // TILE)].astype(F32)
                sig = jax.nn.sigmoid(g)
                silu = g * sig
                dgate = dgate + jnp.sum(dz * silu * u, axis=1, keepdims=True)
                dz = dz * gates[j]
                dg = dz * u * sig * (1.0 + g * (1.0 - sig))
                dgu[c, :, lane_tile(f + j * (2 * FF // TILE))] = dg.astype(BF16)
                dgu[c, :, lane_tile(f + j * (2 * FF // TILE) + FF // TILE)] = (dz * silu).astype(BF16)
                return dgate

            dgate = lax.fori_loop(0, FF // TILE, tile_step, jnp.zeros((total, 1), F32))
            dcs.append(gates[j] * (dgate - outer))
        lane = lax.broadcasted_iota(jnp.int32, (total, LANES), 1)
        low = jnp.zeros((total, LANES), F32)
        for j in range(EXP_DEV):
            high = dcs[j].astype(BF16).astype(F32)
            low = low + jnp.where(lane == j, high, 0.0) + jnp.where(lane == EXP_DEV + j, dcs[j] - high, 0.0)
        dgu[c, :, pl.ds(up_at, LANES)] = low.astype(BF16)

        @pl.loop(0, width // TILE)
        def _(n):
            acc = nt(dgu[c, :, pl.ds(0, 2 * FF)], gu_v[0, lane_tile(n), :])
            for j in range(1, EXP_DEV):
                acc = acc + nt(dgu[c, :, pl.ds(j * 2 * FF, 2 * FF)], gu_v[j, lane_tile(n), :])
            for j in range(EXP_DEV):
                acc = acc + dcs[j] * router_ref[pl.ds(j, 1), lane_tile(n)]
            parts[c, :, lane_tile(n)] = acc.astype(BF16)

        plane.side_copy(c).start()
        return carry

    lax.fori_loop(0, LINE, step, 0)

    def store_gu(n):
        return [pltpu.make_async_copy(
            grad_gu.at[j, lane_tile(n)], grad_gu_hbm.at[j, lane_tile(n)], store_sem.at[0, j, n])
            for j in range(EXP_DEV)]

    def store_down(n):
        return pltpu.make_async_copy(
            grad_down.at[lane_tile(n)], grad_down_hbm.at[lane_tile(n)], store_sem.at[1, 0, n])

    def grad_gu_rows(n):
        for j in range(EXP_DEV):
            acc = tn(fwd_rows[0, :, lane_tile(n)], dgu[0, :, pl.ds(j * 2 * FF, 2 * FF)])
            for c in range(1, LINE):
                acc = acc + tn(fwd_rows[c, :, lane_tile(n)], dgu[c, :, pl.ds(j * 2 * FF, 2 * FF)])
            grad_gu[j, lane_tile(n), :] = acc.astype(BF16)
        acc = tn(fwd_rows[0, :, lane_tile(n)], dgu[0, :, pl.ds(up_at, LANES)])
        for c in range(1, LINE):
            acc = acc + tn(fwd_rows[c, :, lane_tile(n)], dgu[c, :, pl.ds(up_at, LANES)])
        grad_router_ref[lane_tile(n), :] = acc
        for store in store_gu(n):
            store.start()

    def grad_down_rows(n):
        acc = tn(scaled[0, :, lane_tile(n)], gathered[0, :, pl.ds(0, width)])
        for c in range(1, LINE):
            acc = acc + tn(scaled[c, :, lane_tile(n)], gathered[c, :, pl.ds(0, width)])
        grad_down[lane_tile(n), :] = acc.astype(BF16)
        store_down(n).start()

    gu_steps, down_steps = width // TILE, EXP_DEV * FF // TILE

    def sum_step(t, carry):
        pl.loop(2 * t, 2 * t + 2)(grad_gu_rows)
        plane.pass_sum(chunk_order(plane.z, LINE - 1 - t))
        return carry

    lax.fori_loop(0, LINE - 1, sum_step, 0)
    pl.loop(0, down_steps)(grad_down_rows)
    plane.finish_sum(db_ref)
    plane.drain()
    for n in range(gu_steps):
        for store in store_gu(n):
            store.wait()
    for n in range(down_steps):
        store_down(n).wait()


def moe_backward(layer, block, router, gu, down, rows_kept, kept, scaled, experts, collective_id):
    rows, wide = block.shape
    width = wide - LANES
    total = SIDE * rows
    any_spec = pl.BlockSpec(memory_space=pl.ANY)
    vmem = pl.BlockSpec(memory_space=pltpu.VMEM)
    return pl.pallas_call(
        functools.partial(moe_backward_kernel, layer, experts, rows, width),
        name="moe_backward",
        out_shape=(
            jax.ShapeDtypeStruct((rows, width), F32),
            jax.ShapeDtypeStruct((EXP_DEV, width, 2 * FF), BF16),
            jax.ShapeDtypeStruct((EXP_DEV * FF, width), BF16),
            jax.ShapeDtypeStruct((width, LANES), F32),
        ),
        in_specs=[vmem, vmem] + [any_spec] * 5,
        out_specs=(vmem, any_spec, any_spec, vmem),
        scratch_shapes=[
            pltpu.VMEM((EXP_DEV, width, 2 * FF), BF16),
            pltpu.VMEM((EXP_DEV * FF, width), BF16),
            pltpu.VMEM((LINE, total, wide), BF16),
            pltpu.VMEM((LINE, total, EXP_DEV * 2 * FF), BF16),
            pltpu.VMEM((LINE, total, EXP_DEV * FF), BF16),
            pltpu.VMEM((LINE, total, EXP_DEV * 2 * FF + LANES), BF16),
            pltpu.VMEM((EXP_DEV, width, 2 * FF), BF16),
            pltpu.VMEM((EXP_DEV * FF, width), BF16),
            pltpu.SemaphoreType.DMA((6,)),
            pltpu.SemaphoreType.DMA((3, LINE)),
            pltpu.SemaphoreType.DMA((2, EXP_DEV, max(width, EXP_DEV * FF) // TILE)),
        ] + plane_scratch(rows, width, wide),
        compiler_params=pltpu.CompilerParams(
            collective_id=collective_id, has_side_effects=True, vmem_limit_bytes=VMEM_BYTES),
    )(block, router, gu, down, rows_kept, kept, scaled)


def split_terms(values):
    high = values.astype(BF16)
    return high, (values - high.astype(F32)).astype(BF16)


def with_lanes(block, columns):
    extra = jnp.concatenate(columns, axis=1)
    extra = jnp.pad(extra, ((0, 0), (0, LANES - extra.shape[1])))
    return jnp.concatenate([block, extra], axis=1)


def dot(a, b, dims):
    return lax.dot_general(a, b, (dims, ((), ())), preferred_element_type=F32)


def rms_scale(values):
    return lax.rsqrt(jnp.mean(values * values, axis=-1, keepdims=True) + EPS)


def swap_cores(value):
    return lax.ppermute(value, "section", [(0, 1), (1, 0)])


def both_layers(own):
    return lax.all_gather(own, "section", axis=0, tiled=False)


def document_mask(sequence_lengths, rows):
    pos = jnp.arange(rows, dtype=jnp.int32)
    ends = jnp.cumsum(sequence_lengths)
    doc = jnp.sum((pos[:, None] >= ends[None, :]).astype(jnp.int32), axis=1)
    return (doc[:, None] == doc[None, :]) & (pos[None, :] <= pos[:, None])


def attention_forward(qkv, allowed, heads, kv_heads):
    rows = qkv.shape[0]
    group = heads // kv_heads
    q = qkv[:, : heads * HEAD_SIZE].reshape(rows, kv_heads, group, HEAD_SIZE)
    k = qkv[:, heads * HEAD_SIZE : (heads + kv_heads) * HEAD_SIZE].reshape(rows, kv_heads, HEAD_SIZE)
    v = qkv[:, (heads + kv_heads) * HEAD_SIZE :].reshape(rows, kv_heads, HEAD_SIZE)
    s = jnp.einsum("qhgd,khd->hgqk", q, k, preferred_element_type=F32) * HEAD_SIZE ** (-0.5)
    s = jnp.where(allowed[None, None], s, MASKED_SCORE)
    ex = jnp.exp(s - jnp.max(s, axis=-1, keepdims=True))
    p = ex / jnp.sum(ex, axis=-1, keepdims=True)
    o = jnp.einsum("hgqk,khd->qhgd", p.astype(BF16), v, preferred_element_type=F32)
    return o.reshape(rows, heads * HEAD_SIZE).astype(BF16), p, (q, k, v)


def attention_backward(do, p, heads_in):
    q, k, v = heads_in
    rows = q.shape[0]
    dh = do.reshape(q.shape)
    dv = jnp.einsum("hgqk,qhgd->khd", p.astype(BF16), dh, preferred_element_type=F32)
    dp = jnp.einsum("qhgd,khd->hgqk", dh, v, preferred_element_type=F32)
    ds = (p * (dp - jnp.sum(p * dp, axis=-1, keepdims=True))).astype(BF16)
    dq = jnp.einsum("hgqk,khd->qhgd", ds, k, preferred_element_type=F32) * HEAD_SIZE ** (-0.5)
    dk = jnp.einsum("hgqk,qhgd->khd", ds, q, preferred_element_type=F32) * HEAD_SIZE ** (-0.5)
    return jnp.concatenate(
        [dq.reshape(rows, -1), dk.reshape(rows, -1), dv.reshape(rows, -1)], axis=1
    ).astype(BF16)


def column_parts(n, j):
    qw, kw = QUERY_WIDTH // n, KV_WIDTH // n
    return (
        (j * qw, qw),
        (QUERY_WIDTH + j * kw, kw),
        (QUERY_WIDTH + KV_WIDTH + j * kw, kw),
    )


def shards(
    edge_inputs, seq_lengths, routes, w_qkv, w_out, w_router, gain_attn, gain_moe, w_gate_up, w_down
):
    sec = lax.axis_index("section")
    owner = lax.axis_index("expert")
    shard_pos = lax.axis_index("shard")
    n_shard = lax.axis_size("shard")
    n_owner = lax.axis_size("expert")
    rows, width = edge_inputs.shape[2], edge_inputs.shape[3]
    experts = w_router.shape[2]
    group_rows = rows * n_shard
    half = width // n_shard
    heads, kv_heads = QUERY_HEADS // n_shard, KEY_VALUE_HEADS // n_shard

    def pick(array, index):
        return lax.dynamic_index_in_dim(array, index, 0, keepdims=False)

    own_edge, other_edge = pick(edge_inputs[0], sec), swap_cores(pick(edge_inputs[0], 1 - sec))
    x_in = jnp.where(sec == 0, own_edge, other_edge)
    dy = jnp.where(sec == 0, other_edge, own_edge)
    own_routes, other_routes = pick(routes[0], sec), swap_cores(pick(routes[0], 1 - sec))
    layer_routes = (
        jnp.where(sec == 0, own_routes, other_routes),
        jnp.where(sec == 0, other_routes, own_routes),
    )
    allowed = document_mask(pick(seq_lengths, sec)[0], group_rows)
    wq = both_layers(w_qkv[0])
    wo = both_layers(w_out[0])
    small = jnp.concatenate([w_router[0], gain_attn[0][:, None], gain_moe[0][:, None]], axis=1)
    small = lax.all_gather(both_layers(small), "shard", axis=1, tiled=True)
    wgu = both_layers(w_gate_up[0])
    wd = both_layers(w_down[0])
    columns = jnp.arange(experts, dtype=jnp.int32)
    route_masks = [
        jnp.any(r[:, :, None] == columns[None, None, :], axis=1).astype(BF16) for r in layer_routes
    ]
    kernels = n_owner == LINE * SIDE
    if not kernels:
        plane_masks = [lax.all_gather(m, "expert", axis=0, tiled=True) for m in route_masks]

    def token_gates(b, router, mask):
        logits = jnp.where(mask, dot(b, router, ((1,), (0,))), MASKED_SCORE)
        ex = jnp.where(mask, jnp.exp(logits - jnp.max(logits, axis=1, keepdims=True)), 0.0)
        return ex / jnp.sum(ex, axis=1, keepdims=True)

    def forward(layer, h):
        gain_a = small[layer, :, experts].astype(F32)[None, :]
        gain_m = small[layer, :, experts + 1].astype(F32)[None, :]
        router = small[layer, :, :experts]
        r1 = rms_scale(h)
        a = (h * r1 * gain_a).astype(BF16)
        a_half = lax.all_to_all(
            a.reshape(rows, n_shard, half), "shard", split_axis=1, concat_axis=0, tiled=True
        ).reshape(group_rows, half)
        blocks = []
        for j in range(n_shard):
            blocks.append(
                jnp.concatenate(
                    [
                        dot(a_half, wq[layer, :, at : at + size], ((1,), (0,)))
                        for at, size in column_parts(n_shard, j)
                    ],
                    axis=1,
                ).astype(BF16)
            )
        qkv = lax.psum_scatter(jnp.stack(blocks), "shard", scatter_dimension=0, tiled=False)
        o, p, heads_in = attention_forward(qkv, allowed, heads, kv_heads)
        part = dot(o, wo[layer], ((1,), (0,))).astype(BF16)
        h1 = h + lax.psum_scatter(part, "shard", scatter_dimension=0, tiled=True).astype(F32)
        r2 = rms_scale(h1)
        b = (h1 * r2 * gain_m).astype(BF16)
        first = (h, r1, a_half, p, heads_in, o, h1, r2)
        if kernels:
            gates = token_gates(b, router, route_masks[layer].astype(F32) > 0)
            block = with_lanes(b, split_terms(gates))
            moe, *kept = moe_forward(layer, block, wgu, wd, experts, 1 + layer)
            return h1 + moe, first + (moe, kept)
        b_all = lax.all_gather(b, "expert", axis=0, tiled=True)
        gates = token_gates(b_all, router, plane_masks[layer].astype(F32) > 0)
        own_gates = lax.dynamic_slice_in_dim(gates, owner * EXP_DEV, EXP_DEV, 1)
        kept, scaled = [], []
        for j in range(EXP_DEV):
            gu = dot(b_all, wgu[layer, j], ((1,), (0,)))
            g, u = gu[:, :FF], gu[:, FF:]
            scaled.append((g * jax.nn.sigmoid(g) * u * own_gates[:, j : j + 1]).astype(BF16))
            kept.append(gu.astype(BF16))
        scaled = jnp.concatenate(scaled, axis=1)
        moe_part = dot(scaled, wd[layer].reshape(EXP_DEV * FF, width), ((1,), (0,))).astype(BF16)
        moe = lax.psum_scatter(moe_part, "expert", scatter_dimension=0, tiled=True).astype(F32)
        return h1 + moe, first + (moe, (b_all, own_gates, kept, scaled))

    def experts_backward(layer, dout, dout_low, moe, kept_state):
        router = small[layer, :, :experts]
        own_router = lax.dynamic_slice_in_dim(router, owner * EXP_DEV, EXP_DEV, 1)
        outer = jnp.sum(dout * moe, axis=1)
        if kernels:
            block = with_lanes(dout_low, split_terms(outer[:, None]))
            rows_of_router = jnp.pad(own_router.T.astype(F32), ((0, 8 - EXP_DEV), (0, 0)))
            db, grad_gu, grad_down, grad_router = moe_backward(
                layer, block, rows_of_router, wgu, wd, *kept_state, experts, 3 + layer
            )
            grad_router = (grad_router[:, :EXP_DEV] + grad_router[:, EXP_DEV : 2 * EXP_DEV]).T
            return db, grad_gu, grad_down.reshape(EXP_DEV, FF, width), grad_router
        b_all, own_gates, kept, scaled = kept_state
        total = lax.all_gather(outer, "expert", axis=0, tiled=True)
        dout_all = lax.all_gather(dout_low, "expert", axis=0, tiled=True)
        dgus, dcs = [], []
        for j in range(EXP_DEV):
            gate = own_gates[:, j : j + 1]
            g, u = kept[j][:, :FF].astype(F32), kept[j][:, FF:].astype(F32)
            sig = jax.nn.sigmoid(g)
            silu = g * sig
            dz = dot(dout_all, wd[layer, j], ((1,), (1,)))
            dgate = jnp.sum(dz * silu * u, axis=1, keepdims=True)
            dcs.append(gate * (dgate - total[:, None]))
            dz = dz * gate
            dgus.append(
                jnp.concatenate(
                    [dz * u * sig * (1.0 + g * (1.0 - sig)), dz * silu], axis=1
                ).astype(BF16)
            )
        dc = jnp.concatenate(dcs, axis=1)
        db_part = sum(dot(dgus[j], wgu[layer, j], ((1,), (1,))) for j in range(EXP_DEV))
        for j in range(EXP_DEV):
            db_part = db_part + dc[:, j : j + 1] * own_router[:, j].astype(F32)[None, :]
        db = lax.psum_scatter(
            db_part.astype(BF16), "expert", scatter_dimension=0, tiled=True
        ).astype(F32)
        grad_down = dot(scaled, dout_all, ((0,), (0,))).reshape(EXP_DEV, FF, width)
        grad_gu = jnp.stack([dot(b_all, dgus[j], ((0,), (0,))) for j in range(EXP_DEV)])
        grad_router = lax.dot_general(
            dc, b_all.astype(F32), (((0,), (0,)), ((), ())), precision=lax.Precision.HIGHEST
        )
        return db, grad_gu, grad_down, grad_router

    def backward(layer, dout, dout_low, state):
        h, r1, a_half, p, heads_in, o, h1, r2, moe, kept_state = state
        gain_a = small[layer, :, experts].astype(F32)[None, :]
        gain_m = small[layer, :, experts + 1].astype(F32)[None, :]
        db, grad_gu, grad_down, grad_router = experts_backward(
            layer, dout, dout_low, moe, kept_state
        )
        normed = h1 * r2
        grad_gain_m = jnp.sum(db * normed, axis=0)
        scaled_db = db * gain_m
        dh1 = dout + r2 * (scaled_db - normed * jnp.mean(scaled_db * normed, axis=1, keepdims=True))
        dattn = lax.all_gather(dh1.astype(BF16), "shard", axis=0, tiled=True)
        do = dot(dattn, wo[layer], ((1,), (1,))).astype(BF16)
        grad_out = dot(o, dattn, ((0,), (0,)))
        dqkv = lax.all_gather(attention_backward(do, p, heads_in), "shard", axis=0, tiled=False)
        da = 0.0
        grad_qkv = []
        for part in range(3):
            grad_qkv.append([])
        for j in range(n_shard):
            at_local = 0
            for part, (at, size) in enumerate(column_parts(n_shard, j)):
                piece = dqkv[j, :, at_local : at_local + size]
                at_local += size
                da = da + dot(piece, wq[layer, :, at : at + size], ((1,), (1,)))
                grad_qkv[part].append(dot(a_half, piece, ((0,), (0,))))
        grad_qkv = jnp.concatenate([x for part in grad_qkv for x in part], axis=1)
        da = lax.all_to_all(
            da.astype(BF16), "shard", split_axis=0, concat_axis=1, tiled=True
        ).astype(F32)
        normed = h * r1
        grad_gain_a = jnp.sum(da * normed, axis=0)
        scaled_da = da * gain_a
        dh = dh1 + r1 * (scaled_da - normed * jnp.mean(scaled_da * normed, axis=1, keepdims=True))
        return dh, (grad_qkv, grad_out, grad_router, grad_gain_a, grad_gain_m, grad_gu, grad_down)

    out0, state0 = forward(0, x_in.astype(F32))
    mid = out0.astype(BF16).astype(F32)
    final, state1 = forward(1, mid)
    dh_one, grads1 = backward(1, dy.astype(F32), dy, state1)
    low = dh_one.astype(BF16)
    dh_zero, grads0 = backward(0, low.astype(F32), low, state0)

    def half_sum(grad):
        low_grad = grad.astype(BF16)
        halves = low_grad.reshape((2, -1) + low_grad.shape[1:])
        got = swap_cores(pick(halves, 1 - sec))
        return (pick(halves, sec).astype(F32) + got.astype(F32)).astype(BF16)

    def to_owner(half0, half1):
        keep = jnp.where(sec == 0, half0, half1)
        got = swap_cores(jnp.where(sec == 0, half1, half0))
        first = jnp.where(sec == 0, keep, got)
        second = jnp.where(sec == 0, got, keep)
        return jnp.concatenate([first, second], axis=0).astype(F32)

    def shard_sum(value):
        if n_shard != 2:
            return lax.psum(value, "shard")
        got = lax.ppermute(value, "shard", [(0, 1), (1, 0)])
        return (value.astype(F32) + got.astype(F32)).astype(BF16)

    def small_sum(grads):
        hot = jnp.arange(experts)[:, None] == owner * EXP_DEV + jnp.arange(EXP_DEV)[None, :]
        router = sum(
            jnp.where(hot[:, j : j + 1], grads[2][j][None, :], 0.0) for j in range(EXP_DEV)
        )
        tiny = jnp.concatenate([router, grads[3][None, :], grads[4][None, :]], axis=0)
        if n_shard != 2:
            tiny = lax.psum_scatter(tiny, "shard", scatter_dimension=1, tiled=True)
        else:
            mine = lax.dynamic_slice_in_dim(tiny, shard_pos * half, half, 1)
            others = lax.dynamic_slice_in_dim(tiny, (1 - shard_pos) * half, half, 1)
            tiny = mine + lax.ppermute(others, "shard", [(0, 1), (1, 0)])
        return tiny + swap_cores(tiny)

    columns_attn = w_qkv.shape[2] + w_out.shape[2]
    small_count = (experts + 2) * half
    small_rows = -(-small_count // columns_attn)

    def attn_sum(grads, before):
        attn = half_sum(jnp.concatenate([grads[0], grads[1]], axis=1))
        tiny = small_sum(grads).reshape(-1).astype(BF16)
        tiny = jnp.pad(tiny, (0, small_rows * columns_attn - small_count))
        joined = jnp.concatenate([attn, tiny.reshape(small_rows, columns_attn)], axis=0)
        if before is not None:
            joined, _ = lax.optimization_barrier((joined, before))
        return lax.psum(joined, "expert")

    sums1 = attn_sum(grads1, None)
    exp1 = tuple(shard_sum(half_sum(g)) for g in (grads1[5], grads1[6]))
    exp0 = tuple(shard_sum(half_sum(g)) for g in (grads0[5], grads0[6]))
    sums0 = attn_sum(grads0, sums1)
    attn_rows = half // 2
    attn = to_owner(sums0[:attn_rows], sums1[:attn_rows])
    grad_qkv, grad_out = attn[:, : w_qkv.shape[2]], attn[:, w_qkv.shape[2] :]
    grad_gu = to_owner(exp0[0], exp1[0])
    grad_down = to_owner(exp0[1], exp1[1])
    tiny = jnp.where(sec == 0, sums0[attn_rows:], sums1[attn_rows:]).astype(F32)
    tiny = tiny.reshape(-1)[:small_count].reshape(experts + 2, half)

    send = jnp.where(sec == 0, final, dh_zero)
    keep = jnp.where(sec == 0, dh_zero, final)
    got = swap_cores(send)
    edge = jnp.where(sec == 0, jnp.stack([keep, got]), jnp.stack([got, keep]))
    return (
        edge[None],
        grad_qkv[None],
        grad_out[None],
        tiny[:experts].T[None],
        tiny[experts][None],
        tiny[experts + 1][None],
        grad_gu[None],
        grad_down[None],
    )


def solution(mesh):
    in_specs = (
        P("section", None, ("expert", "shard"), None),
        P(None, "expert", None),
        P("section", None, ("expert", "shard"), None),
        P("section", "shard", None),
        P("section", "shard", None),
        P("section", "shard", None),
        P("section", "shard"),
        P("section", "shard"),
        P("section", "expert", None, None),
        P("section", "expert", None, None),
    )
    out_specs = (
        P("section", None, ("expert", "shard"), None),
        P("section", "shard", None),
        P("section", "shard", None),
        P("section", "shard", None),
        P("section", "shard"),
        P("section", "shard"),
        P("section", "expert", None, None),
        P("section", "expert", None, None),
    )
    return jax.shard_map(shards, mesh=mesh, in_specs=in_specs, out_specs=out_specs, check_vma=False)
```

```python
import functools

import jax
import jax.numpy as jnp
from jax import lax
from jax.experimental import pallas as pl
from jax.experimental.pallas import tpu as pltpu
from jax.sharding import PartitionSpec as P

QUERY_HEADS = 24
KEY_VALUE_HEADS = 8
HEAD_SIZE = 64
FF = 512
TOP = 8
EXP_DEV = 2
EPS = 1e-05
MASKED_SCORE = -1e30
QUERY_WIDTH = QUERY_HEADS * HEAD_SIZE
KV_WIDTH = KEY_VALUE_HEADS * HEAD_SIZE
F32 = jnp.float32
BF16 = jnp.bfloat16
MESH = pl.DeviceIdType.MESH
LINE = 4
SIDE = 2
LANES = 128
HALVES = 2
TILE = 256
VMEM_BYTES = 60 * 2**20


def chunk_order(z, t):
    near = z + 1 - 2 * lax.rem(z, 2)
    third = jnp.where(z < 2, 2, 1)
    last = jnp.where(z < 2, 3, 0)
    return jnp.where(t == 0, z, jnp.where(t == 1, near, jnp.where(t == 2, third, last)))


def sum_order(z, i):
    first = jnp.where((z == 0) | (z == 2), 1, 2)
    second = jnp.where(z == 0, 2, jnp.where(z == 1, 3, jnp.where(z == 2, 0, 1)))
    third = jnp.where(z == 0, 3, jnp.where(z == 1, 0, jnp.where(z == 2, 3, 0)))
    return jnp.where(i == 0, first, jnp.where(i == 1, second, third))


class Plane:
    def __init__(self, rows, refs):
        (self.gathered, self.parts, self.from_side, self.from_low, self.from_high, self.sums,
         self.line_send, self.gather_recv, self.side_send, self.side_recv,
         self.sum_send, self.low_recv, self.high_recv) = refs
        self.sub = rows // HALVES
        self.both = SIDE * self.sub
        self.sec, self.owner, self.shard = (lax.axis_index(n) for n in ("section", "expert", "shard"))
        self.z, self.x = lax.div(self.owner, SIDE), lax.rem(self.owner, SIDE)
        self.inner = ((self.z > 0) & (self.z < LINE - 1)).astype(jnp.int32)

    def device(self, z, x):
        return (self.sec, z * SIDE + x, self.shard)

    def chunk(self, c, h):
        return pl.ds(pl.multiple_of((c * HALVES + h) * self.both, self.both), self.both)

    def block(self, c, h, x):
        return pl.ds(pl.multiple_of((c * HALVES + h) * self.both + x * self.sub, self.sub), self.sub)

    def barrier(self):
        z, x = self.z, self.x
        sem = pltpu.get_barrier_semaphore()

        def greet(device):
            pl.semaphore_signal(sem, inc=1, device_id=device, device_id_type=MESH)

        greet(self.device(z, 1 - x))
        pl.when(z > 0)(lambda: greet(self.device(z - 1, x)))
        pl.when(z < LINE - 1)(lambda: greet(self.device(z + 1, x)))
        pl.semaphore_wait(sem, 2 + self.inner)

    def place(self, block_ref):
        for h in range(HALVES):
            self.gathered[self.block(self.z, h, self.x)] = block_ref[pl.ds(h * self.sub, self.sub)]

    def gather_copy(self, way, c, h, x, device):
        ref = self.gathered.at[self.block(c, h, x)]
        q = c * HALVES + h
        return pltpu.make_async_remote_copy(
            src_ref=ref, dst_ref=ref, send_sem=self.line_send.at[way, q],
            recv_sem=self.gather_recv.at[q, x], device_id=device, device_id_type=MESH)

    def forward_up(self, c, h):
        return self.gather_copy(0, c, h, self.x, self.device(self.z + 1, self.x))

    def forward_down(self, c, h):
        return self.gather_copy(1, c, h, self.x, self.device(self.z - 1, self.x))

    def forward_side(self, c, h):
        return self.gather_copy(2, c, h, self.x, self.device(self.z, 1 - self.x))

    def start_gather(self):
        z = self.z
        for h in range(HALVES):
            pl.when(z < LINE - 1)(lambda h=h: self.forward_up(z, h).start())
            pl.when(z > 0)(lambda h=h: self.forward_down(z, h).start())
            self.forward_side(z, h).start()

    def relay(self, t, h):
        z = self.z

        @pl.when((t > 0) & (z - t >= 0))
        def _():
            c = z - t
            self.forward_side(c, h).wait_recv()
            pl.when(z < LINE - 1)(lambda: self.forward_up(c, h).start())
            self.forward_side(c, h).start()

        @pl.when((t > 0) & (z + t <= LINE - 1))
        def _():
            c = z + t
            self.forward_side(c, h).wait_recv()
            pl.when(z > 0)(lambda: self.forward_down(c, h).start())
            self.forward_side(c, h).start()

    def wait_side_block(self, c, h):
        self.gather_copy(2, c, h, 1 - self.x, self.device(self.z, 1 - self.x)).wait_recv()

    def side_copy(self, c, h):
        q = c * HALVES + h
        return pltpu.make_async_remote_copy(
            src_ref=self.parts.at[self.block(c, h, 1 - self.x)], dst_ref=self.from_side.at[q],
            send_sem=self.side_send.at[q], recv_sem=self.side_recv.at[q],
            device_id=self.device(self.z, 1 - self.x), device_id_type=MESH)

    def up_copy(self, c, h):
        q = c * HALVES + h
        return pltpu.make_async_remote_copy(
            src_ref=self.sums.at[q], dst_ref=self.from_low.at[q], send_sem=self.sum_send.at[q],
            recv_sem=self.low_recv.at[q], device_id=self.device(self.z + 1, self.x), device_id_type=MESH)

    def down_copy(self, c, h):
        q = c * HALVES + h
        return pltpu.make_async_remote_copy(
            src_ref=self.sums.at[q], dst_ref=self.from_high.at[q], send_sem=self.sum_send.at[q],
            recv_sem=self.high_recv.at[q], device_id=self.device(self.z - 1, self.x), device_id_type=MESH)

    def own_part(self, c, h):
        return (self.parts[self.block(c, h, self.x)].astype(F32)
                + self.from_side[c * HALVES + h].astype(F32))

    def pass_sum(self, t, h):
        i = t - 3 - self.inner
        pl.when((i >= 0) & (i < LINE - 1))(lambda: self.pass_chunk(sum_order(self.z, i), h))

    def pass_chunk(self, c, h):
        z = self.z
        q = c * HALVES + h
        self.side_copy(c, h).wait_recv()

        @pl.when(c > z)
        def _():
            @pl.when(z > 0)
            def _():
                self.up_copy(c, h).wait_recv()
                self.sums[q] = (self.own_part(c, h) + self.from_low[q].astype(F32)).astype(BF16)

            @pl.when(z == 0)
            def _():
                self.sums[q] = self.own_part(c, h).astype(BF16)

            self.up_copy(c, h).start()

        @pl.when(c < z)
        def _():
            @pl.when(z < LINE - 1)
            def _():
                self.down_copy(c, h).wait_recv()
                self.sums[q] = (self.own_part(c, h) + self.from_high[q].astype(F32)).astype(BF16)

            @pl.when(z == LINE - 1)
            def _():
                self.sums[q] = self.own_part(c, h).astype(BF16)

            self.down_copy(c, h).start()

    def finish_sum(self, h, out_ref):
        z = self.z
        q = z * HALVES + h
        rows = pl.ds(pl.multiple_of(h * self.sub, self.sub), self.sub)
        self.side_copy(z, h).wait_recv()
        out_ref[rows] = self.own_part(z, h)

        @pl.when(z > 0)
        def _():
            self.up_copy(z, h).wait_recv()
            out_ref[rows] += self.from_low[q].astype(F32)

        @pl.when(z < LINE - 1)
        def _():
            self.down_copy(z, h).wait_recv()
            out_ref[rows] += self.from_high[q].astype(F32)

    def drain(self):
        z = self.z

        def one(q, carry):
            c, h = lax.div(q, HALVES), lax.rem(q, HALVES)
            pl.when((z < LINE - 1) & (c <= z))(lambda: self.forward_up(c, h).wait_send())
            pl.when((z > 0) & (c >= z))(lambda: self.forward_down(c, h).wait_send())
            self.forward_side(c, h).wait_send()
            self.side_copy(c, h).wait_send()
            pl.when(c > z)(lambda: self.up_copy(c, h).wait_send())
            pl.when(c < z)(lambda: self.down_copy(c, h).wait_send())
            return carry

        lax.fori_loop(0, LINE * HALVES, one, 0)


def plane_scratch(rows, width, wide):
    count = LINE * HALVES
    block = pltpu.VMEM((count, rows // HALVES, width), BF16)
    return [
        pltpu.VMEM((LINE * SIDE * rows, wide), BF16),
        pltpu.VMEM((LINE * SIDE * rows, width), BF16),
        block, block, block, block,
        pltpu.SemaphoreType.DMA((3, count)),
        pltpu.SemaphoreType.DMA((count, SIDE)),
        pltpu.SemaphoreType.DMA((count,)),
        pltpu.SemaphoreType.DMA((count,)),
        pltpu.SemaphoreType.DMA((count,)),
        pltpu.SemaphoreType.DMA((count,)),
        pltpu.SemaphoreType.DMA((count,)),
    ]


def lane_tile(at, size=TILE):
    return pl.ds(pl.multiple_of(at * size, size), size)


def nn(a, b):
    return jnp.dot(a, b, preferred_element_type=F32)


def nt(a, b):
    return lax.dot_general(a, b, (((1,), (1,)), ((), ())), preferred_element_type=F32)


def tn(a, b):
    return lax.dot_general(a, b, (((0,), (0,)), ((), ())), preferred_element_type=F32)


def pick_lane(block, wanted):
    lane = lax.broadcasted_iota(jnp.int32, block.shape, 1)
    hot = lane == wanted[0]
    for other in wanted[1:]:
        hot = hot | (lane == other)
    return jnp.sum(jnp.where(hot, block, 0.0), axis=1, keepdims=True)


def own_gates(block, owner, experts):
    block = block.astype(F32)
    return [
        pick_lane(block, (owner * EXP_DEV + j, experts + owner * EXP_DEV + j)) for j in range(EXP_DEV)
    ]


def load_layer(layer, sec, own, other, dst, sem):
    copies = [pltpu.make_async_copy(own, dst, sem), pltpu.make_async_copy(other, dst, sem)]
    pl.when(sec == layer)(lambda: copies[0].start())
    pl.when(sec != layer)(lambda: copies[1].start())
    return copies[0]


def load_experts(layer, sec, gu, gu_other, down, down_other, gu_v, down_v, sems):
    loads = [load_layer(layer, sec, gu, gu_other, gu_v, sems.at[0])]
    for j in range(EXP_DEV):
        loads.append(load_layer(
            layer, sec, down.at[j], down_other.at[j], down_v.at[pl.ds(j * FF, FF)], sems.at[1 + j]))
    return loads


def moe_forward_kernel(layer, experts, rows, width, block_ref, gu_hbm, gu_other, down_hbm, down_other,
                       moe_ref, rows_hbm, kept_hbm, scaled_hbm,
                       gu_v, down_v, kept, scaled, load_sem, store_sem, *plane_refs):
    plane = Plane(rows, plane_refs)
    gathered, parts = plane.gathered, plane.parts
    loads = load_experts(layer, plane.sec, gu_hbm, gu_other, down_hbm, down_other, gu_v, down_v, load_sem)
    plane.place(block_ref)
    plane.barrier()
    plane.start_gather()
    for load in loads:
        load.wait()

    def stores(c, h):
        q, at = c * HALVES + h, plane.chunk(c, h)
        return [
            pltpu.make_async_copy(gathered.at[at], rows_hbm.at[at], store_sem.at[0, q]),
            pltpu.make_async_copy(kept.at[at], kept_hbm.at[at], store_sem.at[1, q]),
            pltpu.make_async_copy(scaled.at[at], scaled_hbm.at[at], store_sem.at[2, q]),
        ]

    def step(k, carry):
        t, h = lax.div(k, HALVES), lax.rem(k, HALVES)
        plane.relay(t, h)
        plane.pass_sum(t, h)
        pl.when(t > 0)(lambda: work(chunk_order(plane.z, t - 1), h))
        return carry

    def work(c, h):
        at = plane.chunk(c, h)
        plane.wait_side_block(c, h)
        gates = own_gates(gathered[at, pl.ds(width, LANES)], plane.owner, experts)
        for j in range(EXP_DEV):
            for f in range(FF // TILE):
                data = gathered[at, pl.ds(0, width)]
                low, high = j * 2 * FF + f * TILE, j * 2 * FF + FF + f * TILE
                g = nn(data, gu_v[j, :, pl.ds(f * TILE, TILE)])
                u = nn(data, gu_v[j, :, pl.ds(FF + f * TILE, TILE)])
                z = g * jax.nn.sigmoid(g) * u * gates[j]
                scaled[at, pl.ds(j * FF + f * TILE, TILE)] = z.astype(BF16)
                kept[at, pl.ds(low, TILE)] = g.astype(BF16)
                kept[at, pl.ds(high, TILE)] = u.astype(BF16)
        for n in range(width // TILE):
            parts[at, pl.ds(n * TILE, TILE)] = nn(
                scaled[at, :], down_v[:, pl.ds(n * TILE, TILE)]).astype(BF16)
        plane.side_copy(c, h).start()
        for store in stores(c, h):
            store.start()

    lax.fori_loop(0, (LINE + 1) * HALVES, step, 0)

    def tail(k, carry):
        plane.pass_sum(lax.div(k, HALVES), lax.rem(k, HALVES))
        return carry

    lax.fori_loop((LINE + 1) * HALVES, (LINE + 3) * HALVES, tail, 0)

    def finish(h, carry):
        plane.finish_sum(h, moe_ref)
        return carry

    lax.fori_loop(0, HALVES, finish, 0)
    plane.drain()

    def stored(q, carry):
        for store in stores(lax.div(q, HALVES), lax.rem(q, HALVES)):
            store.wait()
        return carry

    lax.fori_loop(0, LINE * HALVES, stored, 0)


def moe_forward(layer, block, weights, experts, collective_id):
    rows, wide = block.shape
    width = wide - LANES
    total = LINE * SIDE * rows
    any_spec = pl.BlockSpec(memory_space=pl.ANY)
    vmem = pl.BlockSpec(memory_space=pltpu.VMEM)
    return pl.pallas_call(
        functools.partial(moe_forward_kernel, layer, experts, rows, width),
        name="moe_forward",
        out_shape=(
            jax.ShapeDtypeStruct((rows, width), F32),
            jax.ShapeDtypeStruct((total, wide), BF16),
            jax.ShapeDtypeStruct((total, EXP_DEV * 2 * FF), BF16),
            jax.ShapeDtypeStruct((total, EXP_DEV * FF), BF16),
        ),
        in_specs=[vmem] + [any_spec] * 4,
        out_specs=(vmem, any_spec, any_spec, any_spec),
        scratch_shapes=[
            pltpu.VMEM((EXP_DEV, width, 2 * FF), BF16),
            pltpu.VMEM((EXP_DEV * FF, width), BF16),
            pltpu.VMEM((total, EXP_DEV * 2 * FF), BF16),
            pltpu.VMEM((total, EXP_DEV * FF), BF16),
            pltpu.SemaphoreType.DMA((1 + EXP_DEV,)),
            pltpu.SemaphoreType.DMA((3, LINE * HALVES)),
        ] + plane_scratch(rows, width, wide),
        compiler_params=pltpu.CompilerParams(
            collective_id=collective_id, has_side_effects=True, vmem_limit_bytes=VMEM_BYTES),
    )(block, *weights)


def moe_backward_kernel(layer, experts, rows, width, block_ref, router_ref, gu_hbm, gu_other, down_hbm, down_other,
                        rows_hbm, kept_hbm, scaled_hbm, db_ref, grad_gu_hbm, grad_down_hbm, grad_router_ref,
                        gu_v, down_v, fwd_rows, kept, scaled, dgu, grad_gu, grad_down, load_sem, store_sem,
                        *plane_refs):
    plane = Plane(rows, plane_refs)
    gathered, parts = plane.gathered, plane.parts
    loads = load_experts(layer, plane.sec, gu_hbm, gu_other, down_hbm, down_other, gu_v, down_v, load_sem)
    loads.append(pltpu.make_async_copy(rows_hbm, fwd_rows, load_sem.at[3]))
    loads.append(pltpu.make_async_copy(kept_hbm, kept, load_sem.at[4]))
    loads.append(pltpu.make_async_copy(scaled_hbm, scaled, load_sem.at[5]))
    for load in loads[3:]:
        load.start()
    plane.place(block_ref)
    plane.barrier()
    plane.start_gather()
    for load in loads:
        load.wait()
    total = plane.both
    up_at = EXP_DEV * 2 * FF

    def step(k, carry):
        t, h = lax.div(k, HALVES), lax.rem(k, HALVES)
        plane.relay(t, h)
        plane.pass_sum(t, h)
        pl.when(t > 0)(lambda: work(chunk_order(plane.z, t - 1), h))
        return carry

    def work(c, h):
        at = plane.chunk(c, h)
        plane.wait_side_block(c, h)
        gates = own_gates(fwd_rows[at, pl.ds(width, LANES)], plane.owner, experts)
        outer = jnp.sum(gathered[at, pl.ds(width, LANES)].astype(F32), axis=1, keepdims=True)
        dcs = []
        for j in range(EXP_DEV):
            dgate = jnp.zeros((total, 1), F32)
            for f in range(FF // TILE):
                low, high = pl.ds(j * 2 * FF + f * TILE, TILE), pl.ds(j * 2 * FF + FF + f * TILE, TILE)
                dz = nt(gathered[at, pl.ds(0, width)], down_v[pl.ds(j * FF + f * TILE, TILE), :])
                g = kept[at, low].astype(F32)
                u = kept[at, high].astype(F32)
                sig = jax.nn.sigmoid(g)
                silu = g * sig
                dgate = dgate + jnp.sum(dz * silu * u, axis=1, keepdims=True)
                dz = dz * gates[j]
                dgu[at, low] = (dz * u * sig * (1.0 + g * (1.0 - sig))).astype(BF16)
                dgu[at, high] = (dz * silu).astype(BF16)
            dcs.append(gates[j] * (dgate - outer))
        lane = lax.broadcasted_iota(jnp.int32, (total, LANES), 1)
        extra = jnp.zeros((total, LANES), F32)
        for j in range(EXP_DEV):
            top = dcs[j].astype(BF16).astype(F32)
            extra = extra + jnp.where(lane == j, top, 0.0) + jnp.where(lane == EXP_DEV + j, dcs[j] - top, 0.0)
        dgu[at, pl.ds(up_at, LANES)] = extra.astype(BF16)
        for n in range(width // TILE):
            cols = pl.ds(n * TILE, TILE)
            acc = nt(dgu[at, pl.ds(0, 2 * FF)], gu_v[0, cols, :])
            for j in range(1, EXP_DEV):
                acc = acc + nt(dgu[at, pl.ds(j * 2 * FF, 2 * FF)], gu_v[j, cols, :])
            for j in range(EXP_DEV):
                acc = acc + dcs[j] * router_ref[pl.ds(j, 1), cols]
            parts[at, cols] = acc.astype(BF16)
        plane.side_copy(c, h).start()

    lax.fori_loop(0, (LINE + 1) * HALVES, step, 0)

    def store_gu(n):
        return [pltpu.make_async_copy(
            grad_gu.at[j, lane_tile(n)], grad_gu_hbm.at[j, lane_tile(n)], store_sem.at[j, n])
            for j in range(EXP_DEV)]

    def store_down(n):
        return pltpu.make_async_copy(
            grad_down.at[lane_tile(n)], grad_down_hbm.at[lane_tile(n)], store_sem.at[EXP_DEV, n])

    def grad_gu_rows(n):
        rows_t = fwd_rows[:, lane_tile(n)]
        for j in range(EXP_DEV):
            grad_gu[j, lane_tile(n), :] = tn(rows_t, dgu[:, pl.ds(j * 2 * FF, 2 * FF)]).astype(BF16)
        grad_router_ref[lane_tile(n), :] = tn(rows_t, dgu[:, pl.ds(up_at, LANES)])
        for store in store_gu(n):
            store.start()

    def grad_down_rows(n):
        grad_down[lane_tile(n), :] = tn(scaled[:, lane_tile(n)], gathered[:, pl.ds(0, width)]).astype(BF16)
        store_down(n).start()

    gu_steps, down_steps = width // TILE, EXP_DEV * FF // TILE
    slots = 2 * HALVES

    def tail(k, carry):
        pl.loop(lax.div(k * gu_steps, slots), lax.div((k + 1) * gu_steps, slots))(grad_gu_rows)
        plane.pass_sum(LINE + 1 + lax.div(k, HALVES), lax.rem(k, HALVES))
        return carry

    lax.fori_loop(0, slots, tail, 0)
    pl.loop(0, down_steps)(grad_down_rows)

    def finish(h, carry):
        plane.finish_sum(h, db_ref)
        return carry

    lax.fori_loop(0, HALVES, finish, 0)
    plane.drain()
    for n in range(gu_steps):
        for store in store_gu(n):
            store.wait()
    for n in range(down_steps):
        store_down(n).wait()


def moe_backward(layer, block, router, weights, kept, experts, collective_id):
    rows, wide = block.shape
    width = wide - LANES
    total = LINE * SIDE * rows
    any_spec = pl.BlockSpec(memory_space=pl.ANY)
    vmem = pl.BlockSpec(memory_space=pltpu.VMEM)
    return pl.pallas_call(
        functools.partial(moe_backward_kernel, layer, experts, rows, width),
        name="moe_backward",
        out_shape=(
            jax.ShapeDtypeStruct((rows, width), F32),
            jax.ShapeDtypeStruct((EXP_DEV, width, 2 * FF), BF16),
            jax.ShapeDtypeStruct((EXP_DEV * FF, width), BF16),
            jax.ShapeDtypeStruct((width, LANES), F32),
        ),
        in_specs=[vmem, vmem] + [any_spec] * 7,
        out_specs=(vmem, any_spec, any_spec, vmem),
        scratch_shapes=[
            pltpu.VMEM((EXP_DEV, width, 2 * FF), BF16),
            pltpu.VMEM((EXP_DEV * FF, width), BF16),
            pltpu.VMEM((total, wide), BF16),
            pltpu.VMEM((total, EXP_DEV * 2 * FF), BF16),
            pltpu.VMEM((total, EXP_DEV * FF), BF16),
            pltpu.VMEM((total, EXP_DEV * 2 * FF + LANES), BF16),
            pltpu.VMEM((EXP_DEV, width, 2 * FF), BF16),
            pltpu.VMEM((EXP_DEV * FF, width), BF16),
            pltpu.SemaphoreType.DMA((6,)),
            pltpu.SemaphoreType.DMA((1 + EXP_DEV, max(width, EXP_DEV * FF) // TILE)),
        ] + plane_scratch(rows, width, wide),
        compiler_params=pltpu.CompilerParams(
            collective_id=collective_id, has_side_effects=True, vmem_limit_bytes=VMEM_BYTES),
    )(block, router, *weights, *kept)


def split_terms(values):
    high = values.astype(BF16)
    return high, (values - high.astype(F32)).astype(BF16)


def with_lanes(block, columns):
    extra = jnp.concatenate(columns, axis=1)
    extra = jnp.pad(extra, ((0, 0), (0, LANES - extra.shape[1])))
    return jnp.concatenate([block, extra], axis=1)


PAIRS = 2
GROUP = QUERY_HEADS // KEY_VALUE_HEADS
SCALE = HEAD_SIZE ** (-0.5)


class Pair:
    def __init__(self):
        self.sec, self.owner, self.me = (lax.axis_index(n) for n in ("section", "expert", "shard"))
        self.peer = 1 - self.me

    def barrier(self):
        sem = pltpu.get_barrier_semaphore()
        pl.semaphore_signal(
            sem, inc=1, device_id=(self.sec, self.owner, self.peer), device_id_type=MESH)
        pl.semaphore_wait(sem, 1)

    def send(self, src, dst, send_sem, recv_sem):
        return pltpu.make_async_remote_copy(
            src_ref=src, dst_ref=dst, send_sem=send_sem, recv_sem=recv_sem,
            device_id=(self.sec, self.owner, self.peer), device_id_type=MESH)


def head_columns(shard):
    kv_pair = KEY_VALUE_HEADS // 2 // PAIRS * HEAD_SIZE
    q_pair = kv_pair * GROUP
    wide = q_pair + 2 * kv_pair
    spans = []
    for i in range(PAIRS):
        at = shard * PAIRS + i
        spans.append((at * q_pair, i * wide, q_pair))
        spans.append((QUERY_WIDTH + at * kv_pair, i * wide + q_pair, kv_pair))
        spans.append((QUERY_WIDTH + KV_WIDTH + at * kv_pair, i * wide + q_pair + kv_pair, kv_pair))
    return spans


def head_at(i, n, g):
    kv_pair = KEY_VALUE_HEADS // 2 // PAIRS * HEAD_SIZE
    q_pair = kv_pair * GROUP
    base = i * (q_pair + 2 * kv_pair)
    return (
        pl.ds(base + (n * GROUP + g) * HEAD_SIZE, HEAD_SIZE),
        pl.ds(base + q_pair + n * HEAD_SIZE, HEAD_SIZE),
        pl.ds(base + q_pair + kv_pair + n * HEAD_SIZE, HEAD_SIZE),
    )


KV_IN_PAIR = KEY_VALUE_HEADS // 2 // PAIRS


def load_attention(layer, sec, wq, wq_other, wo, wo_other, wq_v, wo_v, sems):
    loads = []
    for j in range(2):
        for at, local, size in head_columns(j):
            loads.append(load_layer(
                layer, sec, wq.at[:, pl.ds(at, size)], wq_other.at[:, pl.ds(at, size)],
                wq_v.at[j, :, pl.ds(local, size)], sems.at[len(loads)]))
    loads.append(load_layer(layer, sec, wo, wo_other, wo_v, sems.at[len(loads)]))
    return loads


LOADS = 2 * PAIRS * 3 + 1


def attention_forward_kernel(layer, rows, width, h_ref, allowed_ref, gains_ref, router_ref, mask_ref, wq, wq_other,
                             wo, wo_other, block_ref, h1_ref, a_ref, qkv_ref, p_ref, o_ref,
                             wq_v, wo_v, a_parts, a_half, part_send, got_part, out_send, got_out,
                             load_sem, send_sem, recv_sem):
    pair = Pair()
    me, peer = pair.me, pair.peer
    half = width // 2
    loads = load_attention(layer, pair.sec, wq, wq_other, wo, wo_other, wq_v, wo_v, load_sem)
    pair.barrier()

    def span(who):
        return pl.ds(pl.multiple_of(who * rows, rows), rows)

    h = h_ref[...].astype(F32)
    r1 = lax.rsqrt(jnp.mean(h * h, axis=1, keepdims=True) + EPS)
    a = (h * r1 * gains_ref[pl.ds(0, 1), :]).astype(BF16)
    for j in range(2):
        a_parts[j] = a[:, j * half : (j + 1) * half]
    send_a = pair.send(a_parts.at[peer], a_half.at[span(me)], send_sem.at[0], recv_sem.at[0])
    send_a.start()
    a_half[span(me)] = a_parts[me]
    for load in loads[:-1]:
        load.wait()
    part_send[span(me)] = nn(a_parts[me], wq_v[peer]).astype(BF16)
    send_own = pair.send(part_send.at[span(me)], got_part.at[span(me)], send_sem.at[1], recv_sem.at[1])
    send_own.start()
    send_a.wait_recv()
    part_send[span(peer)] = nn(a_half[span(peer)], wq_v[peer]).astype(BF16)
    send_other = pair.send(
        part_send.at[span(peer)], got_part.at[span(peer)], send_sem.at[2], recv_sem.at[2])
    send_other.start()
    mine = nn(a_half[...], wq_v[me])
    a_ref[...] = a_half[...]
    send_own.wait_recv()
    send_other.wait_recv()
    qkv_ref[...] = (mine + got_part[...].astype(F32)).astype(BF16)
    allowed = allowed_ref[...] > 0
    for i in range(PAIRS):
        for n in range(KV_IN_PAIR):
            for g in range(GROUP):
                q_at, k_at, v_at = head_at(i, n, g)
                j = (i * KV_IN_PAIR + n) * GROUP + g
                s = nt(qkv_ref[:, q_at], qkv_ref[:, k_at]) * SCALE
                s = jnp.where(allowed, s, MASKED_SCORE)
                ex = jnp.exp(s - jnp.max(s, axis=1, keepdims=True))
                p = (ex / jnp.sum(ex, axis=1, keepdims=True)).astype(BF16)
                p_ref[j] = p
                o_ref[:, pl.ds(j * HEAD_SIZE, HEAD_SIZE)] = nn(p, qkv_ref[:, v_at]).astype(BF16)
    loads[-1].wait()
    out_send[...] = nn(o_ref[span(peer)], wo_v[...]).astype(BF16)
    send_out = pair.send(out_send, got_out, send_sem.at[3], recv_sem.at[3])
    send_out.start()
    own = nn(o_ref[span(me)], wo_v[...])
    send_out.wait_recv()
    h1 = h + own + got_out[...].astype(F32)
    h1_ref[...] = h1
    r2 = lax.rsqrt(jnp.mean(h1 * h1, axis=1, keepdims=True) + EPS)
    b = (h1 * r2 * gains_ref[pl.ds(1, 1), :]).astype(BF16)
    block_ref[:, pl.ds(0, width)] = b
    mask = mask_ref[...] > 0
    logits = jnp.where(mask, nt(b, router_ref[...]), MASKED_SCORE)
    ex = jnp.where(mask, jnp.exp(logits - jnp.max(logits, axis=1, keepdims=True)), 0.0)
    gates = ex / (0.5 * jnp.sum(ex, axis=1, keepdims=True))
    high = gates.astype(BF16).astype(F32)
    block_ref[:, pl.ds(width, LANES)] = jnp.where(mask_ref[...] > 1, gates - high, high).astype(BF16)
    for send in (send_a, send_own, send_other, send_out):
        send.wait_send()


def attention_forward(layer, h, allowed, gains, router, mask, weights, collective_id):
    rows, width = h.shape
    half, group = width // 2, 2 * rows
    qkv = (QUERY_WIDTH + 2 * KV_WIDTH) // 2
    heads = QUERY_HEADS // 2
    any_spec = pl.BlockSpec(memory_space=pl.ANY)
    vmem = pl.BlockSpec(memory_space=pltpu.VMEM)
    return pl.pallas_call(
        functools.partial(attention_forward_kernel, layer, rows, width),
        name="attention_forward",
        out_shape=(
            jax.ShapeDtypeStruct((rows, width + LANES), BF16),
            jax.ShapeDtypeStruct((rows, width), F32),
            jax.ShapeDtypeStruct((group, half), BF16),
            jax.ShapeDtypeStruct((group, qkv), BF16),
            jax.ShapeDtypeStruct((heads, group, group), BF16),
            jax.ShapeDtypeStruct((group, QUERY_WIDTH // 2), BF16),
        ),
        in_specs=[vmem] * 5 + [any_spec] * 4,
        out_specs=(vmem,) * 6,
        scratch_shapes=[
            pltpu.VMEM((2, half, qkv), BF16),
            pltpu.VMEM((QUERY_WIDTH // 2, width), BF16),
            pltpu.VMEM((2, rows, half), BF16),
            pltpu.VMEM((group, half), BF16),
            pltpu.VMEM((group, qkv), BF16),
            pltpu.VMEM((group, qkv), BF16),
            pltpu.VMEM((rows, width), BF16),
            pltpu.VMEM((rows, width), BF16),
            pltpu.SemaphoreType.DMA((LOADS,)),
            pltpu.SemaphoreType.DMA((4,)),
            pltpu.SemaphoreType.DMA((4,)),
        ],
        compiler_params=pltpu.CompilerParams(
            collective_id=collective_id, has_side_effects=True, vmem_limit_bytes=VMEM_BYTES),
    )(h, allowed, gains, router, mask, *weights)


def attention_backward_kernel(layer, rows, width, db_ref, dout_ref, h1_ref, h_ref, gains_ref, a_ref, qkv_ref,
                              p_ref, o_ref, wq, wq_other, wo, wo_other, dh_ref, gain_grads_ref, grad_hbm,
                              wq_v, wo_v, d_all, do, dqkv, got_dqkv, da_send, got_da, dh1_v, grad_q, grad_o,
                              load_sem, store_sem, send_sem, recv_sem):
    pair = Pair()
    me, peer = pair.me, pair.peer
    half = width // 2
    qkv_cols = dqkv.shape[1]
    pair_cols = qkv_cols // PAIRS
    loads = load_attention(layer, pair.sec, wq, wq_other, wo, wo_other, wq_v, wo_v, load_sem)
    pair.barrier()

    def span(who):
        return pl.ds(pl.multiple_of(who * rows, rows), rows)

    h1 = h1_ref[...]
    r2 = lax.rsqrt(jnp.mean(h1 * h1, axis=1, keepdims=True) + EPS)
    normed = h1 * r2
    db = db_ref[...]
    scaled = db * gains_ref[pl.ds(1, 1), :]
    gain_grads_ref[...] = jnp.zeros_like(gain_grads_ref)
    gain_grads_ref[pl.ds(1, 1), :] = jnp.sum(db * normed, axis=0, keepdims=True)
    dh1 = dout_ref[...].astype(F32) + r2 * (
        scaled - normed * jnp.mean(scaled * normed, axis=1, keepdims=True))
    dh1_v[...] = dh1
    d_all[span(me)] = dh1.astype(BF16)
    send_d = pair.send(d_all.at[span(me)], d_all.at[span(me)], send_sem.at[0], recv_sem.at[0])
    send_d.start()
    for load in loads:
        load.wait()
    do[span(me)] = nt(d_all[span(me)], wo_v[...]).astype(BF16)
    send_d.wait_recv()
    do[span(peer)] = nt(d_all[span(peer)], wo_v[...]).astype(BF16)
    sends = [send_d]
    for i in range(PAIRS):
        cols = pl.ds(i * pair_cols, pair_cols)
        for n in range(KV_IN_PAIR):
            dk = dv = None
            for g in range(GROUP):
                q_at, k_at, v_at = head_at(i, n, g)
                j = (i * KV_IN_PAIR + n) * GROUP + g
                p_low = p_ref[j]
                p = p_low.astype(F32)
                d_head = do[:, pl.ds(j * HEAD_SIZE, HEAD_SIZE)]
                weighted = p * nt(d_head, qkv_ref[:, v_at])
                ds = (weighted - p * jnp.sum(weighted, axis=1, keepdims=True)).astype(BF16)
                dqkv[:, q_at] = (nn(ds, qkv_ref[:, k_at]) * SCALE).astype(BF16)
                dk_part, dv_part = tn(ds, qkv_ref[:, q_at]), tn(p_low, d_head)
                dk = dk_part if dk is None else dk + dk_part
                dv = dv_part if dv is None else dv + dv_part
            dqkv[:, k_at] = (dk * SCALE).astype(BF16)
            dqkv[:, v_at] = dv.astype(BF16)
        send = pair.send(dqkv.at[:, cols], got_dqkv.at[:, cols], send_sem.at[1 + i], recv_sem.at[1 + i])
        send.start()
        sends.append(send)
    da = nt(dqkv[...], wq_v[me])
    grad_q[me] = tn(a_ref[...], dqkv[...]).astype(BF16)
    grad_o[...] = tn(o_ref[...], d_all[...]).astype(BF16)
    store_o = pltpu.make_async_copy(
        grad_o, grad_hbm.at[:, pl.ds(QUERY_WIDTH + 2 * KV_WIDTH, width)], store_sem.at[LOADS - 1])
    store_o.start()
    for send in sends[1:]:
        send.wait_recv()
    da = da + nt(got_dqkv[...], wq_v[peer])
    da_send[...] = jnp.where(me == 0, da[rows:], da[:rows]).astype(BF16)
    send_da = pair.send(da_send, got_da, send_sem.at[1 + PAIRS], recv_sem.at[1 + PAIRS])
    send_da.start()
    own_da = jnp.where(me == 0, da[:rows], da[rows:])
    grad_q[peer] = tn(a_ref[...], got_dqkv[...]).astype(BF16)
    stores = [store_o]
    for j in range(2):
        for at, local, size in head_columns(j):
            store = pltpu.make_async_copy(
                grad_q.at[j, :, pl.ds(local, size)], grad_hbm.at[:, pl.ds(at, size)],
                store_sem.at[len(stores) - 1])
            store.start()
            stores.append(store)
    send_da.wait_recv()
    other_da = got_da[...].astype(F32)
    h = h_ref[...].astype(F32)
    r1 = lax.rsqrt(jnp.mean(h * h, axis=1, keepdims=True) + EPS)
    halves = []
    total = jnp.zeros((rows, 1), F32)
    for j in range(2):
        cols = pl.ds(j * half, half)
        da_j = jnp.where(me == j, own_da, other_da)
        normed = h[:, j * half : (j + 1) * half] * r1
        gain_grads_ref[pl.ds(0, 1), cols] = jnp.sum(da_j * normed, axis=0, keepdims=True)
        scaled = da_j * gains_ref[pl.ds(0, 1), cols]
        total = total + jnp.sum(scaled * normed, axis=1, keepdims=True)
        halves.append((cols, scaled, normed))
    for cols, scaled, normed in halves:
        dh_ref[:, cols] = dh1_v[:, cols] + r1 * (scaled - normed * (total / width))
    for send in sends + [send_da]:
        send.wait_send()
    for store in stores:
        store.wait()


def attention_backward(layer, db, dout, h1, h, gains, a_half, qkv, p, o, weights, collective_id):
    rows, width = db.shape
    half, group = width // 2, 2 * rows
    cols = (QUERY_WIDTH + 2 * KV_WIDTH) // 2
    any_spec = pl.BlockSpec(memory_space=pl.ANY)
    vmem = pl.BlockSpec(memory_space=pltpu.VMEM)
    return pl.pallas_call(
        functools.partial(attention_backward_kernel, layer, rows, width),
        name="attention_backward",
        out_shape=(
            jax.ShapeDtypeStruct((rows, width), F32),
            jax.ShapeDtypeStruct((8, width), F32),
            jax.ShapeDtypeStruct((half, QUERY_WIDTH + 2 * KV_WIDTH + width), BF16),
        ),
        in_specs=[vmem] * 9 + [any_spec] * 4,
        out_specs=(vmem, vmem, any_spec),
        scratch_shapes=[
            pltpu.VMEM((2, half, cols), BF16),
            pltpu.VMEM((QUERY_WIDTH // 2, width), BF16),
            pltpu.VMEM((group, width), BF16),
            pltpu.VMEM((group, QUERY_WIDTH // 2), BF16),
            pltpu.VMEM((group, cols), BF16),
            pltpu.VMEM((group, cols), BF16),
            pltpu.VMEM((rows, half), BF16),
            pltpu.VMEM((rows, half), BF16),
            pltpu.VMEM((rows, width), F32),
            pltpu.VMEM((2, half, cols), BF16),
            pltpu.VMEM((QUERY_WIDTH // 2, width), BF16),
            pltpu.SemaphoreType.DMA((LOADS,)),
            pltpu.SemaphoreType.DMA((LOADS,)),
            pltpu.SemaphoreType.DMA((2 + PAIRS,)),
            pltpu.SemaphoreType.DMA((2 + PAIRS,)),
        ],
        compiler_params=pltpu.CompilerParams(
            collective_id=collective_id, has_side_effects=True, vmem_limit_bytes=VMEM_BYTES),
    )(db, dout, h1, h, gains, a_half, qkv, p, o, *weights)


def dot(a, b, dims):
    return lax.dot_general(a, b, (dims, ((), ())), preferred_element_type=F32)


def rms_scale(values):
    return lax.rsqrt(jnp.mean(values * values, axis=-1, keepdims=True) + EPS)


def swap_cores(value):
    return lax.ppermute(value, "section", [(0, 1), (1, 0)])


def both_layers(own):
    return lax.all_gather(own, "section", axis=0, tiled=False)


def document_mask(sequence_lengths, rows):
    pos = jnp.arange(rows, dtype=jnp.int32)
    ends = jnp.cumsum(sequence_lengths)
    doc = jnp.sum((pos[:, None] >= ends[None, :]).astype(jnp.int32), axis=1)
    return (doc[:, None] == doc[None, :]) & (pos[None, :] <= pos[:, None])


def plain_attention(qkv, allowed, heads, kv_heads):
    rows = qkv.shape[0]
    group = heads // kv_heads
    q = qkv[:, : heads * HEAD_SIZE].reshape(rows, kv_heads, group, HEAD_SIZE)
    k = qkv[:, heads * HEAD_SIZE : (heads + kv_heads) * HEAD_SIZE].reshape(rows, kv_heads, HEAD_SIZE)
    v = qkv[:, (heads + kv_heads) * HEAD_SIZE :].reshape(rows, kv_heads, HEAD_SIZE)
    s = jnp.einsum("qhgd,khd->hgqk", q, k, preferred_element_type=F32) * HEAD_SIZE ** (-0.5)
    s = jnp.where(allowed[None, None], s, MASKED_SCORE)
    ex = jnp.exp(s - jnp.max(s, axis=-1, keepdims=True))
    p = ex / jnp.sum(ex, axis=-1, keepdims=True)
    o = jnp.einsum("hgqk,khd->qhgd", p.astype(BF16), v, preferred_element_type=F32)
    return o.reshape(rows, heads * HEAD_SIZE).astype(BF16), p, (q, k, v)


def plain_attention_backward(do, p, heads_in):
    q, k, v = heads_in
    rows = q.shape[0]
    dh = do.reshape(q.shape)
    dv = jnp.einsum("hgqk,qhgd->khd", p.astype(BF16), dh, preferred_element_type=F32)
    dp = jnp.einsum("qhgd,khd->hgqk", dh, v, preferred_element_type=F32)
    ds = (p * (dp - jnp.sum(p * dp, axis=-1, keepdims=True))).astype(BF16)
    dq = jnp.einsum("hgqk,khd->qhgd", ds, k, preferred_element_type=F32) * HEAD_SIZE ** (-0.5)
    dk = jnp.einsum("hgqk,qhgd->khd", ds, q, preferred_element_type=F32) * HEAD_SIZE ** (-0.5)
    return jnp.concatenate(
        [dq.reshape(rows, -1), dk.reshape(rows, -1), dv.reshape(rows, -1)], axis=1
    ).astype(BF16)


def column_parts(n, j):
    qw, kw = QUERY_WIDTH // n, KV_WIDTH // n
    return (
        (j * qw, qw),
        (QUERY_WIDTH + j * kw, kw),
        (QUERY_WIDTH + KV_WIDTH + j * kw, kw),
    )


def plain_shards(
    edge_inputs, seq_lengths, routes, w_qkv, w_out, w_router, gain_attn, gain_moe, w_gate_up, w_down
):
    sec = lax.axis_index("section")
    owner = lax.axis_index("expert")
    shard_pos = lax.axis_index("shard")
    n_shard = lax.axis_size("shard")
    n_owner = lax.axis_size("expert")
    rows, width = edge_inputs.shape[2], edge_inputs.shape[3]
    experts = w_router.shape[2]
    group_rows = rows * n_shard
    half = width // n_shard
    heads, kv_heads = QUERY_HEADS // n_shard, KEY_VALUE_HEADS // n_shard

    def pick(array, index):
        return lax.dynamic_index_in_dim(array, index, 0, keepdims=False)

    own_edge, other_edge = pick(edge_inputs[0], sec), swap_cores(pick(edge_inputs[0], 1 - sec))
    x_in = jnp.where(sec == 0, own_edge, other_edge)
    dy = jnp.where(sec == 0, other_edge, own_edge)
    own_routes, other_routes = pick(routes[0], sec), swap_cores(pick(routes[0], 1 - sec))
    layer_routes = (
        jnp.where(sec == 0, own_routes, other_routes),
        jnp.where(sec == 0, other_routes, own_routes),
    )
    allowed = document_mask(pick(seq_lengths, sec)[0], group_rows)
    wq = both_layers(w_qkv[0])
    wo = both_layers(w_out[0])
    small = jnp.concatenate([w_router[0], gain_attn[0][:, None], gain_moe[0][:, None]], axis=1)
    small = lax.all_gather(both_layers(small), "shard", axis=1, tiled=True)
    wgu = both_layers(w_gate_up[0])
    wd = both_layers(w_down[0])
    columns = jnp.arange(experts, dtype=jnp.int32)
    route_masks = [
        jnp.any(r[:, :, None] == columns[None, None, :], axis=1).astype(BF16) for r in layer_routes
    ]
    plane_masks = [lax.all_gather(m, "expert", axis=0, tiled=True) for m in route_masks]

    def forward(layer, h):
        gain_a = small[layer, :, experts].astype(F32)[None, :]
        gain_m = small[layer, :, experts + 1].astype(F32)[None, :]
        router = small[layer, :, :experts]
        r1 = rms_scale(h)
        a = (h * r1 * gain_a).astype(BF16)
        a_half = lax.all_to_all(
            a.reshape(rows, n_shard, half), "shard", split_axis=1, concat_axis=0, tiled=True
        ).reshape(group_rows, half)
        blocks = []
        for j in range(n_shard):
            blocks.append(
                jnp.concatenate(
                    [
                        dot(a_half, wq[layer, :, at : at + size], ((1,), (0,)))
                        for at, size in column_parts(n_shard, j)
                    ],
                    axis=1,
                ).astype(BF16)
            )
        qkv = lax.psum_scatter(jnp.stack(blocks), "shard", scatter_dimension=0, tiled=False)
        o, p, heads_in = plain_attention(qkv, allowed, heads, kv_heads)
        part = dot(o, wo[layer], ((1,), (0,))).astype(BF16)
        h1 = h + lax.psum_scatter(part, "shard", scatter_dimension=0, tiled=True).astype(F32)
        r2 = rms_scale(h1)
        b = (h1 * r2 * gain_m).astype(BF16)
        b_all = lax.all_gather(b, "expert", axis=0, tiled=True)
        mask = plane_masks[layer].astype(F32) > 0
        logits = jnp.where(mask, dot(b_all, router, ((1,), (0,))), MASKED_SCORE)
        ex = jnp.where(mask, jnp.exp(logits - jnp.max(logits, axis=1, keepdims=True)), 0.0)
        gates = ex / jnp.sum(ex, axis=1, keepdims=True)
        own_gates = lax.dynamic_slice_in_dim(gates, owner * EXP_DEV, EXP_DEV, 1)
        kept, scaled = [], []
        for j in range(EXP_DEV):
            gu = dot(b_all, wgu[layer, j], ((1,), (0,)))
            g, u = gu[:, :FF], gu[:, FF:]
            scaled.append((g * jax.nn.sigmoid(g) * u * own_gates[:, j : j + 1]).astype(BF16))
            kept.append(gu.astype(BF16))
        scaled = jnp.concatenate(scaled, axis=1)
        moe_part = dot(scaled, wd[layer].reshape(EXP_DEV * FF, width), ((1,), (0,))).astype(BF16)
        moe = lax.psum_scatter(moe_part, "expert", scatter_dimension=0, tiled=True).astype(F32)
        state = (h, r1, a_half, p, heads_in, o, h1, r2, b_all, own_gates, kept, scaled, moe)
        return h1 + moe, state

    def backward(layer, dout, dout_low, state):
        h, r1, a_half, p, heads_in, o, h1, r2, b_all, own_gates, kept, scaled, moe = state
        gain_a = small[layer, :, experts].astype(F32)[None, :]
        gain_m = small[layer, :, experts + 1].astype(F32)[None, :]
        router = small[layer, :, :experts]
        own_router = lax.dynamic_slice_in_dim(router, owner * EXP_DEV, EXP_DEV, 1)
        total = lax.all_gather(jnp.sum(dout * moe, axis=1), "expert", axis=0, tiled=True)
        dout_all = lax.all_gather(dout_low, "expert", axis=0, tiled=True)
        dgus, dcs = [], []
        for j in range(EXP_DEV):
            gate = own_gates[:, j : j + 1]
            g, u = kept[j][:, :FF].astype(F32), kept[j][:, FF:].astype(F32)
            sig = jax.nn.sigmoid(g)
            silu = g * sig
            dz = dot(dout_all, wd[layer, j], ((1,), (1,)))
            dgate = jnp.sum(dz * silu * u, axis=1, keepdims=True)
            dcs.append(gate * (dgate - total[:, None]))
            dz = dz * gate
            dgus.append(
                jnp.concatenate(
                    [dz * u * sig * (1.0 + g * (1.0 - sig)), dz * silu], axis=1
                ).astype(BF16)
            )
        dc = jnp.concatenate(dcs, axis=1)
        db_part = sum(dot(dgus[j], wgu[layer, j], ((1,), (1,))) for j in range(EXP_DEV))
        for j in range(EXP_DEV):
            db_part = db_part + dc[:, j : j + 1] * own_router[:, j].astype(F32)[None, :]
        db = lax.psum_scatter(
            db_part.astype(BF16), "expert", scatter_dimension=0, tiled=True
        ).astype(F32)
        grad_down = dot(scaled, dout_all, ((0,), (0,))).reshape(EXP_DEV, FF, width)
        grad_gu = jnp.stack([dot(b_all, dgus[j], ((0,), (0,))) for j in range(EXP_DEV)])
        grad_router = lax.dot_general(
            dc, b_all.astype(F32), (((0,), (0,)), ((), ())), precision=lax.Precision.HIGHEST
        )
        normed = h1 * r2
        grad_gain_m = jnp.sum(db * normed, axis=0)
        scaled_db = db * gain_m
        dh1 = dout + r2 * (scaled_db - normed * jnp.mean(scaled_db * normed, axis=1, keepdims=True))
        dattn = lax.all_gather(dh1.astype(BF16), "shard", axis=0, tiled=True)
        do = dot(dattn, wo[layer], ((1,), (1,))).astype(BF16)
        grad_out = dot(o, dattn, ((0,), (0,)))
        dqkv = lax.all_gather(plain_attention_backward(do, p, heads_in), "shard", axis=0, tiled=False)
        da = 0.0
        grad_qkv = []
        for part in range(3):
            grad_qkv.append([])
        for j in range(n_shard):
            at_local = 0
            for part, (at, size) in enumerate(column_parts(n_shard, j)):
                piece = dqkv[j, :, at_local : at_local + size]
                at_local += size
                da = da + dot(piece, wq[layer, :, at : at + size], ((1,), (1,)))
                grad_qkv[part].append(dot(a_half, piece, ((0,), (0,))))
        grad_qkv = jnp.concatenate([x for part in grad_qkv for x in part], axis=1)
        da = lax.all_to_all(
            da.astype(BF16), "shard", split_axis=0, concat_axis=1, tiled=True
        ).astype(F32)
        normed = h * r1
        grad_gain_a = jnp.sum(da * normed, axis=0)
        scaled_da = da * gain_a
        dh = dh1 + r1 * (scaled_da - normed * jnp.mean(scaled_da * normed, axis=1, keepdims=True))
        return dh, (grad_qkv, grad_out, grad_router, grad_gain_a, grad_gain_m, grad_gu, grad_down)

    out0, state0 = forward(0, x_in.astype(F32))
    mid = out0.astype(BF16).astype(F32)
    final, state1 = forward(1, mid)
    dh_one, grads1 = backward(1, dy.astype(F32), dy, state1)
    low = dh_one.astype(BF16)
    dh_zero, grads0 = backward(0, low.astype(F32), low, state0)

    def half_sum(grad):
        low_grad = grad.astype(BF16)
        halves = low_grad.reshape((2, -1) + low_grad.shape[1:])
        got = swap_cores(pick(halves, 1 - sec))
        return (pick(halves, sec).astype(F32) + got.astype(F32)).astype(BF16)

    def to_owner(half0, half1):
        keep = jnp.where(sec == 0, half0, half1)
        got = swap_cores(jnp.where(sec == 0, half1, half0))
        first = jnp.where(sec == 0, keep, got)
        second = jnp.where(sec == 0, got, keep)
        return jnp.concatenate([first, second], axis=0).astype(F32)

    attn_halves, exp_halves = [], []
    for grads in (grads0, grads1):
        attn = half_sum(jnp.concatenate([grads[0], grads[1]], axis=1))
        attn_halves.append(lax.psum(attn, "expert"))
        exp_halves.append(tuple(lax.psum(half_sum(g), "shard") for g in (grads[5], grads[6])))
    attn = to_owner(*attn_halves)
    grad_qkv, grad_out = attn[:, : w_qkv.shape[2]], attn[:, w_qkv.shape[2] :]
    grad_gu = to_owner(exp_halves[0][0], exp_halves[1][0])
    grad_down = to_owner(exp_halves[0][1], exp_halves[1][1])

    tiny = []
    for grads in (grads0, grads1):
        hot = jnp.arange(experts)[:, None] == owner * EXP_DEV + jnp.arange(EXP_DEV)[None, :]
        router = sum(
            jnp.where(hot[:, j : j + 1], grads[2][j][None, :], 0.0) for j in range(EXP_DEV)
        )
        tiny.append(jnp.concatenate([router, grads[3][None, :], grads[4][None, :]], axis=0))
    tiny = lax.psum(jnp.stack(tiny), ("section", "expert", "shard"))
    tiny = lax.dynamic_slice_in_dim(pick(tiny, sec), shard_pos * half, half, 1)

    send = jnp.where(sec == 0, final, dh_zero)
    keep = jnp.where(sec == 0, dh_zero, final)
    got = swap_cores(send)
    edge = jnp.where(sec == 0, jnp.stack([keep, got]), jnp.stack([got, keep]))
    return (
        edge[None],
        grad_qkv[None],
        grad_out[None],
        tiny[:experts].T[None],
        tiny[experts][None],
        tiny[experts + 1][None],
        grad_gu[None],
        grad_down[None],
    )


def kernel_shards(
    edge_inputs, seq_lengths, routes, w_qkv, w_out, w_router, gain_attn, gain_moe, w_gate_up, w_down
):
    sec = lax.axis_index("section")
    owner = lax.axis_index("expert")
    shard_pos = lax.axis_index("shard")
    rows, width = edge_inputs.shape[2], edge_inputs.shape[3]
    experts = w_router.shape[2]
    half = width // 2
    attn_cols = w_qkv.shape[2] + w_out.shape[2]

    def pick(array, index):
        return lax.dynamic_index_in_dim(array, index, 0, keepdims=False)

    def swap_shards(value):
        return lax.ppermute(value, "shard", [(0, 1), (1, 0)])

    def by_core(own, other):
        return jnp.where(sec == 0, own, other), jnp.where(sec == 0, other, own)

    small = jnp.concatenate([w_router[0].T, gain_attn, gain_moe], axis=0)
    own_small = jnp.concatenate([small, swap_shards(small)], axis=0)
    own_small = jnp.where(
        shard_pos == 0,
        jnp.concatenate([own_small[: experts + 2], own_small[experts + 2 :]], axis=1),
        jnp.concatenate([own_small[experts + 2 :], own_small[: experts + 2]], axis=1),
    )
    layer_small = by_core(own_small, swap_cores(own_small))
    x_in, dy = by_core(pick(edge_inputs[0], sec), swap_cores(pick(edge_inputs[0], 1 - sec)))
    layer_routes = by_core(pick(routes[0], sec), swap_cores(pick(routes[0], 1 - sec)))
    allowed = document_mask(pick(seq_lengths, sec)[0], 2 * rows).astype(F32)
    attn_weights = (w_qkv[0], swap_cores(w_qkv[0]), w_out[0], swap_cores(w_out[0]))
    expert_weights = (
        w_gate_up[0], swap_cores(w_gate_up[0]), w_down[0], swap_cores(w_down[0])
    )
    gains, routers, masks = [], [], []
    for layer in range(2):
        gains.append(
            jnp.pad(layer_small[layer][experts:].astype(F32), ((0, 8 - 2), (0, 0)))
        )
        router = layer_small[layer][:experts]
        router = jnp.concatenate([router, router], axis=0)
        routers.append(jnp.pad(router, ((0, LANES - 2 * experts), (0, 0))))
        lane = jnp.arange(LANES, dtype=jnp.int32)[None, :]
        hot = jnp.any(layer_routes[layer][:, :, None] == lane[None] % experts, axis=1)
        masks.append(
            jnp.where(hot & (lane < 2 * experts), 1.0 + (lane >= experts), 0.0).astype(F32)
        )

    def forward(layer, h):
        block, h1, *attn_state = attention_forward(
            layer, h, allowed, gains[layer], routers[layer], masks[layer], attn_weights, 1 + layer
        )
        moe, *expert_state = moe_forward(layer, block, expert_weights, experts, 3 + layer)
        return h1 + moe, (h, h1, moe, attn_state, expert_state)

    def backward(layer, dout, state):
        h, h1, moe, attn_state, expert_state = state
        outer = jnp.sum(dout.astype(F32) * moe, axis=1, keepdims=True)
        block = with_lanes(dout, split_terms(outer))
        own_router = lax.dynamic_slice_in_dim(
            layer_small[layer].astype(F32), owner * EXP_DEV, EXP_DEV, 0
        )
        own_router = jnp.pad(own_router, ((0, 8 - EXP_DEV), (0, 0)))
        db, grad_gu, grad_down, grad_router = moe_backward(
            layer, block, own_router, expert_weights, expert_state, experts, 5 + layer
        )
        grad_router = (grad_router[:, :EXP_DEV] + grad_router[:, EXP_DEV : 2 * EXP_DEV]).T
        dh, grad_gains, grad_attn = attention_backward(
            layer, db, dout, h1, h, gains[layer], *attn_state, attn_weights, 7 + layer
        )
        return dh, grad_attn, grad_router, grad_gains, grad_gu, grad_down.reshape(EXP_DEV, FF, width)

    out0, state0 = forward(0, x_in)
    final, state1 = forward(1, out0.astype(BF16))
    dh_one, *grads1 = backward(1, dy, state1)
    dh_zero, *grads0 = backward(0, dh_one.astype(BF16), state0)

    def half_sum(grad):
        halves = grad.reshape((2, -1) + grad.shape[1:])
        got = swap_cores(pick(halves, 1 - sec))
        return (pick(halves, sec).astype(F32) + got.astype(F32)).astype(BF16)

    def to_owner(half0, half1):
        keep = jnp.where(sec == 0, half0, half1)
        got = swap_cores(jnp.where(sec == 0, half1, half0))
        first = jnp.where(sec == 0, keep, got)
        second = jnp.where(sec == 0, got, keep)
        return jnp.concatenate([first, second], axis=0).astype(F32)

    def shard_sum(value):
        return (value.astype(F32) + swap_shards(value).astype(F32)).astype(BF16)

    def small_sum(grad_router, grad_gains):
        hot = jnp.arange(experts)[:, None] == owner * EXP_DEV + jnp.arange(EXP_DEV)[None, :]
        router = sum(
            jnp.where(hot[:, j : j + 1], grad_router[j][None, :], 0.0) for j in range(EXP_DEV)
        )
        tiny = jnp.concatenate([router, grad_gains[:2]], axis=0)
        mine = lax.dynamic_slice_in_dim(tiny, shard_pos * half, half, 1)
        others = lax.dynamic_slice_in_dim(tiny, (1 - shard_pos) * half, half, 1)
        tiny = mine + swap_shards(others)
        return tiny + swap_cores(tiny)

    small_count = (experts + 2) * half
    small_rows = -(-small_count // attn_cols)

    def attn_sum(grads, before):
        tiny = small_sum(grads[1], grads[2]).reshape(-1).astype(BF16)
        tiny = jnp.pad(tiny, (0, small_rows * attn_cols - small_count))
        joined = jnp.concatenate([half_sum(grads[0]), tiny.reshape(small_rows, attn_cols)], axis=0)
        if before is not None:
            joined, _ = lax.optimization_barrier((joined, before))
        return lax.psum(joined, "expert")

    sums1 = attn_sum(grads1, None)
    exp1 = tuple(shard_sum(half_sum(g)) for g in grads1[3:])
    exp0 = tuple(shard_sum(half_sum(g)) for g in grads0[3:])
    sums0 = attn_sum(grads0, sums1)
    attn_rows = half // 2
    attn = to_owner(sums0[:attn_rows], sums1[:attn_rows])
    grad_qkv, grad_out = attn[:, : w_qkv.shape[2]], attn[:, w_qkv.shape[2] :]
    grad_gu = to_owner(exp0[0], exp1[0])
    grad_down = to_owner(exp0[1], exp1[1])
    tiny = jnp.where(sec == 0, sums0[attn_rows:], sums1[attn_rows:]).astype(F32)
    tiny = tiny.reshape(-1)[:small_count].reshape(experts + 2, half)

    send = jnp.where(sec == 0, final, dh_zero)
    keep = jnp.where(sec == 0, dh_zero, final)
    got = swap_cores(send)
    edge = jnp.where(sec == 0, jnp.stack([keep, got]), jnp.stack([got, keep]))
    return (
        edge[None],
        grad_qkv[None],
        grad_out[None],
        tiny[:experts].T[None],
        tiny[experts][None],
        tiny[experts + 1][None],
        grad_gu[None],
        grad_down[None],
    )


def shards(*arrays):
    if lax.axis_size("expert") == LINE * SIDE and lax.axis_size("shard") == 2:
        return kernel_shards(*arrays)
    return plain_shards(*arrays)


def solution(mesh):
    in_specs = (
        P("section", None, ("expert", "shard"), None),
        P(None, "expert", None),
        P("section", None, ("expert", "shard"), None),
        P("section", "shard", None),
        P("section", "shard", None),
        P("section", "shard", None),
        P("section", "shard"),
        P("section", "shard"),
        P("section", "expert", None, None),
        P("section", "expert", None, None),
    )
    out_specs = (
        P("section", None, ("expert", "shard"), None),
        P("section", "shard", None),
        P("section", "shard", None),
        P("section", "shard", None),
        P("section", "shard"),
        P("section", "shard"),
        P("section", "expert", None, None),
        P("section", "expert", None, None),
    )
    return jax.shard_map(shards, mesh=mesh, in_specs=in_specs, out_specs=out_specs, check_vma=False)
```

```python
import functools

import jax
import jax.numpy as jnp
from jax import lax
from jax.experimental import pallas as pl
from jax.experimental.pallas import tpu as pltpu
from jax.sharding import PartitionSpec as P

QUERY_HEADS = 24
KEY_VALUE_HEADS = 8
HEAD_SIZE = 64
FF = 512
TOP = 8
EXP_DEV = 2
EPS = 1e-05
MASKED_SCORE = -1e30
QUERY_WIDTH = QUERY_HEADS * HEAD_SIZE
KV_WIDTH = KEY_VALUE_HEADS * HEAD_SIZE
F32 = jnp.float32
BF16 = jnp.bfloat16
MESH = pl.DeviceIdType.MESH
LINE = 4
SIDE = 2
LANES = 128
HALVES = 2
TILE = 256
VMEM_BYTES = 60 * 2**20
COST = pl.CostEstimate(flops=10**11, bytes_accessed=2**24, transcendentals=0)


def chunk_order(z, t):
    near = z + 1 - 2 * lax.rem(z, 2)
    third = jnp.where(z < 2, 2, 1)
    last = jnp.where(z < 2, 3, 0)
    return jnp.where(t == 0, z, jnp.where(t == 1, near, jnp.where(t == 2, third, last)))


def sum_order(z, i):
    first = jnp.where((z == 0) | (z == 2), 1, 2)
    second = jnp.where(z == 0, 2, jnp.where(z == 1, 3, jnp.where(z == 2, 0, 1)))
    third = jnp.where(z == 0, 3, jnp.where(z == 1, 0, jnp.where(z == 2, 3, 0)))
    return jnp.where(i == 0, first, jnp.where(i == 1, second, third))


class Plane:
    def __init__(self, rows, refs):
        (self.gathered, self.parts, self.from_side, self.from_low, self.from_high, self.sums,
         self.line_send, self.gather_recv, self.side_send, self.side_recv,
         self.sum_send, self.low_recv, self.high_recv) = refs
        self.sub = rows // HALVES
        self.both = SIDE * self.sub
        self.sec, self.owner, self.shard = (lax.axis_index(n) for n in ("section", "expert", "shard"))
        self.z, self.x = lax.div(self.owner, SIDE), lax.rem(self.owner, SIDE)
        self.inner = ((self.z > 0) & (self.z < LINE - 1)).astype(jnp.int32)

    def device(self, z, x):
        return (self.sec, z * SIDE + x, self.shard)

    def other_core(self):
        return (1 - self.sec, self.owner, self.shard)

    def other_shard(self):
        return (self.sec, self.owner, 1 - self.shard)

    def chunk(self, c, h):
        return pl.ds(pl.multiple_of((c * HALVES + h) * self.both, self.both), self.both)

    def block(self, c, h, x):
        return pl.ds(pl.multiple_of((c * HALVES + h) * self.both + x * self.sub, self.sub), self.sub)

    def barrier(self, *others):
        z, x = self.z, self.x
        sem = pltpu.get_barrier_semaphore()

        def greet(device):
            pl.semaphore_signal(sem, inc=1, device_id=device, device_id_type=MESH)

        for other in others:
            greet(other)
        greet(self.device(z, 1 - x))
        pl.when(z > 0)(lambda: greet(self.device(z - 1, x)))
        pl.when(z < LINE - 1)(lambda: greet(self.device(z + 1, x)))
        pl.semaphore_wait(sem, 2 + len(others) + self.inner)

    def place(self, block_ref):
        for h in range(HALVES):
            self.gathered[self.block(self.z, h, self.x)] = block_ref[pl.ds(h * self.sub, self.sub)]

    def gather_copy(self, way, c, h, x, device):
        ref = self.gathered.at[self.block(c, h, x)]
        q = c * HALVES + h
        return pltpu.make_async_remote_copy(
            src_ref=ref, dst_ref=ref, send_sem=self.line_send.at[way, q],
            recv_sem=self.gather_recv.at[q, x], device_id=device, device_id_type=MESH)

    def forward_up(self, c, h):
        return self.gather_copy(0, c, h, self.x, self.device(self.z + 1, self.x))

    def forward_down(self, c, h):
        return self.gather_copy(1, c, h, self.x, self.device(self.z - 1, self.x))

    def forward_side(self, c, h):
        return self.gather_copy(2, c, h, self.x, self.device(self.z, 1 - self.x))

    def start_gather(self):
        z = self.z
        for h in range(HALVES):
            pl.when(z < LINE - 1)(lambda h=h: self.forward_up(z, h).start())
            pl.when(z > 0)(lambda h=h: self.forward_down(z, h).start())
            self.forward_side(z, h).start()

    def relay(self, t, h):
        z = self.z

        @pl.when((t > 0) & (z - t >= 0))
        def _():
            c = z - t
            self.forward_side(c, h).wait_recv()
            pl.when(z < LINE - 1)(lambda: self.forward_up(c, h).start())
            self.forward_side(c, h).start()

        @pl.when((t > 0) & (z + t <= LINE - 1))
        def _():
            c = z + t
            self.forward_side(c, h).wait_recv()
            pl.when(z > 0)(lambda: self.forward_down(c, h).start())
            self.forward_side(c, h).start()

    def wait_side_block(self, c, h):
        self.gather_copy(2, c, h, 1 - self.x, self.device(self.z, 1 - self.x)).wait_recv()

    def side_copy(self, c, h):
        q = c * HALVES + h
        return pltpu.make_async_remote_copy(
            src_ref=self.parts.at[self.block(c, h, 1 - self.x)], dst_ref=self.from_side.at[q],
            send_sem=self.side_send.at[q], recv_sem=self.side_recv.at[q],
            device_id=self.device(self.z, 1 - self.x), device_id_type=MESH)

    def up_copy(self, c, h):
        q = c * HALVES + h
        return pltpu.make_async_remote_copy(
            src_ref=self.sums.at[q], dst_ref=self.from_low.at[q], send_sem=self.sum_send.at[q],
            recv_sem=self.low_recv.at[q], device_id=self.device(self.z + 1, self.x), device_id_type=MESH)

    def down_copy(self, c, h):
        q = c * HALVES + h
        return pltpu.make_async_remote_copy(
            src_ref=self.sums.at[q], dst_ref=self.from_high.at[q], send_sem=self.sum_send.at[q],
            recv_sem=self.high_recv.at[q], device_id=self.device(self.z - 1, self.x), device_id_type=MESH)

    def own_part(self, c, h):
        return (self.parts[self.block(c, h, self.x)].astype(F32)
                + self.from_side[c * HALVES + h].astype(F32))

    def pass_sum(self, t, h):
        i = t - 3 - self.inner
        pl.when((i >= 0) & (i < LINE - 1))(lambda: self.pass_chunk(sum_order(self.z, i), h))

    def pass_chunk(self, c, h):
        z = self.z
        q = c * HALVES + h
        self.side_copy(c, h).wait_recv()

        @pl.when(c > z)
        def _():
            @pl.when(z > 0)
            def _():
                self.up_copy(c, h).wait_recv()
                self.sums[q] = (self.own_part(c, h) + self.from_low[q].astype(F32)).astype(BF16)

            @pl.when(z == 0)
            def _():
                self.sums[q] = self.own_part(c, h).astype(BF16)

            self.up_copy(c, h).start()

        @pl.when(c < z)
        def _():
            @pl.when(z < LINE - 1)
            def _():
                self.down_copy(c, h).wait_recv()
                self.sums[q] = (self.own_part(c, h) + self.from_high[q].astype(F32)).astype(BF16)

            @pl.when(z == LINE - 1)
            def _():
                self.sums[q] = self.own_part(c, h).astype(BF16)

            self.down_copy(c, h).start()

    def finish_sum(self, h, out_ref):
        z = self.z
        q = z * HALVES + h
        rows = pl.ds(pl.multiple_of(h * self.sub, self.sub), self.sub)
        self.side_copy(z, h).wait_recv()
        out_ref[rows] = self.own_part(z, h)

        @pl.when(z > 0)
        def _():
            self.up_copy(z, h).wait_recv()
            out_ref[rows] += self.from_low[q].astype(F32)

        @pl.when(z < LINE - 1)
        def _():
            self.down_copy(z, h).wait_recv()
            out_ref[rows] += self.from_high[q].astype(F32)

    def finish_piece(self, h, out_ref):
        z = self.z
        q = z * HALVES + h
        self.side_copy(z, h).wait_recv()

        @pl.when(z == 0)
        def _():
            self.down_copy(z, h).wait_recv()
            out_ref[h] = (self.own_part(z, h) + self.from_high[q].astype(F32)).astype(BF16)

        @pl.when(z == LINE - 1)
        def _():
            self.up_copy(z, h).wait_recv()
            out_ref[h] = (self.own_part(z, h) + self.from_low[q].astype(F32)).astype(BF16)

        @pl.when((z > 0) & (z < LINE - 1))
        def _():
            self.up_copy(z, h).wait_recv()
            self.down_copy(z, h).wait_recv()
            total = self.own_part(z, h) + self.from_low[q].astype(F32)
            out_ref[h] = (total + self.from_high[q].astype(F32)).astype(BF16)

    def drain(self):
        z = self.z

        def one(q, carry):
            c, h = lax.div(q, HALVES), lax.rem(q, HALVES)
            pl.when((z < LINE - 1) & (c <= z))(lambda: self.forward_up(c, h).wait_send())
            pl.when((z > 0) & (c >= z))(lambda: self.forward_down(c, h).wait_send())
            self.forward_side(c, h).wait_send()
            self.side_copy(c, h).wait_send()
            pl.when(c > z)(lambda: self.up_copy(c, h).wait_send())
            pl.when(c < z)(lambda: self.down_copy(c, h).wait_send())
            return carry

        lax.fori_loop(0, LINE * HALVES, one, 0)


def plane_scratch(rows, width, wide):
    count = LINE * HALVES
    block = pltpu.VMEM((count, rows // HALVES, width), BF16)
    return [
        pltpu.VMEM((LINE * SIDE * rows, wide), BF16),
        pltpu.VMEM((LINE * SIDE * rows, width), BF16),
        block, block, block, block,
        pltpu.SemaphoreType.DMA((3, count)),
        pltpu.SemaphoreType.DMA((count, SIDE)),
        pltpu.SemaphoreType.DMA((count,)),
        pltpu.SemaphoreType.DMA((count,)),
        pltpu.SemaphoreType.DMA((count,)),
        pltpu.SemaphoreType.DMA((count,)),
        pltpu.SemaphoreType.DMA((count,)),
    ]


def lane_tile(at, size=TILE):
    return pl.ds(pl.multiple_of(at * size, size), size)


def nn(a, b):
    return jnp.dot(a, b, preferred_element_type=F32)


def nt(a, b):
    return lax.dot_general(a, b, (((1,), (1,)), ((), ())), preferred_element_type=F32)


def tn(a, b):
    return lax.dot_general(a, b, (((0,), (0,)), ((), ())), preferred_element_type=F32)


def pick_lane(block, wanted):
    lane = lax.broadcasted_iota(jnp.int32, block.shape, 1)
    hot = lane == wanted[0]
    for other in wanted[1:]:
        hot = hot | (lane == other)
    return jnp.sum(jnp.where(hot, block, 0.0), axis=1, keepdims=True)


def own_gates(block, owner, experts):
    block = block.astype(F32)
    return [
        pick_lane(block, (owner * EXP_DEV + j, experts + owner * EXP_DEV + j)) for j in range(EXP_DEV)
    ]


def load_layer(layer, sec, own, other, dst, sem):
    copies = [pltpu.make_async_copy(own, dst, sem), pltpu.make_async_copy(other, dst, sem)]
    pl.when(sec == layer)(lambda: copies[0].start())
    pl.when(sec != layer)(lambda: copies[1].start())
    return copies[0]


def load_experts(layer, sec, gu, gu_other, down, down_other, gu_v, down_v, sems):
    loads = [load_layer(layer, sec, gu, gu_other, gu_v, sems.at[0])]
    for j in range(EXP_DEV):
        loads.append(load_layer(
            layer, sec, down.at[j], down_other.at[j], down_v.at[pl.ds(j * FF, FF)], sems.at[1 + j]))
    return loads


def moe_forward_kernel(layer, experts, rows, width, block_ref, gu_hbm, gu_other, down_hbm, down_other,
                       moe_ref, rows_hbm, kept_hbm, scaled_hbm,
                       gu_v, down_v, kept, scaled, load_sem, store_sem, *plane_refs):
    plane = Plane(rows, plane_refs)
    gathered, parts = plane.gathered, plane.parts
    loads = load_experts(layer, plane.sec, gu_hbm, gu_other, down_hbm, down_other, gu_v, down_v, load_sem)
    plane.place(block_ref)
    plane.barrier()
    plane.start_gather()
    for load in loads:
        load.wait()

    def stores(c, h):
        q, at = c * HALVES + h, plane.chunk(c, h)
        return [
            pltpu.make_async_copy(gathered.at[at], rows_hbm.at[at], store_sem.at[0, q]),
            pltpu.make_async_copy(kept.at[at], kept_hbm.at[at], store_sem.at[1, q]),
            pltpu.make_async_copy(scaled.at[at], scaled_hbm.at[at], store_sem.at[2, q]),
        ]

    def step(k, carry):
        t, h = lax.div(k, HALVES), lax.rem(k, HALVES)
        plane.relay(t, h)
        plane.pass_sum(t, h)
        pl.when(t > 0)(lambda: work(chunk_order(plane.z, t - 1), h))
        return carry

    def work(c, h):
        at = plane.chunk(c, h)
        plane.wait_side_block(c, h)
        gates = own_gates(gathered[at, pl.ds(width, LANES)], plane.owner, experts)
        for j in range(EXP_DEV):
            for f in range(FF // TILE):
                data = gathered[at, pl.ds(0, width)]
                low, high = j * 2 * FF + f * TILE, j * 2 * FF + FF + f * TILE
                g = nn(data, gu_v[j, :, pl.ds(f * TILE, TILE)])
                u = nn(data, gu_v[j, :, pl.ds(FF + f * TILE, TILE)])
                z = g * jax.nn.sigmoid(g) * u * gates[j]
                scaled[at, pl.ds(j * FF + f * TILE, TILE)] = z.astype(BF16)
                kept[at, pl.ds(low, TILE)] = g.astype(BF16)
                kept[at, pl.ds(high, TILE)] = u.astype(BF16)
        for n in range(width // TILE):
            parts[at, pl.ds(n * TILE, TILE)] = nn(
                scaled[at, :], down_v[:, pl.ds(n * TILE, TILE)]).astype(BF16)
        plane.side_copy(c, h).start()
        for store in stores(c, h):
            store.start()

    lax.fori_loop(0, (LINE + 1) * HALVES, step, 0)

    def tail(k, carry):
        plane.pass_sum(lax.div(k, HALVES), lax.rem(k, HALVES))
        return carry

    lax.fori_loop((LINE + 1) * HALVES, (LINE + 3) * HALVES, tail, 0)

    def finish(h, carry):
        plane.finish_sum(h, moe_ref)
        return carry

    lax.fori_loop(0, HALVES, finish, 0)
    plane.drain()

    def stored(q, carry):
        for store in stores(lax.div(q, HALVES), lax.rem(q, HALVES)):
            store.wait()
        return carry

    lax.fori_loop(0, LINE * HALVES, stored, 0)


def moe_forward(layer, block, weights, experts, collective_id):
    rows, wide = block.shape
    width = wide - LANES
    total = LINE * SIDE * rows
    any_spec = pl.BlockSpec(memory_space=pl.ANY)
    vmem = pl.BlockSpec(memory_space=pltpu.VMEM)
    return pl.pallas_call(
        functools.partial(moe_forward_kernel, layer, experts, rows, width),
        name="moe_forward",
        out_shape=(
            jax.ShapeDtypeStruct((rows, width), F32),
            jax.ShapeDtypeStruct((total, wide), BF16),
            jax.ShapeDtypeStruct((total, EXP_DEV * 2 * FF), BF16),
            jax.ShapeDtypeStruct((total, EXP_DEV * FF), BF16),
        ),
        in_specs=[vmem] + [any_spec] * 4,
        out_specs=(vmem, any_spec, any_spec, any_spec),
        scratch_shapes=[
            pltpu.VMEM((EXP_DEV, width, 2 * FF), BF16),
            pltpu.VMEM((EXP_DEV * FF, width), BF16),
            pltpu.VMEM((total, EXP_DEV * 2 * FF), BF16),
            pltpu.VMEM((total, EXP_DEV * FF), BF16),
            pltpu.SemaphoreType.DMA((1 + EXP_DEV,)),
            pltpu.SemaphoreType.DMA((3, LINE * HALVES)),
        ] + plane_scratch(rows, width, wide),
        cost_estimate=COST,
        compiler_params=pltpu.CompilerParams(
            collective_id=collective_id, has_side_effects=True, vmem_limit_bytes=VMEM_BYTES),
    )(block, *weights)


def moe_backward_kernel(layer, experts, rows, width, count, block_ref, router_ref, gu_hbm, gu_other, down_hbm,
                        down_other, rows_hbm, kept_hbm, scaled_hbm, *refs):
    sent, refs = refs[:count], refs[count:]
    (db_ref, grad_gu_hbm, grad_down_hbm, grad_router_ref), refs = refs[:4], refs[4:]
    landed, refs = refs[:count], refs[count:]
    (gu_v, down_v, fwd_rows, kept, scaled, dgu, send_gu, grad_gu, got_gu, send_down, grad_down, got_down,
     load_sem, store_sem, core_send, core_recv, beside_send, beside_recv), plane_refs = refs[:18], refs[18:]
    plane = Plane(rows, plane_refs)
    gathered, parts = plane.gathered, plane.parts
    loads = load_experts(layer, plane.sec, gu_hbm, gu_other, down_hbm, down_other, gu_v, down_v, load_sem)
    loads.append(pltpu.make_async_copy(rows_hbm, fwd_rows, load_sem.at[3]))
    loads.append(pltpu.make_async_copy(kept_hbm, kept, load_sem.at[4]))
    loads.append(pltpu.make_async_copy(scaled_hbm, scaled, load_sem.at[5]))
    for load in loads[3:]:
        load.start()
    plane.place(block_ref)
    plane.barrier(plane.other_core(), *([plane.other_shard()] if count else []))
    plane.start_gather()
    beside = [
        pltpu.make_async_remote_copy(
            src_ref=sent[n], dst_ref=landed[n], send_sem=beside_send.at[n], recv_sem=beside_recv.at[n],
            device_id=plane.other_shard(), device_id_type=MESH)
        for n in range(count)
    ]
    for copy in beside:
        copy.start()
    for load in loads:
        load.wait()
    total = plane.both
    up_at = EXP_DEV * 2 * FF

    def step(k, carry):
        t, h = lax.div(k, HALVES), lax.rem(k, HALVES)
        plane.relay(t, h)
        plane.pass_sum(t, h)
        pl.when(t > 0)(lambda: work(chunk_order(plane.z, t - 1), h))
        return carry

    def work(c, h):
        at = plane.chunk(c, h)
        plane.wait_side_block(c, h)
        gates = own_gates(fwd_rows[at, pl.ds(width, LANES)], plane.owner, experts)
        outer = jnp.sum(gathered[at, pl.ds(width, LANES)].astype(F32), axis=1, keepdims=True)
        dcs = []
        for j in range(EXP_DEV):
            dgate = jnp.zeros((total, 1), F32)
            for f in range(FF // TILE):
                low, high = pl.ds(j * 2 * FF + f * TILE, TILE), pl.ds(j * 2 * FF + FF + f * TILE, TILE)
                dz = nt(gathered[at, pl.ds(0, width)], down_v[pl.ds(j * FF + f * TILE, TILE), :])
                g = kept[at, low].astype(F32)
                u = kept[at, high].astype(F32)
                sig = jax.nn.sigmoid(g)
                silu = g * sig
                dgate = dgate + jnp.sum(dz * silu * u, axis=1, keepdims=True)
                dz = dz * gates[j]
                dgu[at, low] = (dz * u * sig * (1.0 + g * (1.0 - sig))).astype(BF16)
                dgu[at, high] = (dz * silu).astype(BF16)
            dcs.append(gates[j] * (dgate - outer))
        lane = lax.broadcasted_iota(jnp.int32, (total, LANES), 1)
        extra = jnp.zeros((total, LANES), F32)
        for j in range(EXP_DEV):
            top = dcs[j].astype(BF16).astype(F32)
            extra = extra + jnp.where(lane == j, top, 0.0) + jnp.where(lane == EXP_DEV + j, dcs[j] - top, 0.0)
        dgu[at, pl.ds(up_at, LANES)] = extra.astype(BF16)
        for n in range(width // TILE):
            cols = pl.ds(n * TILE, TILE)
            acc = nt(dgu[at, pl.ds(0, 2 * FF)], gu_v[0, cols, :])
            for j in range(1, EXP_DEV):
                acc = acc + nt(dgu[at, pl.ds(j * 2 * FF, 2 * FF)], gu_v[j, cols, :])
            for j in range(EXP_DEV):
                acc = acc + dcs[j] * router_ref[pl.ds(j, 1), cols]
            parts[at, cols] = acc.astype(BF16)
        plane.side_copy(c, h).start()

    lax.fori_loop(0, (LINE + 1) * HALVES, step, 0)

    core = plane.sec
    gu_steps, down_steps = width // TILE, FF // TILE

    def core_gu(n):
        at = lane_tile(n)
        return pltpu.make_async_remote_copy(
            src_ref=send_gu.at[at], dst_ref=got_gu.at[at], send_sem=core_send.at[0, n],
            recv_sem=core_recv.at[0, n], device_id=plane.other_core(), device_id_type=MESH)

    def core_down(n):
        at = lane_tile(n)
        return pltpu.make_async_remote_copy(
            src_ref=send_down.at[at], dst_ref=got_down.at[at], send_sem=core_send.at[1, n],
            recv_sem=core_recv.at[1, n], device_id=plane.other_core(), device_id_type=MESH)

    def store_gu(n):
        return pltpu.make_async_copy(grad_gu.at[lane_tile(n)], grad_gu_hbm.at[lane_tile(n)], store_sem.at[0, n])

    def store_down(n):
        return pltpu.make_async_copy(
            grad_down.at[lane_tile(n)], grad_down_hbm.at[lane_tile(n)], store_sem.at[1, n])

    def expert_cols(j, size):
        return pl.ds(pl.multiple_of(j * size, size), size)

    def grad_gu_rows(n):
        rows_t = fwd_rows[:, lane_tile(n)]
        send_gu[lane_tile(n), :] = tn(rows_t, dgu[:, expert_cols(1 - core, 2 * FF)]).astype(BF16)
        core_gu(n).start()
        grad_gu[lane_tile(n), :] = tn(rows_t, dgu[:, expert_cols(core, 2 * FF)]).astype(BF16)
        grad_router_ref[lane_tile(n), :] = tn(rows_t, dgu[:, pl.ds(up_at, LANES)])

    def grad_down_rows(n):
        def cols(j):
            return pl.ds(pl.multiple_of(j * FF + n * TILE, TILE), TILE)

        data = gathered[:, pl.ds(0, width)]
        send_down[lane_tile(n), :] = tn(scaled[:, cols(1 - core)], data).astype(BF16)
        core_down(n).start()
        grad_down[lane_tile(n), :] = tn(scaled[:, cols(core)], data).astype(BF16)

    def sum_gu_rows(n):
        core_gu(n).wait_recv()
        at = lane_tile(n)
        grad_gu[at, :] = (grad_gu[at, :].astype(F32) + got_gu[at, :].astype(F32)).astype(BF16)
        store_gu(n).start()

    def sum_down_rows(n):
        core_down(n).wait_recv()
        at = lane_tile(n)
        grad_down[at, :] = (grad_down[at, :].astype(F32) + got_down[at, :].astype(F32)).astype(BF16)
        store_down(n).start()

    slots = 2 * HALVES

    def tail(k, carry):
        pl.loop(lax.div(k * gu_steps, slots), lax.div((k + 1) * gu_steps, slots))(grad_gu_rows)
        plane.pass_sum(LINE + 1 + lax.div(k, HALVES), lax.rem(k, HALVES))
        return carry

    lax.fori_loop(0, slots, tail, 0)
    pl.loop(0, down_steps)(grad_down_rows)

    def finish(h, carry):
        plane.finish_sum(h, db_ref)
        return carry

    lax.fori_loop(0, HALVES, finish, 0)
    pl.loop(0, gu_steps)(sum_gu_rows)
    pl.loop(0, down_steps)(sum_down_rows)
    plane.drain()
    for n in range(gu_steps):
        core_gu(n).wait_send()
        store_gu(n).wait()
    for n in range(down_steps):
        core_down(n).wait_send()
        store_down(n).wait()
    for copy in beside:
        copy.wait()


def moe_backward(layer, block, router, weights, kept, beside, experts, collective_id):
    rows, wide = block.shape
    width = wide - LANES
    total = LINE * SIDE * rows
    any_spec = pl.BlockSpec(memory_space=pl.ANY)
    vmem = pl.BlockSpec(memory_space=pltpu.VMEM)
    expert_gu, expert_down = pltpu.VMEM((width, 2 * FF), BF16), pltpu.VMEM((FF, width), BF16)
    return pl.pallas_call(
        functools.partial(moe_backward_kernel, layer, experts, rows, width, len(beside)),
        name="moe_backward",
        out_shape=(
            jax.ShapeDtypeStruct((rows, width), F32),
            jax.ShapeDtypeStruct((width, 2 * FF), BF16),
            jax.ShapeDtypeStruct((FF, width), BF16),
            jax.ShapeDtypeStruct((width, LANES), F32),
        ) + tuple(jax.ShapeDtypeStruct(array.shape, array.dtype) for array in beside),
        in_specs=[vmem, vmem] + [any_spec] * (7 + len(beside)),
        out_specs=(vmem, any_spec, any_spec, vmem) + (any_spec,) * len(beside),
        scratch_shapes=[
            pltpu.VMEM((EXP_DEV, width, 2 * FF), BF16),
            pltpu.VMEM((EXP_DEV * FF, width), BF16),
            pltpu.VMEM((total, wide), BF16),
            pltpu.VMEM((total, EXP_DEV * 2 * FF), BF16),
            pltpu.VMEM((total, EXP_DEV * FF), BF16),
            pltpu.VMEM((total, EXP_DEV * 2 * FF + LANES), BF16),
            expert_gu, expert_gu, expert_gu, expert_down, expert_down, expert_down,
            pltpu.SemaphoreType.DMA((6,)),
            pltpu.SemaphoreType.DMA((2, width // TILE)),
            pltpu.SemaphoreType.DMA((2, width // TILE)),
            pltpu.SemaphoreType.DMA((2, width // TILE)),
            pltpu.SemaphoreType.DMA((max(len(beside), 1),)),
            pltpu.SemaphoreType.DMA((max(len(beside), 1),)),
        ] + plane_scratch(rows, width, wide),
        cost_estimate=COST,
        compiler_params=pltpu.CompilerParams(
            collective_id=collective_id, has_side_effects=True, vmem_limit_bytes=VMEM_BYTES),
    )(block, router, *weights, *kept, *beside)


def split_terms(values):
    high = values.astype(BF16)
    return high, (values - high.astype(F32)).astype(BF16)


def with_lanes(block, columns):
    extra = jnp.concatenate(columns, axis=1)
    extra = jnp.pad(extra, ((0, 0), (0, LANES - extra.shape[1])))
    return jnp.concatenate([block, extra], axis=1)


def far_order(z, i):
    low = jnp.where(i == 0, 3, jnp.where(i == 1, jnp.where(z == 0, 2, 0), jnp.where(z == 0, 1, 2)))
    high = jnp.where(i == 0, 0, jnp.where(i == 1, jnp.where(z == 3, 1, 3), jnp.where(z == 3, 2, 1)))
    return jnp.where(z < 2, low, high)


def reduce_kernel(sub, cols, g1, g0, t1, t0, gu_hbm, down_hbm,
                  sum_hbm, own_gu_hbm, own_down_hbm, got_gu_hbm, got_down_hbm,
                  core_got, small_own, small_got, result, own_gu, other_gu, own_down, other_down,
                  load_sem, core_sem, small_sem, move_sem, expert_sem, core_expert_sem, store_sem, *plane_refs):
    plane = Plane(HALVES * sub, plane_refs)
    gathered, parts = plane.gathered, plane.parts
    core, shard, z, x = plane.sec, plane.shard, plane.z, plane.x
    wide = cols + LANES
    grads, smalls = (g1, g0), (t1, t0)
    diagonal = (1 - core, plane.owner, 1 - shard)
    places = [(c, side) for c in range(LINE) for side in range(SIDE)]

    def remote(src, dst, send_sem, recv_sem, device):
        return pltpu.make_async_remote_copy(
            src_ref=src, dst_ref=dst, send_sem=send_sem, recv_sem=recv_sem,
            device_id=device, device_id_type=MESH)

    loads = []
    for h in range(2):
        for n, (c, side) in enumerate(places):
            loads.append(pltpu.make_async_copy(
                grads[h].at[n, core], parts.at[plane.block(c, h, side), pl.ds(0, cols)], load_sem.at[h, n]))
        loads.append(pltpu.make_async_copy(
            smalls[h].at[shard, :, core], small_own.at[h], load_sem.at[h, len(places)]))
    loads.append(pltpu.make_async_copy(gu_hbm, own_gu, load_sem.at[2, 0]))
    loads.append(pltpu.make_async_copy(down_hbm, own_down, load_sem.at[2, 1]))
    for load in loads:
        load.start()
    plane.barrier(plane.other_core(), plane.other_shard(), diagonal)
    cores = [
        remote(grads[h].at[:, 1 - core], core_got.at[h], core_sem.at[0, h], core_sem.at[1, h], plane.other_core())
        for h in range(2)
    ]
    small = []
    for h in range(2):
        for n, (there, half, device) in enumerate((
            (shard, 1 - core, plane.other_core()),
            (1 - shard, core, plane.other_shard()),
            (1 - shard, 1 - core, diagonal),
        )):
            small.append(remote(
                smalls[h].at[there, :, half], small_got.at[h, n], small_sem.at[0, h, n], small_sem.at[1, h, n],
                device))
    for copy in cores + small:
        copy.start()
    pieces = []
    for n in range(4):
        at = pl.ds(n * (own_gu.shape[0] // 4), own_gu.shape[0] // 4)
        pieces.append((gu_hbm, own_gu, other_gu, own_gu_hbm, got_gu_hbm, at))
    for n in range(2):
        at = pl.ds(n * (own_down.shape[0] // 2), own_down.shape[0] // 2)
        pieces.append((down_hbm, own_down, other_down, own_down_hbm, got_down_hbm, at))
    exchange = [
        remote(hbm.at[at], other.at[at], expert_sem.at[0, n], expert_sem.at[1, n], plane.other_shard())
        for n, (hbm, own, other, own_hbm, got_hbm, at) in enumerate(pieces)
    ]
    for copy in exchange:
        copy.start()
    for load in loads:
        load.wait()
    for h in range(2):
        cores[h].wait_recv()
        for copy in small[3 * h : 3 * h + 3]:
            copy.wait_recv()

        def prepare(k, carry, h=h):
            c = jnp.where(k < 2 * (LINE - 1), far_order(z, lax.div(k, 2)), z)
            side = jnp.where(lax.rem(k, 2) == 0, 1 - x, x)
            n = c * SIDE + side
            at = plane.block(c, h, side)
            parts[at, pl.ds(0, cols)] = (
                parts[at, pl.ds(0, cols)].astype(F32) + core_got[h, n].astype(F32)).astype(BF16)
            total = small_own[h, n].astype(F32)
            for other in range(3):
                total = total + small_got[h, other, n].astype(F32)
            parts[at, pl.ds(cols, LANES)] = total.astype(BF16)
            pl.when(side != x)(lambda: plane.side_copy(c, h).start())
            return carry

        lax.fori_loop(0, LINE * SIDE, prepare, 0)

    def passes(k, carry):
        plane.pass_chunk(far_order(z, lax.div(k, HALVES)), lax.rem(k, HALVES))
        return carry

    lax.fori_loop(0, (LINE - 1) * HALVES, passes, 0)

    def move(h):
        return remote(
            result.at[h], gathered.at[plane.block(z, core, x)], move_sem.at[0], move_sem.at[1], plane.other_core())

    def send_block(h):
        pl.when(z < LINE - 1)(lambda: plane.forward_up(z, h).start())
        pl.when(z > 0)(lambda: plane.forward_down(z, h).start())
        plane.forward_side(z, h).start()

    for h in range(2):
        plane.finish_piece(h, result)
        own_layer = core == 1 - h

        @pl.when(own_layer)
        def _(h=h):
            gathered[plane.block(z, core, x)] = result[h]
            send_block(core)

        pl.when(jnp.logical_not(own_layer))(lambda h=h: move(h).start())

    arrived = remote(
        result.at[0], gathered.at[plane.block(z, 1 - core, x)], move_sem.at[0], move_sem.at[1], plane.other_core())
    arrived.wait_recv()
    send_block(1 - core)

    def out_copy(c, h, side):
        at = pl.multiple_of(((c * SIDE + side) * HALVES + h) * sub, sub)
        return pltpu.make_async_copy(
            gathered.at[plane.block(c, h, side)], sum_hbm.at[pl.ds(at, sub)],
            store_sem.at[(c * SIDE + side) * HALVES + h])

    def gather(k, carry):
        t, turn = lax.div(k, HALVES), lax.rem(k, HALVES)
        h = jnp.where(turn == 0, core, 1 - core)
        plane.relay(t, h)

        @pl.when(t > 0)
        def _():
            c = chunk_order(z, t - 1)
            plane.wait_side_block(c, h)
            out_copy(c, h, x).start()
            out_copy(c, h, 1 - x).start()

        return carry

    lax.fori_loop(0, (LINE + 1) * HALVES, gather, 0)
    count = LINE * SIDE * HALVES
    to_core, keep = [], []
    for n, (hbm, own, other, own_hbm, got_hbm, at) in enumerate(pieces):
        exchange[n].wait_recv()
        own[at] = (own[at].astype(F32) + other[at].astype(F32)).astype(BF16)
        copy = remote(
            own.at[at], got_hbm.at[at], core_expert_sem.at[0, n], core_expert_sem.at[1, n], plane.other_core())
        pl.when(core == 1)(lambda copy=copy: copy.start())
        to_core.append(copy)
        store = pltpu.make_async_copy(own.at[at], own_hbm.at[at], store_sem.at[count + n])
        store.start()
        keep.append(store)
    plane.drain()
    for copy in cores + small + exchange:
        copy.wait_send()
    arrived.wait_send()

    def stored(k, carry):
        out_copy(lax.div(k, SIDE * HALVES), lax.rem(k, HALVES), lax.rem(lax.div(k, HALVES), SIDE)).wait()
        return carry

    lax.fori_loop(0, count, stored, 0)
    for store in keep:
        store.wait()
    for copy in to_core:
        pl.when(core == 1)(lambda copy=copy: copy.wait_send())
        pl.when(core == 0)(lambda copy=copy: copy.wait_recv())


def reduce_gradients(g1, g0, t1, t0, grad_gu, grad_down, collective_id):
    places, halves, sub, cols = g1.shape
    any_spec = pl.BlockSpec(memory_space=pl.ANY)
    wide = cols + LANES
    gu, down = jax.ShapeDtypeStruct(grad_gu.shape, BF16), jax.ShapeDtypeStruct(grad_down.shape, BF16)
    return pl.pallas_call(
        functools.partial(reduce_kernel, sub, cols),
        name="reduce_gradients",
        out_shape=(jax.ShapeDtypeStruct((places * halves * sub, wide), BF16), gu, down, gu, down),
        in_specs=[any_spec] * 6,
        out_specs=(any_spec,) * 5,
        scratch_shapes=[
            pltpu.VMEM((2, places, sub, cols), BF16),
            pltpu.VMEM((2, places, sub, LANES), BF16),
            pltpu.VMEM((2, 3, places, sub, LANES), BF16),
            pltpu.VMEM((2, sub, wide), BF16),
            pltpu.VMEM(grad_gu.shape, BF16),
            pltpu.VMEM(grad_gu.shape, BF16),
            pltpu.VMEM(grad_down.shape, BF16),
            pltpu.VMEM(grad_down.shape, BF16),
            pltpu.SemaphoreType.DMA((3, places + 1)),
            pltpu.SemaphoreType.DMA((2, 2)),
            pltpu.SemaphoreType.DMA((2, 2, 3)),
            pltpu.SemaphoreType.DMA((2,)),
            pltpu.SemaphoreType.DMA((2, 6)),
            pltpu.SemaphoreType.DMA((2, 6)),
            pltpu.SemaphoreType.DMA((places * halves + 6,)),
        ] + plane_scratch(halves * sub, wide, wide),
        compiler_params=pltpu.CompilerParams(
            collective_id=collective_id, has_side_effects=True, vmem_limit_bytes=VMEM_BYTES),
    )(g1, g0, t1, t0, grad_gu, grad_down)


PAIRS = 2
GROUP = QUERY_HEADS // KEY_VALUE_HEADS
SCALE = HEAD_SIZE ** (-0.5)


class Pair:
    def __init__(self):
        self.sec, self.owner, self.me = (lax.axis_index(n) for n in ("section", "expert", "shard"))
        self.peer = 1 - self.me

    def barrier(self):
        sem = pltpu.get_barrier_semaphore()
        pl.semaphore_signal(
            sem, inc=1, device_id=(self.sec, self.owner, self.peer), device_id_type=MESH)
        pl.semaphore_wait(sem, 1)

    def send(self, src, dst, send_sem, recv_sem):
        return pltpu.make_async_remote_copy(
            src_ref=src, dst_ref=dst, send_sem=send_sem, recv_sem=recv_sem,
            device_id=(self.sec, self.owner, self.peer), device_id_type=MESH)


def head_columns(shard):
    kv_pair = KEY_VALUE_HEADS // 2 // PAIRS * HEAD_SIZE
    q_pair = kv_pair * GROUP
    wide = q_pair + 2 * kv_pair
    spans = []
    for i in range(PAIRS):
        at = shard * PAIRS + i
        spans.append((at * q_pair, i * wide, q_pair))
        spans.append((QUERY_WIDTH + at * kv_pair, i * wide + q_pair, kv_pair))
        spans.append((QUERY_WIDTH + KV_WIDTH + at * kv_pair, i * wide + q_pair + kv_pair, kv_pair))
    return spans


def head_at(i, n, g):
    kv_pair = KEY_VALUE_HEADS // 2 // PAIRS * HEAD_SIZE
    q_pair = kv_pair * GROUP
    base = i * (q_pair + 2 * kv_pair)
    return (
        pl.ds(base + (n * GROUP + g) * HEAD_SIZE, HEAD_SIZE),
        pl.ds(base + q_pair + n * HEAD_SIZE, HEAD_SIZE),
        pl.ds(base + q_pair + kv_pair + n * HEAD_SIZE, HEAD_SIZE),
    )


KV_IN_PAIR = KEY_VALUE_HEADS // 2 // PAIRS


def load_attention(layer, sec, wq, wq_other, wo, wo_other, wq_v, wo_v, sems):
    loads = []
    for j in range(2):
        for at, local, size in head_columns(j):
            loads.append(load_layer(
                layer, sec, wq.at[:, pl.ds(at, size)], wq_other.at[:, pl.ds(at, size)],
                wq_v.at[j, :, pl.ds(local, size)], sems.at[len(loads)]))
    loads.append(load_layer(layer, sec, wo, wo_other, wo_v, sems.at[len(loads)]))
    return loads


LOADS = 2 * PAIRS * 3 + 1


def attention_forward_kernel(layer, rows, width, h_ref, allowed_ref, gains_ref, router_ref, mask_ref, wq, wq_other,
                             wo, wo_other, block_ref, h1_ref, a_ref, qkv_ref, p_ref, o_ref,
                             wq_v, wo_v, a_parts, a_half, part_send, got_part, out_send, got_out,
                             load_sem, send_sem, recv_sem):
    pair = Pair()
    me, peer = pair.me, pair.peer
    half = width // 2
    loads = load_attention(layer, pair.sec, wq, wq_other, wo, wo_other, wq_v, wo_v, load_sem)
    pair.barrier()

    def span(who):
        return pl.ds(pl.multiple_of(who * rows, rows), rows)

    h = h_ref[...].astype(F32)
    r1 = lax.rsqrt(jnp.mean(h * h, axis=1, keepdims=True) + EPS)
    a = (h * r1 * gains_ref[pl.ds(0, 1), :]).astype(BF16)
    for j in range(2):
        a_parts[j] = a[:, j * half : (j + 1) * half]
    send_a = pair.send(a_parts.at[peer], a_half.at[span(me)], send_sem.at[0], recv_sem.at[0])
    send_a.start()
    a_half[span(me)] = a_parts[me]
    for load in loads[:-1]:
        load.wait()
    part_send[span(me)] = nn(a_parts[me], wq_v[peer]).astype(BF16)
    send_own = pair.send(part_send.at[span(me)], got_part.at[span(me)], send_sem.at[1], recv_sem.at[1])
    send_own.start()
    send_a.wait_recv()
    part_send[span(peer)] = nn(a_half[span(peer)], wq_v[peer]).astype(BF16)
    send_other = pair.send(
        part_send.at[span(peer)], got_part.at[span(peer)], send_sem.at[2], recv_sem.at[2])
    send_other.start()
    mine = nn(a_half[...], wq_v[me])
    a_ref[...] = a_half[...]
    send_own.wait_recv()
    send_other.wait_recv()
    qkv_ref[...] = (mine + got_part[...].astype(F32)).astype(BF16)
    allowed = allowed_ref[...] > 0
    for i in range(PAIRS):
        for n in range(KV_IN_PAIR):
            for g in range(GROUP):
                q_at, k_at, v_at = head_at(i, n, g)
                j = (i * KV_IN_PAIR + n) * GROUP + g
                s = nt(qkv_ref[:, q_at], qkv_ref[:, k_at]) * SCALE
                s = jnp.where(allowed, s, MASKED_SCORE)
                ex = jnp.exp(s - jnp.max(s, axis=1, keepdims=True))
                p = (ex / jnp.sum(ex, axis=1, keepdims=True)).astype(BF16)
                p_ref[j] = p
                o_ref[:, pl.ds(j * HEAD_SIZE, HEAD_SIZE)] = nn(p, qkv_ref[:, v_at]).astype(BF16)
    loads[-1].wait()
    out_send[...] = nn(o_ref[span(peer)], wo_v[...]).astype(BF16)
    send_out = pair.send(out_send, got_out, send_sem.at[3], recv_sem.at[3])
    send_out.start()
    own = nn(o_ref[span(me)], wo_v[...])
    send_out.wait_recv()
    h1 = h + own + got_out[...].astype(F32)
    h1_ref[...] = h1
    r2 = lax.rsqrt(jnp.mean(h1 * h1, axis=1, keepdims=True) + EPS)
    b = (h1 * r2 * gains_ref[pl.ds(1, 1), :]).astype(BF16)
    block_ref[:, pl.ds(0, width)] = b
    mask = mask_ref[...] > 0
    logits = jnp.where(mask, nt(b, router_ref[...]), MASKED_SCORE)
    ex = jnp.where(mask, jnp.exp(logits - jnp.max(logits, axis=1, keepdims=True)), 0.0)
    gates = ex / (0.5 * jnp.sum(ex, axis=1, keepdims=True))
    high = gates.astype(BF16).astype(F32)
    block_ref[:, pl.ds(width, LANES)] = jnp.where(mask_ref[...] > 1, gates - high, high).astype(BF16)
    for send in (send_a, send_own, send_other, send_out):
        send.wait_send()


def attention_forward(layer, h, allowed, gains, router, mask, weights, collective_id):
    rows, width = h.shape
    half, group = width // 2, 2 * rows
    qkv = (QUERY_WIDTH + 2 * KV_WIDTH) // 2
    heads = QUERY_HEADS // 2
    any_spec = pl.BlockSpec(memory_space=pl.ANY)
    vmem = pl.BlockSpec(memory_space=pltpu.VMEM)
    return pl.pallas_call(
        functools.partial(attention_forward_kernel, layer, rows, width),
        name="attention_forward",
        out_shape=(
            jax.ShapeDtypeStruct((rows, width + LANES), BF16),
            jax.ShapeDtypeStruct((rows, width), F32),
            jax.ShapeDtypeStruct((group, half), BF16),
            jax.ShapeDtypeStruct((group, qkv), BF16),
            jax.ShapeDtypeStruct((heads, group, group), BF16),
            jax.ShapeDtypeStruct((group, QUERY_WIDTH // 2), BF16),
        ),
        in_specs=[vmem] * 5 + [any_spec] * 4,
        out_specs=(vmem,) * 6,
        scratch_shapes=[
            pltpu.VMEM((2, half, qkv), BF16),
            pltpu.VMEM((QUERY_WIDTH // 2, width), BF16),
            pltpu.VMEM((2, rows, half), BF16),
            pltpu.VMEM((group, half), BF16),
            pltpu.VMEM((group, qkv), BF16),
            pltpu.VMEM((group, qkv), BF16),
            pltpu.VMEM((rows, width), BF16),
            pltpu.VMEM((rows, width), BF16),
            pltpu.SemaphoreType.DMA((LOADS,)),
            pltpu.SemaphoreType.DMA((4,)),
            pltpu.SemaphoreType.DMA((4,)),
        ],
        cost_estimate=COST,
        compiler_params=pltpu.CompilerParams(
            collective_id=collective_id, has_side_effects=True, vmem_limit_bytes=VMEM_BYTES),
    )(h, allowed, gains, router, mask, *weights)


def attention_backward_kernel(layer, rows, width, db_ref, dout_ref, h1_ref, h_ref, gains_ref, a_ref, qkv_ref,
                              p_ref, o_ref, wq, wq_other, wo, wo_other, dh_ref, gain_grads_ref, grad_hbm,
                              wq_v, wo_v, d_all, do, dqkv, got_dqkv, da_send, got_da, dh1_v, grad_q, grad_o,
                              load_sem, store_sem, send_sem, recv_sem):
    pair = Pair()
    me, peer = pair.me, pair.peer
    half = width // 2
    qkv_cols = dqkv.shape[1]
    pair_cols = qkv_cols // PAIRS
    loads = load_attention(layer, pair.sec, wq, wq_other, wo, wo_other, wq_v, wo_v, load_sem)
    pair.barrier()

    def span(who):
        return pl.ds(pl.multiple_of(who * rows, rows), rows)

    h1 = h1_ref[...]
    r2 = lax.rsqrt(jnp.mean(h1 * h1, axis=1, keepdims=True) + EPS)
    normed = h1 * r2
    db = db_ref[...]
    scaled = db * gains_ref[pl.ds(1, 1), :]
    gain_grads_ref[...] = jnp.zeros_like(gain_grads_ref)
    gain_grads_ref[pl.ds(1, 1), :] = jnp.sum(db * normed, axis=0, keepdims=True)
    dh1 = dout_ref[...].astype(F32) + r2 * (
        scaled - normed * jnp.mean(scaled * normed, axis=1, keepdims=True))
    dh1_v[...] = dh1
    d_all[span(me)] = dh1.astype(BF16)
    send_d = pair.send(d_all.at[span(me)], d_all.at[span(me)], send_sem.at[0], recv_sem.at[0])
    send_d.start()
    for load in loads:
        load.wait()
    do[span(me)] = nt(d_all[span(me)], wo_v[...]).astype(BF16)
    send_d.wait_recv()
    do[span(peer)] = nt(d_all[span(peer)], wo_v[...]).astype(BF16)
    sends = [send_d]
    for i in range(PAIRS):
        cols = pl.ds(i * pair_cols, pair_cols)
        for n in range(KV_IN_PAIR):
            dk = dv = None
            for g in range(GROUP):
                q_at, k_at, v_at = head_at(i, n, g)
                j = (i * KV_IN_PAIR + n) * GROUP + g
                p_low = p_ref[j]
                p = p_low.astype(F32)
                d_head = do[:, pl.ds(j * HEAD_SIZE, HEAD_SIZE)]
                weighted = p * nt(d_head, qkv_ref[:, v_at])
                ds = (weighted - p * jnp.sum(weighted, axis=1, keepdims=True)).astype(BF16)
                dqkv[:, q_at] = (nn(ds, qkv_ref[:, k_at]) * SCALE).astype(BF16)
                dk_part, dv_part = tn(ds, qkv_ref[:, q_at]), tn(p_low, d_head)
                dk = dk_part if dk is None else dk + dk_part
                dv = dv_part if dv is None else dv + dv_part
            dqkv[:, k_at] = (dk * SCALE).astype(BF16)
            dqkv[:, v_at] = dv.astype(BF16)
        send = pair.send(dqkv.at[:, cols], got_dqkv.at[:, cols], send_sem.at[1 + i], recv_sem.at[1 + i])
        send.start()
        sends.append(send)
    da = nt(dqkv[...], wq_v[me])
    grad_q[me] = tn(a_ref[...], dqkv[...]).astype(BF16)
    grad_o[...] = tn(o_ref[...], d_all[...]).astype(BF16)
    store_o = pltpu.make_async_copy(
        grad_o, grad_hbm.at[:, pl.ds(QUERY_WIDTH + 2 * KV_WIDTH, width)], store_sem.at[LOADS - 1])
    store_o.start()
    for send in sends[1:]:
        send.wait_recv()
    da = da + nt(got_dqkv[...], wq_v[peer])
    da_send[...] = jnp.where(me == 0, da[rows:], da[:rows]).astype(BF16)
    send_da = pair.send(da_send, got_da, send_sem.at[1 + PAIRS], recv_sem.at[1 + PAIRS])
    send_da.start()
    own_da = jnp.where(me == 0, da[:rows], da[rows:])
    grad_q[peer] = tn(a_ref[...], got_dqkv[...]).astype(BF16)
    stores = [store_o]
    for j in range(2):
        for at, local, size in head_columns(j):
            store = pltpu.make_async_copy(
                grad_q.at[j, :, pl.ds(local, size)], grad_hbm.at[:, pl.ds(at, size)],
                store_sem.at[len(stores) - 1])
            store.start()
            stores.append(store)
    send_da.wait_recv()
    other_da = got_da[...].astype(F32)
    h = h_ref[...].astype(F32)
    r1 = lax.rsqrt(jnp.mean(h * h, axis=1, keepdims=True) + EPS)
    halves = []
    total = jnp.zeros((rows, 1), F32)
    for j in range(2):
        cols = pl.ds(j * half, half)
        da_j = jnp.where(me == j, own_da, other_da)
        normed = h[:, j * half : (j + 1) * half] * r1
        gain_grads_ref[pl.ds(0, 1), cols] = jnp.sum(da_j * normed, axis=0, keepdims=True)
        scaled = da_j * gains_ref[pl.ds(0, 1), cols]
        total = total + jnp.sum(scaled * normed, axis=1, keepdims=True)
        halves.append((cols, scaled, normed))
    for cols, scaled, normed in halves:
        dh_ref[:, cols] = dh1_v[:, cols] + r1 * (scaled - normed * (total / width))
    for send in sends + [send_da]:
        send.wait_send()
    for store in stores:
        store.wait()


def attention_backward(layer, db, dout, h1, h, gains, a_half, qkv, p, o, weights, collective_id):
    rows, width = db.shape
    half, group = width // 2, 2 * rows
    cols = (QUERY_WIDTH + 2 * KV_WIDTH) // 2
    any_spec = pl.BlockSpec(memory_space=pl.ANY)
    vmem = pl.BlockSpec(memory_space=pltpu.VMEM)
    return pl.pallas_call(
        functools.partial(attention_backward_kernel, layer, rows, width),
        name="attention_backward",
        out_shape=(
            jax.ShapeDtypeStruct((rows, width), F32),
            jax.ShapeDtypeStruct((8, width), F32),
            jax.ShapeDtypeStruct((half, QUERY_WIDTH + 2 * KV_WIDTH + width), BF16),
        ),
        in_specs=[vmem] * 9 + [any_spec] * 4,
        out_specs=(vmem, vmem, any_spec),
        scratch_shapes=[
            pltpu.VMEM((2, half, cols), BF16),
            pltpu.VMEM((QUERY_WIDTH // 2, width), BF16),
            pltpu.VMEM((group, width), BF16),
            pltpu.VMEM((group, QUERY_WIDTH // 2), BF16),
            pltpu.VMEM((group, cols), BF16),
            pltpu.VMEM((group, cols), BF16),
            pltpu.VMEM((rows, half), BF16),
            pltpu.VMEM((rows, half), BF16),
            pltpu.VMEM((rows, width), F32),
            pltpu.VMEM((2, half, cols), BF16),
            pltpu.VMEM((QUERY_WIDTH // 2, width), BF16),
            pltpu.SemaphoreType.DMA((LOADS,)),
            pltpu.SemaphoreType.DMA((LOADS,)),
            pltpu.SemaphoreType.DMA((2 + PAIRS,)),
            pltpu.SemaphoreType.DMA((2 + PAIRS,)),
        ],
        cost_estimate=COST,
        compiler_params=pltpu.CompilerParams(
            collective_id=collective_id, has_side_effects=True, vmem_limit_bytes=VMEM_BYTES),
    )(db, dout, h1, h, gains, a_half, qkv, p, o, *weights)


def dot(a, b, dims):
    return lax.dot_general(a, b, (dims, ((), ())), preferred_element_type=F32)


def rms_scale(values):
    return lax.rsqrt(jnp.mean(values * values, axis=-1, keepdims=True) + EPS)


def swap_cores(value):
    return lax.ppermute(value, "section", [(0, 1), (1, 0)])


def both_layers(own):
    return lax.all_gather(own, "section", axis=0, tiled=False)


def document_mask(sequence_lengths, rows):
    pos = jnp.arange(rows, dtype=jnp.int32)
    ends = jnp.cumsum(sequence_lengths)
    doc = jnp.sum((pos[:, None] >= ends[None, :]).astype(jnp.int32), axis=1)
    return (doc[:, None] == doc[None, :]) & (pos[None, :] <= pos[:, None])


def plain_attention(qkv, allowed, heads, kv_heads):
    rows = qkv.shape[0]
    group = heads // kv_heads
    q = qkv[:, : heads * HEAD_SIZE].reshape(rows, kv_heads, group, HEAD_SIZE)
    k = qkv[:, heads * HEAD_SIZE : (heads + kv_heads) * HEAD_SIZE].reshape(rows, kv_heads, HEAD_SIZE)
    v = qkv[:, (heads + kv_heads) * HEAD_SIZE :].reshape(rows, kv_heads, HEAD_SIZE)
    s = jnp.einsum("qhgd,khd->hgqk", q, k, preferred_element_type=F32) * HEAD_SIZE ** (-0.5)
    s = jnp.where(allowed[None, None], s, MASKED_SCORE)
    ex = jnp.exp(s - jnp.max(s, axis=-1, keepdims=True))
    p = ex / jnp.sum(ex, axis=-1, keepdims=True)
    o = jnp.einsum("hgqk,khd->qhgd", p.astype(BF16), v, preferred_element_type=F32)
    return o.reshape(rows, heads * HEAD_SIZE).astype(BF16), p, (q, k, v)


def plain_attention_backward(do, p, heads_in):
    q, k, v = heads_in
    rows = q.shape[0]
    dh = do.reshape(q.shape)
    dv = jnp.einsum("hgqk,qhgd->khd", p.astype(BF16), dh, preferred_element_type=F32)
    dp = jnp.einsum("qhgd,khd->hgqk", dh, v, preferred_element_type=F32)
    ds = (p * (dp - jnp.sum(p * dp, axis=-1, keepdims=True))).astype(BF16)
    dq = jnp.einsum("hgqk,khd->qhgd", ds, k, preferred_element_type=F32) * HEAD_SIZE ** (-0.5)
    dk = jnp.einsum("hgqk,qhgd->khd", ds, q, preferred_element_type=F32) * HEAD_SIZE ** (-0.5)
    return jnp.concatenate(
        [dq.reshape(rows, -1), dk.reshape(rows, -1), dv.reshape(rows, -1)], axis=1
    ).astype(BF16)


def column_parts(n, j):
    qw, kw = QUERY_WIDTH // n, KV_WIDTH // n
    return (
        (j * qw, qw),
        (QUERY_WIDTH + j * kw, kw),
        (QUERY_WIDTH + KV_WIDTH + j * kw, kw),
    )


def plain_shards(
    edge_inputs, seq_lengths, routes, w_qkv, w_out, w_router, gain_attn, gain_moe, w_gate_up, w_down
):
    sec = lax.axis_index("section")
    owner = lax.axis_index("expert")
    shard_pos = lax.axis_index("shard")
    n_shard = lax.axis_size("shard")
    n_owner = lax.axis_size("expert")
    rows, width = edge_inputs.shape[2], edge_inputs.shape[3]
    experts = w_router.shape[2]
    group_rows = rows * n_shard
    half = width // n_shard
    heads, kv_heads = QUERY_HEADS // n_shard, KEY_VALUE_HEADS // n_shard

    def pick(array, index):
        return lax.dynamic_index_in_dim(array, index, 0, keepdims=False)

    own_edge, other_edge = pick(edge_inputs[0], sec), swap_cores(pick(edge_inputs[0], 1 - sec))
    x_in = jnp.where(sec == 0, own_edge, other_edge)
    dy = jnp.where(sec == 0, other_edge, own_edge)
    own_routes, other_routes = pick(routes[0], sec), swap_cores(pick(routes[0], 1 - sec))
    layer_routes = (
        jnp.where(sec == 0, own_routes, other_routes),
        jnp.where(sec == 0, other_routes, own_routes),
    )
    allowed = document_mask(pick(seq_lengths, sec)[0], group_rows)
    wq = both_layers(w_qkv[0])
    wo = both_layers(w_out[0])
    small = jnp.concatenate([w_router[0], gain_attn[0][:, None], gain_moe[0][:, None]], axis=1)
    small = lax.all_gather(both_layers(small), "shard", axis=1, tiled=True)
    wgu = both_layers(w_gate_up[0])
    wd = both_layers(w_down[0])
    columns = jnp.arange(experts, dtype=jnp.int32)
    route_masks = [
        jnp.any(r[:, :, None] == columns[None, None, :], axis=1).astype(BF16) for r in layer_routes
    ]
    plane_masks = [lax.all_gather(m, "expert", axis=0, tiled=True) for m in route_masks]

    def forward(layer, h):
        gain_a = small[layer, :, experts].astype(F32)[None, :]
        gain_m = small[layer, :, experts + 1].astype(F32)[None, :]
        router = small[layer, :, :experts]
        r1 = rms_scale(h)
        a = (h * r1 * gain_a).astype(BF16)
        a_half = lax.all_to_all(
            a.reshape(rows, n_shard, half), "shard", split_axis=1, concat_axis=0, tiled=True
        ).reshape(group_rows, half)
        blocks = []
        for j in range(n_shard):
            blocks.append(
                jnp.concatenate(
                    [
                        dot(a_half, wq[layer, :, at : at + size], ((1,), (0,)))
                        for at, size in column_parts(n_shard, j)
                    ],
                    axis=1,
                ).astype(BF16)
            )
        qkv = lax.psum_scatter(jnp.stack(blocks), "shard", scatter_dimension=0, tiled=False)
        o, p, heads_in = plain_attention(qkv, allowed, heads, kv_heads)
        part = dot(o, wo[layer], ((1,), (0,))).astype(BF16)
        h1 = h + lax.psum_scatter(part, "shard", scatter_dimension=0, tiled=True).astype(F32)
        r2 = rms_scale(h1)
        b = (h1 * r2 * gain_m).astype(BF16)
        b_all = lax.all_gather(b, "expert", axis=0, tiled=True)
        mask = plane_masks[layer].astype(F32) > 0
        logits = jnp.where(mask, dot(b_all, router, ((1,), (0,))), MASKED_SCORE)
        ex = jnp.where(mask, jnp.exp(logits - jnp.max(logits, axis=1, keepdims=True)), 0.0)
        gates = ex / jnp.sum(ex, axis=1, keepdims=True)
        own_gates = lax.dynamic_slice_in_dim(gates, owner * EXP_DEV, EXP_DEV, 1)
        kept, scaled = [], []
        for j in range(EXP_DEV):
            gu = dot(b_all, wgu[layer, j], ((1,), (0,)))
            g, u = gu[:, :FF], gu[:, FF:]
            scaled.append((g * jax.nn.sigmoid(g) * u * own_gates[:, j : j + 1]).astype(BF16))
            kept.append(gu.astype(BF16))
        scaled = jnp.concatenate(scaled, axis=1)
        moe_part = dot(scaled, wd[layer].reshape(EXP_DEV * FF, width), ((1,), (0,))).astype(BF16)
        moe = lax.psum_scatter(moe_part, "expert", scatter_dimension=0, tiled=True).astype(F32)
        state = (h, r1, a_half, p, heads_in, o, h1, r2, b_all, own_gates, kept, scaled, moe)
        return h1 + moe, state

    def backward(layer, dout, dout_low, state):
        h, r1, a_half, p, heads_in, o, h1, r2, b_all, own_gates, kept, scaled, moe = state
        gain_a = small[layer, :, experts].astype(F32)[None, :]
        gain_m = small[layer, :, experts + 1].astype(F32)[None, :]
        router = small[layer, :, :experts]
        own_router = lax.dynamic_slice_in_dim(router, owner * EXP_DEV, EXP_DEV, 1)
        total = lax.all_gather(jnp.sum(dout * moe, axis=1), "expert", axis=0, tiled=True)
        dout_all = lax.all_gather(dout_low, "expert", axis=0, tiled=True)
        dgus, dcs = [], []
        for j in range(EXP_DEV):
            gate = own_gates[:, j : j + 1]
            g, u = kept[j][:, :FF].astype(F32), kept[j][:, FF:].astype(F32)
            sig = jax.nn.sigmoid(g)
            silu = g * sig
            dz = dot(dout_all, wd[layer, j], ((1,), (1,)))
            dgate = jnp.sum(dz * silu * u, axis=1, keepdims=True)
            dcs.append(gate * (dgate - total[:, None]))
            dz = dz * gate
            dgus.append(
                jnp.concatenate(
                    [dz * u * sig * (1.0 + g * (1.0 - sig)), dz * silu], axis=1
                ).astype(BF16)
            )
        dc = jnp.concatenate(dcs, axis=1)
        db_part = sum(dot(dgus[j], wgu[layer, j], ((1,), (1,))) for j in range(EXP_DEV))
        for j in range(EXP_DEV):
            db_part = db_part + dc[:, j : j + 1] * own_router[:, j].astype(F32)[None, :]
        db = lax.psum_scatter(
            db_part.astype(BF16), "expert", scatter_dimension=0, tiled=True
        ).astype(F32)
        grad_down = dot(scaled, dout_all, ((0,), (0,))).reshape(EXP_DEV, FF, width)
        grad_gu = jnp.stack([dot(b_all, dgus[j], ((0,), (0,))) for j in range(EXP_DEV)])
        grad_router = lax.dot_general(
            dc, b_all.astype(F32), (((0,), (0,)), ((), ())), precision=lax.Precision.HIGHEST
        )
        normed = h1 * r2
        grad_gain_m = jnp.sum(db * normed, axis=0)
        scaled_db = db * gain_m
        dh1 = dout + r2 * (scaled_db - normed * jnp.mean(scaled_db * normed, axis=1, keepdims=True))
        dattn = lax.all_gather(dh1.astype(BF16), "shard", axis=0, tiled=True)
        do = dot(dattn, wo[layer], ((1,), (1,))).astype(BF16)
        grad_out = dot(o, dattn, ((0,), (0,)))
        dqkv = lax.all_gather(plain_attention_backward(do, p, heads_in), "shard", axis=0, tiled=False)
        da = 0.0
        grad_qkv = []
        for part in range(3):
            grad_qkv.append([])
        for j in range(n_shard):
            at_local = 0
            for part, (at, size) in enumerate(column_parts(n_shard, j)):
                piece = dqkv[j, :, at_local : at_local + size]
                at_local += size
                da = da + dot(piece, wq[layer, :, at : at + size], ((1,), (1,)))
                grad_qkv[part].append(dot(a_half, piece, ((0,), (0,))))
        grad_qkv = jnp.concatenate([x for part in grad_qkv for x in part], axis=1)
        da = lax.all_to_all(
            da.astype(BF16), "shard", split_axis=0, concat_axis=1, tiled=True
        ).astype(F32)
        normed = h * r1
        grad_gain_a = jnp.sum(da * normed, axis=0)
        scaled_da = da * gain_a
        dh = dh1 + r1 * (scaled_da - normed * jnp.mean(scaled_da * normed, axis=1, keepdims=True))
        return dh, (grad_qkv, grad_out, grad_router, grad_gain_a, grad_gain_m, grad_gu, grad_down)

    out0, state0 = forward(0, x_in.astype(F32))
    mid = out0.astype(BF16).astype(F32)
    final, state1 = forward(1, mid)
    dh_one, grads1 = backward(1, dy.astype(F32), dy, state1)
    low = dh_one.astype(BF16)
    dh_zero, grads0 = backward(0, low.astype(F32), low, state0)

    def half_sum(grad):
        low_grad = grad.astype(BF16)
        halves = low_grad.reshape((2, -1) + low_grad.shape[1:])
        got = swap_cores(pick(halves, 1 - sec))
        return (pick(halves, sec).astype(F32) + got.astype(F32)).astype(BF16)

    def to_owner(half0, half1):
        keep = jnp.where(sec == 0, half0, half1)
        got = swap_cores(jnp.where(sec == 0, half1, half0))
        first = jnp.where(sec == 0, keep, got)
        second = jnp.where(sec == 0, got, keep)
        return jnp.concatenate([first, second], axis=0).astype(F32)

    attn_halves, exp_halves = [], []
    for grads in (grads0, grads1):
        attn = half_sum(jnp.concatenate([grads[0], grads[1]], axis=1))
        attn_halves.append(lax.psum(attn, "expert"))
        exp_halves.append(tuple(lax.psum(half_sum(g), "shard") for g in (grads[5], grads[6])))
    attn = to_owner(*attn_halves)
    grad_qkv, grad_out = attn[:, : w_qkv.shape[2]], attn[:, w_qkv.shape[2] :]
    grad_gu = to_owner(exp_halves[0][0], exp_halves[1][0])
    grad_down = to_owner(exp_halves[0][1], exp_halves[1][1])

    tiny = []
    for grads in (grads0, grads1):
        hot = jnp.arange(experts)[:, None] == owner * EXP_DEV + jnp.arange(EXP_DEV)[None, :]
        router = sum(
            jnp.where(hot[:, j : j + 1], grads[2][j][None, :], 0.0) for j in range(EXP_DEV)
        )
        tiny.append(jnp.concatenate([router, grads[3][None, :], grads[4][None, :]], axis=0))
    tiny = lax.psum(jnp.stack(tiny), ("section", "expert", "shard"))
    tiny = lax.dynamic_slice_in_dim(pick(tiny, sec), shard_pos * half, half, 1)

    send = jnp.where(sec == 0, final, dh_zero)
    keep = jnp.where(sec == 0, dh_zero, final)
    got = swap_cores(send)
    edge = jnp.where(sec == 0, jnp.stack([keep, got]), jnp.stack([got, keep]))
    return (
        edge[None],
        grad_qkv[None],
        grad_out[None],
        tiny[:experts].T[None],
        tiny[experts][None],
        tiny[experts + 1][None],
        grad_gu[None],
        grad_down[None],
    )


def kernel_shards(
    edge_inputs, seq_lengths, routes, w_qkv, w_out, w_router, gain_attn, gain_moe, w_gate_up, w_down
):
    sec = lax.axis_index("section")
    owner = lax.axis_index("expert")
    shard_pos = lax.axis_index("shard")
    rows, width = edge_inputs.shape[2], edge_inputs.shape[3]
    experts = w_router.shape[2]
    half = width // 2
    attn_cols = w_qkv.shape[2] + w_out.shape[2]

    def pick(array, index):
        return lax.dynamic_index_in_dim(array, index, 0, keepdims=False)

    def swap_shards(value):
        return lax.ppermute(value, "shard", [(0, 1), (1, 0)])

    def by_core(own, other):
        return jnp.where(sec == 0, own, other), jnp.where(sec == 0, other, own)

    small = jnp.concatenate([w_router[0].T, gain_attn, gain_moe], axis=0)
    own_small = jnp.concatenate([small, swap_shards(small)], axis=0)
    own_small = jnp.where(
        shard_pos == 0,
        jnp.concatenate([own_small[: experts + 2], own_small[experts + 2 :]], axis=1),
        jnp.concatenate([own_small[experts + 2 :], own_small[: experts + 2]], axis=1),
    )
    layer_small = by_core(own_small, swap_cores(own_small))
    x_in, dy = by_core(pick(edge_inputs[0], sec), swap_cores(pick(edge_inputs[0], 1 - sec)))
    layer_routes = by_core(pick(routes[0], sec), swap_cores(pick(routes[0], 1 - sec)))
    allowed = document_mask(pick(seq_lengths, sec)[0], 2 * rows).astype(F32)
    attn_weights = (w_qkv[0], swap_cores(w_qkv[0]), w_out[0], swap_cores(w_out[0]))
    expert_weights = (
        w_gate_up[0], swap_cores(w_gate_up[0]), w_down[0], swap_cores(w_down[0])
    )
    gains, routers, masks = [], [], []
    for layer in range(2):
        gains.append(
            jnp.pad(layer_small[layer][experts:].astype(F32), ((0, 8 - 2), (0, 0)))
        )
        router = layer_small[layer][:experts]
        router = jnp.concatenate([router, router], axis=0)
        routers.append(jnp.pad(router, ((0, LANES - 2 * experts), (0, 0))))
        lane = jnp.arange(LANES, dtype=jnp.int32)[None, :]
        hot = jnp.any(layer_routes[layer][:, :, None] == lane[None] % experts, axis=1)
        masks.append(
            jnp.where(hot & (lane < 2 * experts), 1.0 + (lane >= experts), 0.0).astype(F32)
        )

    def forward(layer, h):
        block, h1, *attn_state = attention_forward(
            layer, h, allowed, gains[layer], routers[layer], masks[layer], attn_weights, 1 + layer
        )
        moe, *expert_state = moe_forward(layer, block, expert_weights, experts, 3 + layer)
        return h1 + moe, (h, h1, moe, attn_state, expert_state)

    def backward(layer, dout, state, beside):
        h, h1, moe, attn_state, expert_state = state
        outer = jnp.sum(dout.astype(F32) * moe, axis=1, keepdims=True)
        block = with_lanes(dout, split_terms(outer))
        own_router = lax.dynamic_slice_in_dim(
            layer_small[layer].astype(F32), owner * EXP_DEV, EXP_DEV, 0
        )
        own_router = jnp.pad(own_router, ((0, 8 - EXP_DEV), (0, 0)))
        db, grad_gu, grad_down, grad_router, *landed = moe_backward(
            layer, block, own_router, expert_weights, expert_state, beside, experts, 5 + layer
        )
        dh, grad_gains, grad_attn = attention_backward(
            layer, db, dout, h1, h, gains[layer], *attn_state, attn_weights, 7 + layer
        )
        lane = jnp.arange(LANES, dtype=jnp.int32)[None, :]
        columns = jnp.where(lane == experts, grad_gains[0][:, None], 0.0)
        columns = jnp.where(lane == experts + 1, grad_gains[1][:, None], columns)
        for j in range(EXP_DEV):
            column = grad_router[:, j : j + 1] + grad_router[:, EXP_DEV + j : EXP_DEV + j + 1]
            columns = jnp.where(lane == owner * EXP_DEV + j, column, columns)
        places = LINE * SIDE
        sub = half // (2 * places)
        grad_attn = grad_attn.reshape(places, 2, sub, attn_cols)
        columns = columns.astype(BF16).reshape(2, places, 2, sub, LANES)
        return dh, grad_attn, columns, (grad_gu, grad_down), landed

    out0, state0 = forward(0, x_in)
    final, state1 = forward(1, out0.astype(BF16))
    dh_one, attn1, columns1, experts1, _ = backward(1, dy, state1, ())
    dh_zero, attn0, columns0, experts0, landed1 = backward(
        0, dh_one.astype(BF16), state0, experts1
    )
    sums1 = [
        (own.astype(F32) + got.astype(F32)).astype(BF16) for own, got in zip(experts1, landed1)
    ]
    moved1 = [lax.ppermute(value, "section", [(0, 1)]) for value in sums1]
    attn, gu_own, down_own, gu_got, down_got = reduce_gradients(
        attn1, attn0, columns1, columns0, *experts0, 9
    )
    attn = attn.astype(F32)
    grad_qkv, grad_out = attn[:, : w_qkv.shape[2]], attn[:, w_qkv.shape[2] : attn_cols]
    tiny = attn[:, attn_cols : attn_cols + experts + 2]

    def both_experts(own, got, layer_one, moved):
        first = jnp.where(sec == 0, own, moved)
        second = jnp.where(sec == 0, got, layer_one)
        return jnp.stack([first, second]).astype(F32)

    grad_gu = both_experts(gu_own, gu_got, sums1[0], moved1[0])
    grad_down = both_experts(down_own, down_got, sums1[1], moved1[1])

    send = jnp.where(sec == 0, final, dh_zero)
    keep = jnp.where(sec == 0, dh_zero, final)
    got = swap_cores(send)
    edge = jnp.where(sec == 0, jnp.stack([keep, got]), jnp.stack([got, keep]))
    return (
        edge[None],
        grad_qkv[None],
        grad_out[None],
        tiny[:, :experts][None],
        tiny[:, experts][None],
        tiny[:, experts + 1][None],
        grad_gu[None],
        grad_down[None],
    )


def shards(*arrays):
    if lax.axis_size("expert") == LINE * SIDE and lax.axis_size("shard") == 2:
        return kernel_shards(*arrays)
    return plain_shards(*arrays)


def solution(mesh):
    in_specs = (
        P("section", None, ("expert", "shard"), None),
        P(None, "expert", None),
        P("section", None, ("expert", "shard"), None),
        P("section", "shard", None),
        P("section", "shard", None),
        P("section", "shard", None),
        P("section", "shard"),
        P("section", "shard"),
        P("section", "expert", None, None),
        P("section", "expert", None, None),
    )
    out_specs = (
        P("section", None, ("expert", "shard"), None),
        P("section", "shard", None),
        P("section", "shard", None),
        P("section", "shard", None),
        P("section", "shard"),
        P("section", "shard"),
        P("section", "expert", None, None),
        P("section", "expert", None, None),
    )
    return jax.shard_map(shards, mesh=mesh, in_specs=in_specs, out_specs=out_specs, check_vma=False)
```

```python
import functools

import jax
import jax.numpy as jnp
from jax import lax
from jax.experimental import pallas as pl
from jax.experimental.pallas import tpu as pltpu
from jax.sharding import PartitionSpec as P

QUERY_HEADS = 24
KEY_VALUE_HEADS = 8
HEAD_SIZE = 64
FF = 512
TOP = 8
EXP_DEV = 2
EPS = 1e-05
MASKED_SCORE = -1e30
QUERY_WIDTH = QUERY_HEADS * HEAD_SIZE
KV_WIDTH = KEY_VALUE_HEADS * HEAD_SIZE
F32 = jnp.float32
BF16 = jnp.bfloat16
MESH = pl.DeviceIdType.MESH
LINE = 4
SIDE = 2
LANES = 128
HALVES = 2
TILE = 256
VMEM_BYTES = 60 * 2**20
COST = pl.CostEstimate(flops=10**11, bytes_accessed=2**24, transcendentals=0)


def chunk_order(z, t):
    near = z + 1 - 2 * lax.rem(z, 2)
    third = jnp.where(z < 2, 2, 1)
    last = jnp.where(z < 2, 3, 0)
    return jnp.where(t == 0, z, jnp.where(t == 1, near, jnp.where(t == 2, third, last)))


def sum_order(z, i):
    first = jnp.where((z == 0) | (z == 2), 1, 2)
    second = jnp.where(z == 0, 2, jnp.where(z == 1, 3, jnp.where(z == 2, 0, 1)))
    third = jnp.where(z == 0, 3, jnp.where(z == 1, 0, jnp.where(z == 2, 3, 0)))
    return jnp.where(i == 0, first, jnp.where(i == 1, second, third))


class Plane:
    def __init__(self, rows, refs):
        (self.gathered, self.parts, self.from_side, self.from_low, self.from_high, self.sums,
         self.line_send, self.gather_recv, self.side_send, self.side_recv,
         self.sum_send, self.low_recv, self.high_recv) = refs
        self.sub = rows // HALVES
        self.both = SIDE * self.sub
        self.sec, self.owner, self.shard = (lax.axis_index(n) for n in ("section", "expert", "shard"))
        self.z, self.x = lax.div(self.owner, SIDE), lax.rem(self.owner, SIDE)
        self.inner = ((self.z > 0) & (self.z < LINE - 1)).astype(jnp.int32)

    def device(self, z, x):
        return (self.sec, z * SIDE + x, self.shard)

    def other_core(self):
        return (1 - self.sec, self.owner, self.shard)

    def other_shard(self):
        return (self.sec, self.owner, 1 - self.shard)

    def chunk(self, c, h):
        return pl.ds(pl.multiple_of((c * HALVES + h) * self.both, self.both), self.both)

    def block(self, c, h, x):
        return pl.ds(pl.multiple_of((c * HALVES + h) * self.both + x * self.sub, self.sub), self.sub)

    def barrier(self, *others):
        z, x = self.z, self.x
        sem = pltpu.get_barrier_semaphore()

        def greet(device):
            pl.semaphore_signal(sem, inc=1, device_id=device, device_id_type=MESH)

        for other in others:
            greet(other)
        greet(self.device(z, 1 - x))
        pl.when(z > 0)(lambda: greet(self.device(z - 1, x)))
        pl.when(z < LINE - 1)(lambda: greet(self.device(z + 1, x)))
        pl.semaphore_wait(sem, 2 + len(others) + self.inner)

    def place(self, block_ref):
        for h in range(HALVES):
            self.gathered[self.block(self.z, h, self.x)] = block_ref[pl.ds(h * self.sub, self.sub)]

    def gather_copy(self, way, c, h, x, device):
        ref = self.gathered.at[self.block(c, h, x)]
        q = c * HALVES + h
        return pltpu.make_async_remote_copy(
            src_ref=ref, dst_ref=ref, send_sem=self.line_send.at[way, q],
            recv_sem=self.gather_recv.at[q, x], device_id=device, device_id_type=MESH)

    def forward_up(self, c, h):
        return self.gather_copy(0, c, h, self.x, self.device(self.z + 1, self.x))

    def forward_down(self, c, h):
        return self.gather_copy(1, c, h, self.x, self.device(self.z - 1, self.x))

    def forward_side(self, c, h):
        return self.gather_copy(2, c, h, self.x, self.device(self.z, 1 - self.x))

    def start_gather(self):
        z = self.z
        for h in range(HALVES):
            pl.when(z < LINE - 1)(lambda h=h: self.forward_up(z, h).start())
            pl.when(z > 0)(lambda h=h: self.forward_down(z, h).start())
            self.forward_side(z, h).start()

    def relay(self, t, h):
        z = self.z

        @pl.when((t > 0) & (z - t >= 0))
        def _():
            c = z - t
            self.forward_side(c, h).wait_recv()
            pl.when(z < LINE - 1)(lambda: self.forward_up(c, h).start())
            self.forward_side(c, h).start()

        @pl.when((t > 0) & (z + t <= LINE - 1))
        def _():
            c = z + t
            self.forward_side(c, h).wait_recv()
            pl.when(z > 0)(lambda: self.forward_down(c, h).start())
            self.forward_side(c, h).start()

    def wait_side_block(self, c, h):
        self.gather_copy(2, c, h, 1 - self.x, self.device(self.z, 1 - self.x)).wait_recv()

    def side_copy(self, c, h):
        q = c * HALVES + h
        return pltpu.make_async_remote_copy(
            src_ref=self.parts.at[self.block(c, h, 1 - self.x)], dst_ref=self.from_side.at[q],
            send_sem=self.side_send.at[q], recv_sem=self.side_recv.at[q],
            device_id=self.device(self.z, 1 - self.x), device_id_type=MESH)

    def up_copy(self, c, h):
        q = c * HALVES + h
        return pltpu.make_async_remote_copy(
            src_ref=self.sums.at[q], dst_ref=self.from_low.at[q], send_sem=self.sum_send.at[q],
            recv_sem=self.low_recv.at[q], device_id=self.device(self.z + 1, self.x), device_id_type=MESH)

    def down_copy(self, c, h):
        q = c * HALVES + h
        return pltpu.make_async_remote_copy(
            src_ref=self.sums.at[q], dst_ref=self.from_high.at[q], send_sem=self.sum_send.at[q],
            recv_sem=self.high_recv.at[q], device_id=self.device(self.z - 1, self.x), device_id_type=MESH)

    def own_part(self, c, h):
        return (self.parts[self.block(c, h, self.x)].astype(F32)
                + self.from_side[c * HALVES + h].astype(F32))

    def pass_sum(self, t, h):
        i = t - 3 - self.inner
        pl.when((i >= 0) & (i < LINE - 1))(lambda: self.pass_chunk(sum_order(self.z, i), h))

    def pass_chunk(self, c, h):
        z = self.z
        q = c * HALVES + h
        self.side_copy(c, h).wait_recv()

        @pl.when(c > z)
        def _():
            @pl.when(z > 0)
            def _():
                self.up_copy(c, h).wait_recv()
                self.sums[q] = (self.own_part(c, h) + self.from_low[q].astype(F32)).astype(BF16)

            @pl.when(z == 0)
            def _():
                self.sums[q] = self.own_part(c, h).astype(BF16)

            self.up_copy(c, h).start()

        @pl.when(c < z)
        def _():
            @pl.when(z < LINE - 1)
            def _():
                self.down_copy(c, h).wait_recv()
                self.sums[q] = (self.own_part(c, h) + self.from_high[q].astype(F32)).astype(BF16)

            @pl.when(z == LINE - 1)
            def _():
                self.sums[q] = self.own_part(c, h).astype(BF16)

            self.down_copy(c, h).start()

    def finish_sum(self, h, out_ref):
        z = self.z
        q = z * HALVES + h
        rows = pl.ds(pl.multiple_of(h * self.sub, self.sub), self.sub)
        self.side_copy(z, h).wait_recv()
        out_ref[rows] = self.own_part(z, h)

        @pl.when(z > 0)
        def _():
            self.up_copy(z, h).wait_recv()
            out_ref[rows] += self.from_low[q].astype(F32)

        @pl.when(z < LINE - 1)
        def _():
            self.down_copy(z, h).wait_recv()
            out_ref[rows] += self.from_high[q].astype(F32)

    def finish_piece(self, h, out_ref):
        z = self.z
        q = z * HALVES + h
        self.side_copy(z, h).wait_recv()

        @pl.when(z == 0)
        def _():
            self.down_copy(z, h).wait_recv()
            out_ref[h] = (self.own_part(z, h) + self.from_high[q].astype(F32)).astype(BF16)

        @pl.when(z == LINE - 1)
        def _():
            self.up_copy(z, h).wait_recv()
            out_ref[h] = (self.own_part(z, h) + self.from_low[q].astype(F32)).astype(BF16)

        @pl.when((z > 0) & (z < LINE - 1))
        def _():
            self.up_copy(z, h).wait_recv()
            self.down_copy(z, h).wait_recv()
            total = self.own_part(z, h) + self.from_low[q].astype(F32)
            out_ref[h] = (total + self.from_high[q].astype(F32)).astype(BF16)

    def drain(self):
        z = self.z

        def one(q, carry):
            c, h = lax.div(q, HALVES), lax.rem(q, HALVES)
            pl.when((z < LINE - 1) & (c <= z))(lambda: self.forward_up(c, h).wait_send())
            pl.when((z > 0) & (c >= z))(lambda: self.forward_down(c, h).wait_send())
            self.forward_side(c, h).wait_send()
            self.side_copy(c, h).wait_send()
            pl.when(c > z)(lambda: self.up_copy(c, h).wait_send())
            pl.when(c < z)(lambda: self.down_copy(c, h).wait_send())
            return carry

        lax.fori_loop(0, LINE * HALVES, one, 0)


def plane_scratch(rows, width, wide):
    count = LINE * HALVES
    block = pltpu.VMEM((count, rows // HALVES, width), BF16)
    return [
        pltpu.VMEM((LINE * SIDE * rows, wide), BF16),
        pltpu.VMEM((LINE * SIDE * rows, width), BF16),
        block, block, block, block,
        pltpu.SemaphoreType.DMA((3, count)),
        pltpu.SemaphoreType.DMA((count, SIDE)),
        pltpu.SemaphoreType.DMA((count,)),
        pltpu.SemaphoreType.DMA((count,)),
        pltpu.SemaphoreType.DMA((count,)),
        pltpu.SemaphoreType.DMA((count,)),
        pltpu.SemaphoreType.DMA((count,)),
    ]


def lane_tile(at, size=TILE):
    return pl.ds(pl.multiple_of(at * size, size), size)


def nn(a, b):
    return jnp.dot(a, b, preferred_element_type=F32)


def nt(a, b):
    return lax.dot_general(a, b, (((1,), (1,)), ((), ())), preferred_element_type=F32)


def tn(a, b):
    return lax.dot_general(a, b, (((0,), (0,)), ((), ())), preferred_element_type=F32)


def pick_lane(block, wanted):
    lane = lax.broadcasted_iota(jnp.int32, block.shape, 1)
    hot = lane == wanted[0]
    for other in wanted[1:]:
        hot = hot | (lane == other)
    return jnp.sum(jnp.where(hot, block, 0.0), axis=1, keepdims=True)


def own_gates(block, owner, experts):
    block = block.astype(F32)
    return [
        pick_lane(block, (owner * EXP_DEV + j, experts + owner * EXP_DEV + j)) for j in range(EXP_DEV)
    ]


def load_layer(layer, sec, own, other, dst, sem):
    copies = [pltpu.make_async_copy(own, dst, sem), pltpu.make_async_copy(other, dst, sem)]
    pl.when(sec == layer)(lambda: copies[0].start())
    pl.when(sec != layer)(lambda: copies[1].start())
    return copies[0]


def load_experts(layer, sec, gu, gu_other, down, down_other, gu_v, down_v, sems):
    loads = [load_layer(layer, sec, gu, gu_other, gu_v, sems.at[0])]
    for j in range(EXP_DEV):
        loads.append(load_layer(
            layer, sec, down.at[j], down_other.at[j], down_v.at[pl.ds(j * FF, FF)], sems.at[1 + j]))
    return loads


def moe_forward_kernel(layer, experts, rows, width, block_ref, gu_hbm, gu_other, down_hbm, down_other,
                       moe_ref, rows_hbm, kept_hbm, scaled_hbm,
                       gu_v, down_v, kept, scaled, load_sem, store_sem, *plane_refs):
    plane = Plane(rows, plane_refs)
    gathered, parts = plane.gathered, plane.parts
    loads = load_experts(layer, plane.sec, gu_hbm, gu_other, down_hbm, down_other, gu_v, down_v, load_sem)
    plane.place(block_ref)
    plane.barrier()
    plane.start_gather()
    for load in loads:
        load.wait()

    def stores(c, h):
        q, at = c * HALVES + h, plane.chunk(c, h)
        return [
            pltpu.make_async_copy(gathered.at[at], rows_hbm.at[at], store_sem.at[0, q]),
            pltpu.make_async_copy(kept.at[at], kept_hbm.at[at], store_sem.at[1, q]),
            pltpu.make_async_copy(scaled.at[at], scaled_hbm.at[at], store_sem.at[2, q]),
        ]

    def step(k, carry):
        t, h = lax.div(k, HALVES), lax.rem(k, HALVES)
        plane.relay(t, h)
        plane.pass_sum(t, h)
        pl.when(t > 0)(lambda: work(chunk_order(plane.z, t - 1), h))
        return carry

    def work(c, h):
        at = plane.chunk(c, h)
        plane.wait_side_block(c, h)
        gates = own_gates(gathered[at, pl.ds(width, LANES)], plane.owner, experts)
        for j in range(EXP_DEV):
            for f in range(FF // TILE):
                data = gathered[at, pl.ds(0, width)]
                low, high = j * 2 * FF + f * TILE, j * 2 * FF + FF + f * TILE
                g = nn(data, gu_v[j, :, pl.ds(f * TILE, TILE)])
                u = nn(data, gu_v[j, :, pl.ds(FF + f * TILE, TILE)])
                z = g * jax.nn.sigmoid(g) * u * gates[j]
                scaled[at, pl.ds(j * FF + f * TILE, TILE)] = z.astype(BF16)
                kept[at, pl.ds(low, TILE)] = g.astype(BF16)
                kept[at, pl.ds(high, TILE)] = u.astype(BF16)
        for n in range(width // TILE):
            parts[at, pl.ds(n * TILE, TILE)] = nn(
                scaled[at, :], down_v[:, pl.ds(n * TILE, TILE)]).astype(BF16)
        plane.side_copy(c, h).start()
        for store in stores(c, h):
            store.start()

    lax.fori_loop(0, (LINE + 1) * HALVES, step, 0)

    def tail(k, carry):
        plane.pass_sum(lax.div(k, HALVES), lax.rem(k, HALVES))
        return carry

    lax.fori_loop((LINE + 1) * HALVES, (LINE + 3) * HALVES, tail, 0)

    def finish(h, carry):
        plane.finish_sum(h, moe_ref)
        return carry

    lax.fori_loop(0, HALVES, finish, 0)
    plane.drain()

    def stored(q, carry):
        for store in stores(lax.div(q, HALVES), lax.rem(q, HALVES)):
            store.wait()
        return carry

    lax.fori_loop(0, LINE * HALVES, stored, 0)


def moe_forward(layer, block, weights, experts, collective_id):
    rows, wide = block.shape
    width = wide - LANES
    total = LINE * SIDE * rows
    any_spec = pl.BlockSpec(memory_space=pl.ANY)
    vmem = pl.BlockSpec(memory_space=pltpu.VMEM)
    return pl.pallas_call(
        functools.partial(moe_forward_kernel, layer, experts, rows, width),
        name="moe_forward",
        out_shape=(
            jax.ShapeDtypeStruct((rows, width), F32),
            jax.ShapeDtypeStruct((total, wide), BF16),
            jax.ShapeDtypeStruct((total, EXP_DEV * 2 * FF), BF16),
            jax.ShapeDtypeStruct((total, EXP_DEV * FF), BF16),
        ),
        in_specs=[vmem] + [any_spec] * 4,
        out_specs=(vmem, any_spec, any_spec, any_spec),
        scratch_shapes=[
            pltpu.VMEM((EXP_DEV, width, 2 * FF), BF16),
            pltpu.VMEM((EXP_DEV * FF, width), BF16),
            pltpu.VMEM((total, EXP_DEV * 2 * FF), BF16),
            pltpu.VMEM((total, EXP_DEV * FF), BF16),
            pltpu.SemaphoreType.DMA((1 + EXP_DEV,)),
            pltpu.SemaphoreType.DMA((3, LINE * HALVES)),
        ] + plane_scratch(rows, width, wide),
        cost_estimate=COST,
        compiler_params=pltpu.CompilerParams(
            collective_id=collective_id, has_side_effects=True, vmem_limit_bytes=VMEM_BYTES),
    )(block, *weights)


def moe_backward_kernel(layer, experts, rows, width, beside, block_ref, router_ref, gu_hbm, gu_other, down_hbm,
                        down_other, rows_hbm, kept_hbm, scaled_hbm, *refs):
    (later, refs) = (refs[:4], refs[4:]) if beside else ((), refs)
    (db_ref, keep_gu_hbm, keep_down_hbm, send_gu_hbm, send_down_hbm, grad_router_ref), refs = refs[:6], refs[6:]
    (later_out, refs) = (refs[:4], refs[4:]) if beside else ((), refs)
    (gu_v, down_v, fwd_rows, kept, scaled, dgu, send_gu, grad_gu, send_down, grad_down,
     load_sem, store_sem), refs = refs[:12], refs[12:]
    (later_v, refs) = (refs[:7], refs[7:]) if beside else ((), refs)
    plane_refs = refs
    plane = Plane(rows, plane_refs)
    gathered, parts = plane.gathered, plane.parts
    loads = load_experts(layer, plane.sec, gu_hbm, gu_other, down_hbm, down_other, gu_v, down_v, load_sem)
    loads.append(pltpu.make_async_copy(rows_hbm, fwd_rows, load_sem.at[3]))
    loads.append(pltpu.make_async_copy(kept_hbm, kept, load_sem.at[4]))
    loads.append(pltpu.make_async_copy(scaled_hbm, scaled, load_sem.at[5]))
    for load in loads[3:]:
        load.start()
    plane.place(block_ref)
    plane.barrier(*([plane.other_shard()] if beside else []))
    plane.start_gather()
    if beside:
        other_layer = LaterExperts(plane, *later, *later_out, *later_v)
        other_layer.start_loads()
    for load in loads:
        load.wait()
    if beside:
        other_layer.send()
    total = plane.both
    up_at = EXP_DEV * 2 * FF

    def step(k, carry):
        t, h = lax.div(k, HALVES), lax.rem(k, HALVES)
        plane.relay(t, h)
        plane.pass_sum(t, h)
        pl.when(t > 0)(lambda: work(chunk_order(plane.z, t - 1), h))
        return carry

    def work(c, h):
        at = plane.chunk(c, h)
        plane.wait_side_block(c, h)
        gates = own_gates(fwd_rows[at, pl.ds(width, LANES)], plane.owner, experts)
        outer = jnp.sum(gathered[at, pl.ds(width, LANES)].astype(F32), axis=1, keepdims=True)
        dcs = []
        for j in range(EXP_DEV):
            dgate = jnp.zeros((total, 1), F32)
            for f in range(FF // TILE):
                low, high = pl.ds(j * 2 * FF + f * TILE, TILE), pl.ds(j * 2 * FF + FF + f * TILE, TILE)
                dz = nt(gathered[at, pl.ds(0, width)], down_v[pl.ds(j * FF + f * TILE, TILE), :])
                g = kept[at, low].astype(F32)
                u = kept[at, high].astype(F32)
                sig = jax.nn.sigmoid(g)
                silu = g * sig
                dgate = dgate + jnp.sum(dz * silu * u, axis=1, keepdims=True)
                dz = dz * gates[j]
                dgu[at, low] = (dz * u * sig * (1.0 + g * (1.0 - sig))).astype(BF16)
                dgu[at, high] = (dz * silu).astype(BF16)
            dcs.append(gates[j] * (dgate - outer))
        lane = lax.broadcasted_iota(jnp.int32, (total, LANES), 1)
        extra = jnp.zeros((total, LANES), F32)
        for j in range(EXP_DEV):
            top = dcs[j].astype(BF16).astype(F32)
            column = plane.owner * EXP_DEV + j
            extra = extra + jnp.where(lane == column, top, 0.0)
            extra = extra + jnp.where(lane == LANES // 2 + column, dcs[j] - top, 0.0)
        dgu[at, pl.ds(up_at, LANES)] = extra.astype(BF16)
        for n in range(width // TILE):
            cols = pl.ds(n * TILE, TILE)
            acc = nt(dgu[at, pl.ds(0, 2 * FF)], gu_v[0, cols, :])
            for j in range(1, EXP_DEV):
                acc = acc + nt(dgu[at, pl.ds(j * 2 * FF, 2 * FF)], gu_v[j, cols, :])
            for j in range(EXP_DEV):
                acc = acc + dcs[j] * router_ref[pl.ds(j, 1), cols]
            parts[at, cols] = acc.astype(BF16)
        plane.side_copy(c, h).start()

    lax.fori_loop(0, (LINE + 1) * HALVES, step, 0)

    core = plane.sec
    gu_steps, down_steps = width // TILE, FF // TILE

    def stores_gu(n):
        at = lane_tile(n)
        return [pltpu.make_async_copy(send_gu.at[at], send_gu_hbm.at[at], store_sem.at[0, n]),
                pltpu.make_async_copy(grad_gu.at[at], keep_gu_hbm.at[at], store_sem.at[1, n])]

    def stores_down(n):
        at = lane_tile(n)
        return [pltpu.make_async_copy(send_down.at[at], send_down_hbm.at[at], store_sem.at[2, n]),
                pltpu.make_async_copy(grad_down.at[at], keep_down_hbm.at[at], store_sem.at[3, n])]

    def expert_cols(j, size):
        return pl.ds(pl.multiple_of(j * size, size), size)

    def grad_gu_rows(n):
        rows_t = fwd_rows[:, lane_tile(n)]
        send_gu[lane_tile(n), :] = tn(rows_t, dgu[:, expert_cols(1 - core, 2 * FF)]).astype(BF16)
        grad_gu[lane_tile(n), :] = tn(rows_t, dgu[:, expert_cols(core, 2 * FF)]).astype(BF16)
        grad_router_ref[lane_tile(n), :] = tn(rows_t, dgu[:, pl.ds(up_at, LANES)])
        for store in stores_gu(n):
            store.start()

    def grad_down_rows(n):
        def cols(j):
            return pl.ds(pl.multiple_of(j * FF + n * TILE, TILE), TILE)

        data = gathered[:, pl.ds(0, width)]
        send_down[lane_tile(n), :] = tn(scaled[:, cols(1 - core)], data).astype(BF16)
        grad_down[lane_tile(n), :] = tn(scaled[:, cols(core)], data).astype(BF16)
        for store in stores_down(n):
            store.start()

    slots = 2 * HALVES

    def tail(k, carry):
        pl.loop(lax.div(k * gu_steps, slots), lax.div((k + 1) * gu_steps, slots))(grad_gu_rows)
        plane.pass_sum(LINE + 1 + lax.div(k, HALVES), lax.rem(k, HALVES))
        return carry

    lax.fori_loop(0, slots, tail, 0)
    pl.loop(0, down_steps)(grad_down_rows)

    def finish(h, carry):
        plane.finish_sum(h, db_ref)
        return carry

    lax.fori_loop(0, HALVES, finish, 0)
    if beside:
        other_layer.finish()
    plane.drain()
    for n in range(gu_steps):
        for store in stores_gu(n):
            store.wait()
    for n in range(down_steps):
        for store in stores_down(n):
            store.wait()


class LaterExperts:
    def __init__(self, plane, keep_gu, keep_down, got_gu, got_down, sum_gu_hbm, sum_down_hbm, land_gu, land_down,
                 gu_a, gu_b, down_a, down_b, load_sem, send_sem, recv_sem):
        self.sems = load_sem
        self.parts = []
        for keep, got, out, land, a, b, count in (
            (keep_gu, got_gu, sum_gu_hbm, land_gu, gu_a, gu_b, 4),
            (keep_down, got_down, sum_down_hbm, land_down, down_a, down_b, 2),
        ):
            size = a.shape[0] // count
            for n in range(count):
                at, k = pl.ds(n * size, size), len(self.parts)
                self.parts.append((
                    a.at[at], b.at[at],
                    pltpu.make_async_copy(keep.at[at], a.at[at], load_sem.at[0, k]),
                    pltpu.make_async_copy(got.at[at], b.at[at], load_sem.at[1, k]),
                    pltpu.make_async_remote_copy(
                        src_ref=a.at[at], dst_ref=land.at[at], send_sem=send_sem.at[k], recv_sem=recv_sem.at[k],
                        device_id=plane.other_shard(), device_id_type=MESH),
                    pltpu.make_async_copy(land.at[at], b.at[at], load_sem.at[2, k]),
                    pltpu.make_async_copy(a.at[at], out.at[at], load_sem.at[3, k]),
                ))

    def start_loads(self):
        for _, _, load_a, load_b, *_ in self.parts:
            load_a.start()
            load_b.start()

    def send(self):
        for a, b, load_a, load_b, copy, _, _ in self.parts:
            load_a.wait()
            load_b.wait()
            a[...] = (a[...].astype(F32) + b[...].astype(F32)).astype(BF16)
            copy.start()

    def finish(self):
        for _, _, _, _, copy, load, _ in self.parts:
            copy.wait()
            load.start()
        for a, b, _, _, _, load, store in self.parts:
            load.wait()
            a[...] = (a[...].astype(F32) + b[...].astype(F32)).astype(BF16)
            store.start()
        for *_, store in self.parts:
            store.wait()


def moe_backward(layer, block, router, weights, kept, later, experts, collective_id):
    rows, wide = block.shape
    width = wide - LANES
    total = LINE * SIDE * rows
    any_spec = pl.BlockSpec(memory_space=pl.ANY)
    vmem = pl.BlockSpec(memory_space=pltpu.VMEM)
    expert_gu, expert_down = pltpu.VMEM((width, 2 * FF), BF16), pltpu.VMEM((FF, width), BF16)
    gu_shape = jax.ShapeDtypeStruct((width, 2 * FF), BF16)
    down_shape = jax.ShapeDtypeStruct((FF, width), BF16)
    later_out, later_scratch = (), []
    if later:
        later_out = (gu_shape, down_shape) * 2
        later_scratch = [
            expert_gu, expert_gu, expert_down, expert_down,
            pltpu.SemaphoreType.DMA((4, 6)), pltpu.SemaphoreType.DMA((6,)), pltpu.SemaphoreType.DMA((6,)),
        ]
    return pl.pallas_call(
        functools.partial(moe_backward_kernel, layer, experts, rows, width, bool(later)),
        name="moe_backward",
        out_shape=(
            jax.ShapeDtypeStruct((rows, width), F32),
            gu_shape, down_shape, gu_shape, down_shape,
            jax.ShapeDtypeStruct((width, LANES), F32),
        ) + later_out,
        in_specs=[vmem, vmem] + [any_spec] * (7 + len(later)),
        out_specs=(vmem,) + (any_spec,) * 4 + (vmem,) + (any_spec,) * len(later_out),
        scratch_shapes=[
            pltpu.VMEM((EXP_DEV, width, 2 * FF), BF16),
            pltpu.VMEM((EXP_DEV * FF, width), BF16),
            pltpu.VMEM((total, wide), BF16),
            pltpu.VMEM((total, EXP_DEV * 2 * FF), BF16),
            pltpu.VMEM((total, EXP_DEV * FF), BF16),
            pltpu.VMEM((total, EXP_DEV * 2 * FF + LANES), BF16),
            expert_gu, expert_gu, expert_down, expert_down,
            pltpu.SemaphoreType.DMA((6,)),
            pltpu.SemaphoreType.DMA((4, width // TILE)),
        ] + later_scratch + plane_scratch(rows, width, wide),
        cost_estimate=COST,
        compiler_params=pltpu.CompilerParams(
            collective_id=collective_id, has_side_effects=True, vmem_limit_bytes=VMEM_BYTES),
    )(block, router, *weights, *kept, *later)


def split_terms(values):
    high = values.astype(BF16)
    return high, (values - high.astype(F32)).astype(BF16)


def with_lanes(block, columns):
    extra = jnp.concatenate(columns, axis=1)
    extra = jnp.pad(extra, ((0, 0), (0, LANES - extra.shape[1])))
    return jnp.concatenate([block, extra], axis=1)


def far_order(z, i):
    low = jnp.where(i == 0, 3, jnp.where(i == 1, jnp.where(z == 0, 2, 0), jnp.where(z == 0, 1, 2)))
    high = jnp.where(i == 0, 0, jnp.where(i == 1, jnp.where(z == 3, 1, 3), jnp.where(z == 3, 2, 1)))
    return jnp.where(z < 2, low, high)


def reduce_kernel(sub, cols, g1, g0, t1, t0, gu_hbm, down_hbm, core_gu_hbm, core_down_hbm,
                  sum_hbm, own_gu_hbm, own_down_hbm, got_gu_hbm, got_down_hbm,
                  core_got, small_own, small_got, result, own_gu, core_gu, other_gu, own_down, core_down, other_down,
                  load_sem, expert_load_sem, core_sem, small_sem, move_sem, expert_sem, core_expert_sem, store_sem,
                  *plane_refs):
    plane = Plane(HALVES * sub, plane_refs)
    gathered, parts = plane.gathered, plane.parts
    core, shard, z, x = plane.sec, plane.shard, plane.z, plane.x
    wide = cols + LANES
    grads, smalls = (g1, g0), (t1, t0)
    diagonal = (1 - core, plane.owner, 1 - shard)
    places = [(c, side) for c in range(LINE) for side in range(SIDE)]

    def remote(src, dst, send_sem, recv_sem, device):
        return pltpu.make_async_remote_copy(
            src_ref=src, dst_ref=dst, send_sem=send_sem, recv_sem=recv_sem,
            device_id=device, device_id_type=MESH)

    loads = []
    for h in range(2):
        for n, (c, side) in enumerate(places):
            loads.append(pltpu.make_async_copy(
                grads[h].at[n, core], parts.at[plane.block(c, h, side), pl.ds(0, cols)], load_sem.at[h, n]))
        loads.append(pltpu.make_async_copy(
            smalls[h].at[shard, :, core], small_own.at[h], load_sem.at[h, len(places)]))
    pieces, expert_loads = [], []
    for hbm, from_core, own, there, other, own_hbm, got_hbm, count in (
        (gu_hbm, core_gu_hbm, own_gu, core_gu, other_gu, own_gu_hbm, got_gu_hbm, 4),
        (down_hbm, core_down_hbm, own_down, core_down, other_down, own_down_hbm, got_down_hbm, 2),
    ):
        size = own.shape[0] // count
        for n in range(count):
            at, k = pl.ds(n * size, size), len(pieces)
            pieces.append((own, there, other, own_hbm, got_hbm, at))
            expert_loads.append(pltpu.make_async_copy(hbm.at[at], own.at[at], expert_load_sem.at[0, k]))
            expert_loads.append(pltpu.make_async_copy(from_core.at[at], there.at[at], expert_load_sem.at[1, k]))
    for load in expert_loads[:2] + loads + expert_loads[2:]:
        load.start()
    plane.barrier(plane.other_core(), plane.other_shard(), diagonal)
    cores = [
        remote(grads[h].at[:, 1 - core], core_got.at[h], core_sem.at[0, h], core_sem.at[1, h], plane.other_core())
        for h in range(2)
    ]
    small = []
    for h in range(2):
        for n, (there, half, device) in enumerate((
            (shard, 1 - core, plane.other_core()),
            (1 - shard, core, plane.other_shard()),
            (1 - shard, 1 - core, diagonal),
        )):
            small.append(remote(
                smalls[h].at[there, :, half], small_got.at[h, n], small_sem.at[0, h, n], small_sem.at[1, h, n],
                device))
    for copy in cores + small:
        copy.start()
    exchange = []

    def send_piece():
        n = len(exchange)
        own, there, other, own_hbm, got_hbm, at = pieces[n]
        for load in expert_loads[2 * n : 2 * n + 2]:
            load.wait()
        own[at] = (own[at].astype(F32) + there[at].astype(F32)).astype(BF16)
        exchange.append(
            remote(own.at[at], other.at[at], expert_sem.at[0, n], expert_sem.at[1, n], plane.other_shard()))
        exchange[-1].start()

    def prepare(h):
        cores[h].wait_recv()
        for copy in small[3 * h : 3 * h + 3]:
            copy.wait_recv()

        def one(k, carry):
            c = jnp.where(k < 2 * (LINE - 1), far_order(z, lax.div(k, 2)), z)
            side = jnp.where(lax.rem(k, 2) == 0, 1 - x, x)
            n = c * SIDE + side
            at = plane.block(c, h, side)
            parts[at, pl.ds(0, cols)] = (
                parts[at, pl.ds(0, cols)].astype(F32) + core_got[h, n].astype(F32)).astype(BF16)
            total = small_own[h, n].astype(F32)
            for other in range(3):
                total = total + small_got[h, other, n].astype(F32)
            parts[at, pl.ds(cols, LANES)] = total.astype(BF16)
            pl.when(side != x)(lambda: plane.side_copy(c, h).start())
            return carry

        lax.fori_loop(0, LINE * SIDE, one, 0)

    send_piece()
    for load in loads:
        load.wait()
    prepare(0)

    def pass_piece(i, h):
        plane.pass_chunk(far_order(z, i), h)

    def move(h):
        return remote(
            result.at[h], gathered.at[plane.block(z, core, x)], move_sem.at[0], move_sem.at[1], plane.other_core())

    def send_block(h):
        pl.when(z < LINE - 1)(lambda: plane.forward_up(z, h).start())
        pl.when(z > 0)(lambda: plane.forward_down(z, h).start())
        plane.forward_side(z, h).start()

    def finish(h):
        plane.finish_piece(h, result)
        own_layer = core == 1 - h
        pl.when(jnp.logical_not(own_layer))(lambda: move(h).start())

        @pl.when(own_layer)
        def _():
            gathered[plane.block(z, core, x)] = result[h]
            send_block(core)
            arrived = remote(
                result.at[h], gathered.at[plane.block(z, 1 - core, x)], move_sem.at[0], move_sem.at[1],
                plane.other_core())
            arrived.wait_recv()
            send_block(1 - core)

    def out_copy(c, h, side):
        at = pl.multiple_of(((c * SIDE + side) * HALVES + h) * sub, sub)
        return pltpu.make_async_copy(
            gathered.at[plane.block(c, h, side)], sum_hbm.at[pl.ds(at, sub)],
            store_sem.at[(c * SIDE + side) * HALVES + h])

    def gather(t):
        for turn in range(HALVES):
            h = core if turn == 0 else 1 - core
            plane.relay(t, h)
            c = chunk_order(z, t - 1)
            plane.wait_side_block(c, h)
            out_copy(c, h, x).start()
            out_copy(c, h, 1 - x).start()

    count = LINE * SIDE * HALVES

    def to_core(n):
        own, there, other, own_hbm, got_hbm, at = pieces[n]
        return remote(
            own.at[at], got_hbm.at[at], core_expert_sem.at[0, n], core_expert_sem.at[1, n], plane.other_core())

    def keep(n):
        own, there, other, own_hbm, got_hbm, at = pieces[n]
        return pltpu.make_async_copy(own.at[at], own_hbm.at[at], store_sem.at[count + n])

    def expert_piece(n):
        own, there, other, own_hbm, got_hbm, at = pieces[n]
        exchange[n].wait()
        own[at] = (own[at].astype(F32) + other[at].astype(F32)).astype(BF16)
        pl.when(core == 1)(lambda: to_core(n).start())
        keep(n).start()

    send_piece()
    pass_piece(0, 0)
    prepare(1)
    send_piece()
    pass_piece(1, 0)
    send_piece()
    pass_piece(2, 0)
    finish(0)
    send_piece()
    send_piece()
    for i in range(LINE - 1):
        pass_piece(i, 1)
        pl.when(core == 1)(lambda i=i: gather(i + 1))
        expert_piece(i)
    finish(1)
    pl.when(core == 1)(lambda: gather(LINE))

    @pl.when(core == 0)
    def _():
        def one(t, carry):
            gather(t)
            return carry

        lax.fori_loop(1, LINE + 1, one, 0)

    for n in range(LINE - 1, len(pieces)):
        expert_piece(n)
    plane.drain()
    for copy in cores + small:
        copy.wait_send()
    move(0).wait_send()

    def stored(k, carry):
        out_copy(lax.div(k, SIDE * HALVES), lax.rem(k, HALVES), lax.rem(lax.div(k, HALVES), SIDE)).wait()
        return carry

    lax.fori_loop(0, count, stored, 0)
    for n in range(len(pieces)):
        keep(n).wait()
        pl.when(core == 1)(lambda n=n: to_core(n).wait_send())
        pl.when(core == 0)(lambda n=n: to_core(n).wait_recv())


def reduce_gradients(g1, g0, t1, t0, grad_gu, grad_down, core_gu, core_down, collective_id):
    places, halves, sub, cols = g1.shape
    any_spec = pl.BlockSpec(memory_space=pl.ANY)
    wide = cols + LANES
    gu, down = jax.ShapeDtypeStruct(grad_gu.shape, BF16), jax.ShapeDtypeStruct(grad_down.shape, BF16)
    return pl.pallas_call(
        functools.partial(reduce_kernel, sub, cols),
        name="reduce_gradients",
        out_shape=(jax.ShapeDtypeStruct((places * halves * sub, wide), BF16), gu, down, gu, down),
        in_specs=[any_spec] * 8,
        out_specs=(any_spec,) * 5,
        scratch_shapes=[
            pltpu.VMEM((2, places, sub, cols), BF16),
            pltpu.VMEM((2, places, sub, LANES), BF16),
            pltpu.VMEM((2, 3, places, sub, LANES), BF16),
            pltpu.VMEM((2, sub, wide), BF16),
            pltpu.VMEM(grad_gu.shape, BF16),
            pltpu.VMEM(grad_gu.shape, BF16),
            pltpu.VMEM(grad_gu.shape, BF16),
            pltpu.VMEM(grad_down.shape, BF16),
            pltpu.VMEM(grad_down.shape, BF16),
            pltpu.VMEM(grad_down.shape, BF16),
            pltpu.SemaphoreType.DMA((2, places + 1)),
            pltpu.SemaphoreType.DMA((2, 6)),
            pltpu.SemaphoreType.DMA((2, 2)),
            pltpu.SemaphoreType.DMA((2, 2, 3)),
            pltpu.SemaphoreType.DMA((2,)),
            pltpu.SemaphoreType.DMA((2, 6)),
            pltpu.SemaphoreType.DMA((2, 6)),
            pltpu.SemaphoreType.DMA((places * halves + 6,)),
        ] + plane_scratch(halves * sub, wide, wide),
        compiler_params=pltpu.CompilerParams(
            collective_id=collective_id, has_side_effects=True, vmem_limit_bytes=VMEM_BYTES),
    )(g1, g0, t1, t0, grad_gu, grad_down, core_gu, core_down)


def finish_kernel(qkv_cols, attn, gu_own, gu_got, gu_one, gu_moved, down_own, down_got, down_one, down_moved,
                  qkv_hbm, out_hbm, gu_hbm, down_hbm, attn_v, gu_v, down_v, qkv_f, out_f, gu_f, down_f,
                  load_sem, store_sem):
    core = lax.axis_index("section")
    steps = []

    def chunks(rows, count):
        return [pl.ds(n * (rows // count), rows // count) for n in range(count)]

    def choose(zero, one, dst, sem):
        copies = [pltpu.make_async_copy(zero, dst, sem), pltpu.make_async_copy(one, dst, sem)]
        pl.when(core == 0)(lambda: copies[0].start())
        pl.when(core == 1)(lambda: copies[1].start())
        return copies[0]

    def add(load, convert, stores):
        steps.append((load, convert, stores))

    def store(src, dst, n):
        return pltpu.make_async_copy(src, dst, store_sem.at[n])

    stored = 0
    for j, (zero, one) in enumerate(((gu_own, gu_moved), (gu_got, gu_one))):
        for at in chunks(gu_f.shape[1], 6):
            def convert(j=j, at=at):
                gu_f[j, at, :] = gu_v[j, at, :].astype(F32)

            load = choose(zero.at[at], one.at[at], gu_v.at[j, at], load_sem.at[len(steps)])
            add(load, convert, [store(gu_f.at[j, at], gu_hbm.at[j, at], stored)])
            stored += 1
    for j, (zero, one) in enumerate(((down_own, down_moved), (down_got, down_one))):
        for at in chunks(down_f.shape[1], 2):
            def convert(j=j, at=at):
                down_f[j, at, :] = down_v[j, at, :].astype(F32)

            load = choose(zero.at[at], one.at[at], down_v.at[j, at], load_sem.at[len(steps)])
            add(load, convert, [store(down_f.at[j, at], down_hbm.at[j, at], stored)])
            stored += 1
    for at in chunks(attn_v.shape[0], 8):
        def convert(at=at):
            qkv_f[at, :] = attn_v[at, pl.ds(0, qkv_cols)].astype(F32)
            out_f[at, :] = attn_v[at, pl.ds(qkv_cols, out_f.shape[1])].astype(F32)

        load = pltpu.make_async_copy(attn.at[at, pl.ds(0, attn_v.shape[1])], attn_v.at[at], load_sem.at[len(steps)])
        load.start()
        add(load, convert, [
            store(qkv_f.at[at], qkv_hbm.at[at], stored), store(out_f.at[at], out_hbm.at[at], stored + 1)])
        stored += 2
    for load, convert, stores in steps:
        load.wait()
        convert()
        for copy in stores:
            copy.start()
    for load, convert, stores in steps:
        for copy in stores:
            copy.wait()


def finish_outputs(attn, gus, downs, qkv_cols, out_cols):
    rows = attn.shape[0]
    gu, down = (EXP_DEV,) + gus[0].shape, (EXP_DEV,) + downs[0].shape
    any_spec = pl.BlockSpec(memory_space=pl.ANY)
    return pl.pallas_call(
        functools.partial(finish_kernel, qkv_cols),
        name="finish_outputs",
        out_shape=(
            jax.ShapeDtypeStruct((rows, qkv_cols), F32),
            jax.ShapeDtypeStruct((rows, out_cols), F32),
            jax.ShapeDtypeStruct(gu, F32),
            jax.ShapeDtypeStruct(down, F32),
        ),
        in_specs=[any_spec] * 9,
        out_specs=(any_spec,) * 4,
        scratch_shapes=[
            pltpu.VMEM((rows, qkv_cols + out_cols), BF16),
            pltpu.VMEM(gu, BF16),
            pltpu.VMEM(down, BF16),
            pltpu.VMEM((rows, qkv_cols), F32),
            pltpu.VMEM((rows, out_cols), F32),
            pltpu.VMEM(gu, F32),
            pltpu.VMEM(down, F32),
            pltpu.SemaphoreType.DMA((24,)),
            pltpu.SemaphoreType.DMA((32,)),
        ],
        compiler_params=pltpu.CompilerParams(vmem_limit_bytes=VMEM_BYTES),
    )(attn, *gus, *downs)


PAIRS = 2
GROUP = QUERY_HEADS // KEY_VALUE_HEADS
SCALE = HEAD_SIZE ** (-0.5)


class Pair:
    def __init__(self):
        self.sec, self.owner, self.me = (lax.axis_index(n) for n in ("section", "expert", "shard"))
        self.peer = 1 - self.me

    def barrier(self, with_core=False):
        sem = pltpu.get_barrier_semaphore()
        pl.semaphore_signal(
            sem, inc=1, device_id=(self.sec, self.owner, self.peer), device_id_type=MESH)
        if with_core:
            pl.semaphore_signal(
                sem, inc=1, device_id=(1 - self.sec, self.owner, self.me), device_id_type=MESH)
        pl.semaphore_wait(sem, 1 + with_core)

    def send(self, src, dst, send_sem, recv_sem):
        return pltpu.make_async_remote_copy(
            src_ref=src, dst_ref=dst, send_sem=send_sem, recv_sem=recv_sem,
            device_id=(self.sec, self.owner, self.peer), device_id_type=MESH)


def head_columns(shard):
    kv_pair = KEY_VALUE_HEADS // 2 // PAIRS * HEAD_SIZE
    q_pair = kv_pair * GROUP
    wide = q_pair + 2 * kv_pair
    spans = []
    for i in range(PAIRS):
        at = shard * PAIRS + i
        spans.append((at * q_pair, i * wide, q_pair))
        spans.append((QUERY_WIDTH + at * kv_pair, i * wide + q_pair, kv_pair))
        spans.append((QUERY_WIDTH + KV_WIDTH + at * kv_pair, i * wide + q_pair + kv_pair, kv_pair))
    return spans


def head_at(i, n, g):
    kv_pair = KEY_VALUE_HEADS // 2 // PAIRS * HEAD_SIZE
    q_pair = kv_pair * GROUP
    base = i * (q_pair + 2 * kv_pair)
    return (
        pl.ds(base + (n * GROUP + g) * HEAD_SIZE, HEAD_SIZE),
        pl.ds(base + q_pair + n * HEAD_SIZE, HEAD_SIZE),
        pl.ds(base + q_pair + kv_pair + n * HEAD_SIZE, HEAD_SIZE),
    )


KV_IN_PAIR = KEY_VALUE_HEADS // 2 // PAIRS


def load_attention(layer, sec, wq, wq_other, wo, wo_other, wq_v, wo_v, sems):
    loads = []
    for j in range(2):
        for at, local, size in head_columns(j):
            loads.append(load_layer(
                layer, sec, wq.at[:, pl.ds(at, size)], wq_other.at[:, pl.ds(at, size)],
                wq_v.at[j, :, pl.ds(local, size)], sems.at[len(loads)]))
    loads.append(load_layer(layer, sec, wo, wo_other, wo_v, sems.at[len(loads)]))
    return loads


LOADS = 2 * PAIRS * 3 + 1


def attention_forward_kernel(layer, rows, width, h_ref, allowed_ref, gains_ref, router_ref, mask_ref, wq, wq_other,
                             wo, wo_other, block_ref, h1_ref, a_ref, qkv_ref, p_ref, o_ref,
                             wq_v, wo_v, a_parts, a_half, part_send, got_part, out_send, got_out,
                             load_sem, send_sem, recv_sem, *turn):
    pair = Pair()
    me, peer = pair.me, pair.peer
    half = width // 2
    loads = load_attention(layer, pair.sec, wq, wq_other, wo, wo_other, wq_v, wo_v, load_sem)
    pair.barrier(bool(turn))

    def span(who):
        return pl.ds(pl.multiple_of(who * rows, rows), rows)

    h = h_ref[...].astype(F32)
    r1 = lax.rsqrt(jnp.mean(h * h, axis=1, keepdims=True) + EPS)
    a = (h * r1 * gains_ref[pl.ds(0, 1), :]).astype(BF16)
    for j in range(2):
        a_parts[j] = a[:, j * half : (j + 1) * half]
    if turn:
        pl.when(pair.sec == 0)(lambda: pl.semaphore_wait(turn[0], 1))
    send_a = pair.send(a_parts.at[peer], a_half.at[span(me)], send_sem.at[0], recv_sem.at[0])
    send_a.start()
    a_half[span(me)] = a_parts[me]
    for load in loads[:-1]:
        load.wait()
    part_send[span(me)] = nn(a_parts[me], wq_v[peer]).astype(BF16)
    send_own = pair.send(part_send.at[span(me)], got_part.at[span(me)], send_sem.at[1], recv_sem.at[1])
    send_own.start()
    send_a.wait_recv()
    part_send[span(peer)] = nn(a_half[span(peer)], wq_v[peer]).astype(BF16)
    send_other = pair.send(
        part_send.at[span(peer)], got_part.at[span(peer)], send_sem.at[2], recv_sem.at[2])
    send_other.start()
    mine = nn(a_half[...], wq_v[me])
    a_ref[...] = a_half[...]
    send_own.wait_recv()
    send_other.wait_recv()
    qkv_ref[...] = (mine + got_part[...].astype(F32)).astype(BF16)
    allowed = allowed_ref[...] > 0
    for i in range(PAIRS):
        for n in range(KV_IN_PAIR):
            for g in range(GROUP):
                q_at, k_at, v_at = head_at(i, n, g)
                j = (i * KV_IN_PAIR + n) * GROUP + g
                s = nt(qkv_ref[:, q_at], qkv_ref[:, k_at]) * SCALE
                s = jnp.where(allowed, s, MASKED_SCORE)
                ex = jnp.exp(s - jnp.max(s, axis=1, keepdims=True))
                p = (ex / jnp.sum(ex, axis=1, keepdims=True)).astype(BF16)
                p_ref[j] = p
                o_ref[:, pl.ds(j * HEAD_SIZE, HEAD_SIZE)] = nn(p, qkv_ref[:, v_at]).astype(BF16)
    loads[-1].wait()
    out_send[...] = nn(o_ref[span(peer)], wo_v[...]).astype(BF16)
    send_out = pair.send(out_send, got_out, send_sem.at[3], recv_sem.at[3])
    send_out.start()
    own = nn(o_ref[span(me)], wo_v[...])
    send_out.wait_recv()
    if turn:
        @pl.when(pair.sec == 1)
        def _():
            pl.semaphore_signal(
                turn[0], inc=1, device_id=(1 - pair.sec, pair.owner, me), device_id_type=MESH)

    h1 = h + own + got_out[...].astype(F32)
    h1_ref[...] = h1
    r2 = lax.rsqrt(jnp.mean(h1 * h1, axis=1, keepdims=True) + EPS)
    b = (h1 * r2 * gains_ref[pl.ds(1, 1), :]).astype(BF16)
    block_ref[:, pl.ds(0, width)] = b
    mask = mask_ref[...] > 0
    logits = jnp.where(mask, nt(b, router_ref[...]), MASKED_SCORE)
    ex = jnp.where(mask, jnp.exp(logits - jnp.max(logits, axis=1, keepdims=True)), 0.0)
    gates = ex / (0.5 * jnp.sum(ex, axis=1, keepdims=True))
    high = gates.astype(BF16).astype(F32)
    block_ref[:, pl.ds(width, LANES)] = jnp.where(mask_ref[...] > 1, gates - high, high).astype(BF16)
    for send in (send_a, send_own, send_other, send_out):
        send.wait_send()


def attention_forward(layer, h, allowed, gains, router, mask, weights, collective_id):
    rows, width = h.shape
    half, group = width // 2, 2 * rows
    qkv = (QUERY_WIDTH + 2 * KV_WIDTH) // 2
    heads = QUERY_HEADS // 2
    any_spec = pl.BlockSpec(memory_space=pl.ANY)
    vmem = pl.BlockSpec(memory_space=pltpu.VMEM)
    return pl.pallas_call(
        functools.partial(attention_forward_kernel, layer, rows, width),
        name="attention_forward",
        out_shape=(
            jax.ShapeDtypeStruct((rows, width + LANES), BF16),
            jax.ShapeDtypeStruct((rows, width), F32),
            jax.ShapeDtypeStruct((group, half), BF16),
            jax.ShapeDtypeStruct((group, qkv), BF16),
            jax.ShapeDtypeStruct((heads, group, group), BF16),
            jax.ShapeDtypeStruct((group, QUERY_WIDTH // 2), BF16),
        ),
        in_specs=[vmem] * 5 + [any_spec] * 4,
        out_specs=(vmem,) * 6,
        scratch_shapes=[
            pltpu.VMEM((2, half, qkv), BF16),
            pltpu.VMEM((QUERY_WIDTH // 2, width), BF16),
            pltpu.VMEM((2, rows, half), BF16),
            pltpu.VMEM((group, half), BF16),
            pltpu.VMEM((group, qkv), BF16),
            pltpu.VMEM((group, qkv), BF16),
            pltpu.VMEM((rows, width), BF16),
            pltpu.VMEM((rows, width), BF16),
            pltpu.SemaphoreType.DMA((LOADS,)),
            pltpu.SemaphoreType.DMA((4,)),
            pltpu.SemaphoreType.DMA((4,)),
        ] + ([pltpu.SemaphoreType.REGULAR] if layer == 0 else []),
        cost_estimate=COST,
        compiler_params=pltpu.CompilerParams(
            collective_id=collective_id, has_side_effects=True, vmem_limit_bytes=VMEM_BYTES),
    )(h, allowed, gains, router, mask, *weights)


def attention_backward_kernel(layer, rows, width, experts, router_grad_ref, db_ref, dout_ref, h1_ref, h_ref, gains_ref, a_ref, qkv_ref,
                              p_ref, o_ref, wq, wq_other, wo, wo_other, dh_ref, columns_ref, grad_hbm,
                              wq_v, wo_v, d_all, do, dqkv, got_dqkv, da_send, got_da, dh1_v, grad_q, grad_o,
                              gain_grads_ref, columns_v, load_sem, store_sem, send_sem, recv_sem):
    pair = Pair()
    me, peer = pair.me, pair.peer
    half = width // 2
    qkv_cols = dqkv.shape[1]
    pair_cols = qkv_cols // PAIRS
    loads = load_attention(layer, pair.sec, wq, wq_other, wo, wo_other, wq_v, wo_v, load_sem)
    pair.barrier()

    def span(who):
        return pl.ds(pl.multiple_of(who * rows, rows), rows)

    h1 = h1_ref[...]
    r2 = lax.rsqrt(jnp.mean(h1 * h1, axis=1, keepdims=True) + EPS)
    normed = h1 * r2
    db = db_ref[...]
    scaled = db * gains_ref[pl.ds(1, 1), :]
    gain_grads_ref[...] = jnp.zeros_like(gain_grads_ref)
    gain_grads_ref[pl.ds(experts + 1, 1), :] = jnp.sum(db * normed, axis=0, keepdims=True)
    dh1 = dout_ref[...].astype(F32) + r2 * (
        scaled - normed * jnp.mean(scaled * normed, axis=1, keepdims=True))
    dh1_v[...] = dh1
    d_all[span(me)] = dh1.astype(BF16)
    send_d = pair.send(d_all.at[span(me)], d_all.at[span(me)], send_sem.at[0], recv_sem.at[0])
    send_d.start()
    router_terms = router_grad_ref[...]
    lane = lax.broadcasted_iota(jnp.int32, router_terms.shape, 1)
    router_terms = router_terms + pltpu.roll(router_terms, LANES // 2, 1)
    columns_v[...] = jnp.where(lane < experts, router_terms, 0.0)
    for load in loads:
        load.wait()
    do[span(me)] = nt(d_all[span(me)], wo_v[...]).astype(BF16)
    send_d.wait_recv()
    do[span(peer)] = nt(d_all[span(peer)], wo_v[...]).astype(BF16)
    sends = [send_d]
    for i in range(PAIRS):
        cols = pl.ds(i * pair_cols, pair_cols)
        for n in range(KV_IN_PAIR):
            dk = dv = None
            for g in range(GROUP):
                q_at, k_at, v_at = head_at(i, n, g)
                j = (i * KV_IN_PAIR + n) * GROUP + g
                p_low = p_ref[j]
                p = p_low.astype(F32)
                d_head = do[:, pl.ds(j * HEAD_SIZE, HEAD_SIZE)]
                weighted = p * nt(d_head, qkv_ref[:, v_at])
                ds = (weighted - p * jnp.sum(weighted, axis=1, keepdims=True)).astype(BF16)
                dqkv[:, q_at] = (nn(ds, qkv_ref[:, k_at]) * SCALE).astype(BF16)
                dk_part, dv_part = tn(ds, qkv_ref[:, q_at]), tn(p_low, d_head)
                dk = dk_part if dk is None else dk + dk_part
                dv = dv_part if dv is None else dv + dv_part
            dqkv[:, k_at] = (dk * SCALE).astype(BF16)
            dqkv[:, v_at] = dv.astype(BF16)
        send = pair.send(dqkv.at[:, cols], got_dqkv.at[:, cols], send_sem.at[1 + i], recv_sem.at[1 + i])
        send.start()
        sends.append(send)
    da = nt(dqkv[...], wq_v[me])
    grad_q[me] = tn(a_ref[...], dqkv[...]).astype(BF16)
    grad_o[...] = tn(o_ref[...], d_all[...]).astype(BF16)
    store_o = pltpu.make_async_copy(
        grad_o, grad_hbm.at[:, pl.ds(QUERY_WIDTH + 2 * KV_WIDTH, width)], store_sem.at[LOADS - 1])
    store_o.start()
    for send in sends[1:]:
        send.wait_recv()
    da = da + nt(got_dqkv[...], wq_v[peer])
    da_send[...] = jnp.where(me == 0, da[rows:], da[:rows]).astype(BF16)
    send_da = pair.send(da_send, got_da, send_sem.at[1 + PAIRS], recv_sem.at[1 + PAIRS])
    send_da.start()
    own_da = jnp.where(me == 0, da[:rows], da[rows:])
    grad_q[peer] = tn(a_ref[...], got_dqkv[...]).astype(BF16)
    stores = [store_o]
    for j in range(2):
        for at, local, size in head_columns(j):
            store = pltpu.make_async_copy(
                grad_q.at[j, :, pl.ds(local, size)], grad_hbm.at[:, pl.ds(at, size)],
                store_sem.at[len(stores) - 1])
            store.start()
            stores.append(store)
    send_da.wait_recv()
    other_da = got_da[...].astype(F32)
    h = h_ref[...].astype(F32)
    r1 = lax.rsqrt(jnp.mean(h * h, axis=1, keepdims=True) + EPS)
    halves = []
    total = jnp.zeros((rows, 1), F32)
    for j in range(2):
        cols = pl.ds(j * half, half)
        da_j = jnp.where(me == j, own_da, other_da)
        normed = h[:, j * half : (j + 1) * half] * r1
        gain_grads_ref[pl.ds(experts, 1), cols] = jnp.sum(da_j * normed, axis=0, keepdims=True)
        scaled = da_j * gains_ref[pl.ds(0, 1), cols]
        total = total + jnp.sum(scaled * normed, axis=1, keepdims=True)
        halves.append((cols, scaled, normed))
    columns = columns_v[...] + jnp.transpose(gain_grads_ref[...])
    columns_ref[...] = columns.astype(BF16)
    for cols, scaled, normed in halves:
        dh_ref[:, cols] = dh1_v[:, cols] + r1 * (scaled - normed * (total / width))
    for send in sends + [send_da]:
        send.wait_send()
    for store in stores:
        store.wait()


def attention_backward(layer, experts, router_grad, db, dout, h1, h, gains, a_half, qkv, p, o, weights, collective_id):
    rows, width = db.shape
    half, group = width // 2, 2 * rows
    cols = (QUERY_WIDTH + 2 * KV_WIDTH) // 2
    any_spec = pl.BlockSpec(memory_space=pl.ANY)
    vmem = pl.BlockSpec(memory_space=pltpu.VMEM)
    return pl.pallas_call(
        functools.partial(attention_backward_kernel, layer, rows, width, experts),
        name="attention_backward",
        out_shape=(
            jax.ShapeDtypeStruct((rows, width), F32),
            jax.ShapeDtypeStruct((width, LANES), BF16),
            jax.ShapeDtypeStruct((half, QUERY_WIDTH + 2 * KV_WIDTH + width), BF16),
        ),
        in_specs=[vmem] * 10 + [any_spec] * 4,
        out_specs=(vmem, vmem, any_spec),
        scratch_shapes=[
            pltpu.VMEM((2, half, cols), BF16),
            pltpu.VMEM((QUERY_WIDTH // 2, width), BF16),
            pltpu.VMEM((group, width), BF16),
            pltpu.VMEM((group, QUERY_WIDTH // 2), BF16),
            pltpu.VMEM((group, cols), BF16),
            pltpu.VMEM((group, cols), BF16),
            pltpu.VMEM((rows, half), BF16),
            pltpu.VMEM((rows, half), BF16),
            pltpu.VMEM((rows, width), F32),
            pltpu.VMEM((2, half, cols), BF16),
            pltpu.VMEM((QUERY_WIDTH // 2, width), BF16),
            pltpu.VMEM((LANES, width), F32),
            pltpu.VMEM((width, LANES), F32),
            pltpu.SemaphoreType.DMA((LOADS,)),
            pltpu.SemaphoreType.DMA((LOADS,)),
            pltpu.SemaphoreType.DMA((2 + PAIRS,)),
            pltpu.SemaphoreType.DMA((2 + PAIRS,)),
        ],
        cost_estimate=COST,
        compiler_params=pltpu.CompilerParams(
            collective_id=collective_id, has_side_effects=True, vmem_limit_bytes=VMEM_BYTES),
    )(router_grad, db, dout, h1, h, gains, a_half, qkv, p, o, *weights)


def dot(a, b, dims):
    return lax.dot_general(a, b, (dims, ((), ())), preferred_element_type=F32)


def rms_scale(values):
    return lax.rsqrt(jnp.mean(values * values, axis=-1, keepdims=True) + EPS)


def swap_cores(value):
    return lax.ppermute(value, "section", [(0, 1), (1, 0)])


def both_layers(own):
    return lax.all_gather(own, "section", axis=0, tiled=False)


def document_mask(sequence_lengths, rows):
    pos = jnp.arange(rows, dtype=jnp.int32)
    ends = jnp.cumsum(sequence_lengths)
    doc = jnp.sum((pos[:, None] >= ends[None, :]).astype(jnp.int32), axis=1)
    return (doc[:, None] == doc[None, :]) & (pos[None, :] <= pos[:, None])


def plain_attention(qkv, allowed, heads, kv_heads):
    rows = qkv.shape[0]
    group = heads // kv_heads
    q = qkv[:, : heads * HEAD_SIZE].reshape(rows, kv_heads, group, HEAD_SIZE)
    k = qkv[:, heads * HEAD_SIZE : (heads + kv_heads) * HEAD_SIZE].reshape(rows, kv_heads, HEAD_SIZE)
    v = qkv[:, (heads + kv_heads) * HEAD_SIZE :].reshape(rows, kv_heads, HEAD_SIZE)
    s = jnp.einsum("qhgd,khd->hgqk", q, k, preferred_element_type=F32) * HEAD_SIZE ** (-0.5)
    s = jnp.where(allowed[None, None], s, MASKED_SCORE)
    ex = jnp.exp(s - jnp.max(s, axis=-1, keepdims=True))
    p = ex / jnp.sum(ex, axis=-1, keepdims=True)
    o = jnp.einsum("hgqk,khd->qhgd", p.astype(BF16), v, preferred_element_type=F32)
    return o.reshape(rows, heads * HEAD_SIZE).astype(BF16), p, (q, k, v)


def plain_attention_backward(do, p, heads_in):
    q, k, v = heads_in
    rows = q.shape[0]
    dh = do.reshape(q.shape)
    dv = jnp.einsum("hgqk,qhgd->khd", p.astype(BF16), dh, preferred_element_type=F32)
    dp = jnp.einsum("qhgd,khd->hgqk", dh, v, preferred_element_type=F32)
    ds = (p * (dp - jnp.sum(p * dp, axis=-1, keepdims=True))).astype(BF16)
    dq = jnp.einsum("hgqk,khd->qhgd", ds, k, preferred_element_type=F32) * HEAD_SIZE ** (-0.5)
    dk = jnp.einsum("hgqk,qhgd->khd", ds, q, preferred_element_type=F32) * HEAD_SIZE ** (-0.5)
    return jnp.concatenate(
        [dq.reshape(rows, -1), dk.reshape(rows, -1), dv.reshape(rows, -1)], axis=1
    ).astype(BF16)


def column_parts(n, j):
    qw, kw = QUERY_WIDTH // n, KV_WIDTH // n
    return (
        (j * qw, qw),
        (QUERY_WIDTH + j * kw, kw),
        (QUERY_WIDTH + KV_WIDTH + j * kw, kw),
    )


def plain_shards(
    edge_inputs, seq_lengths, routes, w_qkv, w_out, w_router, gain_attn, gain_moe, w_gate_up, w_down
):
    sec = lax.axis_index("section")
    owner = lax.axis_index("expert")
    shard_pos = lax.axis_index("shard")
    n_shard = lax.axis_size("shard")
    n_owner = lax.axis_size("expert")
    rows, width = edge_inputs.shape[2], edge_inputs.shape[3]
    experts = w_router.shape[2]
    group_rows = rows * n_shard
    half = width // n_shard
    heads, kv_heads = QUERY_HEADS // n_shard, KEY_VALUE_HEADS // n_shard

    def pick(array, index):
        return lax.dynamic_index_in_dim(array, index, 0, keepdims=False)

    own_edge, other_edge = pick(edge_inputs[0], sec), swap_cores(pick(edge_inputs[0], 1 - sec))
    x_in = jnp.where(sec == 0, own_edge, other_edge)
    dy = jnp.where(sec == 0, other_edge, own_edge)
    own_routes, other_routes = pick(routes[0], sec), swap_cores(pick(routes[0], 1 - sec))
    layer_routes = (
        jnp.where(sec == 0, own_routes, other_routes),
        jnp.where(sec == 0, other_routes, own_routes),
    )
    allowed = document_mask(pick(seq_lengths, sec)[0], group_rows)
    wq = both_layers(w_qkv[0])
    wo = both_layers(w_out[0])
    small = jnp.concatenate([w_router[0], gain_attn[0][:, None], gain_moe[0][:, None]], axis=1)
    small = lax.all_gather(both_layers(small), "shard", axis=1, tiled=True)
    wgu = both_layers(w_gate_up[0])
    wd = both_layers(w_down[0])
    columns = jnp.arange(experts, dtype=jnp.int32)
    route_masks = [
        jnp.any(r[:, :, None] == columns[None, None, :], axis=1).astype(BF16) for r in layer_routes
    ]
    plane_masks = [lax.all_gather(m, "expert", axis=0, tiled=True) for m in route_masks]

    def forward(layer, h):
        gain_a = small[layer, :, experts].astype(F32)[None, :]
        gain_m = small[layer, :, experts + 1].astype(F32)[None, :]
        router = small[layer, :, :experts]
        r1 = rms_scale(h)
        a = (h * r1 * gain_a).astype(BF16)
        a_half = lax.all_to_all(
            a.reshape(rows, n_shard, half), "shard", split_axis=1, concat_axis=0, tiled=True
        ).reshape(group_rows, half)
        blocks = []
        for j in range(n_shard):
            blocks.append(
                jnp.concatenate(
                    [
                        dot(a_half, wq[layer, :, at : at + size], ((1,), (0,)))
                        for at, size in column_parts(n_shard, j)
                    ],
                    axis=1,
                ).astype(BF16)
            )
        qkv = lax.psum_scatter(jnp.stack(blocks), "shard", scatter_dimension=0, tiled=False)
        o, p, heads_in = plain_attention(qkv, allowed, heads, kv_heads)
        part = dot(o, wo[layer], ((1,), (0,))).astype(BF16)
        h1 = h + lax.psum_scatter(part, "shard", scatter_dimension=0, tiled=True).astype(F32)
        r2 = rms_scale(h1)
        b = (h1 * r2 * gain_m).astype(BF16)
        b_all = lax.all_gather(b, "expert", axis=0, tiled=True)
        mask = plane_masks[layer].astype(F32) > 0
        logits = jnp.where(mask, dot(b_all, router, ((1,), (0,))), MASKED_SCORE)
        ex = jnp.where(mask, jnp.exp(logits - jnp.max(logits, axis=1, keepdims=True)), 0.0)
        gates = ex / jnp.sum(ex, axis=1, keepdims=True)
        own_gates = lax.dynamic_slice_in_dim(gates, owner * EXP_DEV, EXP_DEV, 1)
        kept, scaled = [], []
        for j in range(EXP_DEV):
            gu = dot(b_all, wgu[layer, j], ((1,), (0,)))
            g, u = gu[:, :FF], gu[:, FF:]
            scaled.append((g * jax.nn.sigmoid(g) * u * own_gates[:, j : j + 1]).astype(BF16))
            kept.append(gu.astype(BF16))
        scaled = jnp.concatenate(scaled, axis=1)
        moe_part = dot(scaled, wd[layer].reshape(EXP_DEV * FF, width), ((1,), (0,))).astype(BF16)
        moe = lax.psum_scatter(moe_part, "expert", scatter_dimension=0, tiled=True).astype(F32)
        state = (h, r1, a_half, p, heads_in, o, h1, r2, b_all, own_gates, kept, scaled, moe)
        return h1 + moe, state

    def backward(layer, dout, dout_low, state):
        h, r1, a_half, p, heads_in, o, h1, r2, b_all, own_gates, kept, scaled, moe = state
        gain_a = small[layer, :, experts].astype(F32)[None, :]
        gain_m = small[layer, :, experts + 1].astype(F32)[None, :]
        router = small[layer, :, :experts]
        own_router = lax.dynamic_slice_in_dim(router, owner * EXP_DEV, EXP_DEV, 1)
        total = lax.all_gather(jnp.sum(dout * moe, axis=1), "expert", axis=0, tiled=True)
        dout_all = lax.all_gather(dout_low, "expert", axis=0, tiled=True)
        dgus, dcs = [], []
        for j in range(EXP_DEV):
            gate = own_gates[:, j : j + 1]
            g, u = kept[j][:, :FF].astype(F32), kept[j][:, FF:].astype(F32)
            sig = jax.nn.sigmoid(g)
            silu = g * sig
            dz = dot(dout_all, wd[layer, j], ((1,), (1,)))
            dgate = jnp.sum(dz * silu * u, axis=1, keepdims=True)
            dcs.append(gate * (dgate - total[:, None]))
            dz = dz * gate
            dgus.append(
                jnp.concatenate(
                    [dz * u * sig * (1.0 + g * (1.0 - sig)), dz * silu], axis=1
                ).astype(BF16)
            )
        dc = jnp.concatenate(dcs, axis=1)
        db_part = sum(dot(dgus[j], wgu[layer, j], ((1,), (1,))) for j in range(EXP_DEV))
        for j in range(EXP_DEV):
            db_part = db_part + dc[:, j : j + 1] * own_router[:, j].astype(F32)[None, :]
        db = lax.psum_scatter(
            db_part.astype(BF16), "expert", scatter_dimension=0, tiled=True
        ).astype(F32)
        grad_down = dot(scaled, dout_all, ((0,), (0,))).reshape(EXP_DEV, FF, width)
        grad_gu = jnp.stack([dot(b_all, dgus[j], ((0,), (0,))) for j in range(EXP_DEV)])
        grad_router = lax.dot_general(
            dc, b_all.astype(F32), (((0,), (0,)), ((), ())), precision=lax.Precision.HIGHEST
        )
        normed = h1 * r2
        grad_gain_m = jnp.sum(db * normed, axis=0)
        scaled_db = db * gain_m
        dh1 = dout + r2 * (scaled_db - normed * jnp.mean(scaled_db * normed, axis=1, keepdims=True))
        dattn = lax.all_gather(dh1.astype(BF16), "shard", axis=0, tiled=True)
        do = dot(dattn, wo[layer], ((1,), (1,))).astype(BF16)
        grad_out = dot(o, dattn, ((0,), (0,)))
        dqkv = lax.all_gather(plain_attention_backward(do, p, heads_in), "shard", axis=0, tiled=False)
        da = 0.0
        grad_qkv = []
        for part in range(3):
            grad_qkv.append([])
        for j in range(n_shard):
            at_local = 0
            for part, (at, size) in enumerate(column_parts(n_shard, j)):
                piece = dqkv[j, :, at_local : at_local + size]
                at_local += size
                da = da + dot(piece, wq[layer, :, at : at + size], ((1,), (1,)))
                grad_qkv[part].append(dot(a_half, piece, ((0,), (0,))))
        grad_qkv = jnp.concatenate([x for part in grad_qkv for x in part], axis=1)
        da = lax.all_to_all(
            da.astype(BF16), "shard", split_axis=0, concat_axis=1, tiled=True
        ).astype(F32)
        normed = h * r1
        grad_gain_a = jnp.sum(da * normed, axis=0)
        scaled_da = da * gain_a
        dh = dh1 + r1 * (scaled_da - normed * jnp.mean(scaled_da * normed, axis=1, keepdims=True))
        return dh, (grad_qkv, grad_out, grad_router, grad_gain_a, grad_gain_m, grad_gu, grad_down)

    out0, state0 = forward(0, x_in.astype(F32))
    mid = out0.astype(BF16).astype(F32)
    final, state1 = forward(1, mid)
    dh_one, grads1 = backward(1, dy.astype(F32), dy, state1)
    low = dh_one.astype(BF16)
    dh_zero, grads0 = backward(0, low.astype(F32), low, state0)

    def half_sum(grad):
        low_grad = grad.astype(BF16)
        halves = low_grad.reshape((2, -1) + low_grad.shape[1:])
        got = swap_cores(pick(halves, 1 - sec))
        return (pick(halves, sec).astype(F32) + got.astype(F32)).astype(BF16)

    def to_owner(half0, half1):
        keep = jnp.where(sec == 0, half0, half1)
        got = swap_cores(jnp.where(sec == 0, half1, half0))
        first = jnp.where(sec == 0, keep, got)
        second = jnp.where(sec == 0, got, keep)
        return jnp.concatenate([first, second], axis=0).astype(F32)

    attn_halves, exp_halves = [], []
    for grads in (grads0, grads1):
        attn = half_sum(jnp.concatenate([grads[0], grads[1]], axis=1))
        attn_halves.append(lax.psum(attn, "expert"))
        exp_halves.append(tuple(lax.psum(half_sum(g), "shard") for g in (grads[5], grads[6])))
    attn = to_owner(*attn_halves)
    grad_qkv, grad_out = attn[:, : w_qkv.shape[2]], attn[:, w_qkv.shape[2] :]
    grad_gu = to_owner(exp_halves[0][0], exp_halves[1][0])
    grad_down = to_owner(exp_halves[0][1], exp_halves[1][1])

    tiny = []
    for grads in (grads0, grads1):
        hot = jnp.arange(experts)[:, None] == owner * EXP_DEV + jnp.arange(EXP_DEV)[None, :]
        router = sum(
            jnp.where(hot[:, j : j + 1], grads[2][j][None, :], 0.0) for j in range(EXP_DEV)
        )
        tiny.append(jnp.concatenate([router, grads[3][None, :], grads[4][None, :]], axis=0))
    tiny = lax.psum(jnp.stack(tiny), ("section", "expert", "shard"))
    tiny = lax.dynamic_slice_in_dim(pick(tiny, sec), shard_pos * half, half, 1)

    send = jnp.where(sec == 0, final, dh_zero)
    keep = jnp.where(sec == 0, dh_zero, final)
    got = swap_cores(send)
    edge = jnp.where(sec == 0, jnp.stack([keep, got]), jnp.stack([got, keep]))
    return (
        edge[None],
        grad_qkv[None],
        grad_out[None],
        tiny[:experts].T[None],
        tiny[experts][None],
        tiny[experts + 1][None],
        grad_gu[None],
        grad_down[None],
    )


def kernel_shards(
    edge_inputs, seq_lengths, routes, w_qkv, w_out, w_router, gain_attn, gain_moe, w_gate_up, w_down
):
    sec = lax.axis_index("section")
    owner = lax.axis_index("expert")
    shard_pos = lax.axis_index("shard")
    rows, width = edge_inputs.shape[2], edge_inputs.shape[3]
    experts = w_router.shape[2]
    half = width // 2
    attn_cols = w_qkv.shape[2] + w_out.shape[2]

    def pick(array, index):
        return lax.dynamic_index_in_dim(array, index, 0, keepdims=False)

    def swap_shards(value):
        return lax.ppermute(value, "shard", [(0, 1), (1, 0)])

    def by_core(own, other):
        return jnp.where(sec == 0, own, other), jnp.where(sec == 0, other, own)

    small = jnp.concatenate([w_router[0].T, gain_attn, gain_moe], axis=0)
    own_small = jnp.concatenate([small, swap_shards(small)], axis=0)
    own_small = jnp.where(
        shard_pos == 0,
        jnp.concatenate([own_small[: experts + 2], own_small[experts + 2 :]], axis=1),
        jnp.concatenate([own_small[experts + 2 :], own_small[: experts + 2]], axis=1),
    )
    layer_small = by_core(own_small, swap_cores(own_small))
    x_in, dy = by_core(pick(edge_inputs[0], sec), swap_cores(pick(edge_inputs[0], 1 - sec)))
    layer_routes = by_core(pick(routes[0], sec), swap_cores(pick(routes[0], 1 - sec)))
    allowed = document_mask(pick(seq_lengths, sec)[0], 2 * rows).astype(F32)
    attn_weights = (w_qkv[0], swap_cores(w_qkv[0]), w_out[0], swap_cores(w_out[0]))
    expert_weights = (
        w_gate_up[0], swap_cores(w_gate_up[0]), w_down[0], swap_cores(w_down[0])
    )
    gains, routers, masks = [], [], []
    for layer in range(2):
        gains.append(
            jnp.pad(layer_small[layer][experts:].astype(F32), ((0, 8 - 2), (0, 0)))
        )
        router = layer_small[layer][:experts]
        router = jnp.concatenate([router, router], axis=0)
        routers.append(jnp.pad(router, ((0, LANES - 2 * experts), (0, 0))))
        lane = jnp.arange(LANES, dtype=jnp.int32)[None, :]
        hot = jnp.any(layer_routes[layer][:, :, None] == lane[None] % experts, axis=1)
        masks.append(
            jnp.where(hot & (lane < 2 * experts), 1.0 + (lane >= experts), 0.0).astype(F32)
        )

    def forward(layer, h):
        block, h1, *attn_state = attention_forward(
            layer, h, allowed, gains[layer], routers[layer], masks[layer], attn_weights, 1 + layer
        )
        moe, *expert_state = moe_forward(layer, block, expert_weights, experts, 3 + layer)
        return h1 + moe, (h, h1, moe, attn_state, expert_state)

    def backward(layer, dout, state, later):
        h, h1, moe, attn_state, expert_state = state
        outer = jnp.sum(dout.astype(F32) * moe, axis=1, keepdims=True)
        block = with_lanes(dout, split_terms(outer))
        own_router = lax.dynamic_slice_in_dim(
            layer_small[layer].astype(F32), owner * EXP_DEV, EXP_DEV, 0
        )
        own_router = jnp.pad(own_router, ((0, 8 - EXP_DEV), (0, 0)))
        results = moe_backward(
            layer, block, own_router, expert_weights, expert_state, later, experts, 5 + layer
        )
        db, keep_gu, keep_down, send_gu, send_down, grad_router = results[:6]
        got = (swap_cores(send_gu), swap_cores(send_down))
        dh, columns, grad_attn = attention_backward(
            layer, experts, grad_router, db, dout, h1, h, gains[layer], *attn_state, attn_weights,
            7 + layer,
        )
        places = LINE * SIDE
        sub = half // (2 * places)
        grad_attn = grad_attn.reshape(places, 2, sub, attn_cols)
        columns = columns.reshape(2, places, 2, sub, LANES)
        return dh, grad_attn, columns, (keep_gu, keep_down) + got, results[6:8]

    out0, state0 = forward(0, x_in)
    final, state1 = forward(1, out0.astype(BF16))
    dh_one, attn1, columns1, experts1, _ = backward(1, dy, state1, ())
    dh_zero, attn0, columns0, experts0, sums1 = backward(
        0, dh_one.astype(BF16), state0, experts1
    )
    moved1 = [lax.ppermute(value, "section", [(0, 1)]) for value in sums1]
    attn, gu_own, down_own, gu_got, down_got = reduce_gradients(
        attn1, attn0, columns1, columns0, *experts0, 9
    )
    grad_qkv, grad_out, grad_gu, grad_down = finish_outputs(
        attn,
        (gu_own, gu_got, sums1[0], moved1[0]),
        (down_own, down_got, sums1[1], moved1[1]),
        w_qkv.shape[2],
        w_out.shape[2],
    )
    tiny = attn[:, attn_cols : attn_cols + experts + 2].astype(F32)

    send = jnp.where(sec == 0, final, dh_zero)
    keep = jnp.where(sec == 0, dh_zero, final)
    got = swap_cores(send)
    edge = jnp.where(sec == 0, jnp.stack([keep, got]), jnp.stack([got, keep]))
    return (
        edge[None],
        grad_qkv[None],
        grad_out[None],
        tiny[:, :experts][None],
        tiny[:, experts][None],
        tiny[:, experts + 1][None],
        grad_gu[None],
        grad_down[None],
    )


def shards(*arrays):
    if lax.axis_size("expert") == LINE * SIDE and lax.axis_size("shard") == 2:
        return kernel_shards(*arrays)
    return plain_shards(*arrays)


def solution(mesh):
    in_specs = (
        P("section", None, ("expert", "shard"), None),
        P(None, "expert", None),
        P("section", None, ("expert", "shard"), None),
        P("section", "shard", None),
        P("section", "shard", None),
        P("section", "shard", None),
        P("section", "shard"),
        P("section", "shard"),
        P("section", "expert", None, None),
        P("section", "expert", None, None),
    )
    out_specs = (
        P("section", None, ("expert", "shard"), None),
        P("section", "shard", None),
        P("section", "shard", None),
        P("section", "shard", None),
        P("section", "shard"),
        P("section", "shard"),
        P("section", "expert", None, None),
        P("section", "expert", None, None),
    )
    return jax.shard_map(shards, mesh=mesh, in_specs=in_specs, out_specs=out_specs, check_vma=False)
```

```python
import functools

import jax
import jax.numpy as jnp
from jax import lax
from jax.experimental import pallas as pl
from jax.experimental.pallas import tpu as pltpu
from jax.sharding import PartitionSpec as P

QUERY_HEADS = 24
KEY_VALUE_HEADS = 8
HEAD_SIZE = 64
FF = 512
TOP = 8
EXP_DEV = 2
EPS = 1e-05
MASKED_SCORE = -1e30
QUERY_WIDTH = QUERY_HEADS * HEAD_SIZE
KV_WIDTH = KEY_VALUE_HEADS * HEAD_SIZE
F32 = jnp.float32
BF16 = jnp.bfloat16
MESH = pl.DeviceIdType.MESH
LINE = 4
SIDE = 2
LANES = 128
HALVES = 2
TILE = 256
VMEM_BYTES = 60 * 2**20
COST = pl.CostEstimate(flops=10**11, bytes_accessed=2**24, transcendentals=0)


def chunk_order(z, t):
    near = z + 1 - 2 * lax.rem(z, 2)
    third = jnp.where(z < 2, 2, 1)
    last = jnp.where(z < 2, 3, 0)
    return jnp.where(t == 0, z, jnp.where(t == 1, near, jnp.where(t == 2, third, last)))


def sum_order(z, i):
    first = jnp.where((z == 0) | (z == 2), 1, 2)
    second = jnp.where(z == 0, 2, jnp.where(z == 1, 3, jnp.where(z == 2, 0, 1)))
    third = jnp.where(z == 0, 3, jnp.where(z == 1, 0, jnp.where(z == 2, 3, 0)))
    return jnp.where(i == 0, first, jnp.where(i == 1, second, third))


class Plane:
    def __init__(self, rows, refs):
        (self.gathered, self.parts, self.from_side, self.from_low, self.from_high, self.sums,
         self.line_send, self.gather_recv, self.side_send, self.side_recv,
         self.sum_send, self.low_recv, self.high_recv) = refs
        self.sub = rows // HALVES
        self.both = SIDE * self.sub
        self.sec, self.owner, self.shard = (lax.axis_index(n) for n in ("section", "expert", "shard"))
        self.z, self.x = lax.div(self.owner, SIDE), lax.rem(self.owner, SIDE)
        self.inner = ((self.z > 0) & (self.z < LINE - 1)).astype(jnp.int32)

    def device(self, z, x):
        return (self.sec, z * SIDE + x, self.shard)

    def other_core(self):
        return (1 - self.sec, self.owner, self.shard)

    def other_shard(self):
        return (self.sec, self.owner, 1 - self.shard)

    def chunk(self, c, h):
        return pl.ds(pl.multiple_of((c * HALVES + h) * self.both, self.both), self.both)

    def block(self, c, h, x):
        return pl.ds(pl.multiple_of((c * HALVES + h) * self.both + x * self.sub, self.sub), self.sub)

    def barrier(self, *others):
        z, x = self.z, self.x
        sem = pltpu.get_barrier_semaphore()

        def greet(device):
            pl.semaphore_signal(sem, inc=1, device_id=device, device_id_type=MESH)

        for other in others:
            greet(other)
        greet(self.device(z, 1 - x))
        pl.when(z > 0)(lambda: greet(self.device(z - 1, x)))
        pl.when(z < LINE - 1)(lambda: greet(self.device(z + 1, x)))
        pl.semaphore_wait(sem, 2 + len(others) + self.inner)

    def place(self, block_ref):
        for h in range(HALVES):
            self.gathered[self.block(self.z, h, self.x)] = block_ref[pl.ds(h * self.sub, self.sub)]

    def gather_copy(self, way, c, h, x, device):
        ref = self.gathered.at[self.block(c, h, x)]
        q = c * HALVES + h
        return pltpu.make_async_remote_copy(
            src_ref=ref, dst_ref=ref, send_sem=self.line_send.at[way, q],
            recv_sem=self.gather_recv.at[q, x], device_id=device, device_id_type=MESH)

    def forward_up(self, c, h):
        return self.gather_copy(0, c, h, self.x, self.device(self.z + 1, self.x))

    def forward_down(self, c, h):
        return self.gather_copy(1, c, h, self.x, self.device(self.z - 1, self.x))

    def forward_side(self, c, h):
        return self.gather_copy(2, c, h, self.x, self.device(self.z, 1 - self.x))

    def start_gather(self):
        z = self.z
        for h in range(HALVES):
            pl.when(z < LINE - 1)(lambda h=h: self.forward_up(z, h).start())
            pl.when(z > 0)(lambda h=h: self.forward_down(z, h).start())
            self.forward_side(z, h).start()

    def relay(self, t, h):
        z = self.z

        @pl.when((t > 0) & (z - t >= 0))
        def _():
            c = z - t
            self.forward_side(c, h).wait_recv()
            pl.when(z < LINE - 1)(lambda: self.forward_up(c, h).start())
            self.forward_side(c, h).start()

        @pl.when((t > 0) & (z + t <= LINE - 1))
        def _():
            c = z + t
            self.forward_side(c, h).wait_recv()
            pl.when(z > 0)(lambda: self.forward_down(c, h).start())
            self.forward_side(c, h).start()

    def wait_side_block(self, c, h):
        self.gather_copy(2, c, h, 1 - self.x, self.device(self.z, 1 - self.x)).wait_recv()

    def side_copy(self, c, h):
        q = c * HALVES + h
        return pltpu.make_async_remote_copy(
            src_ref=self.parts.at[self.block(c, h, 1 - self.x)], dst_ref=self.from_side.at[q],
            send_sem=self.side_send.at[q], recv_sem=self.side_recv.at[q],
            device_id=self.device(self.z, 1 - self.x), device_id_type=MESH)

    def up_copy(self, c, h):
        q = c * HALVES + h
        return pltpu.make_async_remote_copy(
            src_ref=self.sums.at[q], dst_ref=self.from_low.at[q], send_sem=self.sum_send.at[q],
            recv_sem=self.low_recv.at[q], device_id=self.device(self.z + 1, self.x), device_id_type=MESH)

    def down_copy(self, c, h):
        q = c * HALVES + h
        return pltpu.make_async_remote_copy(
            src_ref=self.sums.at[q], dst_ref=self.from_high.at[q], send_sem=self.sum_send.at[q],
            recv_sem=self.high_recv.at[q], device_id=self.device(self.z - 1, self.x), device_id_type=MESH)

    def own_part(self, c, h):
        return (self.parts[self.block(c, h, self.x)].astype(F32)
                + self.from_side[c * HALVES + h].astype(F32))

    def pass_sum(self, t, h):
        i = t - 3 - self.inner
        pl.when((i >= 0) & (i < LINE - 1))(lambda: self.pass_chunk(sum_order(self.z, i), h))

    def pass_chunk(self, c, h):
        z = self.z
        q = c * HALVES + h
        self.side_copy(c, h).wait_recv()

        @pl.when(c > z)
        def _():
            @pl.when(z > 0)
            def _():
                self.up_copy(c, h).wait_recv()
                self.sums[q] = (self.own_part(c, h) + self.from_low[q].astype(F32)).astype(BF16)

            @pl.when(z == 0)
            def _():
                self.sums[q] = self.own_part(c, h).astype(BF16)

            self.up_copy(c, h).start()

        @pl.when(c < z)
        def _():
            @pl.when(z < LINE - 1)
            def _():
                self.down_copy(c, h).wait_recv()
                self.sums[q] = (self.own_part(c, h) + self.from_high[q].astype(F32)).astype(BF16)

            @pl.when(z == LINE - 1)
            def _():
                self.sums[q] = self.own_part(c, h).astype(BF16)

            self.down_copy(c, h).start()

    def finish_sum(self, h, out_ref):
        z = self.z
        q = z * HALVES + h
        rows = pl.ds(pl.multiple_of(h * self.sub, self.sub), self.sub)
        self.side_copy(z, h).wait_recv()
        out_ref[rows] = self.own_part(z, h)

        @pl.when(z > 0)
        def _():
            self.up_copy(z, h).wait_recv()
            out_ref[rows] += self.from_low[q].astype(F32)

        @pl.when(z < LINE - 1)
        def _():
            self.down_copy(z, h).wait_recv()
            out_ref[rows] += self.from_high[q].astype(F32)

    def finish_piece(self, h, out_ref):
        z = self.z
        q = z * HALVES + h
        self.side_copy(z, h).wait_recv()

        @pl.when(z == 0)
        def _():
            self.down_copy(z, h).wait_recv()
            out_ref[h] = (self.own_part(z, h) + self.from_high[q].astype(F32)).astype(BF16)

        @pl.when(z == LINE - 1)
        def _():
            self.up_copy(z, h).wait_recv()
            out_ref[h] = (self.own_part(z, h) + self.from_low[q].astype(F32)).astype(BF16)

        @pl.when((z > 0) & (z < LINE - 1))
        def _():
            self.up_copy(z, h).wait_recv()
            self.down_copy(z, h).wait_recv()
            total = self.own_part(z, h) + self.from_low[q].astype(F32)
            out_ref[h] = (total + self.from_high[q].astype(F32)).astype(BF16)

    def drain(self):
        z = self.z

        def one(q, carry):
            c, h = lax.div(q, HALVES), lax.rem(q, HALVES)
            pl.when((z < LINE - 1) & (c <= z))(lambda: self.forward_up(c, h).wait_send())
            pl.when((z > 0) & (c >= z))(lambda: self.forward_down(c, h).wait_send())
            self.forward_side(c, h).wait_send()
            self.side_copy(c, h).wait_send()
            pl.when(c > z)(lambda: self.up_copy(c, h).wait_send())
            pl.when(c < z)(lambda: self.down_copy(c, h).wait_send())
            return carry

        lax.fori_loop(0, LINE * HALVES, one, 0)


def plane_scratch(rows, width, wide):
    count = LINE * HALVES
    block = pltpu.VMEM((count, rows // HALVES, width), BF16)
    return [
        pltpu.VMEM((LINE * SIDE * rows, wide), BF16),
        pltpu.VMEM((LINE * SIDE * rows, width), BF16),
        block, block, block, block,
        pltpu.SemaphoreType.DMA((3, count)),
        pltpu.SemaphoreType.DMA((count, SIDE)),
        pltpu.SemaphoreType.DMA((count,)),
        pltpu.SemaphoreType.DMA((count,)),
        pltpu.SemaphoreType.DMA((count,)),
        pltpu.SemaphoreType.DMA((count,)),
        pltpu.SemaphoreType.DMA((count,)),
    ]


def lane_tile(at, size=TILE):
    return pl.ds(pl.multiple_of(at * size, size), size)


def nn(a, b):
    return jnp.dot(a, b, preferred_element_type=F32)


def nt(a, b):
    return lax.dot_general(a, b, (((1,), (1,)), ((), ())), preferred_element_type=F32)


def tn(a, b):
    return lax.dot_general(a, b, (((0,), (0,)), ((), ())), preferred_element_type=F32)


def pick_lane(block, wanted):
    lane = lax.broadcasted_iota(jnp.int32, block.shape, 1)
    hot = lane == wanted[0]
    for other in wanted[1:]:
        hot = hot | (lane == other)
    return jnp.sum(jnp.where(hot, block, 0.0), axis=1, keepdims=True)


def own_gates(block, owner, experts):
    block = block.astype(F32)
    return [
        pick_lane(block, (owner * EXP_DEV + j, experts + owner * EXP_DEV + j)) for j in range(EXP_DEV)
    ]


def load_layer(layer, sec, own, other, dst, sem):
    copies = [pltpu.make_async_copy(own, dst, sem), pltpu.make_async_copy(other, dst, sem)]
    pl.when(sec == layer)(lambda: copies[0].start())
    pl.when(sec != layer)(lambda: copies[1].start())
    return copies[0]


def load_experts(layer, sec, gu, gu_other, down, down_other, gu_v, down_v, sems):
    loads = [load_layer(layer, sec, gu, gu_other, gu_v, sems.at[0])]
    for j in range(EXP_DEV):
        loads.append(load_layer(
            layer, sec, down.at[j], down_other.at[j], down_v.at[pl.ds(j * FF, FF)], sems.at[1 + j]))
    return loads


def moe_forward_kernel(layer, experts, rows, width, block_ref, gu_hbm, gu_other, down_hbm, down_other,
                       moe_ref, rows_hbm, kept_hbm, scaled_hbm,
                       gu_v, down_v, kept, scaled, load_sem, store_sem, *plane_refs):
    plane = Plane(rows, plane_refs)
    gathered, parts = plane.gathered, plane.parts
    loads = load_experts(layer, plane.sec, gu_hbm, gu_other, down_hbm, down_other, gu_v, down_v, load_sem)
    plane.place(block_ref)
    plane.barrier()
    plane.start_gather()
    for load in loads:
        load.wait()

    def stores(c, h):
        q, at = c * HALVES + h, plane.chunk(c, h)
        return [
            pltpu.make_async_copy(gathered.at[at], rows_hbm.at[at], store_sem.at[0, q]),
            pltpu.make_async_copy(kept.at[at], kept_hbm.at[at], store_sem.at[1, q]),
            pltpu.make_async_copy(scaled.at[at], scaled_hbm.at[at], store_sem.at[2, q]),
        ]

    def step(k, carry):
        t, h = lax.div(k, HALVES), lax.rem(k, HALVES)
        plane.relay(t, h)
        plane.pass_sum(t, h)
        pl.when(t > 0)(lambda: work(chunk_order(plane.z, t - 1), h))
        return carry

    def work(c, h):
        at = plane.chunk(c, h)
        plane.wait_side_block(c, h)
        gates = own_gates(gathered[at, pl.ds(width, LANES)], plane.owner, experts)
        for j in range(EXP_DEV):
            for f in range(FF // TILE):
                data = gathered[at, pl.ds(0, width)]
                low, high = j * 2 * FF + f * TILE, j * 2 * FF + FF + f * TILE
                g = nn(data, gu_v[j, :, pl.ds(f * TILE, TILE)])
                u = nn(data, gu_v[j, :, pl.ds(FF + f * TILE, TILE)])
                z = g * jax.nn.sigmoid(g) * u * gates[j]
                scaled[at, pl.ds(j * FF + f * TILE, TILE)] = z.astype(BF16)
                kept[at, pl.ds(low, TILE)] = g.astype(BF16)
                kept[at, pl.ds(high, TILE)] = u.astype(BF16)
        for n in range(width // TILE):
            parts[at, pl.ds(n * TILE, TILE)] = nn(
                scaled[at, :], down_v[:, pl.ds(n * TILE, TILE)]).astype(BF16)
        plane.side_copy(c, h).start()
        for store in stores(c, h):
            store.start()

    lax.fori_loop(0, (LINE + 1) * HALVES, step, 0)

    def tail(k, carry):
        plane.pass_sum(lax.div(k, HALVES), lax.rem(k, HALVES))
        return carry

    lax.fori_loop((LINE + 1) * HALVES, (LINE + 3) * HALVES, tail, 0)

    def finish(h, carry):
        plane.finish_sum(h, moe_ref)
        return carry

    lax.fori_loop(0, HALVES, finish, 0)
    plane.drain()

    def stored(q, carry):
        for store in stores(lax.div(q, HALVES), lax.rem(q, HALVES)):
            store.wait()
        return carry

    lax.fori_loop(0, LINE * HALVES, stored, 0)


def moe_forward(layer, block, weights, experts, collective_id):
    rows, wide = block.shape
    width = wide - LANES
    total = LINE * SIDE * rows
    any_spec = pl.BlockSpec(memory_space=pl.ANY)
    vmem = pl.BlockSpec(memory_space=pltpu.VMEM)
    return pl.pallas_call(
        functools.partial(moe_forward_kernel, layer, experts, rows, width),
        name="moe_forward",
        out_shape=(
            jax.ShapeDtypeStruct((rows, width), F32),
            jax.ShapeDtypeStruct((total, wide), BF16),
            jax.ShapeDtypeStruct((total, EXP_DEV * 2 * FF), BF16),
            jax.ShapeDtypeStruct((total, EXP_DEV * FF), BF16),
        ),
        in_specs=[vmem] + [any_spec] * 4,
        out_specs=(vmem, any_spec, any_spec, any_spec),
        scratch_shapes=[
            pltpu.VMEM((EXP_DEV, width, 2 * FF), BF16),
            pltpu.VMEM((EXP_DEV * FF, width), BF16),
            pltpu.VMEM((total, EXP_DEV * 2 * FF), BF16),
            pltpu.VMEM((total, EXP_DEV * FF), BF16),
            pltpu.SemaphoreType.DMA((1 + EXP_DEV,)),
            pltpu.SemaphoreType.DMA((3, LINE * HALVES)),
        ] + plane_scratch(rows, width, wide),
        cost_estimate=COST,
        compiler_params=pltpu.CompilerParams(
            collective_id=collective_id, has_side_effects=True, vmem_limit_bytes=VMEM_BYTES),
    )(block, *weights)


def moe_backward_kernel(layer, experts, rows, width, beside, block_ref, router_ref, gu_hbm, gu_other, down_hbm,
                        down_other, rows_hbm, kept_hbm, scaled_hbm, *refs):
    (later, refs) = (refs[:4], refs[4:]) if beside else ((), refs)
    (db_ref, keep_gu_hbm, keep_down_hbm, send_gu_hbm, send_down_hbm, grad_router_ref), refs = refs[:6], refs[6:]
    (later_out, refs) = (refs[:3], refs[3:]) if beside else ((), refs)
    (gu_v, down_v, fwd_rows, kept, scaled, dgu, send_gu, grad_gu, send_down, grad_down,
     load_sem, store_sem), refs = refs[:12], refs[12:]
    (later_v, refs) = (refs[:8], refs[8:]) if beside else ((), refs)
    plane_refs = refs
    plane = Plane(rows, plane_refs)
    gathered, parts = plane.gathered, plane.parts
    loads = load_experts(layer, plane.sec, gu_hbm, gu_other, down_hbm, down_other, gu_v, down_v, load_sem)
    loads.append(pltpu.make_async_copy(rows_hbm, fwd_rows, load_sem.at[3]))
    loads.append(pltpu.make_async_copy(kept_hbm, kept, load_sem.at[4]))
    loads.append(pltpu.make_async_copy(scaled_hbm, scaled, load_sem.at[5]))
    for load in loads[3:]:
        load.start()
    plane.place(block_ref)
    plane.barrier(*([plane.other_core(), plane.other_shard()] if beside else []))
    plane.start_gather()
    if beside:
        other_layer = LaterExperts(plane, *later, *later_out, *later_v)
        other_layer.start_loads()
    for load in loads:
        load.wait()
    if beside:
        other_layer.send()
    total = plane.both
    up_at = EXP_DEV * 2 * FF

    def step(k, carry):
        t, h = lax.div(k, HALVES), lax.rem(k, HALVES)
        plane.relay(t, h)
        plane.pass_sum(t, h)
        pl.when(t > 0)(lambda: work(chunk_order(plane.z, t - 1), h))
        return carry

    def work(c, h):
        at = plane.chunk(c, h)
        plane.wait_side_block(c, h)
        gates = own_gates(fwd_rows[at, pl.ds(width, LANES)], plane.owner, experts)
        outer = jnp.sum(gathered[at, pl.ds(width, LANES)].astype(F32), axis=1, keepdims=True)
        dcs = []
        for j in range(EXP_DEV):
            dgate = jnp.zeros((total, 1), F32)
            for f in range(FF // TILE):
                low, high = pl.ds(j * 2 * FF + f * TILE, TILE), pl.ds(j * 2 * FF + FF + f * TILE, TILE)
                dz = nt(gathered[at, pl.ds(0, width)], down_v[pl.ds(j * FF + f * TILE, TILE), :])
                g = kept[at, low].astype(F32)
                u = kept[at, high].astype(F32)
                sig = jax.nn.sigmoid(g)
                silu = g * sig
                dgate = dgate + jnp.sum(dz * silu * u, axis=1, keepdims=True)
                dz = dz * gates[j]
                dgu[at, low] = (dz * u * sig * (1.0 + g * (1.0 - sig))).astype(BF16)
                dgu[at, high] = (dz * silu).astype(BF16)
            dcs.append(gates[j] * (dgate - outer))
        lane = lax.broadcasted_iota(jnp.int32, (total, LANES), 1)
        extra = jnp.zeros((total, LANES), F32)
        for j in range(EXP_DEV):
            top = dcs[j].astype(BF16).astype(F32)
            column = plane.owner * EXP_DEV + j
            extra = extra + jnp.where(lane == column, top, 0.0)
            extra = extra + jnp.where(lane == LANES // 2 + column, dcs[j] - top, 0.0)
        dgu[at, pl.ds(up_at, LANES)] = extra.astype(BF16)
        for n in range(width // TILE):
            cols = pl.ds(n * TILE, TILE)
            acc = nt(dgu[at, pl.ds(0, 2 * FF)], gu_v[0, cols, :])
            for j in range(1, EXP_DEV):
                acc = acc + nt(dgu[at, pl.ds(j * 2 * FF, 2 * FF)], gu_v[j, cols, :])
            for j in range(EXP_DEV):
                acc = acc + dcs[j] * router_ref[pl.ds(j, 1), cols]
            parts[at, cols] = acc.astype(BF16)
        plane.side_copy(c, h).start()

    lax.fori_loop(0, (LINE + 1) * HALVES, step, 0)

    core = plane.sec
    gu_steps, down_steps = width // TILE, FF // TILE

    def stores_gu(n):
        at = lane_tile(n)
        return [pltpu.make_async_copy(send_gu.at[at], send_gu_hbm.at[at], store_sem.at[0, n]),
                pltpu.make_async_copy(grad_gu.at[at], keep_gu_hbm.at[at], store_sem.at[1, n])]

    def stores_down(n):
        at = lane_tile(n)
        return [pltpu.make_async_copy(send_down.at[at], send_down_hbm.at[at], store_sem.at[2, n]),
                pltpu.make_async_copy(grad_down.at[at], keep_down_hbm.at[at], store_sem.at[3, n])]

    def expert_cols(j, size):
        return pl.ds(pl.multiple_of(j * size, size), size)

    def grad_gu_rows(n):
        rows_t = fwd_rows[:, lane_tile(n)]
        send_gu[lane_tile(n), :] = tn(rows_t, dgu[:, expert_cols(1 - core, 2 * FF)]).astype(BF16)
        grad_gu[lane_tile(n), :] = tn(rows_t, dgu[:, expert_cols(core, 2 * FF)]).astype(BF16)
        grad_router_ref[lane_tile(n), :] = tn(rows_t, dgu[:, pl.ds(up_at, LANES)])
        for store in stores_gu(n):
            store.start()

    def grad_down_rows(n):
        def cols(j):
            return pl.ds(pl.multiple_of(j * FF + n * TILE, TILE), TILE)

        data = gathered[:, pl.ds(0, width)]
        send_down[lane_tile(n), :] = tn(scaled[:, cols(1 - core)], data).astype(BF16)
        grad_down[lane_tile(n), :] = tn(scaled[:, cols(core)], data).astype(BF16)
        for store in stores_down(n):
            store.start()

    slots = 2 * HALVES

    def tail(k, carry):
        pl.loop(lax.div(k * gu_steps, slots), lax.div((k + 1) * gu_steps, slots))(grad_gu_rows)
        plane.pass_sum(LINE + 1 + lax.div(k, HALVES), lax.rem(k, HALVES))
        return carry

    lax.fori_loop(0, slots, tail, 0)
    pl.loop(0, down_steps)(grad_down_rows)

    def finish(h, carry):
        plane.finish_sum(h, db_ref)
        return carry

    lax.fori_loop(0, HALVES, finish, 0)
    if beside:
        other_layer.finish()
    plane.drain()
    for n in range(gu_steps):
        for store in stores_gu(n):
            store.wait()
    for n in range(down_steps):
        for store in stores_down(n):
            store.wait()


class LaterExperts:
    def __init__(self, plane, keep_gu, keep_down, send_gu, send_down, sum_gu_hbm, sum_down_hbm, land_gu,
                 gu_a, gu_b, down_a, down_b, load_sem, core_sem, send_sem, recv_sem):
        self.parts = []
        for keep, sent, out, land, a, b, count in (
            (keep_gu, send_gu, sum_gu_hbm, land_gu, gu_a, gu_b, 4),
            (keep_down, send_down, sum_down_hbm, None, down_a, down_b, 2),
        ):
            size = a.shape[0] // count
            for n in range(count):
                at, k = pl.ds(n * size, size), len(self.parts)
                shard_copy = land_copy = None
                if land is not None:
                    shard_copy = pltpu.make_async_remote_copy(
                        src_ref=a.at[at], dst_ref=land.at[at], send_sem=send_sem.at[k], recv_sem=recv_sem.at[k],
                        device_id=plane.other_shard(), device_id_type=MESH)
                    land_copy = pltpu.make_async_copy(land.at[at], b.at[at], load_sem.at[1, k])
                self.parts.append((
                    a.at[at], b.at[at],
                    pltpu.make_async_copy(keep.at[at], a.at[at], load_sem.at[0, k]),
                    pltpu.make_async_remote_copy(
                        src_ref=sent.at[at], dst_ref=b.at[at], send_sem=core_sem.at[0, k],
                        recv_sem=core_sem.at[1, k], device_id=plane.other_core(), device_id_type=MESH),
                    shard_copy, land_copy,
                    pltpu.make_async_copy(a.at[at], out.at[at], load_sem.at[2, k]),
                ))

    def start_loads(self):
        for _, _, load, core_copy, *_ in self.parts:
            load.start()
            core_copy.start()

    def send(self):
        for a, b, load, core_copy, shard_copy, _, store in self.parts:
            load.wait()
            core_copy.wait()
            a[...] = (a[...].astype(F32) + b[...].astype(F32)).astype(BF16)
            if shard_copy is not None:
                shard_copy.start()
            else:
                store.start()

    def finish(self):
        for _, _, _, _, shard_copy, land_copy, _ in self.parts:
            if shard_copy is not None:
                shard_copy.wait()
                land_copy.start()
        for a, b, _, _, shard_copy, land_copy, store in self.parts:
            if shard_copy is not None:
                land_copy.wait()
                a[...] = (a[...].astype(F32) + b[...].astype(F32)).astype(BF16)
                store.start()
        for *_, store in self.parts:
            store.wait()


def moe_backward(layer, block, router, weights, kept, later, experts, collective_id):
    rows, wide = block.shape
    width = wide - LANES
    total = LINE * SIDE * rows
    any_spec = pl.BlockSpec(memory_space=pl.ANY)
    vmem = pl.BlockSpec(memory_space=pltpu.VMEM)
    expert_gu, expert_down = pltpu.VMEM((width, 2 * FF), BF16), pltpu.VMEM((FF, width), BF16)
    gu_shape = jax.ShapeDtypeStruct((width, 2 * FF), BF16)
    down_shape = jax.ShapeDtypeStruct((FF, width), BF16)
    later_out, later_scratch = (), []
    if later:
        later_out = (gu_shape, down_shape, gu_shape)
        later_scratch = [
            expert_gu, expert_gu, expert_down, expert_down,
            pltpu.SemaphoreType.DMA((3, 6)), pltpu.SemaphoreType.DMA((2, 6)),
            pltpu.SemaphoreType.DMA((4,)), pltpu.SemaphoreType.DMA((4,)),
        ]
    return pl.pallas_call(
        functools.partial(moe_backward_kernel, layer, experts, rows, width, bool(later)),
        name="moe_backward",
        out_shape=(
            jax.ShapeDtypeStruct((rows, width), F32),
            gu_shape, down_shape, gu_shape, down_shape,
            jax.ShapeDtypeStruct((width, LANES), F32),
        ) + later_out,
        in_specs=[vmem, vmem] + [any_spec] * (7 + len(later)),
        out_specs=(vmem,) + (any_spec,) * 4 + (vmem,) + (any_spec,) * len(later_out),
        scratch_shapes=[
            pltpu.VMEM((EXP_DEV, width, 2 * FF), BF16),
            pltpu.VMEM((EXP_DEV * FF, width), BF16),
            pltpu.VMEM((total, wide), BF16),
            pltpu.VMEM((total, EXP_DEV * 2 * FF), BF16),
            pltpu.VMEM((total, EXP_DEV * FF), BF16),
            pltpu.VMEM((total, EXP_DEV * 2 * FF + LANES), BF16),
            expert_gu, expert_gu, expert_down, expert_down,
            pltpu.SemaphoreType.DMA((6,)),
            pltpu.SemaphoreType.DMA((4, width // TILE)),
        ] + later_scratch + plane_scratch(rows, width, wide),
        cost_estimate=COST,
        compiler_params=pltpu.CompilerParams(
            collective_id=collective_id, has_side_effects=True, vmem_limit_bytes=VMEM_BYTES),
    )(block, router, *weights, *kept, *later)


def split_terms(values):
    high = values.astype(BF16)
    return high, (values - high.astype(F32)).astype(BF16)


def with_lanes(block, columns):
    extra = jnp.concatenate(columns, axis=1)
    extra = jnp.pad(extra, ((0, 0), (0, LANES - extra.shape[1])))
    return jnp.concatenate([block, extra], axis=1)


def far_order(z, i):
    low = jnp.where(i == 0, 3, jnp.where(i == 1, jnp.where(z == 0, 2, 0), jnp.where(z == 0, 1, 2)))
    high = jnp.where(i == 0, 0, jnp.where(i == 1, jnp.where(z == 3, 1, 3), jnp.where(z == 3, 2, 1)))
    return jnp.where(z < 2, low, high)


def reduce_kernel(sub, cols, g1, g0, t1, t0, gu_hbm, down_hbm, sent_gu_hbm, sent_down_hbm, gu1_hbm, down1_hbm, edge,
                  sum_hbm, own_gu_hbm, own_down_hbm, got_gu_hbm, got_down_hbm, own_down1_hbm, got_gu1_hbm,
                  got_down1_hbm, got_edge,
                  core_got, small_own, small_got, result, own_gu, core_gu, other_gu, own_down, core_down, other_down,
                  own_down1, other_down1,
                  load_sem, expert_load_sem, expert_core_sem, edge_sem, core_sem, small_sem, move_sem, expert_sem, core_expert_sem, store_sem,
                  *plane_refs):
    plane = Plane(HALVES * sub, plane_refs)
    gathered, parts = plane.gathered, plane.parts
    core, shard, z, x = plane.sec, plane.shard, plane.z, plane.x
    wide = cols + LANES
    grads, smalls = (g1, g0), (t1, t0)
    diagonal = (1 - core, plane.owner, 1 - shard)
    places = [(c, side) for c in range(LINE) for side in range(SIDE)]

    def remote(src, dst, send_sem, recv_sem, device):
        return pltpu.make_async_remote_copy(
            src_ref=src, dst_ref=dst, send_sem=send_sem, recv_sem=recv_sem,
            device_id=device, device_id_type=MESH)

    loads = []
    for h in range(2):
        for n, (c, side) in enumerate(places):
            loads.append(pltpu.make_async_copy(
                grads[h].at[n, core], parts.at[plane.block(c, h, side), pl.ds(0, cols)], load_sem.at[h, n]))
        loads.append(pltpu.make_async_copy(
            smalls[h].at[shard, :, core], small_own.at[h], load_sem.at[h, len(places)]))
    pieces, expert_loads = [], []
    for layer, hbm, sent, own, there, other, own_hbm, got_hbm, count in (
        (1, down1_hbm, None, own_down1, None, other_down1, own_down1_hbm, got_down1_hbm, 2),
        (0, gu_hbm, sent_gu_hbm, own_gu, core_gu, other_gu, own_gu_hbm, got_gu_hbm, 4),
        (0, down_hbm, sent_down_hbm, own_down, core_down, other_down, own_down_hbm, got_down_hbm, 2),
    ):
        size = own.shape[0] // count
        for n in range(count):
            at, k = pl.ds(n * size, size), len(pieces)
            pieces.append((layer, own, there, other, own_hbm, got_hbm, at))
            expert_loads.append((
                pltpu.make_async_copy(hbm.at[at], own.at[at], expert_load_sem.at[k]),
                None if sent is None else remote(
                    sent.at[at], there.at[at], expert_core_sem.at[0, k], expert_core_sem.at[1, k],
                    plane.other_core()),
            ))
    for load in [load for load, _ in expert_loads[:2]] + loads + [load for load, _ in expert_loads[2:]]:
        load.start()
    plane.barrier(plane.other_core(), plane.other_shard(), diagonal)
    cores = [
        remote(grads[h].at[:, 1 - core], core_got.at[h], core_sem.at[0, h], core_sem.at[1, h], plane.other_core())
        for h in range(2)
    ]
    small = []
    for h in range(2):
        for n, (there, half, device) in enumerate((
            (shard, 1 - core, plane.other_core()),
            (1 - shard, core, plane.other_shard()),
            (1 - shard, 1 - core, diagonal),
        )):
            small.append(remote(
                smalls[h].at[there, :, half], small_got.at[h, n], small_sem.at[0, h, n], small_sem.at[1, h, n],
                device))
    for copy in cores[:1] + small + cores[1:]:
        copy.start()
    for _, copy in expert_loads:
        if copy is not None:
            copy.start()
    edges = remote(edge, got_edge, edge_sem.at[0], edge_sem.at[1], plane.other_core())
    edges.start()
    gu1_copy = remote(gu1_hbm, got_gu1_hbm, edge_sem.at[2], edge_sem.at[3], plane.other_core())
    pl.when(core == 0)(lambda: gu1_copy.start())
    exchange = []

    def send_piece():
        n = len(exchange)
        layer, own, there, other, own_hbm, got_hbm, at = pieces[n]
        for load in expert_loads[n]:
            if load is not None:
                load.wait()
        if there is not None:
            own[at] = (own[at].astype(F32) + there[at].astype(F32)).astype(BF16)
        exchange.append(
            remote(own.at[at], other.at[at], expert_sem.at[0, n], expert_sem.at[1, n], plane.other_shard()))
        exchange[-1].start()

    def prepare(h):
        cores[h].wait_recv()
        for copy in small[3 * h : 3 * h + 3]:
            copy.wait_recv()

        def one(k, carry):
            c = jnp.where(k < 2 * (LINE - 1), far_order(z, lax.div(k, 2)), z)
            side = jnp.where(lax.rem(k, 2) == 0, 1 - x, x)
            n = c * SIDE + side
            at = plane.block(c, h, side)
            parts[at, pl.ds(0, cols)] = (
                parts[at, pl.ds(0, cols)].astype(F32) + core_got[h, n].astype(F32)).astype(BF16)
            total = small_own[h, n].astype(F32)
            for other in range(3):
                total = total + small_got[h, other, n].astype(F32)
            parts[at, pl.ds(cols, LANES)] = total.astype(BF16)
            pl.when(side != x)(lambda: plane.side_copy(c, h).start())
            return carry

        lax.fori_loop(0, LINE * SIDE, one, 0)

    send_piece()
    send_piece()
    for load in loads:
        load.wait()
    prepare(0)
    send_piece()

    def pass_piece(i, h):
        plane.pass_chunk(far_order(z, i), h)

    def move(h):
        return remote(
            result.at[h], gathered.at[plane.block(z, core, x)], move_sem.at[0], move_sem.at[1], plane.other_core())

    def send_block(h):
        pl.when(z < LINE - 1)(lambda: plane.forward_up(z, h).start())
        pl.when(z > 0)(lambda: plane.forward_down(z, h).start())
        plane.forward_side(z, h).start()

    def finish(h):
        plane.finish_piece(h, result)
        own_layer = core == 1 - h
        pl.when(jnp.logical_not(own_layer))(lambda: move(h).start())

        @pl.when(own_layer)
        def _():
            gathered[plane.block(z, core, x)] = result[h]
            send_block(core)
            arrived = remote(
                result.at[h], gathered.at[plane.block(z, 1 - core, x)], move_sem.at[0], move_sem.at[1],
                plane.other_core())
            arrived.wait_recv()
            send_block(1 - core)

    def out_copy(c, h, side):
        at = pl.multiple_of(((c * SIDE + side) * HALVES + h) * sub, sub)
        return pltpu.make_async_copy(
            gathered.at[plane.block(c, h, side)], sum_hbm.at[pl.ds(at, sub)],
            store_sem.at[(c * SIDE + side) * HALVES + h])

    def gather(t):
        for turn in range(HALVES):
            h = core if turn == 0 else 1 - core
            plane.relay(t, h)
            c = chunk_order(z, t - 1)
            plane.wait_side_block(c, h)
            out_copy(c, h, x).start()
            out_copy(c, h, 1 - x).start()

    count = LINE * SIDE * HALVES

    def to_core(n):
        layer, own, there, other, own_hbm, got_hbm, at = pieces[n]
        return remote(
            own.at[at], got_hbm.at[at], core_expert_sem.at[0, n], core_expert_sem.at[1, n], plane.other_core())

    def keep(n):
        layer, own, there, other, own_hbm, got_hbm, at = pieces[n]
        return pltpu.make_async_copy(own.at[at], own_hbm.at[at], store_sem.at[count + n])

    def expert_piece(n):
        layer, own, there, other, own_hbm, got_hbm, at = pieces[n]
        exchange[n].wait()
        own[at] = (own[at].astype(F32) + other[at].astype(F32)).astype(BF16)
        pl.when(core != layer)(lambda: to_core(n).start())
        keep(n).start()

    pass_piece(0, 0)
    prepare(1)
    send_piece()
    pass_piece(1, 0)
    send_piece()
    pass_piece(2, 0)
    finish(0)
    while len(exchange) < len(pieces):
        send_piece()
    for i in range(LINE - 1):
        pass_piece(i, 1)
        pl.when(core == 1)(lambda i=i: gather(i + 1))
        expert_piece(i)
    finish(1)
    pl.when(core == 1)(lambda: gather(LINE))

    @pl.when(core == 0)
    def _():
        def one(t, carry):
            gather(t)
            return carry

        lax.fori_loop(1, LINE + 1, one, 0)

    for n in range(LINE - 1, len(pieces)):
        expert_piece(n)
    plane.drain()
    for copy in cores + small:
        copy.wait_send()
    move(0).wait_send()

    def stored(k, carry):
        out_copy(lax.div(k, SIDE * HALVES), lax.rem(k, HALVES), lax.rem(lax.div(k, HALVES), SIDE)).wait()
        return carry

    lax.fori_loop(0, count, stored, 0)
    for n in range(len(pieces)):
        keep(n).wait()
        pl.when(core != pieces[n][0])(lambda n=n: to_core(n).wait_send())
        pl.when(core == pieces[n][0])(lambda n=n: to_core(n).wait_recv())
    edges.wait()
    pl.when(core == 0)(lambda: gu1_copy.wait_send())
    pl.when(core == 1)(lambda: gu1_copy.wait_recv())


def reduce_gradients(g1, g0, t1, t0, experts0, gu1, down1, edge, collective_id):
    places, halves, sub, cols = g1.shape
    grad_gu, grad_down = experts0[:2]
    any_spec = pl.BlockSpec(memory_space=pl.ANY)
    wide = cols + LANES
    gu, down = jax.ShapeDtypeStruct(grad_gu.shape, BF16), jax.ShapeDtypeStruct(grad_down.shape, BF16)
    gu_v, down_v = pltpu.VMEM(grad_gu.shape, BF16), pltpu.VMEM(grad_down.shape, BF16)
    return pl.pallas_call(
        functools.partial(reduce_kernel, sub, cols),
        name="reduce_gradients",
        out_shape=(
            jax.ShapeDtypeStruct((places * halves * sub, wide), BF16), gu, down, gu, down, down, gu, down,
            jax.ShapeDtypeStruct(edge.shape, edge.dtype),
        ),
        in_specs=[any_spec] * 11,
        out_specs=(any_spec,) * 9,
        scratch_shapes=[
            pltpu.VMEM((2, places, sub, cols), BF16),
            pltpu.VMEM((2, places, sub, LANES), BF16),
            pltpu.VMEM((2, 3, places, sub, LANES), BF16),
            pltpu.VMEM((2, sub, wide), BF16),
            gu_v, gu_v, gu_v, down_v, down_v, down_v, down_v, down_v,
            pltpu.SemaphoreType.DMA((2, places + 1)),
            pltpu.SemaphoreType.DMA((8,)),
            pltpu.SemaphoreType.DMA((2, 8)),
            pltpu.SemaphoreType.DMA((4,)),
            pltpu.SemaphoreType.DMA((2, 2)),
            pltpu.SemaphoreType.DMA((2, 2, 3)),
            pltpu.SemaphoreType.DMA((2,)),
            pltpu.SemaphoreType.DMA((2, 8)),
            pltpu.SemaphoreType.DMA((2, 8)),
            pltpu.SemaphoreType.DMA((places * halves + 8,)),
        ] + plane_scratch(halves * sub, wide, wide),
        compiler_params=pltpu.CompilerParams(
            collective_id=collective_id, has_side_effects=True, vmem_limit_bytes=VMEM_BYTES),
    )(g1, g0, t1, t0, *experts0, gu1, down1, edge)


def finish_kernel(qkv_cols, attn, gu_own, gu_got, gu_one, gu_moved, down_own, down_got, down_one, down_moved,
                  qkv_hbm, out_hbm, gu_hbm, down_hbm, attn_v, gu_v, down_v, qkv_f, out_f, gu_f, down_f,
                  load_sem, store_sem):
    core = lax.axis_index("section")
    steps = []

    def chunks(rows, count):
        return [pl.ds(n * (rows // count), rows // count) for n in range(count)]

    def choose(zero, one, dst, sem):
        copies = [pltpu.make_async_copy(zero, dst, sem), pltpu.make_async_copy(one, dst, sem)]
        pl.when(core == 0)(lambda: copies[0].start())
        pl.when(core == 1)(lambda: copies[1].start())
        return copies[0]

    def add(load, convert, stores):
        steps.append((load, convert, stores))

    def store(src, dst, n):
        return pltpu.make_async_copy(src, dst, store_sem.at[n])

    stored = 0
    for j, (zero, one) in enumerate(((gu_own, gu_moved), (gu_got, gu_one))):
        for at in chunks(gu_f.shape[1], 6):
            def convert(j=j, at=at):
                gu_f[j, at, :] = gu_v[j, at, :].astype(F32)

            load = choose(zero.at[at], one.at[at], gu_v.at[j, at], load_sem.at[len(steps)])
            add(load, convert, [store(gu_f.at[j, at], gu_hbm.at[j, at], stored)])
            stored += 1
    for j, (zero, one) in enumerate(((down_own, down_moved), (down_got, down_one))):
        for at in chunks(down_f.shape[1], 2):
            def convert(j=j, at=at):
                down_f[j, at, :] = down_v[j, at, :].astype(F32)

            load = choose(zero.at[at], one.at[at], down_v.at[j, at], load_sem.at[len(steps)])
            add(load, convert, [store(down_f.at[j, at], down_hbm.at[j, at], stored)])
            stored += 1
    for at in chunks(attn_v.shape[0], 8):
        def convert(at=at):
            qkv_f[at, :] = attn_v[at, pl.ds(0, qkv_cols)].astype(F32)
            out_f[at, :] = attn_v[at, pl.ds(qkv_cols, out_f.shape[1])].astype(F32)

        load = pltpu.make_async_copy(attn.at[at, pl.ds(0, attn_v.shape[1])], attn_v.at[at], load_sem.at[len(steps)])
        load.start()
        add(load, convert, [
            store(qkv_f.at[at], qkv_hbm.at[at], stored), store(out_f.at[at], out_hbm.at[at], stored + 1)])
        stored += 2
    for load, convert, stores in steps:
        load.wait()
        convert()
        for copy in stores:
            copy.start()
    for load, convert, stores in steps:
        for copy in stores:
            copy.wait()


def finish_outputs(attn, gus, downs, qkv_cols, out_cols):
    rows = attn.shape[0]
    gu, down = (EXP_DEV,) + gus[0].shape, (EXP_DEV,) + downs[0].shape
    any_spec = pl.BlockSpec(memory_space=pl.ANY)
    return pl.pallas_call(
        functools.partial(finish_kernel, qkv_cols),
        name="finish_outputs",
        out_shape=(
            jax.ShapeDtypeStruct((rows, qkv_cols), F32),
            jax.ShapeDtypeStruct((rows, out_cols), F32),
            jax.ShapeDtypeStruct(gu, F32),
            jax.ShapeDtypeStruct(down, F32),
        ),
        in_specs=[any_spec] * 9,
        out_specs=(any_spec,) * 4,
        scratch_shapes=[
            pltpu.VMEM((rows, qkv_cols + out_cols), BF16),
            pltpu.VMEM(gu, BF16),
            pltpu.VMEM(down, BF16),
            pltpu.VMEM((rows, qkv_cols), F32),
            pltpu.VMEM((rows, out_cols), F32),
            pltpu.VMEM(gu, F32),
            pltpu.VMEM(down, F32),
            pltpu.SemaphoreType.DMA((24,)),
            pltpu.SemaphoreType.DMA((32,)),
        ],
        compiler_params=pltpu.CompilerParams(vmem_limit_bytes=VMEM_BYTES),
    )(attn, *gus, *downs)


PAIRS = 2
GROUP = QUERY_HEADS // KEY_VALUE_HEADS
SCALE = HEAD_SIZE ** (-0.5)


class Pair:
    def __init__(self):
        self.sec, self.owner, self.me = (lax.axis_index(n) for n in ("section", "expert", "shard"))
        self.peer = 1 - self.me

    def barrier(self, with_core=False):
        sem = pltpu.get_barrier_semaphore()
        pl.semaphore_signal(
            sem, inc=1, device_id=(self.sec, self.owner, self.peer), device_id_type=MESH)
        if with_core:
            pl.semaphore_signal(
                sem, inc=1, device_id=(1 - self.sec, self.owner, self.me), device_id_type=MESH)
        pl.semaphore_wait(sem, 1 + with_core)

    def send(self, src, dst, send_sem, recv_sem):
        return pltpu.make_async_remote_copy(
            src_ref=src, dst_ref=dst, send_sem=send_sem, recv_sem=recv_sem,
            device_id=(self.sec, self.owner, self.peer), device_id_type=MESH)


def head_columns(shard):
    kv_pair = KEY_VALUE_HEADS // 2 // PAIRS * HEAD_SIZE
    q_pair = kv_pair * GROUP
    wide = q_pair + 2 * kv_pair
    spans = []
    for i in range(PAIRS):
        at = shard * PAIRS + i
        spans.append((at * q_pair, i * wide, q_pair))
        spans.append((QUERY_WIDTH + at * kv_pair, i * wide + q_pair, kv_pair))
        spans.append((QUERY_WIDTH + KV_WIDTH + at * kv_pair, i * wide + q_pair + kv_pair, kv_pair))
    return spans


def head_at(i, n, g):
    kv_pair = KEY_VALUE_HEADS // 2 // PAIRS * HEAD_SIZE
    q_pair = kv_pair * GROUP
    base = i * (q_pair + 2 * kv_pair)
    return (
        pl.ds(base + (n * GROUP + g) * HEAD_SIZE, HEAD_SIZE),
        pl.ds(base + q_pair + n * HEAD_SIZE, HEAD_SIZE),
        pl.ds(base + q_pair + kv_pair + n * HEAD_SIZE, HEAD_SIZE),
    )


KV_IN_PAIR = KEY_VALUE_HEADS // 2 // PAIRS


def load_attention(layer, sec, wq, wq_other, wo, wo_other, wq_v, wo_v, sems):
    loads = []
    for j in range(2):
        for at, local, size in head_columns(j):
            loads.append(load_layer(
                layer, sec, wq.at[:, pl.ds(at, size)], wq_other.at[:, pl.ds(at, size)],
                wq_v.at[j, :, pl.ds(local, size)], sems.at[len(loads)]))
    loads.append(load_layer(layer, sec, wo, wo_other, wo_v, sems.at[len(loads)]))
    return loads


LOADS = 2 * PAIRS * 3 + 1


def attention_forward_kernel(layer, rows, width, h_ref, allowed_ref, gains_ref, router_ref, mask_ref, wq, wq_other,
                             wo, wo_other, block_ref, h1_ref, a_ref, qkv_ref, p_ref, o_ref,
                             wq_v, wo_v, a_parts, a_half, part_send, got_part, out_send, got_out,
                             load_sem, send_sem, recv_sem, *turn):
    pair = Pair()
    me, peer = pair.me, pair.peer
    half = width // 2
    loads = load_attention(layer, pair.sec, wq, wq_other, wo, wo_other, wq_v, wo_v, load_sem)
    pair.barrier(bool(turn))

    def span(who):
        return pl.ds(pl.multiple_of(who * rows, rows), rows)

    h = h_ref[...].astype(F32)
    r1 = lax.rsqrt(jnp.mean(h * h, axis=1, keepdims=True) + EPS)
    a = (h * r1 * gains_ref[pl.ds(0, 1), :]).astype(BF16)
    for j in range(2):
        a_parts[j] = a[:, j * half : (j + 1) * half]
    if turn:
        pl.when(pair.sec == 0)(lambda: pl.semaphore_wait(turn[0], 1))
    send_a = pair.send(a_parts.at[peer], a_half.at[span(me)], send_sem.at[0], recv_sem.at[0])
    send_a.start()
    a_half[span(me)] = a_parts[me]
    for load in loads[:-1]:
        load.wait()
    part_send[span(me)] = nn(a_parts[me], wq_v[peer]).astype(BF16)
    send_own = pair.send(part_send.at[span(me)], got_part.at[span(me)], send_sem.at[1], recv_sem.at[1])
    send_own.start()
    send_a.wait_recv()
    part_send[span(peer)] = nn(a_half[span(peer)], wq_v[peer]).astype(BF16)
    send_other = pair.send(
        part_send.at[span(peer)], got_part.at[span(peer)], send_sem.at[2], recv_sem.at[2])
    send_other.start()
    mine = nn(a_half[...], wq_v[me])
    a_ref[...] = a_half[...]
    send_own.wait_recv()
    send_other.wait_recv()
    qkv_ref[...] = (mine + got_part[...].astype(F32)).astype(BF16)
    allowed = allowed_ref[...] > 0
    for i in range(PAIRS):
        for n in range(KV_IN_PAIR):
            for g in range(GROUP):
                q_at, k_at, v_at = head_at(i, n, g)
                j = (i * KV_IN_PAIR + n) * GROUP + g
                s = nt(qkv_ref[:, q_at], qkv_ref[:, k_at]) * SCALE
                s = jnp.where(allowed, s, MASKED_SCORE)
                ex = jnp.exp(s - jnp.max(s, axis=1, keepdims=True))
                p = (ex / jnp.sum(ex, axis=1, keepdims=True)).astype(BF16)
                p_ref[j] = p
                o_ref[:, pl.ds(j * HEAD_SIZE, HEAD_SIZE)] = nn(p, qkv_ref[:, v_at]).astype(BF16)
    loads[-1].wait()
    out_send[...] = nn(o_ref[span(peer)], wo_v[...]).astype(BF16)
    send_out = pair.send(out_send, got_out, send_sem.at[3], recv_sem.at[3])
    send_out.start()
    own = nn(o_ref[span(me)], wo_v[...])
    send_out.wait_recv()
    if turn:
        @pl.when(pair.sec == 1)
        def _():
            pl.semaphore_signal(
                turn[0], inc=1, device_id=(1 - pair.sec, pair.owner, me), device_id_type=MESH)

    h1 = h + own + got_out[...].astype(F32)
    h1_ref[...] = h1
    r2 = lax.rsqrt(jnp.mean(h1 * h1, axis=1, keepdims=True) + EPS)
    b = (h1 * r2 * gains_ref[pl.ds(1, 1), :]).astype(BF16)
    block_ref[:, pl.ds(0, width)] = b
    mask = mask_ref[...] > 0
    logits = jnp.where(mask, nt(b, router_ref[...]), MASKED_SCORE)
    ex = jnp.where(mask, jnp.exp(logits - jnp.max(logits, axis=1, keepdims=True)), 0.0)
    gates = ex / (0.5 * jnp.sum(ex, axis=1, keepdims=True))
    high = gates.astype(BF16).astype(F32)
    block_ref[:, pl.ds(width, LANES)] = jnp.where(mask_ref[...] > 1, gates - high, high).astype(BF16)
    for send in (send_a, send_own, send_other, send_out):
        send.wait_send()


def attention_forward(layer, h, allowed, gains, router, mask, weights, collective_id):
    rows, width = h.shape
    half, group = width // 2, 2 * rows
    qkv = (QUERY_WIDTH + 2 * KV_WIDTH) // 2
    heads = QUERY_HEADS // 2
    any_spec = pl.BlockSpec(memory_space=pl.ANY)
    vmem = pl.BlockSpec(memory_space=pltpu.VMEM)
    return pl.pallas_call(
        functools.partial(attention_forward_kernel, layer, rows, width),
        name="attention_forward",
        out_shape=(
            jax.ShapeDtypeStruct((rows, width + LANES), BF16),
            jax.ShapeDtypeStruct((rows, width), F32),
            jax.ShapeDtypeStruct((group, half), BF16),
            jax.ShapeDtypeStruct((group, qkv), BF16),
            jax.ShapeDtypeStruct((heads, group, group), BF16),
            jax.ShapeDtypeStruct((group, QUERY_WIDTH // 2), BF16),
        ),
        in_specs=[vmem] * 5 + [any_spec] * 4,
        out_specs=(vmem,) * 6,
        scratch_shapes=[
            pltpu.VMEM((2, half, qkv), BF16),
            pltpu.VMEM((QUERY_WIDTH // 2, width), BF16),
            pltpu.VMEM((2, rows, half), BF16),
            pltpu.VMEM((group, half), BF16),
            pltpu.VMEM((group, qkv), BF16),
            pltpu.VMEM((group, qkv), BF16),
            pltpu.VMEM((rows, width), BF16),
            pltpu.VMEM((rows, width), BF16),
            pltpu.SemaphoreType.DMA((LOADS,)),
            pltpu.SemaphoreType.DMA((4,)),
            pltpu.SemaphoreType.DMA((4,)),
        ] + ([pltpu.SemaphoreType.REGULAR] if layer == 0 else []),
        cost_estimate=COST,
        compiler_params=pltpu.CompilerParams(
            collective_id=collective_id, has_side_effects=True, vmem_limit_bytes=VMEM_BYTES),
    )(h, allowed, gains, router, mask, *weights)


def attention_backward_kernel(layer, rows, width, experts, router_grad_ref, db_ref, dout_ref, h1_ref, h_ref, gains_ref, a_ref, qkv_ref,
                              p_ref, o_ref, wq, wq_other, wo, wo_other, dh_ref, columns_ref, grad_hbm,
                              wq_v, wo_v, d_all, do, dqkv, got_dqkv, da_send, got_da, dh1_v, grad_q, grad_o,
                              gain_grads_ref, columns_v, load_sem, store_sem, send_sem, recv_sem):
    pair = Pair()
    me, peer = pair.me, pair.peer
    half = width // 2
    qkv_cols = dqkv.shape[1]
    pair_cols = qkv_cols // PAIRS
    loads = load_attention(layer, pair.sec, wq, wq_other, wo, wo_other, wq_v, wo_v, load_sem)
    pair.barrier()

    def span(who):
        return pl.ds(pl.multiple_of(who * rows, rows), rows)

    h1 = h1_ref[...]
    r2 = lax.rsqrt(jnp.mean(h1 * h1, axis=1, keepdims=True) + EPS)
    normed = h1 * r2
    db = db_ref[...]
    scaled = db * gains_ref[pl.ds(1, 1), :]
    gain_grads_ref[...] = jnp.zeros_like(gain_grads_ref)
    gain_grads_ref[pl.ds(experts + 1, 1), :] = jnp.sum(db * normed, axis=0, keepdims=True)
    dh1 = dout_ref[...].astype(F32) + r2 * (
        scaled - normed * jnp.mean(scaled * normed, axis=1, keepdims=True))
    dh1_v[...] = dh1
    d_all[span(me)] = dh1.astype(BF16)
    send_d = pair.send(d_all.at[span(me)], d_all.at[span(me)], send_sem.at[0], recv_sem.at[0])
    send_d.start()
    router_terms = router_grad_ref[...]
    lane = lax.broadcasted_iota(jnp.int32, router_terms.shape, 1)
    router_terms = router_terms + pltpu.roll(router_terms, LANES // 2, 1)
    columns_v[...] = jnp.where(lane < experts, router_terms, 0.0)
    for load in loads:
        load.wait()
    do[span(me)] = nt(d_all[span(me)], wo_v[...]).astype(BF16)
    send_d.wait_recv()
    do[span(peer)] = nt(d_all[span(peer)], wo_v[...]).astype(BF16)
    sends = [send_d]
    for i in range(PAIRS):
        cols = pl.ds(i * pair_cols, pair_cols)
        for n in range(KV_IN_PAIR):
            dk = dv = None
            for g in range(GROUP):
                q_at, k_at, v_at = head_at(i, n, g)
                j = (i * KV_IN_PAIR + n) * GROUP + g
                p_low = p_ref[j]
                p = p_low.astype(F32)
                d_head = do[:, pl.ds(j * HEAD_SIZE, HEAD_SIZE)]
                weighted = p * nt(d_head, qkv_ref[:, v_at])
                ds = (weighted - p * jnp.sum(weighted, axis=1, keepdims=True)).astype(BF16)
                dqkv[:, q_at] = (nn(ds, qkv_ref[:, k_at]) * SCALE).astype(BF16)
                dk_part, dv_part = tn(ds, qkv_ref[:, q_at]), tn(p_low, d_head)
                dk = dk_part if dk is None else dk + dk_part
                dv = dv_part if dv is None else dv + dv_part
            dqkv[:, k_at] = (dk * SCALE).astype(BF16)
            dqkv[:, v_at] = dv.astype(BF16)
        send = pair.send(dqkv.at[:, cols], got_dqkv.at[:, cols], send_sem.at[1 + i], recv_sem.at[1 + i])
        send.start()
        sends.append(send)
    da = nt(dqkv[...], wq_v[me])
    grad_q[me] = tn(a_ref[...], dqkv[...]).astype(BF16)
    grad_o[...] = tn(o_ref[...], d_all[...]).astype(BF16)
    store_o = pltpu.make_async_copy(
        grad_o, grad_hbm.at[:, pl.ds(QUERY_WIDTH + 2 * KV_WIDTH, width)], store_sem.at[LOADS - 1])
    store_o.start()
    for send in sends[1:]:
        send.wait_recv()
    da = da + nt(got_dqkv[...], wq_v[peer])
    da_send[...] = jnp.where(me == 0, da[rows:], da[:rows]).astype(BF16)
    send_da = pair.send(da_send, got_da, send_sem.at[1 + PAIRS], recv_sem.at[1 + PAIRS])
    send_da.start()
    own_da = jnp.where(me == 0, da[:rows], da[rows:])
    grad_q[peer] = tn(a_ref[...], got_dqkv[...]).astype(BF16)
    stores = [store_o]
    for j in range(2):
        for at, local, size in head_columns(j):
            store = pltpu.make_async_copy(
                grad_q.at[j, :, pl.ds(local, size)], grad_hbm.at[:, pl.ds(at, size)],
                store_sem.at[len(stores) - 1])
            store.start()
            stores.append(store)
    send_da.wait_recv()
    other_da = got_da[...].astype(F32)
    h = h_ref[...].astype(F32)
    r1 = lax.rsqrt(jnp.mean(h * h, axis=1, keepdims=True) + EPS)
    halves = []
    total = jnp.zeros((rows, 1), F32)
    for j in range(2):
        cols = pl.ds(j * half, half)
        da_j = jnp.where(me == j, own_da, other_da)
        normed = h[:, j * half : (j + 1) * half] * r1
        gain_grads_ref[pl.ds(experts, 1), cols] = jnp.sum(da_j * normed, axis=0, keepdims=True)
        scaled = da_j * gains_ref[pl.ds(0, 1), cols]
        total = total + jnp.sum(scaled * normed, axis=1, keepdims=True)
        halves.append((cols, scaled, normed))
    columns = columns_v[...] + jnp.transpose(gain_grads_ref[...])
    columns_ref[...] = columns.astype(BF16)
    for cols, scaled, normed in halves:
        dh_ref[:, cols] = dh1_v[:, cols] + r1 * (scaled - normed * (total / width))
    for send in sends + [send_da]:
        send.wait_send()
    for store in stores:
        store.wait()


def attention_backward(layer, experts, router_grad, db, dout, h1, h, gains, a_half, qkv, p, o, weights, collective_id):
    rows, width = db.shape
    half, group = width // 2, 2 * rows
    cols = (QUERY_WIDTH + 2 * KV_WIDTH) // 2
    any_spec = pl.BlockSpec(memory_space=pl.ANY)
    vmem = pl.BlockSpec(memory_space=pltpu.VMEM)
    return pl.pallas_call(
        functools.partial(attention_backward_kernel, layer, rows, width, experts),
        name="attention_backward",
        out_shape=(
            jax.ShapeDtypeStruct((rows, width), F32),
            jax.ShapeDtypeStruct((width, LANES), BF16),
            jax.ShapeDtypeStruct((half, QUERY_WIDTH + 2 * KV_WIDTH + width), BF16),
        ),
        in_specs=[vmem] * 10 + [any_spec] * 4,
        out_specs=(vmem, vmem, any_spec),
        scratch_shapes=[
            pltpu.VMEM((2, half, cols), BF16),
            pltpu.VMEM((QUERY_WIDTH // 2, width), BF16),
            pltpu.VMEM((group, width), BF16),
            pltpu.VMEM((group, QUERY_WIDTH // 2), BF16),
            pltpu.VMEM((group, cols), BF16),
            pltpu.VMEM((group, cols), BF16),
            pltpu.VMEM((rows, half), BF16),
            pltpu.VMEM((rows, half), BF16),
            pltpu.VMEM((rows, width), F32),
            pltpu.VMEM((2, half, cols), BF16),
            pltpu.VMEM((QUERY_WIDTH // 2, width), BF16),
            pltpu.VMEM((LANES, width), F32),
            pltpu.VMEM((width, LANES), F32),
            pltpu.SemaphoreType.DMA((LOADS,)),
            pltpu.SemaphoreType.DMA((LOADS,)),
            pltpu.SemaphoreType.DMA((2 + PAIRS,)),
            pltpu.SemaphoreType.DMA((2 + PAIRS,)),
        ],
        cost_estimate=COST,
        compiler_params=pltpu.CompilerParams(
            collective_id=collective_id, has_side_effects=True, vmem_limit_bytes=VMEM_BYTES),
    )(router_grad, db, dout, h1, h, gains, a_half, qkv, p, o, *weights)


def dot(a, b, dims):
    return lax.dot_general(a, b, (dims, ((), ())), preferred_element_type=F32)


def rms_scale(values):
    return lax.rsqrt(jnp.mean(values * values, axis=-1, keepdims=True) + EPS)


def swap_cores(value):
    return lax.ppermute(value, "section", [(0, 1), (1, 0)])


def both_layers(own):
    return lax.all_gather(own, "section", axis=0, tiled=False)


def document_mask(sequence_lengths, rows):
    pos = jnp.arange(rows, dtype=jnp.int32)
    ends = jnp.cumsum(sequence_lengths)
    doc = jnp.sum((pos[:, None] >= ends[None, :]).astype(jnp.int32), axis=1)
    return (doc[:, None] == doc[None, :]) & (pos[None, :] <= pos[:, None])


def plain_attention(qkv, allowed, heads, kv_heads):
    rows = qkv.shape[0]
    group = heads // kv_heads
    q = qkv[:, : heads * HEAD_SIZE].reshape(rows, kv_heads, group, HEAD_SIZE)
    k = qkv[:, heads * HEAD_SIZE : (heads + kv_heads) * HEAD_SIZE].reshape(rows, kv_heads, HEAD_SIZE)
    v = qkv[:, (heads + kv_heads) * HEAD_SIZE :].reshape(rows, kv_heads, HEAD_SIZE)
    s = jnp.einsum("qhgd,khd->hgqk", q, k, preferred_element_type=F32) * HEAD_SIZE ** (-0.5)
    s = jnp.where(allowed[None, None], s, MASKED_SCORE)
    ex = jnp.exp(s - jnp.max(s, axis=-1, keepdims=True))
    p = ex / jnp.sum(ex, axis=-1, keepdims=True)
    o = jnp.einsum("hgqk,khd->qhgd", p.astype(BF16), v, preferred_element_type=F32)
    return o.reshape(rows, heads * HEAD_SIZE).astype(BF16), p, (q, k, v)


def plain_attention_backward(do, p, heads_in):
    q, k, v = heads_in
    rows = q.shape[0]
    dh = do.reshape(q.shape)
    dv = jnp.einsum("hgqk,qhgd->khd", p.astype(BF16), dh, preferred_element_type=F32)
    dp = jnp.einsum("qhgd,khd->hgqk", dh, v, preferred_element_type=F32)
    ds = (p * (dp - jnp.sum(p * dp, axis=-1, keepdims=True))).astype(BF16)
    dq = jnp.einsum("hgqk,khd->qhgd", ds, k, preferred_element_type=F32) * HEAD_SIZE ** (-0.5)
    dk = jnp.einsum("hgqk,qhgd->khd", ds, q, preferred_element_type=F32) * HEAD_SIZE ** (-0.5)
    return jnp.concatenate(
        [dq.reshape(rows, -1), dk.reshape(rows, -1), dv.reshape(rows, -1)], axis=1
    ).astype(BF16)


def column_parts(n, j):
    qw, kw = QUERY_WIDTH // n, KV_WIDTH // n
    return (
        (j * qw, qw),
        (QUERY_WIDTH + j * kw, kw),
        (QUERY_WIDTH + KV_WIDTH + j * kw, kw),
    )


def plain_shards(
    edge_inputs, seq_lengths, routes, w_qkv, w_out, w_router, gain_attn, gain_moe, w_gate_up, w_down
):
    sec = lax.axis_index("section")
    owner = lax.axis_index("expert")
    shard_pos = lax.axis_index("shard")
    n_shard = lax.axis_size("shard")
    n_owner = lax.axis_size("expert")
    rows, width = edge_inputs.shape[2], edge_inputs.shape[3]
    experts = w_router.shape[2]
    group_rows = rows * n_shard
    half = width // n_shard
    heads, kv_heads = QUERY_HEADS // n_shard, KEY_VALUE_HEADS // n_shard

    def pick(array, index):
        return lax.dynamic_index_in_dim(array, index, 0, keepdims=False)

    own_edge, other_edge = pick(edge_inputs[0], sec), swap_cores(pick(edge_inputs[0], 1 - sec))
    x_in = jnp.where(sec == 0, own_edge, other_edge)
    dy = jnp.where(sec == 0, other_edge, own_edge)
    own_routes, other_routes = pick(routes[0], sec), swap_cores(pick(routes[0], 1 - sec))
    layer_routes = (
        jnp.where(sec == 0, own_routes, other_routes),
        jnp.where(sec == 0, other_routes, own_routes),
    )
    allowed = document_mask(pick(seq_lengths, sec)[0], group_rows)
    wq = both_layers(w_qkv[0])
    wo = both_layers(w_out[0])
    small = jnp.concatenate([w_router[0], gain_attn[0][:, None], gain_moe[0][:, None]], axis=1)
    small = lax.all_gather(both_layers(small), "shard", axis=1, tiled=True)
    wgu = both_layers(w_gate_up[0])
    wd = both_layers(w_down[0])
    columns = jnp.arange(experts, dtype=jnp.int32)
    route_masks = [
        jnp.any(r[:, :, None] == columns[None, None, :], axis=1).astype(BF16) for r in layer_routes
    ]
    plane_masks = [lax.all_gather(m, "expert", axis=0, tiled=True) for m in route_masks]

    def forward(layer, h):
        gain_a = small[layer, :, experts].astype(F32)[None, :]
        gain_m = small[layer, :, experts + 1].astype(F32)[None, :]
        router = small[layer, :, :experts]
        r1 = rms_scale(h)
        a = (h * r1 * gain_a).astype(BF16)
        a_half = lax.all_to_all(
            a.reshape(rows, n_shard, half), "shard", split_axis=1, concat_axis=0, tiled=True
        ).reshape(group_rows, half)
        blocks = []
        for j in range(n_shard):
            blocks.append(
                jnp.concatenate(
                    [
                        dot(a_half, wq[layer, :, at : at + size], ((1,), (0,)))
                        for at, size in column_parts(n_shard, j)
                    ],
                    axis=1,
                ).astype(BF16)
            )
        qkv = lax.psum_scatter(jnp.stack(blocks), "shard", scatter_dimension=0, tiled=False)
        o, p, heads_in = plain_attention(qkv, allowed, heads, kv_heads)
        part = dot(o, wo[layer], ((1,), (0,))).astype(BF16)
        h1 = h + lax.psum_scatter(part, "shard", scatter_dimension=0, tiled=True).astype(F32)
        r2 = rms_scale(h1)
        b = (h1 * r2 * gain_m).astype(BF16)
        b_all = lax.all_gather(b, "expert", axis=0, tiled=True)
        mask = plane_masks[layer].astype(F32) > 0
        logits = jnp.where(mask, dot(b_all, router, ((1,), (0,))), MASKED_SCORE)
        ex = jnp.where(mask, jnp.exp(logits - jnp.max(logits, axis=1, keepdims=True)), 0.0)
        gates = ex / jnp.sum(ex, axis=1, keepdims=True)
        own_gates = lax.dynamic_slice_in_dim(gates, owner * EXP_DEV, EXP_DEV, 1)
        kept, scaled = [], []
        for j in range(EXP_DEV):
            gu = dot(b_all, wgu[layer, j], ((1,), (0,)))
            g, u = gu[:, :FF], gu[:, FF:]
            scaled.append((g * jax.nn.sigmoid(g) * u * own_gates[:, j : j + 1]).astype(BF16))
            kept.append(gu.astype(BF16))
        scaled = jnp.concatenate(scaled, axis=1)
        moe_part = dot(scaled, wd[layer].reshape(EXP_DEV * FF, width), ((1,), (0,))).astype(BF16)
        moe = lax.psum_scatter(moe_part, "expert", scatter_dimension=0, tiled=True).astype(F32)
        state = (h, r1, a_half, p, heads_in, o, h1, r2, b_all, own_gates, kept, scaled, moe)
        return h1 + moe, state

    def backward(layer, dout, dout_low, state):
        h, r1, a_half, p, heads_in, o, h1, r2, b_all, own_gates, kept, scaled, moe = state
        gain_a = small[layer, :, experts].astype(F32)[None, :]
        gain_m = small[layer, :, experts + 1].astype(F32)[None, :]
        router = small[layer, :, :experts]
        own_router = lax.dynamic_slice_in_dim(router, owner * EXP_DEV, EXP_DEV, 1)
        total = lax.all_gather(jnp.sum(dout * moe, axis=1), "expert", axis=0, tiled=True)
        dout_all = lax.all_gather(dout_low, "expert", axis=0, tiled=True)
        dgus, dcs = [], []
        for j in range(EXP_DEV):
            gate = own_gates[:, j : j + 1]
            g, u = kept[j][:, :FF].astype(F32), kept[j][:, FF:].astype(F32)
            sig = jax.nn.sigmoid(g)
            silu = g * sig
            dz = dot(dout_all, wd[layer, j], ((1,), (1,)))
            dgate = jnp.sum(dz * silu * u, axis=1, keepdims=True)
            dcs.append(gate * (dgate - total[:, None]))
            dz = dz * gate
            dgus.append(
                jnp.concatenate(
                    [dz * u * sig * (1.0 + g * (1.0 - sig)), dz * silu], axis=1
                ).astype(BF16)
            )
        dc = jnp.concatenate(dcs, axis=1)
        db_part = sum(dot(dgus[j], wgu[layer, j], ((1,), (1,))) for j in range(EXP_DEV))
        for j in range(EXP_DEV):
            db_part = db_part + dc[:, j : j + 1] * own_router[:, j].astype(F32)[None, :]
        db = lax.psum_scatter(
            db_part.astype(BF16), "expert", scatter_dimension=0, tiled=True
        ).astype(F32)
        grad_down = dot(scaled, dout_all, ((0,), (0,))).reshape(EXP_DEV, FF, width)
        grad_gu = jnp.stack([dot(b_all, dgus[j], ((0,), (0,))) for j in range(EXP_DEV)])
        grad_router = lax.dot_general(
            dc, b_all.astype(F32), (((0,), (0,)), ((), ())), precision=lax.Precision.HIGHEST
        )
        normed = h1 * r2
        grad_gain_m = jnp.sum(db * normed, axis=0)
        scaled_db = db * gain_m
        dh1 = dout + r2 * (scaled_db - normed * jnp.mean(scaled_db * normed, axis=1, keepdims=True))
        dattn = lax.all_gather(dh1.astype(BF16), "shard", axis=0, tiled=True)
        do = dot(dattn, wo[layer], ((1,), (1,))).astype(BF16)
        grad_out = dot(o, dattn, ((0,), (0,)))
        dqkv = lax.all_gather(plain_attention_backward(do, p, heads_in), "shard", axis=0, tiled=False)
        da = 0.0
        grad_qkv = []
        for part in range(3):
            grad_qkv.append([])
        for j in range(n_shard):
            at_local = 0
            for part, (at, size) in enumerate(column_parts(n_shard, j)):
                piece = dqkv[j, :, at_local : at_local + size]
                at_local += size
                da = da + dot(piece, wq[layer, :, at : at + size], ((1,), (1,)))
                grad_qkv[part].append(dot(a_half, piece, ((0,), (0,))))
        grad_qkv = jnp.concatenate([x for part in grad_qkv for x in part], axis=1)
        da = lax.all_to_all(
            da.astype(BF16), "shard", split_axis=0, concat_axis=1, tiled=True
        ).astype(F32)
        normed = h * r1
        grad_gain_a = jnp.sum(da * normed, axis=0)
        scaled_da = da * gain_a
        dh = dh1 + r1 * (scaled_da - normed * jnp.mean(scaled_da * normed, axis=1, keepdims=True))
        return dh, (grad_qkv, grad_out, grad_router, grad_gain_a, grad_gain_m, grad_gu, grad_down)

    out0, state0 = forward(0, x_in.astype(F32))
    mid = out0.astype(BF16).astype(F32)
    final, state1 = forward(1, mid)
    dh_one, grads1 = backward(1, dy.astype(F32), dy, state1)
    low = dh_one.astype(BF16)
    dh_zero, grads0 = backward(0, low.astype(F32), low, state0)

    def half_sum(grad):
        low_grad = grad.astype(BF16)
        halves = low_grad.reshape((2, -1) + low_grad.shape[1:])
        got = swap_cores(pick(halves, 1 - sec))
        return (pick(halves, sec).astype(F32) + got.astype(F32)).astype(BF16)

    def to_owner(half0, half1):
        keep = jnp.where(sec == 0, half0, half1)
        got = swap_cores(jnp.where(sec == 0, half1, half0))
        first = jnp.where(sec == 0, keep, got)
        second = jnp.where(sec == 0, got, keep)
        return jnp.concatenate([first, second], axis=0).astype(F32)

    attn_halves, exp_halves = [], []
    for grads in (grads0, grads1):
        attn = half_sum(jnp.concatenate([grads[0], grads[1]], axis=1))
        attn_halves.append(lax.psum(attn, "expert"))
        exp_halves.append(tuple(lax.psum(half_sum(g), "shard") for g in (grads[5], grads[6])))
    attn = to_owner(*attn_halves)
    grad_qkv, grad_out = attn[:, : w_qkv.shape[2]], attn[:, w_qkv.shape[2] :]
    grad_gu = to_owner(exp_halves[0][0], exp_halves[1][0])
    grad_down = to_owner(exp_halves[0][1], exp_halves[1][1])

    tiny = []
    for grads in (grads0, grads1):
        hot = jnp.arange(experts)[:, None] == owner * EXP_DEV + jnp.arange(EXP_DEV)[None, :]
        router = sum(
            jnp.where(hot[:, j : j + 1], grads[2][j][None, :], 0.0) for j in range(EXP_DEV)
        )
        tiny.append(jnp.concatenate([router, grads[3][None, :], grads[4][None, :]], axis=0))
    tiny = lax.psum(jnp.stack(tiny), ("section", "expert", "shard"))
    tiny = lax.dynamic_slice_in_dim(pick(tiny, sec), shard_pos * half, half, 1)

    send = jnp.where(sec == 0, final, dh_zero)
    keep = jnp.where(sec == 0, dh_zero, final)
    got = swap_cores(send)
    edge = jnp.where(sec == 0, jnp.stack([keep, got]), jnp.stack([got, keep]))
    return (
        edge[None],
        grad_qkv[None],
        grad_out[None],
        tiny[:experts].T[None],
        tiny[experts][None],
        tiny[experts + 1][None],
        grad_gu[None],
        grad_down[None],
    )


def kernel_shards(
    edge_inputs, seq_lengths, routes, w_qkv, w_out, w_router, gain_attn, gain_moe, w_gate_up, w_down
):
    sec = lax.axis_index("section")
    owner = lax.axis_index("expert")
    shard_pos = lax.axis_index("shard")
    rows, width = edge_inputs.shape[2], edge_inputs.shape[3]
    experts = w_router.shape[2]
    half = width // 2
    attn_cols = w_qkv.shape[2] + w_out.shape[2]

    def pick(array, index):
        return lax.dynamic_index_in_dim(array, index, 0, keepdims=False)

    def swap_shards(value):
        return lax.ppermute(value, "shard", [(0, 1), (1, 0)])

    def by_core(own, other):
        return jnp.where(sec == 0, own, other), jnp.where(sec == 0, other, own)

    small = jnp.concatenate([w_router[0].T, gain_attn, gain_moe], axis=0)
    across = lax.ppermute(small, ("section", "shard"), [(0, 3), (1, 2), (2, 1), (3, 0)])

    def joined(mine, other):
        return jnp.where(
            shard_pos == 0,
            jnp.concatenate([mine, other], axis=1),
            jnp.concatenate([other, mine], axis=1),
        )

    layer_small = by_core(joined(small, swap_shards(small)), joined(swap_cores(small), across))
    x_in, dy = by_core(pick(edge_inputs[0], sec), swap_cores(pick(edge_inputs[0], 1 - sec)))
    layer_routes = by_core(pick(routes[0], sec), swap_cores(pick(routes[0], 1 - sec)))
    allowed = document_mask(pick(seq_lengths, sec)[0], 2 * rows).astype(F32)
    attn_weights = (w_qkv[0], swap_cores(w_qkv[0]), w_out[0], swap_cores(w_out[0]))
    expert_weights = (
        w_gate_up[0], swap_cores(w_gate_up[0]), w_down[0], swap_cores(w_down[0])
    )
    gains, routers, masks = [], [], []
    for layer in range(2):
        gains.append(
            jnp.pad(layer_small[layer][experts:].astype(F32), ((0, 8 - 2), (0, 0)))
        )
        router = layer_small[layer][:experts]
        router = jnp.concatenate([router, router], axis=0)
        routers.append(jnp.pad(router, ((0, LANES - 2 * experts), (0, 0))))
        lane = jnp.arange(LANES, dtype=jnp.int32)[None, :]
        hot = jnp.any(layer_routes[layer][:, :, None] == lane[None] % experts, axis=1)
        masks.append(
            jnp.where(hot & (lane < 2 * experts), 1.0 + (lane >= experts), 0.0).astype(F32)
        )

    def forward(layer, h):
        block, h1, *attn_state = attention_forward(
            layer, h, allowed, gains[layer], routers[layer], masks[layer], attn_weights, 1 + layer
        )
        moe, *expert_state = moe_forward(layer, block, expert_weights, experts, 3 + layer)
        return h1 + moe, (h, h1, moe, attn_state, expert_state)

    def backward(layer, dout, state, later):
        h, h1, moe, attn_state, expert_state = state
        outer = jnp.sum(dout.astype(F32) * moe, axis=1, keepdims=True)
        block = with_lanes(dout, split_terms(outer))
        own_router = lax.dynamic_slice_in_dim(
            layer_small[layer].astype(F32), owner * EXP_DEV, EXP_DEV, 0
        )
        own_router = jnp.pad(own_router, ((0, 8 - EXP_DEV), (0, 0)))
        results = moe_backward(
            layer, block, own_router, expert_weights, expert_state, later, experts, 5 + layer
        )
        db, keep_gu, keep_down, send_gu, send_down, grad_router = results[:6]
        dh, columns, grad_attn = attention_backward(
            layer, experts, grad_router, db, dout, h1, h, gains[layer], *attn_state, attn_weights,
            7 + layer,
        )
        places = LINE * SIDE
        sub = half // (2 * places)
        grad_attn = grad_attn.reshape(places, 2, sub, attn_cols)
        columns = columns.reshape(2, places, 2, sub, LANES)
        return dh, grad_attn, columns, (keep_gu, keep_down, send_gu, send_down), results[6:8]

    out0, state0 = forward(0, x_in)
    final, state1 = forward(1, out0.astype(BF16))
    dh_one, attn1, columns1, experts1, _ = backward(1, dy, state1, ())
    dh_zero, attn0, columns0, experts0, sums1 = backward(
        0, dh_one.astype(BF16), state0, experts1
    )
    send = jnp.where(sec == 0, final, dh_zero)
    attn, gu_own, down_own, gu_got, down_got, down_one, gu_moved, down_moved, got = reduce_gradients(
        attn1, attn0, columns1, columns0, experts0, *sums1, send, 9
    )
    grad_qkv, grad_out, grad_gu, grad_down = finish_outputs(
        attn,
        (gu_own, gu_got, sums1[0], gu_moved),
        (down_own, down_got, down_one, down_moved),
        w_qkv.shape[2],
        w_out.shape[2],
    )
    tiny = attn[:, attn_cols : attn_cols + experts + 2].astype(F32)
    keep = jnp.where(sec == 0, dh_zero, final)
    edge = jnp.where(sec == 0, jnp.stack([keep, got]), jnp.stack([got, keep]))
    return (
        edge[None],
        grad_qkv[None],
        grad_out[None],
        tiny[:, :experts][None],
        tiny[:, experts][None],
        tiny[:, experts + 1][None],
        grad_gu[None],
        grad_down[None],
    )


def shards(*arrays):
    if lax.axis_size("expert") == LINE * SIDE and lax.axis_size("shard") == 2:
        return kernel_shards(*arrays)
    return plain_shards(*arrays)


def solution(mesh):
    in_specs = (
        P("section", None, ("expert", "shard"), None),
        P(None, "expert", None),
        P("section", None, ("expert", "shard"), None),
        P("section", "shard", None),
        P("section", "shard", None),
        P("section", "shard", None),
        P("section", "shard"),
        P("section", "shard"),
        P("section", "expert", None, None),
        P("section", "expert", None, None),
    )
    out_specs = (
        P("section", None, ("expert", "shard"), None),
        P("section", "shard", None),
        P("section", "shard", None),
        P("section", "shard", None),
        P("section", "shard"),
        P("section", "shard"),
        P("section", "expert", None, None),
        P("section", "expert", None, None),
    )
    return jax.shard_map(shards, mesh=mesh, in_specs=in_specs, out_specs=out_specs, check_vma=False)
```

```python
import functools

import jax
import jax.numpy as jnp
from jax import lax
from jax.experimental import pallas as pl
from jax.experimental.pallas import tpu as pltpu
from jax.sharding import PartitionSpec as P

QUERY_HEADS = 24
KEY_VALUE_HEADS = 8
HEAD_SIZE = 64
FF = 512
TOP = 8
EXP_DEV = 2
EPS = 1e-05
MASKED_SCORE = -1e30
QUERY_WIDTH = QUERY_HEADS * HEAD_SIZE
KV_WIDTH = KEY_VALUE_HEADS * HEAD_SIZE
F32 = jnp.float32
BF16 = jnp.bfloat16
MESH = pl.DeviceIdType.MESH
LINE = 4
SIDE = 2
LANES = 128
HALVES = 2
LATER_CROSS = 5
TILE = 256
VMEM_BYTES = 60 * 2**20
COST = pl.CostEstimate(flops=10**11, bytes_accessed=2**24, transcendentals=0)


def chunk_order(z, t):
    near = z + 1 - 2 * lax.rem(z, 2)
    third = jnp.where(z < 2, 2, 1)
    last = jnp.where(z < 2, 3, 0)
    return jnp.where(t == 0, z, jnp.where(t == 1, near, jnp.where(t == 2, third, last)))


def sum_order(z, i):
    first = jnp.where((z == 0) | (z == 2), 1, 2)
    second = jnp.where(z == 0, 2, jnp.where(z == 1, 3, jnp.where(z == 2, 0, 1)))
    third = jnp.where(z == 0, 3, jnp.where(z == 1, 0, jnp.where(z == 2, 3, 0)))
    return jnp.where(i == 0, first, jnp.where(i == 1, second, third))


class Plane:
    def __init__(self, rows, refs):
        (self.gathered, self.parts, self.from_side, self.from_low, self.from_high, self.sums,
         self.line_send, self.gather_recv, self.side_send, self.side_recv,
         self.sum_send, self.low_recv, self.high_recv) = refs
        self.sub = rows // HALVES
        self.both = SIDE * self.sub
        self.sec, self.owner, self.shard = (lax.axis_index(n) for n in ("section", "expert", "shard"))
        self.z, self.x = lax.div(self.owner, SIDE), lax.rem(self.owner, SIDE)
        self.inner = ((self.z > 0) & (self.z < LINE - 1)).astype(jnp.int32)

    def device(self, z, x):
        return (self.sec, z * SIDE + x, self.shard)

    def other_core(self):
        return (1 - self.sec, self.owner, self.shard)

    def other_shard(self):
        return (self.sec, self.owner, 1 - self.shard)

    def chunk(self, c, h):
        return pl.ds(pl.multiple_of((c * HALVES + h) * self.both, self.both), self.both)

    def block(self, c, h, x):
        return pl.ds(pl.multiple_of((c * HALVES + h) * self.both + x * self.sub, self.sub), self.sub)

    def barrier(self, *others):
        z, x = self.z, self.x
        sem = pltpu.get_barrier_semaphore()

        def greet(device):
            pl.semaphore_signal(sem, inc=1, device_id=device, device_id_type=MESH)

        for other in others:
            greet(other)
        greet(self.device(z, 1 - x))
        pl.when(z > 0)(lambda: greet(self.device(z - 1, x)))
        pl.when(z < LINE - 1)(lambda: greet(self.device(z + 1, x)))
        pl.semaphore_wait(sem, 2 + len(others) + self.inner)

    def place(self, block_ref):
        for h in range(HALVES):
            self.gathered[self.block(self.z, h, self.x)] = block_ref[pl.ds(h * self.sub, self.sub)]

    def gather_copy(self, way, c, h, x, device):
        ref = self.gathered.at[self.block(c, h, x)]
        q = c * HALVES + h
        return pltpu.make_async_remote_copy(
            src_ref=ref, dst_ref=ref, send_sem=self.line_send.at[way, q],
            recv_sem=self.gather_recv.at[q, x], device_id=device, device_id_type=MESH)

    def forward_up(self, c, h):
        return self.gather_copy(0, c, h, self.x, self.device(self.z + 1, self.x))

    def forward_down(self, c, h):
        return self.gather_copy(1, c, h, self.x, self.device(self.z - 1, self.x))

    def forward_side(self, c, h):
        return self.gather_copy(2, c, h, self.x, self.device(self.z, 1 - self.x))

    def start_gather(self):
        z = self.z
        for h in range(HALVES):
            pl.when(z < LINE - 1)(lambda h=h: self.forward_up(z, h).start())
            pl.when(z > 0)(lambda h=h: self.forward_down(z, h).start())
            self.forward_side(z, h).start()

    def relay(self, t, h):
        z = self.z

        @pl.when((t > 0) & (z - t >= 0))
        def _():
            c = z - t
            self.forward_side(c, h).wait_recv()
            pl.when(z < LINE - 1)(lambda: self.forward_up(c, h).start())
            self.forward_side(c, h).start()

        @pl.when((t > 0) & (z + t <= LINE - 1))
        def _():
            c = z + t
            self.forward_side(c, h).wait_recv()
            pl.when(z > 0)(lambda: self.forward_down(c, h).start())
            self.forward_side(c, h).start()

    def wait_side_block(self, c, h):
        self.gather_copy(2, c, h, 1 - self.x, self.device(self.z, 1 - self.x)).wait_recv()

    def side_copy(self, c, h):
        q = c * HALVES + h
        return pltpu.make_async_remote_copy(
            src_ref=self.parts.at[self.block(c, h, 1 - self.x)], dst_ref=self.from_side.at[q],
            send_sem=self.side_send.at[q], recv_sem=self.side_recv.at[q],
            device_id=self.device(self.z, 1 - self.x), device_id_type=MESH)

    def up_copy(self, c, h):
        q = c * HALVES + h
        return pltpu.make_async_remote_copy(
            src_ref=self.sums.at[q], dst_ref=self.from_low.at[q], send_sem=self.sum_send.at[q],
            recv_sem=self.low_recv.at[q], device_id=self.device(self.z + 1, self.x), device_id_type=MESH)

    def down_copy(self, c, h):
        q = c * HALVES + h
        return pltpu.make_async_remote_copy(
            src_ref=self.sums.at[q], dst_ref=self.from_high.at[q], send_sem=self.sum_send.at[q],
            recv_sem=self.high_recv.at[q], device_id=self.device(self.z - 1, self.x), device_id_type=MESH)

    def own_part(self, c, h, side=True):
        part = self.parts[self.block(c, h, self.x)].astype(F32)
        return part + self.from_side[c * HALVES + h].astype(F32) if side else part

    def pass_sum(self, t, h):
        i = t - 3 - self.inner
        pl.when((i >= 0) & (i < LINE - 1))(lambda: self.pass_chunk(sum_order(self.z, i), h))

    def pass_chunk(self, c, h, side=True, send=True):
        z = self.z
        q = c * HALVES + h
        if side:
            self.side_copy(c, h).wait_recv()

        @pl.when(c > z)
        def _():
            @pl.when(z > 0)
            def _():
                self.up_copy(c, h).wait_recv()
                self.sums[q] = (self.own_part(c, h, side) + self.from_low[q].astype(F32)).astype(BF16)

            @pl.when(z == 0)
            def _():
                self.sums[q] = self.own_part(c, h, side).astype(BF16)

        @pl.when(c < z)
        def _():
            @pl.when(z < LINE - 1)
            def _():
                self.down_copy(c, h).wait_recv()
                self.sums[q] = (self.own_part(c, h, side) + self.from_high[q].astype(F32)).astype(BF16)

            @pl.when(z == LINE - 1)
            def _():
                self.sums[q] = self.own_part(c, h, side).astype(BF16)

        if send:
            self.send_sum(c, h)

    def send_sum(self, c, h):
        pl.when(c > self.z)(lambda: self.up_copy(c, h).start())
        pl.when(c < self.z)(lambda: self.down_copy(c, h).start())

    def wait_sent_sum(self, c, h):
        pl.when(c > self.z)(lambda: self.up_copy(c, h).wait_send())
        pl.when(c < self.z)(lambda: self.down_copy(c, h).wait_send())

    def finish_sum(self, h, out_ref):
        z = self.z
        q = z * HALVES + h
        rows = pl.ds(pl.multiple_of(h * self.sub, self.sub), self.sub)
        self.side_copy(z, h).wait_recv()
        out_ref[rows] = self.own_part(z, h)

        @pl.when(z > 0)
        def _():
            self.up_copy(z, h).wait_recv()
            out_ref[rows] += self.from_low[q].astype(F32)

        @pl.when(z < LINE - 1)
        def _():
            self.down_copy(z, h).wait_recv()
            out_ref[rows] += self.from_high[q].astype(F32)

    def finish_piece(self, h, out_ref, side=True):
        z = self.z
        q = z * HALVES + h
        if side:
            self.side_copy(z, h).wait_recv()

        @pl.when(z == 0)
        def _():
            self.down_copy(z, h).wait_recv()
            out_ref[h] = (self.own_part(z, h, side) + self.from_high[q].astype(F32)).astype(BF16)

        @pl.when(z == LINE - 1)
        def _():
            self.up_copy(z, h).wait_recv()
            out_ref[h] = (self.own_part(z, h, side) + self.from_low[q].astype(F32)).astype(BF16)

        @pl.when((z > 0) & (z < LINE - 1))
        def _():
            self.up_copy(z, h).wait_recv()
            self.down_copy(z, h).wait_recv()
            total = self.own_part(z, h, side) + self.from_low[q].astype(F32)
            out_ref[h] = (total + self.from_high[q].astype(F32)).astype(BF16)

    def drain_gather(self):
        z = self.z

        def one(q, carry):
            c, h = lax.div(q, HALVES), lax.rem(q, HALVES)
            pl.when((z < LINE - 1) & (c <= z))(lambda: self.forward_up(c, h).wait_send())
            pl.when((z > 0) & (c >= z))(lambda: self.forward_down(c, h).wait_send())
            self.forward_side(c, h).wait_send()
            return carry

        lax.fori_loop(0, LINE * HALVES, one, 0)

    def drain(self):
        z = self.z

        def one(q, carry):
            c, h = lax.div(q, HALVES), lax.rem(q, HALVES)
            pl.when((z < LINE - 1) & (c <= z))(lambda: self.forward_up(c, h).wait_send())
            pl.when((z > 0) & (c >= z))(lambda: self.forward_down(c, h).wait_send())
            self.forward_side(c, h).wait_send()
            self.side_copy(c, h).wait_send()
            pl.when(c > z)(lambda: self.up_copy(c, h).wait_send())
            pl.when(c < z)(lambda: self.down_copy(c, h).wait_send())
            return carry

        lax.fori_loop(0, LINE * HALVES, one, 0)


def plane_scratch(rows, width, wide):
    count = LINE * HALVES
    block = pltpu.VMEM((count, rows // HALVES, width), BF16)
    return [
        pltpu.VMEM((LINE * SIDE * rows, wide), BF16),
        pltpu.VMEM((LINE * SIDE * rows, width), BF16),
        block, block, block, block,
        pltpu.SemaphoreType.DMA((3, count)),
        pltpu.SemaphoreType.DMA((count, SIDE)),
        pltpu.SemaphoreType.DMA((count,)),
        pltpu.SemaphoreType.DMA((count,)),
        pltpu.SemaphoreType.DMA((count,)),
        pltpu.SemaphoreType.DMA((count,)),
        pltpu.SemaphoreType.DMA((count,)),
    ]


def lane_tile(at, size=TILE):
    return pl.ds(pl.multiple_of(at * size, size), size)


def nn(a, b):
    return jnp.dot(a, b, preferred_element_type=F32)


def nt(a, b):
    return lax.dot_general(a, b, (((1,), (1,)), ((), ())), preferred_element_type=F32)


def tn(a, b):
    return lax.dot_general(a, b, (((0,), (0,)), ((), ())), preferred_element_type=F32)


def pick_lane(block, wanted):
    lane = lax.broadcasted_iota(jnp.int32, block.shape, 1)
    hot = lane == wanted[0]
    for other in wanted[1:]:
        hot = hot | (lane == other)
    return jnp.sum(jnp.where(hot, block, 0.0), axis=1, keepdims=True)


def own_gates(block, owner, experts):
    block = block.astype(F32)
    return [
        pick_lane(block, (owner * EXP_DEV + j, experts + owner * EXP_DEV + j)) for j in range(EXP_DEV)
    ]


def load_layer(layer, sec, own, other, dst, sem):
    copies = [pltpu.make_async_copy(own, dst, sem), pltpu.make_async_copy(other, dst, sem)]
    pl.when(sec == layer)(lambda: copies[0].start())
    pl.when(sec != layer)(lambda: copies[1].start())
    return copies[0]


def load_experts(layer, sec, gu, gu_other, down, down_other, gu_v, down_v, sems):
    loads = [load_layer(layer, sec, gu, gu_other, gu_v, sems.at[0])]
    for j in range(EXP_DEV):
        loads.append(load_layer(
            layer, sec, down.at[j], down_other.at[j], down_v.at[pl.ds(j * FF, FF)], sems.at[1 + j]))
    return loads


def moe_forward_kernel(layer, experts, rows, width, block_ref, gu_hbm, gu_other, down_hbm, down_other,
                       moe_ref, rows_hbm, kept_hbm, scaled_hbm,
                       gu_v, down_v, kept, scaled, load_sem, store_sem, *plane_refs):
    plane = Plane(rows, plane_refs)
    gathered, parts = plane.gathered, plane.parts
    loads = load_experts(layer, plane.sec, gu_hbm, gu_other, down_hbm, down_other, gu_v, down_v, load_sem)
    plane.place(block_ref)
    plane.barrier()
    plane.start_gather()
    for load in loads:
        load.wait()

    def stores(c, h):
        q, at = c * HALVES + h, plane.chunk(c, h)
        return [
            pltpu.make_async_copy(gathered.at[at], rows_hbm.at[at], store_sem.at[0, q]),
            pltpu.make_async_copy(kept.at[at], kept_hbm.at[at], store_sem.at[1, q]),
            pltpu.make_async_copy(scaled.at[at], scaled_hbm.at[at], store_sem.at[2, q]),
        ]

    def step(k, carry):
        t, h = lax.div(k, HALVES), lax.rem(k, HALVES)
        plane.relay(t, h)
        plane.pass_sum(t, h)
        pl.when(t > 0)(lambda: work(chunk_order(plane.z, t - 1), h))
        return carry

    def work(c, h):
        at = plane.chunk(c, h)
        plane.wait_side_block(c, h)
        gates = own_gates(gathered[at, pl.ds(width, LANES)], plane.owner, experts)
        for j in range(EXP_DEV):
            for f in range(FF // TILE):
                data = gathered[at, pl.ds(0, width)]
                low, high = j * 2 * FF + f * TILE, j * 2 * FF + FF + f * TILE
                g = nn(data, gu_v[j, :, pl.ds(f * TILE, TILE)])
                u = nn(data, gu_v[j, :, pl.ds(FF + f * TILE, TILE)])
                z = g * jax.nn.sigmoid(g) * u * gates[j]
                scaled[at, pl.ds(j * FF + f * TILE, TILE)] = z.astype(BF16)
                kept[at, pl.ds(low, TILE)] = g.astype(BF16)
                kept[at, pl.ds(high, TILE)] = u.astype(BF16)
        for n in range(width // TILE):
            parts[at, pl.ds(n * TILE, TILE)] = nn(
                scaled[at, :], down_v[:, pl.ds(n * TILE, TILE)]).astype(BF16)
        plane.side_copy(c, h).start()
        for store in stores(c, h):
            store.start()

    lax.fori_loop(0, (LINE + 1) * HALVES, step, 0)

    def tail(k, carry):
        plane.pass_sum(lax.div(k, HALVES), lax.rem(k, HALVES))
        return carry

    lax.fori_loop((LINE + 1) * HALVES, (LINE + 3) * HALVES, tail, 0)

    def finish(h, carry):
        plane.finish_sum(h, moe_ref)
        return carry

    lax.fori_loop(0, HALVES, finish, 0)
    plane.drain()

    def stored(q, carry):
        for store in stores(lax.div(q, HALVES), lax.rem(q, HALVES)):
            store.wait()
        return carry

    lax.fori_loop(0, LINE * HALVES, stored, 0)


def moe_forward(layer, block, weights, experts, collective_id):
    rows, wide = block.shape
    width = wide - LANES
    total = LINE * SIDE * rows
    any_spec = pl.BlockSpec(memory_space=pl.ANY)
    vmem = pl.BlockSpec(memory_space=pltpu.VMEM)
    return pl.pallas_call(
        functools.partial(moe_forward_kernel, layer, experts, rows, width),
        name="moe_forward",
        out_shape=(
            jax.ShapeDtypeStruct((rows, width), F32),
            jax.ShapeDtypeStruct((total, wide), BF16),
            jax.ShapeDtypeStruct((total, EXP_DEV * 2 * FF), BF16),
            jax.ShapeDtypeStruct((total, EXP_DEV * FF), BF16),
        ),
        in_specs=[vmem] + [any_spec] * 4,
        out_specs=(vmem, any_spec, any_spec, any_spec),
        scratch_shapes=[
            pltpu.VMEM((EXP_DEV, width, 2 * FF), BF16),
            pltpu.VMEM((EXP_DEV * FF, width), BF16),
            pltpu.VMEM((total, EXP_DEV * 2 * FF), BF16),
            pltpu.VMEM((total, EXP_DEV * FF), BF16),
            pltpu.SemaphoreType.DMA((1 + EXP_DEV,)),
            pltpu.SemaphoreType.DMA((3, LINE * HALVES)),
        ] + plane_scratch(rows, width, wide),
        cost_estimate=COST,
        compiler_params=pltpu.CompilerParams(
            collective_id=collective_id, has_side_effects=True, vmem_limit_bytes=VMEM_BYTES),
    )(block, *weights)


def moe_backward_kernel(layer, experts, rows, width, beside, block_ref, router_ref, gu_hbm, gu_other, down_hbm,
                        down_other, rows_hbm, kept_hbm, scaled_hbm, *refs):
    (later, refs) = (refs[:4], refs[4:]) if beside else ((), refs)
    (db_ref, keep_gu_hbm, keep_down_hbm, send_gu_hbm, send_down_hbm, grad_router_ref), refs = refs[:6], refs[6:]
    (later_out, refs) = (refs[:4], refs[4:]) if beside else ((), refs)
    (gu_v, down_v, fwd_rows, kept, scaled, dgu, send_gu, grad_gu, send_down, grad_down,
     load_sem, store_sem), refs = refs[:12], refs[12:]
    (later_v, refs) = (refs[:8], refs[8:]) if beside else ((), refs)
    plane_refs = refs
    plane = Plane(rows, plane_refs)
    gathered, parts = plane.gathered, plane.parts
    loads = load_experts(layer, plane.sec, gu_hbm, gu_other, down_hbm, down_other, gu_v, down_v, load_sem)
    loads.append(pltpu.make_async_copy(rows_hbm, fwd_rows, load_sem.at[3]))
    loads.append(pltpu.make_async_copy(kept_hbm, kept, load_sem.at[4]))
    loads.append(pltpu.make_async_copy(scaled_hbm, scaled, load_sem.at[5]))
    for load in loads[3:]:
        load.start()
    plane.place(block_ref)
    plane.barrier(*([plane.other_core(), plane.other_shard()] if beside else []))
    plane.start_gather()
    if beside:
        other_layer = LaterExperts(plane, *later, *later_out, *later_v)
        other_layer.start_loads()
    for load in loads:
        load.wait()
    if beside:
        other_layer.send()
    total = plane.both
    up_at = EXP_DEV * 2 * FF

    def step(k, carry):
        t, h = lax.div(k, HALVES), lax.rem(k, HALVES)
        plane.relay(t, h)
        plane.pass_sum(t, h)
        pl.when(t > 0)(lambda: work(chunk_order(plane.z, t - 1), h))
        return carry

    def work(c, h):
        at = plane.chunk(c, h)
        plane.wait_side_block(c, h)
        gates = own_gates(fwd_rows[at, pl.ds(width, LANES)], plane.owner, experts)
        outer = jnp.sum(gathered[at, pl.ds(width, LANES)].astype(F32), axis=1, keepdims=True)
        dcs = []
        for j in range(EXP_DEV):
            dgate = jnp.zeros((total, 1), F32)
            for f in range(FF // TILE):
                low, high = pl.ds(j * 2 * FF + f * TILE, TILE), pl.ds(j * 2 * FF + FF + f * TILE, TILE)
                dz = nt(gathered[at, pl.ds(0, width)], down_v[pl.ds(j * FF + f * TILE, TILE), :])
                g = kept[at, low].astype(F32)
                u = kept[at, high].astype(F32)
                sig = jax.nn.sigmoid(g)
                silu = g * sig
                dgate = dgate + jnp.sum(dz * silu * u, axis=1, keepdims=True)
                dz = dz * gates[j]
                dgu[at, low] = (dz * u * sig * (1.0 + g * (1.0 - sig))).astype(BF16)
                dgu[at, high] = (dz * silu).astype(BF16)
            dcs.append(gates[j] * (dgate - outer))
        lane = lax.broadcasted_iota(jnp.int32, (total, LANES), 1)
        extra = jnp.zeros((total, LANES), F32)
        for j in range(EXP_DEV):
            top = dcs[j].astype(BF16).astype(F32)
            column = plane.owner * EXP_DEV + j
            extra = extra + jnp.where(lane == column, top, 0.0)
            extra = extra + jnp.where(lane == LANES // 2 + column, dcs[j] - top, 0.0)
        dgu[at, pl.ds(up_at, LANES)] = extra.astype(BF16)
        for n in range(width // TILE):
            cols = pl.ds(n * TILE, TILE)
            acc = nt(dgu[at, pl.ds(0, 2 * FF)], gu_v[0, cols, :])
            for j in range(1, EXP_DEV):
                acc = acc + nt(dgu[at, pl.ds(j * 2 * FF, 2 * FF)], gu_v[j, cols, :])
            for j in range(EXP_DEV):
                acc = acc + dcs[j] * router_ref[pl.ds(j, 1), cols]
            parts[at, cols] = acc.astype(BF16)
        plane.side_copy(c, h).start()

    lax.fori_loop(0, (LINE + 1) * HALVES, step, 0)

    core = plane.sec
    gu_steps, down_steps = width // TILE, FF // TILE

    def stores_gu(n):
        at = lane_tile(n)
        return [pltpu.make_async_copy(send_gu.at[at], send_gu_hbm.at[at], store_sem.at[0, n]),
                pltpu.make_async_copy(grad_gu.at[at], keep_gu_hbm.at[at], store_sem.at[1, n])]

    def stores_down(n):
        at = lane_tile(n)
        return [pltpu.make_async_copy(send_down.at[at], send_down_hbm.at[at], store_sem.at[2, n]),
                pltpu.make_async_copy(grad_down.at[at], keep_down_hbm.at[at], store_sem.at[3, n])]

    def expert_cols(j, size):
        return pl.ds(pl.multiple_of(j * size, size), size)

    def grad_gu_rows(n):
        rows_t = fwd_rows[:, lane_tile(n)]
        send_gu[lane_tile(n), :] = tn(rows_t, dgu[:, expert_cols(1 - core, 2 * FF)]).astype(BF16)
        grad_gu[lane_tile(n), :] = tn(rows_t, dgu[:, expert_cols(core, 2 * FF)]).astype(BF16)
        grad_router_ref[lane_tile(n), :] = tn(rows_t, dgu[:, pl.ds(up_at, LANES)])
        for store in stores_gu(n):
            store.start()

    def grad_down_rows(n):
        def cols(j):
            return pl.ds(pl.multiple_of(j * FF + n * TILE, TILE), TILE)

        data = gathered[:, pl.ds(0, width)]
        send_down[lane_tile(n), :] = tn(scaled[:, cols(1 - core)], data).astype(BF16)
        grad_down[lane_tile(n), :] = tn(scaled[:, cols(core)], data).astype(BF16)
        for store in stores_down(n):
            store.start()

    slots = 2 * HALVES

    def tail(k, carry):
        pl.loop(lax.div(k * gu_steps, slots), lax.div((k + 1) * gu_steps, slots))(grad_gu_rows)
        plane.pass_sum(LINE + 1 + lax.div(k, HALVES), lax.rem(k, HALVES))
        return carry

    lax.fori_loop(0, slots, tail, 0)
    pl.loop(0, down_steps)(grad_down_rows)

    def finish(h, carry):
        plane.finish_sum(h, db_ref)
        return carry

    lax.fori_loop(0, HALVES, finish, 0)
    if beside:
        other_layer.finish()
    plane.drain()
    for n in range(gu_steps):
        for store in stores_gu(n):
            store.wait()
    for n in range(down_steps):
        for store in stores_down(n):
            store.wait()


class LaterExperts:
    def __init__(self, plane, keep_gu, keep_down, send_gu, send_down, sum_gu_hbm, sum_down_hbm, land_gu, land_down,
                 gu_a, gu_b, down_a, down_b, load_sem, core_sem, send_sem, recv_sem):
        self.parts = []
        for keep, sent, out, land, a, b, count in (
            (keep_gu, send_gu, sum_gu_hbm, land_gu, gu_a, gu_b, 4),
            (keep_down, send_down, sum_down_hbm, land_down, down_a, down_b, 2),
        ):
            size = a.shape[0] // count
            for n in range(count):
                at, k = pl.ds(n * size, size), len(self.parts)
                shard_copy = land_copy = None
                if k < LATER_CROSS:
                    shard_copy = pltpu.make_async_remote_copy(
                        src_ref=a.at[at], dst_ref=land.at[at], send_sem=send_sem.at[k], recv_sem=recv_sem.at[k],
                        device_id=plane.other_shard(), device_id_type=MESH)
                    land_copy = pltpu.make_async_copy(land.at[at], b.at[at], load_sem.at[1, k])
                self.parts.append((
                    a.at[at], b.at[at],
                    pltpu.make_async_copy(keep.at[at], a.at[at], load_sem.at[0, k]),
                    pltpu.make_async_remote_copy(
                        src_ref=sent.at[at], dst_ref=b.at[at], send_sem=core_sem.at[0, k],
                        recv_sem=core_sem.at[1, k], device_id=plane.other_core(), device_id_type=MESH),
                    shard_copy, land_copy,
                    pltpu.make_async_copy(a.at[at], out.at[at], load_sem.at[2, k]),
                ))

    def start_loads(self):
        for _, _, load, core_copy, *_ in self.parts:
            load.start()
            core_copy.start()

    def send(self):
        for a, b, load, core_copy, shard_copy, _, store in self.parts:
            load.wait()
            core_copy.wait()
            a[...] = (a[...].astype(F32) + b[...].astype(F32)).astype(BF16)
            if shard_copy is not None:
                shard_copy.start()
            else:
                store.start()

    def finish(self):
        for _, _, _, _, shard_copy, land_copy, _ in self.parts:
            if shard_copy is not None:
                shard_copy.wait()
                land_copy.start()
        for a, b, _, _, shard_copy, land_copy, store in self.parts:
            if shard_copy is not None:
                land_copy.wait()
                a[...] = (a[...].astype(F32) + b[...].astype(F32)).astype(BF16)
                store.start()
        for *_, store in self.parts:
            store.wait()


def moe_backward(layer, block, router, weights, kept, later, experts, collective_id):
    rows, wide = block.shape
    width = wide - LANES
    total = LINE * SIDE * rows
    any_spec = pl.BlockSpec(memory_space=pl.ANY)
    vmem = pl.BlockSpec(memory_space=pltpu.VMEM)
    expert_gu, expert_down = pltpu.VMEM((width, 2 * FF), BF16), pltpu.VMEM((FF, width), BF16)
    gu_shape = jax.ShapeDtypeStruct((width, 2 * FF), BF16)
    down_shape = jax.ShapeDtypeStruct((FF, width), BF16)
    later_out, later_scratch = (), []
    if later:
        later_out = (gu_shape, down_shape) * 2
        later_scratch = [
            expert_gu, expert_gu, expert_down, expert_down,
            pltpu.SemaphoreType.DMA((3, 6)), pltpu.SemaphoreType.DMA((2, 6)),
            pltpu.SemaphoreType.DMA((LATER_CROSS,)), pltpu.SemaphoreType.DMA((LATER_CROSS,)),
        ]
    return pl.pallas_call(
        functools.partial(moe_backward_kernel, layer, experts, rows, width, bool(later)),
        name="moe_backward",
        out_shape=(
            jax.ShapeDtypeStruct((rows, width), F32),
            gu_shape, down_shape, gu_shape, down_shape,
            jax.ShapeDtypeStruct((width, LANES), F32),
        ) + later_out,
        in_specs=[vmem, vmem] + [any_spec] * (7 + len(later)),
        out_specs=(vmem,) + (any_spec,) * 4 + (vmem,) + (any_spec,) * len(later_out),
        scratch_shapes=[
            pltpu.VMEM((EXP_DEV, width, 2 * FF), BF16),
            pltpu.VMEM((EXP_DEV * FF, width), BF16),
            pltpu.VMEM((total, wide), BF16),
            pltpu.VMEM((total, EXP_DEV * 2 * FF), BF16),
            pltpu.VMEM((total, EXP_DEV * FF), BF16),
            pltpu.VMEM((total, EXP_DEV * 2 * FF + LANES), BF16),
            expert_gu, expert_gu, expert_down, expert_down,
            pltpu.SemaphoreType.DMA((6,)),
            pltpu.SemaphoreType.DMA((4, width // TILE)),
        ] + later_scratch + plane_scratch(rows, width, wide),
        cost_estimate=COST,
        compiler_params=pltpu.CompilerParams(
            collective_id=collective_id, has_side_effects=True, vmem_limit_bytes=VMEM_BYTES),
    )(block, router, *weights, *kept, *later)


def split_terms(values):
    high = values.astype(BF16)
    return high, (values - high.astype(F32)).astype(BF16)


def with_lanes(block, columns):
    extra = jnp.concatenate(columns, axis=1)
    extra = jnp.pad(extra, ((0, 0), (0, LANES - extra.shape[1])))
    return jnp.concatenate([block, extra], axis=1)


def far_order(z, i):
    low = jnp.where(i == 0, 3, jnp.where(i == 1, jnp.where(z == 0, 2, 0), jnp.where(z == 0, 1, 2)))
    high = jnp.where(i == 0, 0, jnp.where(i == 1, jnp.where(z == 3, 1, 3), jnp.where(z == 3, 2, 1)))
    return jnp.where(z < 2, low, high)


def remote_copy(src, dst, send_sem, recv_sem, device):
    return pltpu.make_async_remote_copy(
        src_ref=src, dst_ref=dst, send_sem=send_sem, recv_sem=recv_sem, device_id=device, device_id_type=MESH)


class GradientSum:
    def __init__(self, plane, h, cols, grad, small, core_got, small_own, small_got, load_sem, core_sem, small_sem):
        self.plane, self.h, self.cols = plane, h, cols
        self.core_got, self.small_own, self.small_got = core_got, small_own, small_got
        core, shard = plane.sec, plane.shard
        places = [(c, side) for c in range(LINE) for side in range(SIDE)]
        self.loads = [
            pltpu.make_async_copy(
                grad.at[n, core], plane.parts.at[plane.block(c, h, side), pl.ds(0, cols)], load_sem.at[n])
            for n, (c, side) in enumerate(places)
        ]
        self.loads.append(pltpu.make_async_copy(small.at[shard, :, core], small_own, load_sem.at[len(places)]))
        self.copies = [
            remote_copy(grad.at[:, 1 - core], core_got, core_sem.at[0], core_sem.at[1], plane.other_core())
        ]
        for n, (there, half, device) in enumerate((
            (shard, 1 - core, plane.other_core()),
            (1 - shard, core, plane.other_shard()),
            (1 - shard, 1 - core, self.diagonal(plane)),
        )):
            self.copies.append(remote_copy(
                small.at[there, :, half], small_got.at[n], small_sem.at[0, n], small_sem.at[1, n], device))

    @staticmethod
    def diagonal(plane):
        return (1 - plane.sec, plane.owner, 1 - plane.shard)

    def start_loads(self):
        for load in self.loads:
            load.start()

    def start_copies(self):
        for copy in self.copies:
            copy.start()

    def wait_terms(self):
        for load in self.loads:
            load.wait()
        for copy in self.copies:
            copy.wait_recv()

    def prepare(self, first, last):
        plane, h, cols = self.plane, self.h, self.cols

        def one(k, carry):
            c = jnp.where(k < 2 * (LINE - 1), far_order(plane.z, lax.div(k, 2)), plane.z)
            side = jnp.where(lax.rem(k, 2) == 0, 1 - plane.x, plane.x)
            n = c * SIDE + side
            at = plane.block(c, h, side)
            plane.parts[at, pl.ds(0, cols)] = (
                plane.parts[at, pl.ds(0, cols)].astype(F32) + self.core_got[n].astype(F32)).astype(BF16)
            total = self.small_own[n].astype(F32)
            for other in range(3):
                total = total + self.small_got[other, n].astype(F32)
            plane.parts[at, pl.ds(cols, LANES)] = total.astype(BF16)
            pl.when(side != plane.x)(lambda: plane.side_copy(c, h).start())
            return carry

        lax.fori_loop(first, last, one, 0)

    def pass_on(self, i):
        self.plane.pass_chunk(far_order(self.plane.z, i), self.h)

    def hand_over(self, out_ref):
        plane, h = self.plane, self.h
        second, third = far_order(plane.z, 1), far_order(plane.z, 2)
        plane.pass_chunk(second, h, send=False)
        out_ref[0] = plane.sums[second * HALVES + h]
        for n, c in ((1, third), (2, plane.z)):
            plane.side_copy(c, h).wait_recv()
            out_ref[n] = plane.own_part(c, h).astype(BF16)

    def drain(self, chunks=LINE - 1):
        plane, h = self.plane, self.h
        for copy in self.copies:
            copy.wait_send()

        def one(c, carry):
            plane.side_copy(c, h).wait_send()
            return carry

        lax.fori_loop(0, LINE, one, 0)
        for i in range(chunks):
            plane.wait_sent_sum(far_order(plane.z, i), h)


def sum_scratch(places, sub, cols):
    plane = plane_scratch(HALVES * sub, cols + LANES, cols + LANES)
    own = [
        pltpu.VMEM((places, sub, cols), BF16),
        pltpu.VMEM((places, sub, LANES), BF16),
        pltpu.VMEM((3, places, sub, LANES), BF16),
        pltpu.SemaphoreType.DMA((places + 1,)),
        pltpu.SemaphoreType.DMA((2,)),
        pltpu.SemaphoreType.DMA((2, 3)),
    ]
    return own, plane


def reduce_kernel(sub, cols, g0, t0, shares1, gu_hbm, down_hbm, sent_gu_hbm, sent_down_hbm, gu1_hbm, down1_hbm, tail1_hbm, edge,
                  sum_hbm, own_gu_hbm, own_down_hbm, got_gu_hbm, got_down_hbm, own_down1_hbm, got_gu1_hbm,
                  got_down1_hbm, got_edge,
                  core_got, small_own, small_got, load_sem, core_sem, small_sem,
                  result, own_gu, core_gu, other_gu, own_down, core_down, other_down,
                  share_sem, expert_load_sem, expert_core_sem, edge_sem, move_sem, expert_sem,
                  core_expert_sem, store_sem, *plane_refs):
    plane = Plane(HALVES * sub, plane_refs)
    gathered = plane.gathered
    core, z, x = plane.sec, plane.z, plane.x
    remote = remote_copy
    sums = GradientSum(plane, 1, cols, g0, t0, core_got, small_own, small_got, load_sem, core_sem, small_sem)
    pieces, expert_loads = [], []
    for layer, hbm, sent, own, there, other, own_hbm, got_hbm, count, first in (
        (0, gu_hbm, sent_gu_hbm, own_gu, core_gu, other_gu, own_gu_hbm, got_gu_hbm, 4, 0),
        (0, down_hbm, sent_down_hbm, own_down, core_down, other_down, own_down_hbm, got_down_hbm, 2, 0),
    ):
        size = own.shape[0] // count
        for n in range(first, count):
            at, k = pl.ds(n * size, size), len(pieces)
            pieces.append((layer, own, there, other, own_hbm, got_hbm, at))
            expert_loads.append((
                pltpu.make_async_copy(hbm.at[at], own.at[at], expert_load_sem.at[k]),
                None if sent is None else remote(
                    sent.at[at], there.at[at], expert_core_sem.at[0, k], expert_core_sem.at[1, k],
                    plane.other_core()),
            ))
    count = LINE * SIDE * HALVES
    split = tail1_hbm.shape[0]
    low, high = pl.ds(0, split), pl.ds(split, split)
    ready_copies = [
        pltpu.make_async_copy(down1_hbm.at[low], own_down1_hbm.at[low], store_sem.at[count + 6]),
        pltpu.make_async_copy(tail1_hbm, own_down1_hbm.at[high], store_sem.at[count + 7]),
    ]
    second, third = far_order(z, 1), far_order(z, 2)
    load_shares = [
        pltpu.make_async_copy(shares1.at[0], plane.sums.at[second * HALVES], share_sem.at[0]),
        pltpu.make_async_copy(shares1.at[1], plane.parts.at[plane.block(third, 0, x)], share_sem.at[1]),
        pltpu.make_async_copy(shares1.at[2], plane.parts.at[plane.block(z, 0, x)], share_sem.at[2]),
    ]
    for load in load_shares:
        load.start()
    expert_loads[0][0].start()
    sums.start_loads()
    for load, _ in expert_loads[1:]:
        load.start()
    plane.barrier(plane.other_core(), plane.other_shard(), sums.diagonal(plane))
    sums.start_copies()
    for _, copy in expert_loads:
        if copy is not None:
            copy.start()

    def move(h):
        return remote(
            result.at[h], gathered.at[plane.block(z, core, x)], move_sem.at[0], move_sem.at[1], plane.other_core())

    def send_block(h):
        pl.when(z < LINE - 1)(lambda: plane.forward_up(z, h).start())
        pl.when(z > 0)(lambda: plane.forward_down(z, h).start())
        plane.forward_side(z, h).start()

    def begin_gather(h):
        own_layer = core == 1 - h
        pl.when(jnp.logical_not(own_layer))(lambda: move(h).start())

        @pl.when(own_layer)
        def _():
            gathered[plane.block(z, core, x)] = result[h]
            send_block(core)
            arrived = remote(
                result.at[h], gathered.at[plane.block(z, 1 - core, x)], move_sem.at[0], move_sem.at[1],
                plane.other_core())
            arrived.wait_recv()
            send_block(1 - core)

    exchange = []

    def send_piece():
        n = len(exchange)
        layer, own, there, other, own_hbm, got_hbm, at = pieces[n]
        for load in expert_loads[n]:
            if load is not None:
                load.wait()
        if there is not None:
            own[at] = (own[at].astype(F32) + there[at].astype(F32)).astype(BF16)
        exchange.append(
            remote(own.at[at], other.at[at], expert_sem.at[0, n], expert_sem.at[1, n], plane.other_shard()))
        exchange[-1].start()

    send_piece()
    for load in load_shares:
        load.wait()
    plane.send_sum(second, 0)
    edges = remote(edge, got_edge, edge_sem.at[0], edge_sem.at[1], plane.other_core())
    edges.start()
    later_copies = [
        remote(gu1_hbm, got_gu1_hbm, edge_sem.at[2], edge_sem.at[3], plane.other_core()),
        remote(down1_hbm.at[low], got_down1_hbm.at[low], edge_sem.at[4], edge_sem.at[5], plane.other_core()),
        remote(tail1_hbm, got_down1_hbm.at[high], edge_sem.at[6], edge_sem.at[7], plane.other_core()),
    ]
    for copy in later_copies:
        pl.when(core == 0)(lambda copy=copy: copy.start())
    for copy in ready_copies:
        copy.start()

    def out_copy(c, h, side):
        at = pl.multiple_of(((c * SIDE + side) * HALVES + h) * sub, sub)
        return pltpu.make_async_copy(
            gathered.at[plane.block(c, h, side)], sum_hbm.at[pl.ds(at, sub)],
            store_sem.at[(c * SIDE + side) * HALVES + h])

    def gather(t):
        for turn in range(HALVES):
            h = core if turn == 0 else 1 - core
            plane.relay(t, h)
            c = chunk_order(z, t - 1)
            plane.wait_side_block(c, h)
            out_copy(c, h, x).start()
            out_copy(c, h, 1 - x).start()

    def to_core(n):
        layer, own, there, other, own_hbm, got_hbm, at = pieces[n]
        return remote(
            own.at[at], got_hbm.at[at], core_expert_sem.at[0, n], core_expert_sem.at[1, n], plane.other_core())

    def keep(n):
        layer, own, there, other, own_hbm, got_hbm, at = pieces[n]
        return pltpu.make_async_copy(own.at[at], own_hbm.at[at], store_sem.at[count + n])

    def expert_piece(n):
        layer, own, there, other, own_hbm, got_hbm, at = pieces[n]
        exchange[n].wait()
        own[at] = (own[at].astype(F32) + other[at].astype(F32)).astype(BF16)
        pl.when(core != layer)(lambda: to_core(n).start())
        keep(n).start()

    sums.wait_terms()
    sums.prepare(0, LINE)
    plane.pass_chunk(third, 0, side=False)
    send_piece()
    sums.prepare(LINE, LINE * SIDE)
    sums.pass_on(0)
    send_piece()
    plane.finish_piece(0, result, side=False)
    begin_gather(0)
    for i in range(1, LINE - 1):
        sums.pass_on(i)
        send_piece()
        pl.when(core == 1)(lambda i=i: gather(i))
    while len(exchange) < len(pieces):
        send_piece()
    plane.finish_piece(1, result)
    begin_gather(1)
    for n in range(2):
        expert_piece(n)

    @pl.when(core == 1)
    def _():
        gather(LINE - 1)
        gather(LINE)

    @pl.when(core == 0)
    def _():
        def one(t, carry):
            gather(t)
            return carry

        lax.fori_loop(1, LINE + 1, one, 0)

    for n in range(2, len(pieces)):
        expert_piece(n)
    sums.drain()
    plane.wait_sent_sum(second, 0)
    plane.wait_sent_sum(third, 0)
    plane.drain_gather()
    move(0).wait_send()

    def stored(k, carry):
        out_copy(lax.div(k, SIDE * HALVES), lax.rem(k, HALVES), lax.rem(lax.div(k, HALVES), SIDE)).wait()
        return carry

    lax.fori_loop(0, count, stored, 0)
    for n in range(len(pieces)):
        keep(n).wait()
        pl.when(core != pieces[n][0])(lambda n=n: to_core(n).wait_send())
        pl.when(core == pieces[n][0])(lambda n=n: to_core(n).wait_recv())
    edges.wait()
    for copy in ready_copies:
        copy.wait()
    for copy in later_copies:
        pl.when(core == 0)(lambda copy=copy: copy.wait_send())
        pl.when(core == 1)(lambda copy=copy: copy.wait_recv())


def reduce_gradients(g0, t0, shares1, experts0, gu1, down1, tail1, edge, collective_id):
    places, halves, sub, cols = g0.shape
    grad_gu, grad_down = experts0[:2]
    any_spec = pl.BlockSpec(memory_space=pl.ANY)
    wide = cols + LANES
    gu, down = jax.ShapeDtypeStruct(grad_gu.shape, BF16), jax.ShapeDtypeStruct(grad_down.shape, BF16)
    gu_v, down_v = pltpu.VMEM(grad_gu.shape, BF16), pltpu.VMEM(grad_down.shape, BF16)
    own, plane = sum_scratch(places, sub, cols)
    return pl.pallas_call(
        functools.partial(reduce_kernel, sub, cols),
        name="reduce_gradients",
        out_shape=(
            jax.ShapeDtypeStruct((places * halves * sub, wide), BF16), gu, down, gu, down, down, gu, down,
            jax.ShapeDtypeStruct(edge.shape, edge.dtype),
        ),
        in_specs=[any_spec] * 11,
        out_specs=(any_spec,) * 9,
        scratch_shapes=own + [
            pltpu.VMEM((2, sub, wide), BF16),
            gu_v, gu_v, gu_v, down_v, down_v, down_v,
            pltpu.SemaphoreType.DMA((3,)),
            pltpu.SemaphoreType.DMA((6,)),
            pltpu.SemaphoreType.DMA((2, 6)),
            pltpu.SemaphoreType.DMA((8,)),
            pltpu.SemaphoreType.DMA((2,)),
            pltpu.SemaphoreType.DMA((2, 6)),
            pltpu.SemaphoreType.DMA((2, 6)),
            pltpu.SemaphoreType.DMA((places * halves + 8,)),
        ] + plane,
        compiler_params=pltpu.CompilerParams(
            collective_id=collective_id, has_side_effects=True, vmem_limit_bytes=VMEM_BYTES),
    )(g0, t0, shares1, *experts0, gu1, down1, tail1, edge)


def finish_kernel(qkv_cols, attn, gu_own, gu_got, gu_one, gu_moved, down_own, down_got, down_one, down_moved,
                  qkv_hbm, out_hbm, gu_hbm, down_hbm, attn_v, gu_v, down_v, qkv_f, out_f, gu_f, down_f,
                  load_sem, store_sem):
    core = lax.axis_index("section")
    steps = []

    def chunks(rows, count):
        return [pl.ds(n * (rows // count), rows // count) for n in range(count)]

    def choose(zero, one, dst, sem):
        copies = [pltpu.make_async_copy(zero, dst, sem), pltpu.make_async_copy(one, dst, sem)]
        pl.when(core == 0)(lambda: copies[0].start())
        pl.when(core == 1)(lambda: copies[1].start())
        return copies[0]

    def add(load, convert, stores):
        steps.append((load, convert, stores))

    def store(src, dst, n):
        return pltpu.make_async_copy(src, dst, store_sem.at[n])

    stored = 0
    for j, (zero, one) in enumerate(((gu_own, gu_moved), (gu_got, gu_one))):
        for at in chunks(gu_f.shape[1], 6):
            def convert(j=j, at=at):
                gu_f[j, at, :] = gu_v[j, at, :].astype(F32)

            load = choose(zero.at[at], one.at[at], gu_v.at[j, at], load_sem.at[len(steps)])
            add(load, convert, [store(gu_f.at[j, at], gu_hbm.at[j, at], stored)])
            stored += 1
    for j, (zero, one) in enumerate(((down_own, down_moved), (down_got, down_one))):
        for at in chunks(down_f.shape[1], 2):
            def convert(j=j, at=at):
                down_f[j, at, :] = down_v[j, at, :].astype(F32)

            load = choose(zero.at[at], one.at[at], down_v.at[j, at], load_sem.at[len(steps)])
            add(load, convert, [store(down_f.at[j, at], down_hbm.at[j, at], stored)])
            stored += 1
    for at in chunks(attn_v.shape[0], 8):
        def convert(at=at):
            qkv_f[at, :] = attn_v[at, pl.ds(0, qkv_cols)].astype(F32)
            out_f[at, :] = attn_v[at, pl.ds(qkv_cols, out_f.shape[1])].astype(F32)

        load = pltpu.make_async_copy(attn.at[at, pl.ds(0, attn_v.shape[1])], attn_v.at[at], load_sem.at[len(steps)])
        load.start()
        add(load, convert, [
            store(qkv_f.at[at], qkv_hbm.at[at], stored), store(out_f.at[at], out_hbm.at[at], stored + 1)])
        stored += 2
    for load, convert, stores in steps:
        load.wait()
        convert()
        for copy in stores:
            copy.start()
    for load, convert, stores in steps:
        for copy in stores:
            copy.wait()


def finish_outputs(attn, gus, downs, qkv_cols, out_cols):
    rows = attn.shape[0]
    gu, down = (EXP_DEV,) + gus[0].shape, (EXP_DEV,) + downs[0].shape
    any_spec = pl.BlockSpec(memory_space=pl.ANY)
    return pl.pallas_call(
        functools.partial(finish_kernel, qkv_cols),
        name="finish_outputs",
        out_shape=(
            jax.ShapeDtypeStruct((rows, qkv_cols), F32),
            jax.ShapeDtypeStruct((rows, out_cols), F32),
            jax.ShapeDtypeStruct(gu, F32),
            jax.ShapeDtypeStruct(down, F32),
        ),
        in_specs=[any_spec] * 9,
        out_specs=(any_spec,) * 4,
        scratch_shapes=[
            pltpu.VMEM((rows, qkv_cols + out_cols), BF16),
            pltpu.VMEM(gu, BF16),
            pltpu.VMEM(down, BF16),
            pltpu.VMEM((rows, qkv_cols), F32),
            pltpu.VMEM((rows, out_cols), F32),
            pltpu.VMEM(gu, F32),
            pltpu.VMEM(down, F32),
            pltpu.SemaphoreType.DMA((24,)),
            pltpu.SemaphoreType.DMA((32,)),
        ],
        compiler_params=pltpu.CompilerParams(vmem_limit_bytes=VMEM_BYTES),
    )(attn, *gus, *downs)


PAIRS = 2
GROUP = QUERY_HEADS // KEY_VALUE_HEADS
SCALE = HEAD_SIZE ** (-0.5)


class Pair:
    def __init__(self):
        self.sec, self.owner, self.me = (lax.axis_index(n) for n in ("section", "expert", "shard"))
        self.peer = 1 - self.me

    def barrier(self, with_core=False):
        sem = pltpu.get_barrier_semaphore()
        pl.semaphore_signal(
            sem, inc=1, device_id=(self.sec, self.owner, self.peer), device_id_type=MESH)
        if with_core:
            pl.semaphore_signal(
                sem, inc=1, device_id=(1 - self.sec, self.owner, self.me), device_id_type=MESH)
        pl.semaphore_wait(sem, 1 + with_core)

    def send(self, src, dst, send_sem, recv_sem):
        return pltpu.make_async_remote_copy(
            src_ref=src, dst_ref=dst, send_sem=send_sem, recv_sem=recv_sem,
            device_id=(self.sec, self.owner, self.peer), device_id_type=MESH)


def head_columns(shard):
    kv_pair = KEY_VALUE_HEADS // 2 // PAIRS * HEAD_SIZE
    q_pair = kv_pair * GROUP
    wide = q_pair + 2 * kv_pair
    spans = []
    for i in range(PAIRS):
        at = shard * PAIRS + i
        spans.append((at * q_pair, i * wide, q_pair))
        spans.append((QUERY_WIDTH + at * kv_pair, i * wide + q_pair, kv_pair))
        spans.append((QUERY_WIDTH + KV_WIDTH + at * kv_pair, i * wide + q_pair + kv_pair, kv_pair))
    return spans


def head_at(i, n, g):
    kv_pair = KEY_VALUE_HEADS // 2 // PAIRS * HEAD_SIZE
    q_pair = kv_pair * GROUP
    base = i * (q_pair + 2 * kv_pair)
    return (
        pl.ds(base + (n * GROUP + g) * HEAD_SIZE, HEAD_SIZE),
        pl.ds(base + q_pair + n * HEAD_SIZE, HEAD_SIZE),
        pl.ds(base + q_pair + kv_pair + n * HEAD_SIZE, HEAD_SIZE),
    )


KV_IN_PAIR = KEY_VALUE_HEADS // 2 // PAIRS


def load_attention(layer, sec, wq, wq_other, wo, wo_other, wq_v, wo_v, sems):
    loads = []
    for j in range(2):
        for at, local, size in head_columns(j):
            loads.append(load_layer(
                layer, sec, wq.at[:, pl.ds(at, size)], wq_other.at[:, pl.ds(at, size)],
                wq_v.at[j, :, pl.ds(local, size)], sems.at[len(loads)]))
    loads.append(load_layer(layer, sec, wo, wo_other, wo_v, sems.at[len(loads)]))
    return loads


LOADS = 2 * PAIRS * 3 + 1


def attention_forward_kernel(layer, rows, width, h_ref, allowed_ref, gains_ref, router_ref, mask_ref, wq, wq_other,
                             wo, wo_other, block_ref, h1_ref, a_ref, qkv_ref, p_ref, o_ref,
                             wq_v, wo_v, a_parts, a_half, part_send, got_part, out_send, got_out,
                             load_sem, send_sem, recv_sem, *turn):
    pair = Pair()
    me, peer = pair.me, pair.peer
    half = width // 2
    loads = load_attention(layer, pair.sec, wq, wq_other, wo, wo_other, wq_v, wo_v, load_sem)
    pair.barrier(bool(turn))

    def span(who):
        return pl.ds(pl.multiple_of(who * rows, rows), rows)

    h = h_ref[...].astype(F32)
    r1 = lax.rsqrt(jnp.mean(h * h, axis=1, keepdims=True) + EPS)
    a = (h * r1 * gains_ref[pl.ds(0, 1), :]).astype(BF16)
    for j in range(2):
        a_parts[j] = a[:, j * half : (j + 1) * half]
    a_half[span(me)] = a_parts[me]
    for load in loads[:-1]:
        load.wait()
    part_send[span(me)] = nn(a_parts[me], wq_v[peer]).astype(BF16)
    if turn:
        pl.when(pair.sec == 0)(lambda: pl.semaphore_wait(turn[0], 1))
    send_a = pair.send(a_parts.at[peer], a_half.at[span(me)], send_sem.at[0], recv_sem.at[0])
    send_a.start()
    send_own = pair.send(part_send.at[span(me)], got_part.at[span(me)], send_sem.at[1], recv_sem.at[1])
    send_own.start()
    send_a.wait_recv()
    part_send[span(peer)] = nn(a_half[span(peer)], wq_v[peer]).astype(BF16)
    send_other = pair.send(
        part_send.at[span(peer)], got_part.at[span(peer)], send_sem.at[2], recv_sem.at[2])
    send_other.start()
    mine = nn(a_half[...], wq_v[me])
    a_ref[...] = a_half[...]
    send_own.wait_recv()
    send_other.wait_recv()
    qkv_ref[...] = (mine + got_part[...].astype(F32)).astype(BF16)
    allowed = allowed_ref[...] > 0
    for i in range(PAIRS):
        for n in range(KV_IN_PAIR):
            for g in range(GROUP):
                q_at, k_at, v_at = head_at(i, n, g)
                j = (i * KV_IN_PAIR + n) * GROUP + g
                s = nt(qkv_ref[:, q_at], qkv_ref[:, k_at]) * SCALE
                s = jnp.where(allowed, s, MASKED_SCORE)
                ex = jnp.exp(s - jnp.max(s, axis=1, keepdims=True))
                p = (ex / jnp.sum(ex, axis=1, keepdims=True)).astype(BF16)
                p_ref[j] = p
                o_ref[:, pl.ds(j * HEAD_SIZE, HEAD_SIZE)] = nn(p, qkv_ref[:, v_at]).astype(BF16)
    loads[-1].wait()
    out_send[...] = nn(o_ref[span(peer)], wo_v[...]).astype(BF16)
    send_out = pair.send(out_send, got_out, send_sem.at[3], recv_sem.at[3])
    send_out.start()
    own = nn(o_ref[span(me)], wo_v[...])
    send_out.wait_recv()
    if turn:
        @pl.when(pair.sec == 1)
        def _():
            pl.semaphore_signal(
                turn[0], inc=1, device_id=(1 - pair.sec, pair.owner, me), device_id_type=MESH)

    h1 = h + own + got_out[...].astype(F32)
    h1_ref[...] = h1
    r2 = lax.rsqrt(jnp.mean(h1 * h1, axis=1, keepdims=True) + EPS)
    b = (h1 * r2 * gains_ref[pl.ds(1, 1), :]).astype(BF16)
    block_ref[:, pl.ds(0, width)] = b
    mask = mask_ref[...] > 0
    logits = jnp.where(mask, nt(b, router_ref[...]), MASKED_SCORE)
    ex = jnp.where(mask, jnp.exp(logits - jnp.max(logits, axis=1, keepdims=True)), 0.0)
    gates = ex / (0.5 * jnp.sum(ex, axis=1, keepdims=True))
    high = gates.astype(BF16).astype(F32)
    block_ref[:, pl.ds(width, LANES)] = jnp.where(mask_ref[...] > 1, gates - high, high).astype(BF16)
    for send in (send_a, send_own, send_other, send_out):
        send.wait_send()


def attention_forward(layer, h, allowed, gains, router, mask, weights, collective_id):
    rows, width = h.shape
    half, group = width // 2, 2 * rows
    qkv = (QUERY_WIDTH + 2 * KV_WIDTH) // 2
    heads = QUERY_HEADS // 2
    any_spec = pl.BlockSpec(memory_space=pl.ANY)
    vmem = pl.BlockSpec(memory_space=pltpu.VMEM)
    return pl.pallas_call(
        functools.partial(attention_forward_kernel, layer, rows, width),
        name="attention_forward",
        out_shape=(
            jax.ShapeDtypeStruct((rows, width + LANES), BF16),
            jax.ShapeDtypeStruct((rows, width), F32),
            jax.ShapeDtypeStruct((group, half), BF16),
            jax.ShapeDtypeStruct((group, qkv), BF16),
            jax.ShapeDtypeStruct((heads, group, group), BF16),
            jax.ShapeDtypeStruct((group, QUERY_WIDTH // 2), BF16),
        ),
        in_specs=[vmem] * 5 + [any_spec] * 4,
        out_specs=(vmem,) * 6,
        scratch_shapes=[
            pltpu.VMEM((2, half, qkv), BF16),
            pltpu.VMEM((QUERY_WIDTH // 2, width), BF16),
            pltpu.VMEM((2, rows, half), BF16),
            pltpu.VMEM((group, half), BF16),
            pltpu.VMEM((group, qkv), BF16),
            pltpu.VMEM((group, qkv), BF16),
            pltpu.VMEM((rows, width), BF16),
            pltpu.VMEM((rows, width), BF16),
            pltpu.SemaphoreType.DMA((LOADS,)),
            pltpu.SemaphoreType.DMA((4,)),
            pltpu.SemaphoreType.DMA((4,)),
        ] + ([pltpu.SemaphoreType.REGULAR] if layer == 0 else []),
        cost_estimate=COST,
        compiler_params=pltpu.CompilerParams(
            collective_id=collective_id, has_side_effects=True, vmem_limit_bytes=VMEM_BYTES),
    )(h, allowed, gains, router, mask, *weights)


ATTENTION_BACKWARD_REFS = 20


def attention_backward_kernel(layer, rows, width, experts, router_grad_ref, db_ref, dout_ref, h1_ref, h_ref, gains_ref, a_ref, qkv_ref,
                              p_ref, o_ref, wq, wq_other, wo, wo_other, *refs):
    beside = len(refs) > ATTENTION_BACKWARD_REFS
    (later, refs) = (refs[:3], refs[3:]) if beside else ((), refs)
    (dh_ref, columns_ref, grad_hbm), refs = refs[:3], refs[3:]
    (later_out, refs) = (refs[:2], refs[2:]) if beside else ((), refs)
    (wq_v, wo_v, d_all, do, dqkv, got_dqkv, da_send, got_da, dh1_v, grad_q, grad_o,
     gain_grads_ref, columns_v, load_sem, store_sem, send_sem, recv_sem), refs = refs[:17], refs[17:]
    pair = Pair()
    me, peer = pair.me, pair.peer
    half = width // 2
    qkv_cols = dqkv.shape[1]
    pair_cols = qkv_cols // PAIRS
    loads = load_attention(layer, pair.sec, wq, wq_other, wo, wo_other, wq_v, wo_v, load_sem)
    if beside:
        sub, cols_all = later[0].shape[2:]
        plane = Plane(HALVES * sub, (None,) + tuple(refs[10:]))
        sums = GradientSum(plane, 0, cols_all, *later[:2], *refs[:6])
        tail_own, tail_got, tail_load, tail_sem = refs[6:10]
        tail_rows = tail_own.shape[0]
        load_tail = pltpu.make_async_copy(later[2].at[pl.ds(tail_rows, tail_rows)], tail_own, tail_load)
        load_tail.start()
        sums.start_loads()
        plane.barrier(plane.other_core(), plane.other_shard(), sums.diagonal(plane))
        sums.start_copies()
        load_tail.wait()
        tail_copy = pair.send(tail_own, tail_got, tail_sem.at[0], tail_sem.at[1])
    else:
        pair.barrier()

    def span(who):
        return pl.ds(pl.multiple_of(who * rows, rows), rows)

    h1 = h1_ref[...]
    r2 = lax.rsqrt(jnp.mean(h1 * h1, axis=1, keepdims=True) + EPS)
    normed = h1 * r2
    db = db_ref[...]
    scaled = db * gains_ref[pl.ds(1, 1), :]
    gain_grads_ref[...] = jnp.zeros_like(gain_grads_ref)
    gain_grads_ref[pl.ds(experts + 1, 1), :] = jnp.sum(db * normed, axis=0, keepdims=True)
    dh1 = dout_ref[...].astype(F32) + r2 * (
        scaled - normed * jnp.mean(scaled * normed, axis=1, keepdims=True))
    dh1_v[...] = dh1
    d_all[span(me)] = dh1.astype(BF16)
    send_d = pair.send(d_all.at[span(me)], d_all.at[span(me)], send_sem.at[0], recv_sem.at[0])
    send_d.start()
    router_terms = router_grad_ref[...]
    lane = lax.broadcasted_iota(jnp.int32, router_terms.shape, 1)
    router_terms = router_terms + pltpu.roll(router_terms, LANES // 2, 1)
    columns_v[...] = jnp.where(lane < experts, router_terms, 0.0)
    if beside:
        sums.wait_terms()
        sums.prepare(0, LINE)
    for load in loads:
        load.wait()
    do[span(me)] = nt(d_all[span(me)], wo_v[...]).astype(BF16)
    send_d.wait_recv()
    do[span(peer)] = nt(d_all[span(peer)], wo_v[...]).astype(BF16)
    sends = [send_d]
    if beside:
        tail_copy.start()
        pl.when(plane.inner == 0)(lambda: sums.pass_on(0))
        sums.prepare(LINE, LINE * SIDE)
    for i in range(PAIRS):
        cols = pl.ds(i * pair_cols, pair_cols)
        for n in range(KV_IN_PAIR):
            dk = dv = None
            for g in range(GROUP):
                q_at, k_at, v_at = head_at(i, n, g)
                j = (i * KV_IN_PAIR + n) * GROUP + g
                p_low = p_ref[j]
                p = p_low.astype(F32)
                d_head = do[:, pl.ds(j * HEAD_SIZE, HEAD_SIZE)]
                weighted = p * nt(d_head, qkv_ref[:, v_at])
                ds = (weighted - p * jnp.sum(weighted, axis=1, keepdims=True)).astype(BF16)
                dqkv[:, q_at] = (nn(ds, qkv_ref[:, k_at]) * SCALE).astype(BF16)
                dk_part, dv_part = tn(ds, qkv_ref[:, q_at]), tn(p_low, d_head)
                dk = dk_part if dk is None else dk + dk_part
                dv = dv_part if dv is None else dv + dv_part
            dqkv[:, k_at] = (dk * SCALE).astype(BF16)
            dqkv[:, v_at] = dv.astype(BF16)
        send = pair.send(dqkv.at[:, cols], got_dqkv.at[:, cols], send_sem.at[1 + i], recv_sem.at[1 + i])
        send.start()
        sends.append(send)
        if beside and i == 0:
            pl.when(plane.inner == 1)(lambda: sums.pass_on(0))
    da = nt(dqkv[...], wq_v[me])
    grad_q[me] = tn(a_ref[...], dqkv[...]).astype(BF16)
    grad_o[...] = tn(o_ref[...], d_all[...]).astype(BF16)
    store_o = pltpu.make_async_copy(
        grad_o, grad_hbm.at[:, pl.ds(QUERY_WIDTH + 2 * KV_WIDTH, width)], store_sem.at[LOADS - 1])
    store_o.start()
    for send in sends[1:]:
        send.wait_recv()
    da = da + nt(got_dqkv[...], wq_v[peer])
    da_send[...] = jnp.where(me == 0, da[rows:], da[:rows]).astype(BF16)
    send_da = pair.send(da_send, got_da, send_sem.at[1 + PAIRS], recv_sem.at[1 + PAIRS])
    send_da.start()
    own_da = jnp.where(me == 0, da[:rows], da[rows:])
    grad_q[peer] = tn(a_ref[...], got_dqkv[...]).astype(BF16)
    stores = [store_o]
    for j in range(2):
        for at, local, size in head_columns(j):
            store = pltpu.make_async_copy(
                grad_q.at[j, :, pl.ds(local, size)], grad_hbm.at[:, pl.ds(at, size)],
                store_sem.at[len(stores) - 1])
            store.start()
            stores.append(store)
    send_da.wait_recv()
    other_da = got_da[...].astype(F32)
    h = h_ref[...].astype(F32)
    r1 = lax.rsqrt(jnp.mean(h * h, axis=1, keepdims=True) + EPS)
    halves = []
    total = jnp.zeros((rows, 1), F32)
    for j in range(2):
        cols = pl.ds(j * half, half)
        da_j = jnp.where(me == j, own_da, other_da)
        normed = h[:, j * half : (j + 1) * half] * r1
        gain_grads_ref[pl.ds(experts, 1), cols] = jnp.sum(da_j * normed, axis=0, keepdims=True)
        scaled = da_j * gains_ref[pl.ds(0, 1), cols]
        total = total + jnp.sum(scaled * normed, axis=1, keepdims=True)
        halves.append((cols, scaled, normed))
    columns = columns_v[...] + jnp.transpose(gain_grads_ref[...])
    columns_ref[...] = columns.astype(BF16)
    for cols, scaled, normed in halves:
        dh_ref[:, cols] = dh1_v[:, cols] + r1 * (scaled - normed * (total / width))
    if beside:
        sums.hand_over(later_out[0])
        tail_copy.wait()
        later_out[1][...] = (tail_own[...].astype(F32) + tail_got[...].astype(F32)).astype(BF16)
        sums.drain(1)
    for send in sends + [send_da]:
        send.wait_send()
    for store in stores:
        store.wait()


def attention_backward(layer, experts, router_grad, db, dout, h1, h, gains, a_half, qkv, p, o, weights, later,
                       collective_id):
    rows, width = db.shape
    half, group = width // 2, 2 * rows
    cols = (QUERY_WIDTH + 2 * KV_WIDTH) // 2
    any_spec = pl.BlockSpec(memory_space=pl.ANY)
    vmem = pl.BlockSpec(memory_space=pltpu.VMEM)
    later_out, later_scratch = (), []
    if later:
        places, _, sub, later_cols = later[0].shape
        own, plane = sum_scratch(places, sub, later_cols)
        tail_shape = (later[2].shape[0] // 2, later[2].shape[1])
        later_out = (
            jax.ShapeDtypeStruct((3, sub, later_cols + LANES), BF16),
            jax.ShapeDtypeStruct(tail_shape, BF16),
        )
        later_scratch = own + [
            pltpu.VMEM(tail_shape, BF16),
            pltpu.VMEM(tail_shape, BF16),
            pltpu.SemaphoreType.DMA,
            pltpu.SemaphoreType.DMA((2,)),
        ] + plane[1:]
    return pl.pallas_call(
        functools.partial(attention_backward_kernel, layer, rows, width, experts),
        name="attention_backward",
        out_shape=(
            jax.ShapeDtypeStruct((rows, width), F32),
            jax.ShapeDtypeStruct((width, LANES), BF16),
            jax.ShapeDtypeStruct((half, QUERY_WIDTH + 2 * KV_WIDTH + width), BF16),
        ) + later_out,
        in_specs=[vmem] * 10 + [any_spec] * (4 + len(later)),
        out_specs=(vmem, vmem, any_spec) + (vmem,) * len(later_out),
        scratch_shapes=[
            pltpu.VMEM((2, half, cols), BF16),
            pltpu.VMEM((QUERY_WIDTH // 2, width), BF16),
            pltpu.VMEM((group, width), BF16),
            pltpu.VMEM((group, QUERY_WIDTH // 2), BF16),
            pltpu.VMEM((group, cols), BF16),
            pltpu.VMEM((group, cols), BF16),
            pltpu.VMEM((rows, half), BF16),
            pltpu.VMEM((rows, half), BF16),
            pltpu.VMEM((rows, width), F32),
            pltpu.VMEM((2, half, cols), BF16),
            pltpu.VMEM((QUERY_WIDTH // 2, width), BF16),
            pltpu.VMEM((LANES, width), F32),
            pltpu.VMEM((width, LANES), F32),
            pltpu.SemaphoreType.DMA((LOADS,)),
            pltpu.SemaphoreType.DMA((LOADS,)),
            pltpu.SemaphoreType.DMA((2 + PAIRS,)),
            pltpu.SemaphoreType.DMA((2 + PAIRS,)),
        ] + later_scratch,
        cost_estimate=COST,
        compiler_params=pltpu.CompilerParams(
            collective_id=collective_id, has_side_effects=True, vmem_limit_bytes=VMEM_BYTES),
    )(router_grad, db, dout, h1, h, gains, a_half, qkv, p, o, *weights, *later)


def dot(a, b, dims):
    return lax.dot_general(a, b, (dims, ((), ())), preferred_element_type=F32)


def rms_scale(values):
    return lax.rsqrt(jnp.mean(values * values, axis=-1, keepdims=True) + EPS)


def swap_cores(value):
    return lax.ppermute(value, "section", [(0, 1), (1, 0)])


def both_layers(own):
    return lax.all_gather(own, "section", axis=0, tiled=False)


def document_mask(sequence_lengths, rows):
    pos = jnp.arange(rows, dtype=jnp.int32)
    ends = jnp.cumsum(sequence_lengths)
    doc = jnp.sum((pos[:, None] >= ends[None, :]).astype(jnp.int32), axis=1)
    return (doc[:, None] == doc[None, :]) & (pos[None, :] <= pos[:, None])


def plain_attention(qkv, allowed, heads, kv_heads):
    rows = qkv.shape[0]
    group = heads // kv_heads
    q = qkv[:, : heads * HEAD_SIZE].reshape(rows, kv_heads, group, HEAD_SIZE)
    k = qkv[:, heads * HEAD_SIZE : (heads + kv_heads) * HEAD_SIZE].reshape(rows, kv_heads, HEAD_SIZE)
    v = qkv[:, (heads + kv_heads) * HEAD_SIZE :].reshape(rows, kv_heads, HEAD_SIZE)
    s = jnp.einsum("qhgd,khd->hgqk", q, k, preferred_element_type=F32) * HEAD_SIZE ** (-0.5)
    s = jnp.where(allowed[None, None], s, MASKED_SCORE)
    ex = jnp.exp(s - jnp.max(s, axis=-1, keepdims=True))
    p = ex / jnp.sum(ex, axis=-1, keepdims=True)
    o = jnp.einsum("hgqk,khd->qhgd", p.astype(BF16), v, preferred_element_type=F32)
    return o.reshape(rows, heads * HEAD_SIZE).astype(BF16), p, (q, k, v)


def plain_attention_backward(do, p, heads_in):
    q, k, v = heads_in
    rows = q.shape[0]
    dh = do.reshape(q.shape)
    dv = jnp.einsum("hgqk,qhgd->khd", p.astype(BF16), dh, preferred_element_type=F32)
    dp = jnp.einsum("qhgd,khd->hgqk", dh, v, preferred_element_type=F32)
    ds = (p * (dp - jnp.sum(p * dp, axis=-1, keepdims=True))).astype(BF16)
    dq = jnp.einsum("hgqk,khd->qhgd", ds, k, preferred_element_type=F32) * HEAD_SIZE ** (-0.5)
    dk = jnp.einsum("hgqk,qhgd->khd", ds, q, preferred_element_type=F32) * HEAD_SIZE ** (-0.5)
    return jnp.concatenate(
        [dq.reshape(rows, -1), dk.reshape(rows, -1), dv.reshape(rows, -1)], axis=1
    ).astype(BF16)


def column_parts(n, j):
    qw, kw = QUERY_WIDTH // n, KV_WIDTH // n
    return (
        (j * qw, qw),
        (QUERY_WIDTH + j * kw, kw),
        (QUERY_WIDTH + KV_WIDTH + j * kw, kw),
    )


def plain_shards(
    edge_inputs, seq_lengths, routes, w_qkv, w_out, w_router, gain_attn, gain_moe, w_gate_up, w_down
):
    sec = lax.axis_index("section")
    owner = lax.axis_index("expert")
    shard_pos = lax.axis_index("shard")
    n_shard = lax.axis_size("shard")
    n_owner = lax.axis_size("expert")
    rows, width = edge_inputs.shape[2], edge_inputs.shape[3]
    experts = w_router.shape[2]
    group_rows = rows * n_shard
    half = width // n_shard
    heads, kv_heads = QUERY_HEADS // n_shard, KEY_VALUE_HEADS // n_shard

    def pick(array, index):
        return lax.dynamic_index_in_dim(array, index, 0, keepdims=False)

    own_edge, other_edge = pick(edge_inputs[0], sec), swap_cores(pick(edge_inputs[0], 1 - sec))
    x_in = jnp.where(sec == 0, own_edge, other_edge)
    dy = jnp.where(sec == 0, other_edge, own_edge)
    own_routes, other_routes = pick(routes[0], sec), swap_cores(pick(routes[0], 1 - sec))
    layer_routes = (
        jnp.where(sec == 0, own_routes, other_routes),
        jnp.where(sec == 0, other_routes, own_routes),
    )
    allowed = document_mask(pick(seq_lengths, sec)[0], group_rows)
    wq = both_layers(w_qkv[0])
    wo = both_layers(w_out[0])
    small = jnp.concatenate([w_router[0], gain_attn[0][:, None], gain_moe[0][:, None]], axis=1)
    small = lax.all_gather(both_layers(small), "shard", axis=1, tiled=True)
    wgu = both_layers(w_gate_up[0])
    wd = both_layers(w_down[0])
    columns = jnp.arange(experts, dtype=jnp.int32)
    route_masks = [
        jnp.any(r[:, :, None] == columns[None, None, :], axis=1).astype(BF16) for r in layer_routes
    ]
    plane_masks = [lax.all_gather(m, "expert", axis=0, tiled=True) for m in route_masks]

    def forward(layer, h):
        gain_a = small[layer, :, experts].astype(F32)[None, :]
        gain_m = small[layer, :, experts + 1].astype(F32)[None, :]
        router = small[layer, :, :experts]
        r1 = rms_scale(h)
        a = (h * r1 * gain_a).astype(BF16)
        a_half = lax.all_to_all(
            a.reshape(rows, n_shard, half), "shard", split_axis=1, concat_axis=0, tiled=True
        ).reshape(group_rows, half)
        blocks = []
        for j in range(n_shard):
            blocks.append(
                jnp.concatenate(
                    [
                        dot(a_half, wq[layer, :, at : at + size], ((1,), (0,)))
                        for at, size in column_parts(n_shard, j)
                    ],
                    axis=1,
                ).astype(BF16)
            )
        qkv = lax.psum_scatter(jnp.stack(blocks), "shard", scatter_dimension=0, tiled=False)
        o, p, heads_in = plain_attention(qkv, allowed, heads, kv_heads)
        part = dot(o, wo[layer], ((1,), (0,))).astype(BF16)
        h1 = h + lax.psum_scatter(part, "shard", scatter_dimension=0, tiled=True).astype(F32)
        r2 = rms_scale(h1)
        b = (h1 * r2 * gain_m).astype(BF16)
        b_all = lax.all_gather(b, "expert", axis=0, tiled=True)
        mask = plane_masks[layer].astype(F32) > 0
        logits = jnp.where(mask, dot(b_all, router, ((1,), (0,))), MASKED_SCORE)
        ex = jnp.where(mask, jnp.exp(logits - jnp.max(logits, axis=1, keepdims=True)), 0.0)
        gates = ex / jnp.sum(ex, axis=1, keepdims=True)
        own_gates = lax.dynamic_slice_in_dim(gates, owner * EXP_DEV, EXP_DEV, 1)
        kept, scaled = [], []
        for j in range(EXP_DEV):
            gu = dot(b_all, wgu[layer, j], ((1,), (0,)))
            g, u = gu[:, :FF], gu[:, FF:]
            scaled.append((g * jax.nn.sigmoid(g) * u * own_gates[:, j : j + 1]).astype(BF16))
            kept.append(gu.astype(BF16))
        scaled = jnp.concatenate(scaled, axis=1)
        moe_part = dot(scaled, wd[layer].reshape(EXP_DEV * FF, width), ((1,), (0,))).astype(BF16)
        moe = lax.psum_scatter(moe_part, "expert", scatter_dimension=0, tiled=True).astype(F32)
        state = (h, r1, a_half, p, heads_in, o, h1, r2, b_all, own_gates, kept, scaled, moe)
        return h1 + moe, state

    def backward(layer, dout, dout_low, state):
        h, r1, a_half, p, heads_in, o, h1, r2, b_all, own_gates, kept, scaled, moe = state
        gain_a = small[layer, :, experts].astype(F32)[None, :]
        gain_m = small[layer, :, experts + 1].astype(F32)[None, :]
        router = small[layer, :, :experts]
        own_router = lax.dynamic_slice_in_dim(router, owner * EXP_DEV, EXP_DEV, 1)
        total = lax.all_gather(jnp.sum(dout * moe, axis=1), "expert", axis=0, tiled=True)
        dout_all = lax.all_gather(dout_low, "expert", axis=0, tiled=True)
        dgus, dcs = [], []
        for j in range(EXP_DEV):
            gate = own_gates[:, j : j + 1]
            g, u = kept[j][:, :FF].astype(F32), kept[j][:, FF:].astype(F32)
            sig = jax.nn.sigmoid(g)
            silu = g * sig
            dz = dot(dout_all, wd[layer, j], ((1,), (1,)))
            dgate = jnp.sum(dz * silu * u, axis=1, keepdims=True)
            dcs.append(gate * (dgate - total[:, None]))
            dz = dz * gate
            dgus.append(
                jnp.concatenate(
                    [dz * u * sig * (1.0 + g * (1.0 - sig)), dz * silu], axis=1
                ).astype(BF16)
            )
        dc = jnp.concatenate(dcs, axis=1)
        db_part = sum(dot(dgus[j], wgu[layer, j], ((1,), (1,))) for j in range(EXP_DEV))
        for j in range(EXP_DEV):
            db_part = db_part + dc[:, j : j + 1] * own_router[:, j].astype(F32)[None, :]
        db = lax.psum_scatter(
            db_part.astype(BF16), "expert", scatter_dimension=0, tiled=True
        ).astype(F32)
        grad_down = dot(scaled, dout_all, ((0,), (0,))).reshape(EXP_DEV, FF, width)
        grad_gu = jnp.stack([dot(b_all, dgus[j], ((0,), (0,))) for j in range(EXP_DEV)])
        grad_router = lax.dot_general(
            dc, b_all.astype(F32), (((0,), (0,)), ((), ())), precision=lax.Precision.HIGHEST
        )
        normed = h1 * r2
        grad_gain_m = jnp.sum(db * normed, axis=0)
        scaled_db = db * gain_m
        dh1 = dout + r2 * (scaled_db - normed * jnp.mean(scaled_db * normed, axis=1, keepdims=True))
        dattn = lax.all_gather(dh1.astype(BF16), "shard", axis=0, tiled=True)
        do = dot(dattn, wo[layer], ((1,), (1,))).astype(BF16)
        grad_out = dot(o, dattn, ((0,), (0,)))
        dqkv = lax.all_gather(plain_attention_backward(do, p, heads_in), "shard", axis=0, tiled=False)
        da = 0.0
        grad_qkv = []
        for part in range(3):
            grad_qkv.append([])
        for j in range(n_shard):
            at_local = 0
            for part, (at, size) in enumerate(column_parts(n_shard, j)):
                piece = dqkv[j, :, at_local : at_local + size]
                at_local += size
                da = da + dot(piece, wq[layer, :, at : at + size], ((1,), (1,)))
                grad_qkv[part].append(dot(a_half, piece, ((0,), (0,))))
        grad_qkv = jnp.concatenate([x for part in grad_qkv for x in part], axis=1)
        da = lax.all_to_all(
            da.astype(BF16), "shard", split_axis=0, concat_axis=1, tiled=True
        ).astype(F32)
        normed = h * r1
        grad_gain_a = jnp.sum(da * normed, axis=0)
        scaled_da = da * gain_a
        dh = dh1 + r1 * (scaled_da - normed * jnp.mean(scaled_da * normed, axis=1, keepdims=True))
        return dh, (grad_qkv, grad_out, grad_router, grad_gain_a, grad_gain_m, grad_gu, grad_down)

    out0, state0 = forward(0, x_in.astype(F32))
    mid = out0.astype(BF16).astype(F32)
    final, state1 = forward(1, mid)
    dh_one, grads1 = backward(1, dy.astype(F32), dy, state1)
    low = dh_one.astype(BF16)
    dh_zero, grads0 = backward(0, low.astype(F32), low, state0)

    def half_sum(grad):
        low_grad = grad.astype(BF16)
        halves = low_grad.reshape((2, -1) + low_grad.shape[1:])
        got = swap_cores(pick(halves, 1 - sec))
        return (pick(halves, sec).astype(F32) + got.astype(F32)).astype(BF16)

    def to_owner(half0, half1):
        keep = jnp.where(sec == 0, half0, half1)
        got = swap_cores(jnp.where(sec == 0, half1, half0))
        first = jnp.where(sec == 0, keep, got)
        second = jnp.where(sec == 0, got, keep)
        return jnp.concatenate([first, second], axis=0).astype(F32)

    attn_halves, exp_halves = [], []
    for grads in (grads0, grads1):
        attn = half_sum(jnp.concatenate([grads[0], grads[1]], axis=1))
        attn_halves.append(lax.psum(attn, "expert"))
        exp_halves.append(tuple(lax.psum(half_sum(g), "shard") for g in (grads[5], grads[6])))
    attn = to_owner(*attn_halves)
    grad_qkv, grad_out = attn[:, : w_qkv.shape[2]], attn[:, w_qkv.shape[2] :]
    grad_gu = to_owner(exp_halves[0][0], exp_halves[1][0])
    grad_down = to_owner(exp_halves[0][1], exp_halves[1][1])

    tiny = []
    for grads in (grads0, grads1):
        hot = jnp.arange(experts)[:, None] == owner * EXP_DEV + jnp.arange(EXP_DEV)[None, :]
        router = sum(
            jnp.where(hot[:, j : j + 1], grads[2][j][None, :], 0.0) for j in range(EXP_DEV)
        )
        tiny.append(jnp.concatenate([router, grads[3][None, :], grads[4][None, :]], axis=0))
    tiny = lax.psum(jnp.stack(tiny), ("section", "expert", "shard"))
    tiny = lax.dynamic_slice_in_dim(pick(tiny, sec), shard_pos * half, half, 1)

    send = jnp.where(sec == 0, final, dh_zero)
    keep = jnp.where(sec == 0, dh_zero, final)
    got = swap_cores(send)
    edge = jnp.where(sec == 0, jnp.stack([keep, got]), jnp.stack([got, keep]))
    return (
        edge[None],
        grad_qkv[None],
        grad_out[None],
        tiny[:experts].T[None],
        tiny[experts][None],
        tiny[experts + 1][None],
        grad_gu[None],
        grad_down[None],
    )


def kernel_shards(
    edge_inputs, seq_lengths, routes, w_qkv, w_out, w_router, gain_attn, gain_moe, w_gate_up, w_down
):
    sec = lax.axis_index("section")
    owner = lax.axis_index("expert")
    shard_pos = lax.axis_index("shard")
    rows, width = edge_inputs.shape[2], edge_inputs.shape[3]
    experts = w_router.shape[2]
    half = width // 2
    attn_cols = w_qkv.shape[2] + w_out.shape[2]

    def pick(array, index):
        return lax.dynamic_index_in_dim(array, index, 0, keepdims=False)

    def swap_shards(value):
        return lax.ppermute(value, "shard", [(0, 1), (1, 0)])

    def by_core(own, other):
        return jnp.where(sec == 0, own, other), jnp.where(sec == 0, other, own)

    small = jnp.concatenate([w_router[0].T, gain_attn, gain_moe], axis=0)
    across = lax.ppermute(small, ("section", "shard"), [(0, 3), (1, 2), (2, 1), (3, 0)])

    def joined(mine, other):
        return jnp.where(
            shard_pos == 0,
            jnp.concatenate([mine, other], axis=1),
            jnp.concatenate([other, mine], axis=1),
        )

    layer_small = by_core(joined(small, swap_shards(small)), joined(swap_cores(small), across))
    x_in, dy = by_core(pick(edge_inputs[0], sec), swap_cores(pick(edge_inputs[0], 1 - sec)))
    layer_routes = by_core(pick(routes[0], sec), swap_cores(pick(routes[0], 1 - sec)))
    allowed = document_mask(pick(seq_lengths, sec)[0], 2 * rows).astype(F32)
    attn_weights = (w_qkv[0], swap_cores(w_qkv[0]), w_out[0], swap_cores(w_out[0]))
    expert_weights = (
        w_gate_up[0], swap_cores(w_gate_up[0]), w_down[0], swap_cores(w_down[0])
    )
    gains, routers, masks = [], [], []
    for layer in range(2):
        gains.append(
            jnp.pad(layer_small[layer][experts:].astype(F32), ((0, 8 - 2), (0, 0)))
        )
        router = layer_small[layer][:experts]
        router = jnp.concatenate([router, router], axis=0)
        routers.append(jnp.pad(router, ((0, LANES - 2 * experts), (0, 0))))
        lane = jnp.arange(LANES, dtype=jnp.int32)[None, :]
        hot = jnp.any(layer_routes[layer][:, :, None] == lane[None] % experts, axis=1)
        masks.append(
            jnp.where(hot & (lane < 2 * experts), 1.0 + (lane >= experts), 0.0).astype(F32)
        )

    def forward(layer, h):
        block, h1, *attn_state = attention_forward(
            layer, h, allowed, gains[layer], routers[layer], masks[layer], attn_weights, 1 + layer
        )
        moe, *expert_state = moe_forward(layer, block, expert_weights, experts, 3 + layer)
        return h1 + moe, (h, h1, moe, attn_state, expert_state)

    def backward(layer, dout, state, later, later_attn):
        h, h1, moe, attn_state, expert_state = state
        outer = jnp.sum(dout.astype(F32) * moe, axis=1, keepdims=True)
        block = with_lanes(dout, split_terms(outer))
        own_router = lax.dynamic_slice_in_dim(
            layer_small[layer].astype(F32), owner * EXP_DEV, EXP_DEV, 0
        )
        own_router = jnp.pad(own_router, ((0, 8 - EXP_DEV), (0, 0)))
        results = moe_backward(
            layer, block, own_router, expert_weights, expert_state, later, experts, 5 + layer
        )
        db, keep_gu, keep_down, send_gu, send_down, grad_router = results[:6]
        dh, columns, grad_attn, *piece = attention_backward(
            layer, experts, grad_router, db, dout, h1, h, gains[layer], *attn_state, attn_weights,
            later_attn + tuple(results[7:8]) if later else (), 7 + layer,
        )
        places = LINE * SIDE
        sub = half // (2 * places)
        grad_attn = grad_attn.reshape(places, 2, sub, attn_cols)
        columns = columns.reshape(2, places, 2, sub, LANES)
        return dh, grad_attn, columns, (keep_gu, keep_down, send_gu, send_down), results[6:8], piece

    out0, state0 = forward(0, x_in)
    final, state1 = forward(1, out0.astype(BF16))
    dh_one, attn1, columns1, experts1, *_ = backward(1, dy, state1, (), ())
    dh_zero, attn0, columns0, experts0, sums1, (shares1, tail1) = backward(
        0, dh_one.astype(BF16), state0, experts1, (attn1, columns1)
    )
    send = jnp.where(sec == 0, final, dh_zero)
    attn, gu_own, down_own, gu_got, down_got, down_one, gu_moved, down_moved, got = reduce_gradients(
        attn0, columns0, shares1, experts0, *sums1, tail1, send, 9
    )
    grad_qkv, grad_out, grad_gu, grad_down = finish_outputs(
        attn,
        (gu_own, gu_got, sums1[0], gu_moved),
        (down_own, down_got, down_one, down_moved),
        w_qkv.shape[2],
        w_out.shape[2],
    )
    tiny = attn[:, attn_cols : attn_cols + experts + 2].astype(F32)
    keep = jnp.where(sec == 0, dh_zero, final)
    edge = jnp.where(sec == 0, jnp.stack([keep, got]), jnp.stack([got, keep]))
    return (
        edge[None],
        grad_qkv[None],
        grad_out[None],
        tiny[:, :experts][None],
        tiny[:, experts][None],
        tiny[:, experts + 1][None],
        grad_gu[None],
        grad_down[None],
    )


def shards(*arrays):
    if lax.axis_size("expert") == LINE * SIDE and lax.axis_size("shard") == 2:
        return kernel_shards(*arrays)
    return plain_shards(*arrays)


def solution(mesh):
    in_specs = (
        P("section", None, ("expert", "shard"), None),
        P(None, "expert", None),
        P("section", None, ("expert", "shard"), None),
        P("section", "shard", None),
        P("section", "shard", None),
        P("section", "shard", None),
        P("section", "shard"),
        P("section", "shard"),
        P("section", "expert", None, None),
        P("section", "expert", None, None),
    )
    out_specs = (
        P("section", None, ("expert", "shard"), None),
        P("section", "shard", None),
        P("section", "shard", None),
        P("section", "shard", None),
        P("section", "shard"),
        P("section", "shard"),
        P("section", "expert", None, None),
        P("section", "expert", None, None),
    )
    return jax.shard_map(shards, mesh=mesh, in_specs=in_specs, out_specs=out_specs, check_vma=False)
```

```python
import functools

import jax
import jax.numpy as jnp
from jax import lax
from jax.experimental import pallas as pl
from jax.experimental.pallas import tpu as pltpu
from jax.sharding import PartitionSpec as P

QUERY_HEADS = 24
KEY_VALUE_HEADS = 8
HEAD_SIZE = 64
FF = 512
TOP = 8
EXP_DEV = 2
EPS = 1e-05
MASKED_SCORE = -1e30
QUERY_WIDTH = QUERY_HEADS * HEAD_SIZE
KV_WIDTH = KEY_VALUE_HEADS * HEAD_SIZE
F32 = jnp.float32
BF16 = jnp.bfloat16
MESH = pl.DeviceIdType.MESH
LINE = 4
SIDE = 2
LANES = 128
HALVES = 2
LATER_CROSS = 5
TILE = 256
VMEM_BYTES = 60 * 2**20
COST = pl.CostEstimate(flops=10**11, bytes_accessed=2**24, transcendentals=0)


def chunk_order(z, t):
    near = z + 1 - 2 * lax.rem(z, 2)
    third = jnp.where(z < 2, 2, 1)
    last = jnp.where(z < 2, 3, 0)
    return jnp.where(t == 0, z, jnp.where(t == 1, near, jnp.where(t == 2, third, last)))


def sum_order(z, i):
    first = jnp.where((z == 0) | (z == 2), 1, 2)
    second = jnp.where(z == 0, 2, jnp.where(z == 1, 3, jnp.where(z == 2, 0, 1)))
    third = jnp.where(z == 0, 3, jnp.where(z == 1, 0, jnp.where(z == 2, 3, 0)))
    return jnp.where(i == 0, first, jnp.where(i == 1, second, third))


class Plane:
    def __init__(self, rows, refs):
        (self.gathered, self.parts, self.from_side, self.from_low, self.from_high, self.sums,
         self.line_send, self.gather_recv, self.side_send, self.side_recv,
         self.sum_send, self.low_recv, self.high_recv) = refs
        self.sub = rows // HALVES
        self.both = SIDE * self.sub
        self.sec, self.owner, self.shard = (lax.axis_index(n) for n in ("section", "expert", "shard"))
        self.z, self.x = lax.div(self.owner, SIDE), lax.rem(self.owner, SIDE)
        self.inner = ((self.z > 0) & (self.z < LINE - 1)).astype(jnp.int32)

    def device(self, z, x):
        return (self.sec, z * SIDE + x, self.shard)

    def other_core(self):
        return (1 - self.sec, self.owner, self.shard)

    def other_shard(self):
        return (self.sec, self.owner, 1 - self.shard)

    def chunk(self, c, h):
        return pl.ds(pl.multiple_of((c * HALVES + h) * self.both, self.both), self.both)

    def block(self, c, h, x):
        return pl.ds(pl.multiple_of((c * HALVES + h) * self.both + x * self.sub, self.sub), self.sub)

    def barrier(self, *others):
        z, x = self.z, self.x
        sem = pltpu.get_barrier_semaphore()

        def greet(device):
            pl.semaphore_signal(sem, inc=1, device_id=device, device_id_type=MESH)

        for other in others:
            greet(other)
        greet(self.device(z, 1 - x))
        pl.when(z > 0)(lambda: greet(self.device(z - 1, x)))
        pl.when(z < LINE - 1)(lambda: greet(self.device(z + 1, x)))
        pl.semaphore_wait(sem, 2 + len(others) + self.inner)

    def place(self, block_ref):
        for h in range(HALVES):
            self.gathered[self.block(self.z, h, self.x)] = block_ref[pl.ds(h * self.sub, self.sub)]

    def gather_copy(self, way, c, h, x, device):
        ref = self.gathered.at[self.block(c, h, x)]
        q = c * HALVES + h
        return pltpu.make_async_remote_copy(
            src_ref=ref, dst_ref=ref, send_sem=self.line_send.at[way, q],
            recv_sem=self.gather_recv.at[q, x], device_id=device, device_id_type=MESH)

    def forward_up(self, c, h):
        return self.gather_copy(0, c, h, self.x, self.device(self.z + 1, self.x))

    def forward_down(self, c, h):
        return self.gather_copy(1, c, h, self.x, self.device(self.z - 1, self.x))

    def forward_side(self, c, h):
        return self.gather_copy(2, c, h, self.x, self.device(self.z, 1 - self.x))

    def start_gather(self):
        z = self.z
        for h in range(HALVES):
            pl.when(z < LINE - 1)(lambda h=h: self.forward_up(z, h).start())
            pl.when(z > 0)(lambda h=h: self.forward_down(z, h).start())
            self.forward_side(z, h).start()

    def relay(self, t, h):
        z = self.z

        @pl.when((t > 0) & (z - t >= 0))
        def _():
            c = z - t
            self.forward_side(c, h).wait_recv()
            pl.when(z < LINE - 1)(lambda: self.forward_up(c, h).start())
            self.forward_side(c, h).start()

        @pl.when((t > 0) & (z + t <= LINE - 1))
        def _():
            c = z + t
            self.forward_side(c, h).wait_recv()
            pl.when(z > 0)(lambda: self.forward_down(c, h).start())
            self.forward_side(c, h).start()

    def wait_side_block(self, c, h):
        self.gather_copy(2, c, h, 1 - self.x, self.device(self.z, 1 - self.x)).wait_recv()

    def side_copy(self, c, h):
        q = c * HALVES + h
        return pltpu.make_async_remote_copy(
            src_ref=self.parts.at[self.block(c, h, 1 - self.x)], dst_ref=self.from_side.at[q],
            send_sem=self.side_send.at[q], recv_sem=self.side_recv.at[q],
            device_id=self.device(self.z, 1 - self.x), device_id_type=MESH)

    def up_copy(self, c, h):
        q = c * HALVES + h
        return pltpu.make_async_remote_copy(
            src_ref=self.sums.at[q], dst_ref=self.from_low.at[q], send_sem=self.sum_send.at[q],
            recv_sem=self.low_recv.at[q],
            device_id=self.device(jnp.minimum(self.z + 1, LINE - 1), self.x), device_id_type=MESH)

    def down_copy(self, c, h):
        q = c * HALVES + h
        return pltpu.make_async_remote_copy(
            src_ref=self.sums.at[q], dst_ref=self.from_high.at[q], send_sem=self.sum_send.at[q],
            recv_sem=self.high_recv.at[q],
            device_id=self.device(jnp.maximum(self.z - 1, 0), self.x), device_id_type=MESH)

    def own_part(self, c, h, side=True):
        part = self.parts[self.block(c, h, self.x)].astype(F32)
        return part + self.from_side[c * HALVES + h].astype(F32) if side else part

    def pass_sum(self, t, h):
        i = t - 3 - self.inner
        pl.when((i >= 0) & (i < LINE - 1))(lambda: self.pass_chunk(sum_order(self.z, i), h))

    def pass_chunk(self, c, h, side=True, send=True):
        z = self.z
        q = c * HALVES + h
        if side:
            self.side_copy(c, h).wait_recv()

        @pl.when(c > z)
        def _():
            @pl.when(z > 0)
            def _():
                self.up_copy(c, h).wait_recv()
                self.sums[q] = (self.own_part(c, h, side) + self.from_low[q].astype(F32)).astype(BF16)

            @pl.when(z == 0)
            def _():
                self.sums[q] = self.own_part(c, h, side).astype(BF16)

        @pl.when(c < z)
        def _():
            @pl.when(z < LINE - 1)
            def _():
                self.down_copy(c, h).wait_recv()
                self.sums[q] = (self.own_part(c, h, side) + self.from_high[q].astype(F32)).astype(BF16)

            @pl.when(z == LINE - 1)
            def _():
                self.sums[q] = self.own_part(c, h, side).astype(BF16)

        if send:
            self.send_sum(c, h)

    def send_sum(self, c, h):
        pl.when(c > self.z)(lambda: self.up_copy(c, h).start())
        pl.when(c < self.z)(lambda: self.down_copy(c, h).start())

    def wait_sent_sum(self, c, h):
        pl.when(c > self.z)(lambda: self.up_copy(c, h).wait_send())
        pl.when(c < self.z)(lambda: self.down_copy(c, h).wait_send())

    def finish_sum(self, h, out_ref):
        z = self.z
        q = z * HALVES + h
        rows = pl.ds(pl.multiple_of(h * self.sub, self.sub), self.sub)
        self.side_copy(z, h).wait_recv()
        out_ref[rows] = self.own_part(z, h)

        @pl.when(z > 0)
        def _():
            self.up_copy(z, h).wait_recv()
            out_ref[rows] += self.from_low[q].astype(F32)

        @pl.when(z < LINE - 1)
        def _():
            self.down_copy(z, h).wait_recv()
            out_ref[rows] += self.from_high[q].astype(F32)

    def finish_piece(self, h, out_ref, side=True):
        z = self.z
        q = z * HALVES + h
        if side:
            self.side_copy(z, h).wait_recv()

        @pl.when(z == 0)
        def _():
            self.down_copy(z, h).wait_recv()
            out_ref[h] = (self.own_part(z, h, side) + self.from_high[q].astype(F32)).astype(BF16)

        @pl.when(z == LINE - 1)
        def _():
            self.up_copy(z, h).wait_recv()
            out_ref[h] = (self.own_part(z, h, side) + self.from_low[q].astype(F32)).astype(BF16)

        @pl.when((z > 0) & (z < LINE - 1))
        def _():
            self.up_copy(z, h).wait_recv()
            self.down_copy(z, h).wait_recv()
            total = self.own_part(z, h, side) + self.from_low[q].astype(F32)
            out_ref[h] = (total + self.from_high[q].astype(F32)).astype(BF16)

    def drain_gather(self):
        z = self.z

        def one(q, carry):
            c, h = lax.div(q, HALVES), lax.rem(q, HALVES)
            pl.when((z < LINE - 1) & (c <= z))(lambda: self.forward_up(c, h).wait_send())
            pl.when((z > 0) & (c >= z))(lambda: self.forward_down(c, h).wait_send())
            self.forward_side(c, h).wait_send()
            return carry

        lax.fori_loop(0, LINE * HALVES, one, 0)

    def drain(self):
        z = self.z

        def one(q, carry):
            c, h = lax.div(q, HALVES), lax.rem(q, HALVES)
            pl.when((z < LINE - 1) & (c <= z))(lambda: self.forward_up(c, h).wait_send())
            pl.when((z > 0) & (c >= z))(lambda: self.forward_down(c, h).wait_send())
            self.forward_side(c, h).wait_send()
            self.side_copy(c, h).wait_send()
            pl.when(c > z)(lambda: self.up_copy(c, h).wait_send())
            pl.when(c < z)(lambda: self.down_copy(c, h).wait_send())
            return carry

        lax.fori_loop(0, LINE * HALVES, one, 0)


def plane_scratch(rows, width, wide):
    count = LINE * HALVES
    block = pltpu.VMEM((count, rows // HALVES, width), BF16)
    return [
        pltpu.VMEM((LINE * SIDE * rows, wide), BF16),
        pltpu.VMEM((LINE * SIDE * rows, width), BF16),
        block, block, block, block,
        pltpu.SemaphoreType.DMA((3, count)),
        pltpu.SemaphoreType.DMA((count, SIDE)),
        pltpu.SemaphoreType.DMA((count,)),
        pltpu.SemaphoreType.DMA((count,)),
        pltpu.SemaphoreType.DMA((count,)),
        pltpu.SemaphoreType.DMA((count,)),
        pltpu.SemaphoreType.DMA((count,)),
    ]


def lane_tile(at, size=TILE):
    return pl.ds(pl.multiple_of(at * size, size), size)


def nn(a, b):
    return jnp.dot(a, b, preferred_element_type=F32)


def nt(a, b):
    return lax.dot_general(a, b, (((1,), (1,)), ((), ())), preferred_element_type=F32)


def tn(a, b):
    return lax.dot_general(a, b, (((0,), (0,)), ((), ())), preferred_element_type=F32)


def pick_lane(block, wanted):
    lane = lax.broadcasted_iota(jnp.int32, block.shape, 1)
    hot = lane == wanted[0]
    for other in wanted[1:]:
        hot = hot | (lane == other)
    return jnp.sum(jnp.where(hot, block, 0.0), axis=1, keepdims=True)


def own_gates(block, owner, experts):
    block = block.astype(F32)
    return [
        pick_lane(block, (owner * EXP_DEV + j, experts + owner * EXP_DEV + j)) for j in range(EXP_DEV)
    ]


def load_layer(layer, sec, own, other, dst, sem):
    copies = [pltpu.make_async_copy(own, dst, sem), pltpu.make_async_copy(other, dst, sem)]
    pl.when(sec == layer)(lambda: copies[0].start())
    pl.when(sec != layer)(lambda: copies[1].start())
    return copies[0]


def load_experts(layer, sec, gu, gu_other, down, down_other, gu_v, down_v, sems):
    loads = [load_layer(layer, sec, gu, gu_other, gu_v, sems.at[0])]
    for j in range(EXP_DEV):
        loads.append(load_layer(
            layer, sec, down.at[j], down_other.at[j], down_v.at[pl.ds(j * FF, FF)], sems.at[1 + j]))
    return loads


def moe_forward_kernel(layer, experts, rows, width, block_ref, h1_ref, gu_hbm, gu_other, down_hbm, down_other,
                       moe_ref, out_ref, rows_hbm, kept_hbm, scaled_hbm,
                       gu_v, down_v, kept, scaled, load_sem, store_sem, *plane_refs):
    plane = Plane(rows, plane_refs)
    gathered, parts = plane.gathered, plane.parts
    loads = load_experts(layer, plane.sec, gu_hbm, gu_other, down_hbm, down_other, gu_v, down_v, load_sem)
    plane.place(block_ref)
    plane.barrier()
    plane.start_gather()
    for load in loads:
        load.wait()

    def stores(c, h):
        q, at = c * HALVES + h, plane.chunk(c, h)
        return [
            pltpu.make_async_copy(gathered.at[at], rows_hbm.at[at], store_sem.at[0, q]),
            pltpu.make_async_copy(kept.at[at], kept_hbm.at[at], store_sem.at[1, q]),
            pltpu.make_async_copy(scaled.at[at], scaled_hbm.at[at], store_sem.at[2, q]),
        ]

    def step(k, carry):
        t, h = lax.div(k, HALVES), lax.rem(k, HALVES)
        plane.relay(t, h)
        plane.pass_sum(t, h)
        pl.when(t > 0)(lambda: work(chunk_order(plane.z, t - 1), h))
        return carry

    def work(c, h):
        at = plane.chunk(c, h)
        plane.wait_side_block(c, h)
        gates = own_gates(gathered[at, pl.ds(width, LANES)], plane.owner, experts)
        for j in range(EXP_DEV):
            for f in range(FF // TILE):
                data = gathered[at, pl.ds(0, width)]
                low, high = j * 2 * FF + f * TILE, j * 2 * FF + FF + f * TILE
                g = nn(data, gu_v[j, :, pl.ds(f * TILE, TILE)])
                u = nn(data, gu_v[j, :, pl.ds(FF + f * TILE, TILE)])
                z = g * jax.nn.sigmoid(g) * u * gates[j]
                scaled[at, pl.ds(j * FF + f * TILE, TILE)] = z.astype(BF16)
                kept[at, pl.ds(low, TILE)] = g.astype(BF16)
                kept[at, pl.ds(high, TILE)] = u.astype(BF16)
        for n in range(width // TILE):
            parts[at, pl.ds(n * TILE, TILE)] = nn(
                scaled[at, :], down_v[:, pl.ds(n * TILE, TILE)]).astype(BF16)
        plane.side_copy(c, h).start()
        for store in stores(c, h):
            store.start()

    lax.fori_loop(0, (LINE + 1) * HALVES, step, 0)

    def tail(k, carry):
        plane.pass_sum(lax.div(k, HALVES), lax.rem(k, HALVES))
        return carry

    lax.fori_loop((LINE + 1) * HALVES, (LINE + 3) * HALVES, tail, 0)

    def finish(h, carry):
        plane.finish_sum(h, moe_ref)
        return carry

    lax.fori_loop(0, HALVES, finish, 0)
    out_ref[...] = (h1_ref[...] + moe_ref[...]).astype(out_ref.dtype)
    plane.drain()

    def stored(q, carry):
        for store in stores(lax.div(q, HALVES), lax.rem(q, HALVES)):
            store.wait()
        return carry

    lax.fori_loop(0, LINE * HALVES, stored, 0)


def moe_forward(layer, block, h1, weights, experts, out_type, collective_id):
    rows, wide = block.shape
    width = wide - LANES
    total = LINE * SIDE * rows
    any_spec = pl.BlockSpec(memory_space=pl.ANY)
    vmem = pl.BlockSpec(memory_space=pltpu.VMEM)
    return pl.pallas_call(
        functools.partial(moe_forward_kernel, layer, experts, rows, width),
        name="moe_forward",
        out_shape=(
            jax.ShapeDtypeStruct((rows, width), F32),
            jax.ShapeDtypeStruct((rows, width), out_type),
            jax.ShapeDtypeStruct((total, wide), BF16),
            jax.ShapeDtypeStruct((total, EXP_DEV * 2 * FF), BF16),
            jax.ShapeDtypeStruct((total, EXP_DEV * FF), BF16),
        ),
        in_specs=[vmem] * 2 + [any_spec] * 4,
        out_specs=(vmem, vmem, any_spec, any_spec, any_spec),
        scratch_shapes=[
            pltpu.VMEM((EXP_DEV, width, 2 * FF), BF16),
            pltpu.VMEM((EXP_DEV * FF, width), BF16),
            pltpu.VMEM((total, EXP_DEV * 2 * FF), BF16),
            pltpu.VMEM((total, EXP_DEV * FF), BF16),
            pltpu.SemaphoreType.DMA((1 + EXP_DEV,)),
            pltpu.SemaphoreType.DMA((3, LINE * HALVES)),
        ] + plane_scratch(rows, width, wide),
        cost_estimate=COST,
        compiler_params=pltpu.CompilerParams(
            collective_id=collective_id, has_side_effects=True, vmem_limit_bytes=VMEM_BYTES),
    )(block, h1, *weights)


def moe_backward_kernel(layer, experts, rows, width, beside, dout_ref, moe_ref, small_ref, gu_hbm, gu_other, down_hbm,
                        down_other, rows_hbm, kept_hbm, scaled_hbm, *refs):
    (later, refs) = (refs[:4], refs[4:]) if beside else ((), refs)
    (db_ref, keep_gu_hbm, keep_down_hbm, send_gu_hbm, send_down_hbm, grad_router_ref), refs = refs[:6], refs[6:]
    (later_out, refs) = (refs[:4], refs[4:]) if beside else ((), refs)
    (gu_v, down_v, fwd_rows, kept, scaled, dgu, send_gu, grad_gu, send_down, grad_down, router,
     load_sem, store_sem), refs = refs[:13], refs[13:]
    (later_v, refs) = (refs[:8], refs[8:]) if beside else ((), refs)
    plane_refs = refs
    plane = Plane(rows, plane_refs)
    gathered, parts = plane.gathered, plane.parts
    if beside:
        other_layer = LaterExperts(plane, *later, *later_out, *later_v)
        other_layer.start_loads()
    loads = load_experts(layer, plane.sec, gu_hbm, gu_other, down_hbm, down_other, gu_v, down_v, load_sem)
    loads.append(pltpu.make_async_copy(rows_hbm, fwd_rows, load_sem.at[3]))
    loads.append(pltpu.make_async_copy(kept_hbm, kept, load_sem.at[4]))
    loads.append(pltpu.make_async_copy(scaled_hbm, scaled, load_sem.at[5]))
    for load in loads[3:]:
        load.start()
    dout = dout_ref[...]
    outer = jnp.sum(dout.astype(F32) * moe_ref[...], axis=1, keepdims=True)
    top = outer.astype(BF16).astype(F32)
    lane = lax.broadcasted_iota(jnp.int32, (rows, LANES), 1)
    terms = (jnp.where(lane == 0, top, 0.0) + jnp.where(lane == 1, outer - top, 0.0)).astype(BF16)
    for h in range(HALVES):
        at, part = plane.block(plane.z, h, plane.x), slice(h * plane.sub, (h + 1) * plane.sub)
        gathered[at, pl.ds(0, width)] = dout[part]
        gathered[at, pl.ds(width, LANES)] = terms[part]
    router[...] = small_ref[pl.ds(0, experts)].astype(F32)
    plane.barrier(*([plane.other_core(), plane.other_shard()] if beside else []))
    plane.start_gather()
    if beside:
        other_layer.start_copies()
        other_layer.send()
    for load in loads:
        load.wait()
    total = plane.both
    up_at = EXP_DEV * 2 * FF

    def step(k, carry):
        t, h = lax.div(k, HALVES), lax.rem(k, HALVES)
        plane.relay(t, h)
        plane.pass_sum(t, h)
        pl.when(t > 0)(lambda: work(chunk_order(plane.z, t - 1), h))
        return carry

    def work(c, h):
        at = plane.chunk(c, h)
        plane.wait_side_block(c, h)
        gates = own_gates(fwd_rows[at, pl.ds(width, LANES)], plane.owner, experts)
        outer = jnp.sum(gathered[at, pl.ds(width, LANES)].astype(F32), axis=1, keepdims=True)
        dcs = []
        for j in range(EXP_DEV):
            dgate = jnp.zeros((total, 1), F32)
            for f in range(FF // TILE):
                low, high = pl.ds(j * 2 * FF + f * TILE, TILE), pl.ds(j * 2 * FF + FF + f * TILE, TILE)
                dz = nt(gathered[at, pl.ds(0, width)], down_v[pl.ds(j * FF + f * TILE, TILE), :])
                g = kept[at, low].astype(F32)
                u = kept[at, high].astype(F32)
                sig = jax.nn.sigmoid(g)
                silu = g * sig
                dgate = dgate + jnp.sum(dz * silu * u, axis=1, keepdims=True)
                dz = dz * gates[j]
                dgu[at, low] = (dz * u * sig * (1.0 + g * (1.0 - sig))).astype(BF16)
                dgu[at, high] = (dz * silu).astype(BF16)
            dcs.append(gates[j] * (dgate - outer))
        lane = lax.broadcasted_iota(jnp.int32, (total, LANES), 1)
        extra = jnp.zeros((total, LANES), F32)
        for j in range(EXP_DEV):
            top = dcs[j].astype(BF16).astype(F32)
            column = plane.owner * EXP_DEV + j
            extra = extra + jnp.where(lane == column, top, 0.0)
            extra = extra + jnp.where(lane == LANES // 2 + column, dcs[j] - top, 0.0)
        dgu[at, pl.ds(up_at, LANES)] = extra.astype(BF16)
        for n in range(width // TILE):
            cols = pl.ds(n * TILE, TILE)
            acc = nt(dgu[at, pl.ds(0, 2 * FF)], gu_v[0, cols, :])
            for j in range(1, EXP_DEV):
                acc = acc + nt(dgu[at, pl.ds(j * 2 * FF, 2 * FF)], gu_v[j, cols, :])
            for j in range(EXP_DEV):
                acc = acc + dcs[j] * router[pl.ds(plane.owner * EXP_DEV + j, 1), cols]
            parts[at, cols] = acc.astype(BF16)
        plane.side_copy(c, h).start()

    lax.fori_loop(0, (LINE + 1) * HALVES, step, 0)

    core = plane.sec
    gu_steps, down_steps = width // TILE, FF // TILE

    def stores_gu(n):
        at = lane_tile(n)
        return [pltpu.make_async_copy(send_gu.at[at], send_gu_hbm.at[at], store_sem.at[0, n]),
                pltpu.make_async_copy(grad_gu.at[at], keep_gu_hbm.at[at], store_sem.at[1, n])]

    def stores_down(n):
        at = lane_tile(n)
        return [pltpu.make_async_copy(send_down.at[at], send_down_hbm.at[at], store_sem.at[2, n]),
                pltpu.make_async_copy(grad_down.at[at], keep_down_hbm.at[at], store_sem.at[3, n])]

    def expert_cols(j, size):
        return pl.ds(pl.multiple_of(j * size, size), size)

    def grad_gu_rows(n):
        rows_t = fwd_rows[:, lane_tile(n)]
        send_gu[lane_tile(n), :] = tn(rows_t, dgu[:, expert_cols(1 - core, 2 * FF)]).astype(BF16)
        grad_gu[lane_tile(n), :] = tn(rows_t, dgu[:, expert_cols(core, 2 * FF)]).astype(BF16)
        grad_router_ref[lane_tile(n), :] = tn(rows_t, dgu[:, pl.ds(up_at, LANES)])
        for store in stores_gu(n):
            store.start()

    def grad_down_rows(n):
        def cols(j):
            return pl.ds(pl.multiple_of(j * FF + n * TILE, TILE), TILE)

        data = gathered[:, pl.ds(0, width)]
        send_down[lane_tile(n), :] = tn(scaled[:, cols(1 - core)], data).astype(BF16)
        grad_down[lane_tile(n), :] = tn(scaled[:, cols(core)], data).astype(BF16)
        for store in stores_down(n):
            store.start()

    slots = 2 * HALVES

    def tail(k, carry):
        pl.loop(lax.div(k * gu_steps, slots), lax.div((k + 1) * gu_steps, slots))(grad_gu_rows)
        plane.pass_sum(LINE + 1 + lax.div(k, HALVES), lax.rem(k, HALVES))
        return carry

    lax.fori_loop(0, slots, tail, 0)
    pl.loop(0, down_steps)(grad_down_rows)

    def finish(h, carry):
        plane.finish_sum(h, db_ref)
        return carry

    lax.fori_loop(0, HALVES, finish, 0)
    if beside:
        other_layer.finish()
    plane.drain()
    for n in range(gu_steps):
        for store in stores_gu(n):
            store.wait()
    for n in range(down_steps):
        for store in stores_down(n):
            store.wait()


class LaterExperts:
    def __init__(self, plane, keep_gu, keep_down, send_gu, send_down, sum_gu_hbm, sum_down_hbm, land_gu, land_down,
                 gu_a, gu_b, down_a, down_b, load_sem, core_sem, send_sem, recv_sem):
        self.parts = []
        for keep, sent, out, land, a, b, count in (
            (keep_gu, send_gu, sum_gu_hbm, land_gu, gu_a, gu_b, 4),
            (keep_down, send_down, sum_down_hbm, land_down, down_a, down_b, 2),
        ):
            size = a.shape[0] // count
            for n in range(count):
                at, k = pl.ds(n * size, size), len(self.parts)
                shard_copy = land_copy = None
                if k < LATER_CROSS:
                    shard_copy = pltpu.make_async_remote_copy(
                        src_ref=a.at[at], dst_ref=land.at[at], send_sem=send_sem.at[k], recv_sem=recv_sem.at[k],
                        device_id=plane.other_shard(), device_id_type=MESH)
                    land_copy = pltpu.make_async_copy(land.at[at], b.at[at], load_sem.at[1, k])
                self.parts.append((
                    a.at[at], b.at[at],
                    pltpu.make_async_copy(keep.at[at], a.at[at], load_sem.at[0, k]),
                    pltpu.make_async_remote_copy(
                        src_ref=sent.at[at], dst_ref=b.at[at], send_sem=core_sem.at[0, k],
                        recv_sem=core_sem.at[1, k], device_id=plane.other_core(), device_id_type=MESH),
                    shard_copy, land_copy,
                    pltpu.make_async_copy(a.at[at], out.at[at], load_sem.at[2, k]),
                ))

    def start_loads(self):
        for _, _, load, *_ in self.parts:
            load.start()

    def start_copies(self):
        for _, _, _, core_copy, *_ in self.parts:
            core_copy.start()

    def send(self):
        for a, b, load, core_copy, shard_copy, _, store in self.parts:
            load.wait()
            core_copy.wait()
            a[...] = (a[...].astype(F32) + b[...].astype(F32)).astype(BF16)
            if shard_copy is not None:
                shard_copy.start()
            else:
                store.start()

    def finish(self):
        for _, _, _, _, shard_copy, land_copy, _ in self.parts:
            if shard_copy is not None:
                shard_copy.wait()
                land_copy.start()
        for a, b, _, _, shard_copy, land_copy, store in self.parts:
            if shard_copy is not None:
                land_copy.wait()
                a[...] = (a[...].astype(F32) + b[...].astype(F32)).astype(BF16)
                store.start()
        for *_, store in self.parts:
            store.wait()


def moe_backward(layer, dout, moe, small, weights, kept, later, experts, collective_id):
    rows, width = dout.shape
    wide = width + LANES
    total = LINE * SIDE * rows
    any_spec = pl.BlockSpec(memory_space=pl.ANY)
    vmem = pl.BlockSpec(memory_space=pltpu.VMEM)
    expert_gu, expert_down = pltpu.VMEM((width, 2 * FF), BF16), pltpu.VMEM((FF, width), BF16)
    gu_shape = jax.ShapeDtypeStruct((width, 2 * FF), BF16)
    down_shape = jax.ShapeDtypeStruct((FF, width), BF16)
    later_out, later_scratch = (), []
    if later:
        later_out = (gu_shape, down_shape) * 2
        later_scratch = [
            expert_gu, expert_gu, expert_down, expert_down,
            pltpu.SemaphoreType.DMA((3, 6)), pltpu.SemaphoreType.DMA((2, 6)),
            pltpu.SemaphoreType.DMA((LATER_CROSS,)), pltpu.SemaphoreType.DMA((LATER_CROSS,)),
        ]
    return pl.pallas_call(
        functools.partial(moe_backward_kernel, layer, experts, rows, width, bool(later)),
        name="moe_backward",
        out_shape=(
            jax.ShapeDtypeStruct((rows, width), F32),
            gu_shape, down_shape, gu_shape, down_shape,
            jax.ShapeDtypeStruct((width, LANES), F32),
        ) + later_out,
        in_specs=[vmem] * 3 + [any_spec] * (7 + len(later)),
        out_specs=(vmem,) + (any_spec,) * 4 + (vmem,) + (any_spec,) * len(later_out),
        scratch_shapes=[
            pltpu.VMEM((EXP_DEV, width, 2 * FF), BF16),
            pltpu.VMEM((EXP_DEV * FF, width), BF16),
            pltpu.VMEM((total, wide), BF16),
            pltpu.VMEM((total, EXP_DEV * 2 * FF), BF16),
            pltpu.VMEM((total, EXP_DEV * FF), BF16),
            pltpu.VMEM((total, EXP_DEV * 2 * FF + LANES), BF16),
            expert_gu, expert_gu, expert_down, expert_down,
            pltpu.VMEM((experts, width), F32),
            pltpu.SemaphoreType.DMA((6,)),
            pltpu.SemaphoreType.DMA((4, width // TILE)),
        ] + later_scratch + plane_scratch(rows, width, wide),
        cost_estimate=COST,
        compiler_params=pltpu.CompilerParams(
            collective_id=collective_id, has_side_effects=True, vmem_limit_bytes=VMEM_BYTES),
    )(dout, moe, small, *weights, *kept, *later)


def split_terms(values):
    high = values.astype(BF16)
    return high, (values - high.astype(F32)).astype(BF16)


def with_lanes(block, columns):
    extra = jnp.concatenate(columns, axis=1)
    extra = jnp.pad(extra, ((0, 0), (0, LANES - extra.shape[1])))
    return jnp.concatenate([block, extra], axis=1)


def far_order(z, i):
    low = jnp.where(i == 0, 3, jnp.where(i == 1, jnp.where(z == 0, 2, 0), jnp.where(z == 0, 1, 2)))
    high = jnp.where(i == 0, 0, jnp.where(i == 1, jnp.where(z == 3, 1, 3), jnp.where(z == 3, 2, 1)))
    return jnp.where(z < 2, low, high)


def remote_copy(src, dst, send_sem, recv_sem, device):
    return pltpu.make_async_remote_copy(
        src_ref=src, dst_ref=dst, send_sem=send_sem, recv_sem=recv_sem, device_id=device, device_id_type=MESH)


class GradientSum:
    def __init__(self, plane, h, cols, grad, small, core_got, small_own, small_got, load_sem, core_sem, small_sem):
        self.plane, self.h, self.cols = plane, h, cols
        self.core_got, self.small_own, self.small_got = core_got, small_own, small_got
        core, shard = plane.sec, plane.shard
        places = [(c, side) for c in range(LINE) for side in range(SIDE)]
        self.loads = [
            pltpu.make_async_copy(
                grad.at[n, core], plane.parts.at[plane.block(c, h, side), pl.ds(0, cols)], load_sem.at[n])
            for n, (c, side) in enumerate(places)
        ]
        self.loads.append(pltpu.make_async_copy(small.at[shard, :, core], small_own, load_sem.at[len(places)]))
        self.copies = [
            remote_copy(grad.at[:, 1 - core], core_got, core_sem.at[0], core_sem.at[1], plane.other_core())
        ]
        for n, (there, half, device) in enumerate((
            (shard, 1 - core, plane.other_core()),
            (1 - shard, core, plane.other_shard()),
            (1 - shard, 1 - core, self.diagonal(plane)),
        )):
            self.copies.append(remote_copy(
                small.at[there, :, half], small_got.at[n], small_sem.at[0, n], small_sem.at[1, n], device))

    @staticmethod
    def diagonal(plane):
        return (1 - plane.sec, plane.owner, 1 - plane.shard)

    def start_loads(self):
        for load in self.loads:
            load.start()

    def start_copies(self):
        for copy in self.copies:
            copy.start()

    def wait_terms(self):
        for load in self.loads:
            load.wait()
        for copy in self.copies:
            copy.wait_recv()

    def prepare(self, first, last):
        plane, h, cols = self.plane, self.h, self.cols

        def one(k, carry):
            c = jnp.where(k < 2 * (LINE - 1), far_order(plane.z, lax.div(k, 2)), plane.z)
            side = jnp.where(lax.rem(k, 2) == 0, 1 - plane.x, plane.x)
            n = c * SIDE + side
            at = plane.block(c, h, side)
            plane.parts[at, pl.ds(0, cols)] = (
                plane.parts[at, pl.ds(0, cols)].astype(F32) + self.core_got[n].astype(F32)).astype(BF16)
            total = self.small_own[n].astype(F32)
            for other in range(3):
                total = total + self.small_got[other, n].astype(F32)
            plane.parts[at, pl.ds(cols, LANES)] = total.astype(BF16)
            pl.when(side != plane.x)(lambda: plane.side_copy(c, h).start())
            return carry

        lax.fori_loop(first, last, one, 0)

    def pass_on(self, i):
        self.plane.pass_chunk(far_order(self.plane.z, i), self.h)

    def hand_over(self, out_ref):
        plane, h = self.plane, self.h
        second, third = far_order(plane.z, 1), far_order(plane.z, 2)
        plane.pass_chunk(second, h, send=False)
        out_ref[0] = plane.sums[second * HALVES + h]
        for n, c in ((1, third), (2, plane.z)):
            plane.side_copy(c, h).wait_recv()
            out_ref[n] = plane.own_part(c, h).astype(BF16)

    def drain(self, chunks=LINE - 1):
        plane, h = self.plane, self.h
        for copy in self.copies:
            copy.wait_send()

        def one(c, carry):
            plane.side_copy(c, h).wait_send()
            return carry

        lax.fori_loop(0, LINE, one, 0)
        for i in range(chunks):
            plane.wait_sent_sum(far_order(plane.z, i), h)


def sum_scratch(places, sub, cols):
    plane = plane_scratch(HALVES * sub, cols + LANES, cols + LANES)
    own = [
        pltpu.VMEM((places, sub, cols), BF16),
        pltpu.VMEM((places, sub, LANES), BF16),
        pltpu.VMEM((3, places, sub, LANES), BF16),
        pltpu.SemaphoreType.DMA((places + 1,)),
        pltpu.SemaphoreType.DMA((2,)),
        pltpu.SemaphoreType.DMA((2, 3)),
    ]
    return own, plane


def reduce_kernel(sub, cols, g0, t0, shares1, gu_hbm, down_hbm, sent_gu_hbm, sent_down_hbm, gu1_hbm, down1_hbm, tail1_hbm, edge,
                  sum_hbm, own_gu_hbm, own_down_hbm, got_gu_hbm, got_down_hbm, own_down1_hbm, got_gu1_hbm,
                  got_down1_hbm, got_edge,
                  core_got, small_own, small_got, load_sem, core_sem, small_sem,
                  result, own_gu, core_gu, other_gu, own_down, core_down, other_down,
                  share_sem, expert_load_sem, expert_core_sem, edge_sem, move_sem, expert_sem,
                  core_expert_sem, store_sem, *plane_refs):
    plane = Plane(HALVES * sub, plane_refs)
    gathered = plane.gathered
    core, z, x = plane.sec, plane.z, plane.x
    remote = remote_copy
    sums = GradientSum(plane, 1, cols, g0, t0, core_got, small_own, small_got, load_sem, core_sem, small_sem)
    pieces, expert_loads = [], []
    for layer, hbm, sent, own, there, other, own_hbm, got_hbm, count, first in (
        (0, gu_hbm, sent_gu_hbm, own_gu, core_gu, other_gu, own_gu_hbm, got_gu_hbm, 4, 0),
        (0, down_hbm, sent_down_hbm, own_down, core_down, other_down, own_down_hbm, got_down_hbm, 2, 0),
    ):
        size = own.shape[0] // count
        for n in range(first, count):
            at, k = pl.ds(n * size, size), len(pieces)
            pieces.append((layer, own, there, other, own_hbm, got_hbm, at))
            expert_loads.append((
                pltpu.make_async_copy(hbm.at[at], own.at[at], expert_load_sem.at[k]),
                None if sent is None else remote(
                    sent.at[at], there.at[at], expert_core_sem.at[0, k], expert_core_sem.at[1, k],
                    plane.other_core()),
            ))
    count = LINE * SIDE * HALVES
    split = tail1_hbm.shape[0]
    low, high = pl.ds(0, split), pl.ds(split, split)
    ready_copies = [
        pltpu.make_async_copy(down1_hbm.at[low], own_down1_hbm.at[low], store_sem.at[count + 6]),
        pltpu.make_async_copy(tail1_hbm, own_down1_hbm.at[high], store_sem.at[count + 7]),
    ]
    second, third = far_order(z, 1), far_order(z, 2)
    load_shares = [
        pltpu.make_async_copy(shares1.at[0], plane.sums.at[second * HALVES], share_sem.at[0]),
        pltpu.make_async_copy(shares1.at[1], plane.parts.at[plane.block(third, 0, x)], share_sem.at[1]),
        pltpu.make_async_copy(shares1.at[2], plane.parts.at[plane.block(z, 0, x)], share_sem.at[2]),
    ]
    for load in load_shares:
        load.start()
    expert_loads[0][0].start()
    sums.start_loads()
    for load, _ in expert_loads[1:]:
        load.start()
    plane.barrier(plane.other_core(), plane.other_shard(), sums.diagonal(plane))
    expert_loads[0][1].start()
    sums.start_copies()
    for _, copy in expert_loads[1:]:
        copy.start()

    def move(h):
        return remote(
            result.at[h], gathered.at[plane.block(z, core, x)], move_sem.at[0], move_sem.at[1], plane.other_core())

    def send_block(h):
        pl.when(z < LINE - 1)(lambda: plane.forward_up(z, h).start())
        pl.when(z > 0)(lambda: plane.forward_down(z, h).start())
        plane.forward_side(z, h).start()

    def begin_gather(h):
        own_layer = core == 1 - h
        pl.when(jnp.logical_not(own_layer))(lambda: move(h).start())

        @pl.when(own_layer)
        def _():
            gathered[plane.block(z, core, x)] = result[h]
            send_block(core)
            arrived = remote(
                result.at[h], gathered.at[plane.block(z, 1 - core, x)], move_sem.at[0], move_sem.at[1],
                plane.other_core())
            arrived.wait_recv()
            send_block(1 - core)

    exchange = []

    def send_piece():
        n = len(exchange)
        layer, own, there, other, own_hbm, got_hbm, at = pieces[n]
        for load in expert_loads[n]:
            if load is not None:
                load.wait()
        if there is not None:
            own[at] = (own[at].astype(F32) + there[at].astype(F32)).astype(BF16)
        exchange.append(
            remote(own.at[at], other.at[at], expert_sem.at[0, n], expert_sem.at[1, n], plane.other_shard()))
        exchange[-1].start()

    send_piece()
    for load in load_shares:
        load.wait()
    plane.send_sum(second, 0)
    edges = remote(edge, got_edge, edge_sem.at[0], edge_sem.at[1], plane.other_core())
    edges.start()
    later_copies = [
        remote(gu1_hbm, got_gu1_hbm, edge_sem.at[2], edge_sem.at[3], plane.other_core()),
        remote(down1_hbm.at[low], got_down1_hbm.at[low], edge_sem.at[4], edge_sem.at[5], plane.other_core()),
        remote(tail1_hbm, got_down1_hbm.at[high], edge_sem.at[6], edge_sem.at[7], plane.other_core()),
    ]
    for copy in later_copies:
        pl.when(core == 0)(lambda copy=copy: copy.start())
    for copy in ready_copies:
        copy.start()

    def out_copy(c, h, side):
        at = pl.multiple_of(((c * SIDE + side) * HALVES + h) * sub, sub)
        return pltpu.make_async_copy(
            gathered.at[plane.block(c, h, side)], sum_hbm.at[pl.ds(at, sub)],
            store_sem.at[(c * SIDE + side) * HALVES + h])

    def gather(t):
        for turn in range(HALVES):
            h = core if turn == 0 else 1 - core
            plane.relay(t, h)
            c = chunk_order(z, t - 1)
            plane.wait_side_block(c, h)
            out_copy(c, h, x).start()
            out_copy(c, h, 1 - x).start()

    def to_core(n):
        layer, own, there, other, own_hbm, got_hbm, at = pieces[n]
        return remote(
            own.at[at], got_hbm.at[at], core_expert_sem.at[0, n], core_expert_sem.at[1, n], plane.other_core())

    def keep(n):
        layer, own, there, other, own_hbm, got_hbm, at = pieces[n]
        return pltpu.make_async_copy(own.at[at], own_hbm.at[at], store_sem.at[count + n])

    def expert_piece(n):
        layer, own, there, other, own_hbm, got_hbm, at = pieces[n]
        exchange[n].wait()
        own[at] = (own[at].astype(F32) + other[at].astype(F32)).astype(BF16)
        pl.when(core != layer)(lambda: to_core(n).start())
        keep(n).start()

    sums.wait_terms()
    sums.prepare(0, LINE)
    plane.pass_chunk(third, 0, side=False)
    send_piece()
    sums.prepare(LINE, LINE * SIDE)
    sums.pass_on(0)
    send_piece()
    plane.finish_piece(0, result, side=False)
    begin_gather(0)
    for i in range(1, LINE - 1):
        sums.pass_on(i)
        send_piece()
        pl.when(core == 1)(lambda i=i: gather(i))
    while len(exchange) < len(pieces):
        send_piece()
    plane.finish_piece(1, result)
    begin_gather(1)
    for n in range(2):
        expert_piece(n)

    @pl.when(core == 1)
    def _():
        gather(LINE - 1)
        gather(LINE)

    @pl.when(core == 0)
    def _():
        def one(t, carry):
            gather(t)
            return carry

        lax.fori_loop(1, LINE + 1, one, 0)

    for n in range(2, len(pieces)):
        expert_piece(n)
    sums.drain()
    plane.wait_sent_sum(second, 0)
    plane.wait_sent_sum(third, 0)
    plane.drain_gather()
    move(0).wait_send()

    def stored(k, carry):
        out_copy(lax.div(k, SIDE * HALVES), lax.rem(k, HALVES), lax.rem(lax.div(k, HALVES), SIDE)).wait()
        return carry

    lax.fori_loop(0, count, stored, 0)
    for n in range(len(pieces)):
        keep(n).wait()
        pl.when(core != pieces[n][0])(lambda n=n: to_core(n).wait_send())
        pl.when(core == pieces[n][0])(lambda n=n: to_core(n).wait_recv())
    edges.wait()
    for copy in ready_copies:
        copy.wait()
    for copy in later_copies:
        pl.when(core == 0)(lambda copy=copy: copy.wait_send())
        pl.when(core == 1)(lambda copy=copy: copy.wait_recv())


def reduce_gradients(g0, t0, shares1, experts0, gu1, down1, tail1, edge, collective_id):
    places, halves, sub, cols = g0.shape
    grad_gu, grad_down = experts0[:2]
    any_spec = pl.BlockSpec(memory_space=pl.ANY)
    wide = cols + LANES
    gu, down = jax.ShapeDtypeStruct(grad_gu.shape, BF16), jax.ShapeDtypeStruct(grad_down.shape, BF16)
    gu_v, down_v = pltpu.VMEM(grad_gu.shape, BF16), pltpu.VMEM(grad_down.shape, BF16)
    own, plane = sum_scratch(places, sub, cols)
    return pl.pallas_call(
        functools.partial(reduce_kernel, sub, cols),
        name="reduce_gradients",
        out_shape=(
            jax.ShapeDtypeStruct((places * halves * sub, wide), BF16), gu, down, gu, down, down, gu, down,
            jax.ShapeDtypeStruct(edge.shape, edge.dtype),
        ),
        in_specs=[any_spec] * 11,
        out_specs=(any_spec,) * 9,
        scratch_shapes=own + [
            pltpu.VMEM((2, sub, wide), BF16),
            gu_v, gu_v, gu_v, down_v, down_v, down_v,
            pltpu.SemaphoreType.DMA((3,)),
            pltpu.SemaphoreType.DMA((6,)),
            pltpu.SemaphoreType.DMA((2, 6)),
            pltpu.SemaphoreType.DMA((8,)),
            pltpu.SemaphoreType.DMA((2,)),
            pltpu.SemaphoreType.DMA((2, 6)),
            pltpu.SemaphoreType.DMA((2, 6)),
            pltpu.SemaphoreType.DMA((places * halves + 8,)),
        ] + plane,
        compiler_params=pltpu.CompilerParams(
            collective_id=collective_id, has_side_effects=True, vmem_limit_bytes=VMEM_BYTES),
    )(g0, t0, shares1, *experts0, gu1, down1, tail1, edge)


def finish_kernel(qkv_cols, attn, gu_own, gu_got, gu_one, gu_moved, down_own, down_got, down_one, down_moved,
                  qkv_hbm, out_hbm, gu_hbm, down_hbm, attn_v, gu_v, down_v, qkv_f, out_f, gu_f, down_f,
                  load_sem, store_sem):
    core = lax.axis_index("section")
    steps = []

    def chunks(rows, count):
        return [pl.ds(n * (rows // count), rows // count) for n in range(count)]

    def choose(zero, one, dst, sem):
        copies = [pltpu.make_async_copy(zero, dst, sem), pltpu.make_async_copy(one, dst, sem)]
        pl.when(core == 0)(lambda: copies[0].start())
        pl.when(core == 1)(lambda: copies[1].start())
        return copies[0]

    def add(load, convert, stores):
        steps.append((load, convert, stores))

    def store(src, dst, n):
        return pltpu.make_async_copy(src, dst, store_sem.at[n])

    stored = 0
    for j, (zero, one) in enumerate(((gu_own, gu_moved), (gu_got, gu_one))):
        for at in chunks(gu_f.shape[1], 6):
            def convert(j=j, at=at):
                gu_f[j, at, :] = gu_v[j, at, :].astype(F32)

            load = choose(zero.at[at], one.at[at], gu_v.at[j, at], load_sem.at[len(steps)])
            add(load, convert, [store(gu_f.at[j, at], gu_hbm.at[j, at], stored)])
            stored += 1
    for j, (zero, one) in enumerate(((down_own, down_moved), (down_got, down_one))):
        for at in chunks(down_f.shape[1], 2):
            def convert(j=j, at=at):
                down_f[j, at, :] = down_v[j, at, :].astype(F32)

            load = choose(zero.at[at], one.at[at], down_v.at[j, at], load_sem.at[len(steps)])
            add(load, convert, [store(down_f.at[j, at], down_hbm.at[j, at], stored)])
            stored += 1
    for at in chunks(attn_v.shape[0], 8):
        def convert(at=at):
            qkv_f[at, :] = attn_v[at, pl.ds(0, qkv_cols)].astype(F32)
            out_f[at, :] = attn_v[at, pl.ds(qkv_cols, out_f.shape[1])].astype(F32)

        load = pltpu.make_async_copy(attn.at[at, pl.ds(0, attn_v.shape[1])], attn_v.at[at], load_sem.at[len(steps)])
        load.start()
        add(load, convert, [
            store(qkv_f.at[at], qkv_hbm.at[at], stored), store(out_f.at[at], out_hbm.at[at], stored + 1)])
        stored += 2
    for load, convert, stores in steps:
        load.wait()
        convert()
        for copy in stores:
            copy.start()
    for load, convert, stores in steps:
        for copy in stores:
            copy.wait()


def finish_outputs(attn, gus, downs, qkv_cols, out_cols):
    rows = attn.shape[0]
    gu, down = (EXP_DEV,) + gus[0].shape, (EXP_DEV,) + downs[0].shape
    any_spec = pl.BlockSpec(memory_space=pl.ANY)
    return pl.pallas_call(
        functools.partial(finish_kernel, qkv_cols),
        name="finish_outputs",
        out_shape=(
            jax.ShapeDtypeStruct((rows, qkv_cols), F32),
            jax.ShapeDtypeStruct((rows, out_cols), F32),
            jax.ShapeDtypeStruct(gu, F32),
            jax.ShapeDtypeStruct(down, F32),
        ),
        in_specs=[any_spec] * 9,
        out_specs=(any_spec,) * 4,
        scratch_shapes=[
            pltpu.VMEM((rows, qkv_cols + out_cols), BF16),
            pltpu.VMEM(gu, BF16),
            pltpu.VMEM(down, BF16),
            pltpu.VMEM((rows, qkv_cols), F32),
            pltpu.VMEM((rows, out_cols), F32),
            pltpu.VMEM(gu, F32),
            pltpu.VMEM(down, F32),
            pltpu.SemaphoreType.DMA((24,)),
            pltpu.SemaphoreType.DMA((32,)),
        ],
        compiler_params=pltpu.CompilerParams(vmem_limit_bytes=VMEM_BYTES),
    )(attn, *gus, *downs)


PAIRS = 2
GROUP = QUERY_HEADS // KEY_VALUE_HEADS
SCALE = HEAD_SIZE ** (-0.5)


class Pair:
    def __init__(self):
        self.sec, self.owner, self.me = (lax.axis_index(n) for n in ("section", "expert", "shard"))
        self.peer = 1 - self.me

    def barrier(self, with_core=False):
        sem = pltpu.get_barrier_semaphore()
        pl.semaphore_signal(
            sem, inc=1, device_id=(self.sec, self.owner, self.peer), device_id_type=MESH)
        if with_core:
            pl.semaphore_signal(
                sem, inc=1, device_id=(1 - self.sec, self.owner, self.me), device_id_type=MESH)
        pl.semaphore_wait(sem, 1 + with_core)

    def send(self, src, dst, send_sem, recv_sem):
        return pltpu.make_async_remote_copy(
            src_ref=src, dst_ref=dst, send_sem=send_sem, recv_sem=recv_sem,
            device_id=(self.sec, self.owner, self.peer), device_id_type=MESH)


def head_columns(shard):
    kv_pair = KEY_VALUE_HEADS // 2 // PAIRS * HEAD_SIZE
    q_pair = kv_pair * GROUP
    wide = q_pair + 2 * kv_pair
    spans = []
    for i in range(PAIRS):
        at = shard * PAIRS + i
        spans.append((at * q_pair, i * wide, q_pair))
        spans.append((QUERY_WIDTH + at * kv_pair, i * wide + q_pair, kv_pair))
        spans.append((QUERY_WIDTH + KV_WIDTH + at * kv_pair, i * wide + q_pair + kv_pair, kv_pair))
    return spans


def head_at(i, n, g):
    kv_pair = KEY_VALUE_HEADS // 2 // PAIRS * HEAD_SIZE
    q_pair = kv_pair * GROUP
    base = i * (q_pair + 2 * kv_pair)
    return (
        pl.ds(base + (n * GROUP + g) * HEAD_SIZE, HEAD_SIZE),
        pl.ds(base + q_pair + n * HEAD_SIZE, HEAD_SIZE),
        pl.ds(base + q_pair + kv_pair + n * HEAD_SIZE, HEAD_SIZE),
    )


KV_IN_PAIR = KEY_VALUE_HEADS // 2 // PAIRS


def load_attention(layer, sec, wq, wq_other, wo, wo_other, wq_v, wo_v, sems):
    loads = []
    for j in range(2):
        for at, local, size in head_columns(j):
            loads.append(load_layer(
                layer, sec, wq.at[:, pl.ds(at, size)], wq_other.at[:, pl.ds(at, size)],
                wq_v.at[j, :, pl.ds(local, size)], sems.at[len(loads)]))
    loads.append(load_layer(layer, sec, wo, wo_other, wo_v, sems.at[len(loads)]))
    return loads


LOADS = 2 * PAIRS * 3 + 1


def attention_forward_kernel(layer, experts, rows, width, lens_ref, h_ref, small_ref, routes_ref, wq, wq_other,
                             wo, wo_other, block_ref, h1_ref, a_ref, qkv_ref, p_ref, o_ref,
                             router_v, wq_v, wo_v, a_parts, a_half, part_send, got_part, out_send, got_out,
                             load_sem, send_sem, recv_sem, *turn):
    pair = Pair()
    me, peer = pair.me, pair.peer
    half = width // 2
    loads = load_attention(layer, pair.sec, wq, wq_other, wo, wo_other, wq_v, wo_v, load_sem)
    pair.barrier(bool(turn))

    def span(who):
        return pl.ds(pl.multiple_of(who * rows, rows), rows)

    h = h_ref[...].astype(F32)
    r1 = lax.rsqrt(jnp.mean(h * h, axis=1, keepdims=True) + EPS)
    gains = small_ref[pl.ds(experts, 2)].astype(F32)
    a = (h * r1 * gains[0:1]).astype(BF16)
    for j in range(2):
        a_parts[j] = a[:, j * half : (j + 1) * half]
    a_half[span(me)] = a_parts[me]
    for load in loads[:-1]:
        load.wait()
    part_send[span(me)] = nn(a_parts[me], wq_v[peer]).astype(BF16)
    if turn:
        pl.when(pair.sec == 0)(lambda: pl.semaphore_wait(turn[0], 1))
    send_a = pair.send(a_parts.at[peer], a_half.at[span(me)], send_sem.at[0], recv_sem.at[0])
    send_a.start()
    send_own = pair.send(part_send.at[span(me)], got_part.at[span(me)], send_sem.at[1], recv_sem.at[1])
    send_own.start()
    send_a.wait_recv()
    part_send[span(peer)] = nn(a_half[span(peer)], wq_v[peer]).astype(BF16)
    send_other = pair.send(
        part_send.at[span(peer)], got_part.at[span(peer)], send_sem.at[2], recv_sem.at[2])
    send_other.start()
    mine = nn(a_half[...], wq_v[me])
    a_ref[...] = a_half[...]
    send_own.wait_recv()
    send_other.wait_recv()
    qkv_ref[...] = (mine + got_part[...].astype(F32)).astype(BF16)
    query = lax.broadcasted_iota(jnp.int32, (2 * rows, 2 * rows), 0)
    key = lax.broadcasted_iota(jnp.int32, (2 * rows, 2 * rows), 1)
    allowed = key <= query
    end = 0
    for n in range(lens_ref.shape[0]):
        end = end + lens_ref[n]
        allowed = allowed & ((query >= end) == (key >= end))
    for i in range(PAIRS):
        for n in range(KV_IN_PAIR):
            for g in range(GROUP):
                q_at, k_at, v_at = head_at(i, n, g)
                j = (i * KV_IN_PAIR + n) * GROUP + g
                s = nt(qkv_ref[:, q_at], qkv_ref[:, k_at]) * SCALE
                s = jnp.where(allowed, s, MASKED_SCORE)
                ex = jnp.exp(s - jnp.max(s, axis=1, keepdims=True))
                p = (ex / jnp.sum(ex, axis=1, keepdims=True)).astype(BF16)
                p_ref[j] = p
                o_ref[:, pl.ds(j * HEAD_SIZE, HEAD_SIZE)] = nn(p, qkv_ref[:, v_at]).astype(BF16)
    loads[-1].wait()
    out_send[...] = nn(o_ref[span(peer)], wo_v[...]).astype(BF16)
    send_out = pair.send(out_send, got_out, send_sem.at[3], recv_sem.at[3])
    send_out.start()
    own = nn(o_ref[span(me)], wo_v[...])
    send_out.wait_recv()
    if turn:
        @pl.when(pair.sec == 1)
        def _():
            pl.semaphore_signal(
                turn[0], inc=1, device_id=(1 - pair.sec, pair.owner, me), device_id_type=MESH)

    h1 = h + own + got_out[...].astype(F32)
    h1_ref[...] = h1
    r2 = lax.rsqrt(jnp.mean(h1 * h1, axis=1, keepdims=True) + EPS)
    b = (h1 * r2 * gains[1:2]).astype(BF16)
    block_ref[:, pl.ds(0, width)] = b
    router_v[...] = jnp.zeros_like(router_v)
    for copy in range(2):
        router_v[pl.ds(copy * experts, experts)] = small_ref[pl.ds(0, experts)]
    lane = lax.broadcasted_iota(jnp.int32, (rows, LANES), 1)
    column = jnp.where(lane < experts, lane, lane - experts)
    routes = routes_ref[...]
    mask = routes[:, 0:1] == column
    for n in range(1, TOP):
        mask = mask | (routes[:, n : n + 1] == column)
    mask = mask & (lane < 2 * experts)
    logits = jnp.where(mask, nt(b, router_v[...]), MASKED_SCORE)
    ex = jnp.where(mask, jnp.exp(logits - jnp.max(logits, axis=1, keepdims=True)), 0.0)
    gates = ex / (0.5 * jnp.sum(ex, axis=1, keepdims=True))
    high = gates.astype(BF16).astype(F32)
    block_ref[:, pl.ds(width, LANES)] = jnp.where(lane >= experts, gates - high, high).astype(BF16)
    for send in (send_a, send_own, send_other, send_out):
        send.wait_send()


def attention_forward(layer, experts, lens, h, small, routes, weights, collective_id):
    rows, width = h.shape
    half, group = width // 2, 2 * rows
    qkv = (QUERY_WIDTH + 2 * KV_WIDTH) // 2
    heads = QUERY_HEADS // 2
    any_spec = pl.BlockSpec(memory_space=pl.ANY)
    vmem = pl.BlockSpec(memory_space=pltpu.VMEM)
    return pl.pallas_call(
        functools.partial(attention_forward_kernel, layer, experts, rows, width),
        name="attention_forward",
        out_shape=(
            jax.ShapeDtypeStruct((rows, width + LANES), BF16),
            jax.ShapeDtypeStruct((rows, width), F32),
            jax.ShapeDtypeStruct((group, half), BF16),
            jax.ShapeDtypeStruct((group, qkv), BF16),
            jax.ShapeDtypeStruct((heads, group, group), BF16),
            jax.ShapeDtypeStruct((group, QUERY_WIDTH // 2), BF16),
        ),
        in_specs=[pl.BlockSpec(memory_space=pltpu.SMEM)] + [vmem] * 3 + [any_spec] * 4,
        out_specs=(vmem,) * 6,
        scratch_shapes=[
            pltpu.VMEM((LANES, width), BF16),
            pltpu.VMEM((2, half, qkv), BF16),
            pltpu.VMEM((QUERY_WIDTH // 2, width), BF16),
            pltpu.VMEM((2, rows, half), BF16),
            pltpu.VMEM((group, half), BF16),
            pltpu.VMEM((group, qkv), BF16),
            pltpu.VMEM((group, qkv), BF16),
            pltpu.VMEM((rows, width), BF16),
            pltpu.VMEM((rows, width), BF16),
            pltpu.SemaphoreType.DMA((LOADS,)),
            pltpu.SemaphoreType.DMA((4,)),
            pltpu.SemaphoreType.DMA((4,)),
        ] + ([pltpu.SemaphoreType.REGULAR] if layer == 0 else []),
        cost_estimate=COST,
        compiler_params=pltpu.CompilerParams(
            collective_id=collective_id, has_side_effects=True, vmem_limit_bytes=VMEM_BYTES),
    )(lens, h, small, routes, *weights)


ATTENTION_BACKWARD_REFS = 20


def attention_backward_kernel(layer, rows, width, experts, router_grad_ref, db_ref, dout_ref, h1_ref, h_ref, small_ref, a_ref, qkv_ref,
                              p_ref, o_ref, wq, wq_other, wo, wo_other, *refs):
    beside = len(refs) > ATTENTION_BACKWARD_REFS
    (later, refs) = (refs[:3], refs[3:]) if beside else ((), refs)
    (dh_ref, columns_ref, grad_hbm), refs = refs[:3], refs[3:]
    (later_out, refs) = (refs[:2], refs[2:]) if beside else ((), refs)
    (wq_v, wo_v, d_all, do, dqkv, got_dqkv, da_send, got_da, dh1_v, grad_q, grad_o,
     gain_grads_ref, columns_v, load_sem, store_sem, send_sem, recv_sem), refs = refs[:17], refs[17:]
    pair = Pair()
    me, peer = pair.me, pair.peer
    half = width // 2
    qkv_cols = dqkv.shape[1]
    pair_cols = qkv_cols // PAIRS
    loads = load_attention(layer, pair.sec, wq, wq_other, wo, wo_other, wq_v, wo_v, load_sem)
    if beside:
        sub, cols_all = later[0].shape[2:]
        plane = Plane(HALVES * sub, (None,) + tuple(refs[10:]))
        sums = GradientSum(plane, 0, cols_all, *later[:2], *refs[:6])
        tail_own, tail_got, tail_load, tail_sem = refs[6:10]
        tail_rows = tail_own.shape[0]
        load_tail = pltpu.make_async_copy(later[2].at[pl.ds(tail_rows, tail_rows)], tail_own, tail_load)
        load_tail.start()
        sums.start_loads()
        plane.barrier(plane.other_core(), plane.other_shard(), sums.diagonal(plane))
        sums.start_copies()
        load_tail.wait()
        tail_copies = []
        for n in range(2):
            at = pl.ds(n * (tail_rows // 2), tail_rows // 2)
            tail_copies.append(pair.send(tail_own.at[at], tail_got.at[at], tail_sem.at[0, n], tail_sem.at[1, n]))
        tail_copies[0].start()
    else:
        pair.barrier()

    def span(who):
        return pl.ds(pl.multiple_of(who * rows, rows), rows)

    h1 = h1_ref[...]
    r2 = lax.rsqrt(jnp.mean(h1 * h1, axis=1, keepdims=True) + EPS)
    normed = h1 * r2
    db = db_ref[...]
    gains = small_ref[pl.ds(experts, 2)].astype(F32)
    scaled = db * gains[1:2]
    gain_grads_ref[...] = jnp.zeros_like(gain_grads_ref)
    gain_grads_ref[pl.ds(experts + 1, 1), :] = jnp.sum(db * normed, axis=0, keepdims=True)
    dh1 = dout_ref[...].astype(F32) + r2 * (
        scaled - normed * jnp.mean(scaled * normed, axis=1, keepdims=True))
    dh1_v[...] = dh1
    d_all[span(me)] = dh1.astype(BF16)
    send_d = pair.send(d_all.at[span(me)], d_all.at[span(me)], send_sem.at[0], recv_sem.at[0])
    send_d.start()
    router_terms = router_grad_ref[...]
    lane = lax.broadcasted_iota(jnp.int32, router_terms.shape, 1)
    router_terms = router_terms + pltpu.roll(router_terms, LANES // 2, 1)
    columns_v[...] = jnp.where(lane < experts, router_terms, 0.0)
    if beside:
        sums.wait_terms()
        sums.prepare(0, LINE)
    for load in loads:
        load.wait()
    do[span(me)] = nt(d_all[span(me)], wo_v[...]).astype(BF16)
    send_d.wait_recv()
    do[span(peer)] = nt(d_all[span(peer)], wo_v[...]).astype(BF16)
    sends = [send_d]
    if beside:
        tail_copies[1].start()
        pl.when(plane.inner == 0)(lambda: sums.pass_on(0))
        sums.prepare(LINE, LINE * SIDE)
    for i in range(PAIRS):
        cols = pl.ds(i * pair_cols, pair_cols)
        for n in range(KV_IN_PAIR):
            dk = dv = None
            for g in range(GROUP):
                q_at, k_at, v_at = head_at(i, n, g)
                j = (i * KV_IN_PAIR + n) * GROUP + g
                p_low = p_ref[j]
                p = p_low.astype(F32)
                d_head = do[:, pl.ds(j * HEAD_SIZE, HEAD_SIZE)]
                weighted = p * nt(d_head, qkv_ref[:, v_at])
                ds = (weighted - p * jnp.sum(weighted, axis=1, keepdims=True)).astype(BF16)
                dqkv[:, q_at] = (nn(ds, qkv_ref[:, k_at]) * SCALE).astype(BF16)
                dk_part, dv_part = tn(ds, qkv_ref[:, q_at]), tn(p_low, d_head)
                dk = dk_part if dk is None else dk + dk_part
                dv = dv_part if dv is None else dv + dv_part
            dqkv[:, k_at] = (dk * SCALE).astype(BF16)
            dqkv[:, v_at] = dv.astype(BF16)
        send = pair.send(dqkv.at[:, cols], got_dqkv.at[:, cols], send_sem.at[1 + i], recv_sem.at[1 + i])
        send.start()
        sends.append(send)
        if beside and i == 0:
            pl.when(plane.inner == 1)(lambda: sums.pass_on(0))
    da = nt(dqkv[...], wq_v[me])
    grad_q[me] = tn(a_ref[...], dqkv[...]).astype(BF16)
    grad_o[...] = tn(o_ref[...], d_all[...]).astype(BF16)
    store_o = pltpu.make_async_copy(
        grad_o, grad_hbm.at[:, pl.ds(QUERY_WIDTH + 2 * KV_WIDTH, width)], store_sem.at[LOADS - 1])
    store_o.start()
    for send in sends[1:]:
        send.wait_recv()
    da = da + nt(got_dqkv[...], wq_v[peer])
    da_send[...] = jnp.where(me == 0, da[rows:], da[:rows]).astype(BF16)
    send_da = pair.send(da_send, got_da, send_sem.at[1 + PAIRS], recv_sem.at[1 + PAIRS])
    send_da.start()
    own_da = jnp.where(me == 0, da[:rows], da[rows:])
    grad_q[peer] = tn(a_ref[...], got_dqkv[...]).astype(BF16)
    stores = [store_o]
    for j in range(2):
        for at, local, size in head_columns(j):
            store = pltpu.make_async_copy(
                grad_q.at[j, :, pl.ds(local, size)], grad_hbm.at[:, pl.ds(at, size)],
                store_sem.at[len(stores) - 1])
            store.start()
            stores.append(store)
    send_da.wait_recv()
    other_da = got_da[...].astype(F32)
    h = h_ref[...].astype(F32)
    r1 = lax.rsqrt(jnp.mean(h * h, axis=1, keepdims=True) + EPS)
    halves = []
    total = jnp.zeros((rows, 1), F32)
    for j in range(2):
        cols = pl.ds(j * half, half)
        da_j = jnp.where(me == j, own_da, other_da)
        normed = h[:, j * half : (j + 1) * half] * r1
        gain_grads_ref[pl.ds(experts, 1), cols] = jnp.sum(da_j * normed, axis=0, keepdims=True)
        scaled = da_j * gains[0:1, j * half : (j + 1) * half]
        total = total + jnp.sum(scaled * normed, axis=1, keepdims=True)
        halves.append((cols, scaled, normed))
    columns = columns_v[...] + jnp.transpose(gain_grads_ref[...])
    columns_ref[...] = columns.astype(BF16)
    for cols, scaled, normed in halves:
        dh_ref[:, cols] = (dh1_v[:, cols] + r1 * (scaled - normed * (total / width))).astype(dh_ref.dtype)
    if beside:
        sums.hand_over(later_out[0])
        for copy in tail_copies:
            copy.wait()
        later_out[1][...] = (tail_own[...].astype(F32) + tail_got[...].astype(F32)).astype(BF16)
        sums.drain(1)
    for send in sends + [send_da]:
        send.wait_send()
    for store in stores:
        store.wait()


def attention_backward(layer, experts, router_grad, db, dout, h1, h, small, a_half, qkv, p, o, weights, later,
                       collective_id):
    rows, width = db.shape
    half, group = width // 2, 2 * rows
    cols = (QUERY_WIDTH + 2 * KV_WIDTH) // 2
    any_spec = pl.BlockSpec(memory_space=pl.ANY)
    vmem = pl.BlockSpec(memory_space=pltpu.VMEM)
    later_out, later_scratch = (), []
    if later:
        places, _, sub, later_cols = later[0].shape
        own, plane = sum_scratch(places, sub, later_cols)
        tail_shape = (later[2].shape[0] // 2, later[2].shape[1])
        later_out = (
            jax.ShapeDtypeStruct((3, sub, later_cols + LANES), BF16),
            jax.ShapeDtypeStruct(tail_shape, BF16),
        )
        later_scratch = own + [
            pltpu.VMEM(tail_shape, BF16),
            pltpu.VMEM(tail_shape, BF16),
            pltpu.SemaphoreType.DMA,
            pltpu.SemaphoreType.DMA((2, 2)),
        ] + plane[1:]
    return pl.pallas_call(
        functools.partial(attention_backward_kernel, layer, rows, width, experts),
        name="attention_backward",
        out_shape=(
            jax.ShapeDtypeStruct((rows, width), F32 if layer == 0 else BF16),
            jax.ShapeDtypeStruct((width, LANES), BF16),
            jax.ShapeDtypeStruct((half, QUERY_WIDTH + 2 * KV_WIDTH + width), BF16),
        ) + later_out,
        in_specs=[vmem] * 10 + [any_spec] * (4 + len(later)),
        out_specs=(vmem, vmem, any_spec) + (vmem,) * len(later_out),
        scratch_shapes=[
            pltpu.VMEM((2, half, cols), BF16),
            pltpu.VMEM((QUERY_WIDTH // 2, width), BF16),
            pltpu.VMEM((group, width), BF16),
            pltpu.VMEM((group, QUERY_WIDTH // 2), BF16),
            pltpu.VMEM((group, cols), BF16),
            pltpu.VMEM((group, cols), BF16),
            pltpu.VMEM((rows, half), BF16),
            pltpu.VMEM((rows, half), BF16),
            pltpu.VMEM((rows, width), F32),
            pltpu.VMEM((2, half, cols), BF16),
            pltpu.VMEM((QUERY_WIDTH // 2, width), BF16),
            pltpu.VMEM((LANES, width), F32),
            pltpu.VMEM((width, LANES), F32),
            pltpu.SemaphoreType.DMA((LOADS,)),
            pltpu.SemaphoreType.DMA((LOADS,)),
            pltpu.SemaphoreType.DMA((2 + PAIRS,)),
            pltpu.SemaphoreType.DMA((2 + PAIRS,)),
        ] + later_scratch,
        cost_estimate=COST,
        compiler_params=pltpu.CompilerParams(
            collective_id=collective_id, has_side_effects=True, vmem_limit_bytes=VMEM_BYTES),
    )(router_grad, db, dout, h1, h, small, a_half, qkv, p, o, *weights, *later)


def dot(a, b, dims):
    return lax.dot_general(a, b, (dims, ((), ())), preferred_element_type=F32)


def rms_scale(values):
    return lax.rsqrt(jnp.mean(values * values, axis=-1, keepdims=True) + EPS)


def swap_cores(value):
    return lax.ppermute(value, "section", [(0, 1), (1, 0)])


def both_layers(own):
    return lax.all_gather(own, "section", axis=0, tiled=False)


def document_mask(sequence_lengths, rows):
    pos = jnp.arange(rows, dtype=jnp.int32)
    ends = jnp.cumsum(sequence_lengths)
    doc = jnp.sum((pos[:, None] >= ends[None, :]).astype(jnp.int32), axis=1)
    return (doc[:, None] == doc[None, :]) & (pos[None, :] <= pos[:, None])


def plain_attention(qkv, allowed, heads, kv_heads):
    rows = qkv.shape[0]
    group = heads // kv_heads
    q = qkv[:, : heads * HEAD_SIZE].reshape(rows, kv_heads, group, HEAD_SIZE)
    k = qkv[:, heads * HEAD_SIZE : (heads + kv_heads) * HEAD_SIZE].reshape(rows, kv_heads, HEAD_SIZE)
    v = qkv[:, (heads + kv_heads) * HEAD_SIZE :].reshape(rows, kv_heads, HEAD_SIZE)
    s = jnp.einsum("qhgd,khd->hgqk", q, k, preferred_element_type=F32) * HEAD_SIZE ** (-0.5)
    s = jnp.where(allowed[None, None], s, MASKED_SCORE)
    ex = jnp.exp(s - jnp.max(s, axis=-1, keepdims=True))
    p = ex / jnp.sum(ex, axis=-1, keepdims=True)
    o = jnp.einsum("hgqk,khd->qhgd", p.astype(BF16), v, preferred_element_type=F32)
    return o.reshape(rows, heads * HEAD_SIZE).astype(BF16), p, (q, k, v)


def plain_attention_backward(do, p, heads_in):
    q, k, v = heads_in
    rows = q.shape[0]
    dh = do.reshape(q.shape)
    dv = jnp.einsum("hgqk,qhgd->khd", p.astype(BF16), dh, preferred_element_type=F32)
    dp = jnp.einsum("qhgd,khd->hgqk", dh, v, preferred_element_type=F32)
    ds = (p * (dp - jnp.sum(p * dp, axis=-1, keepdims=True))).astype(BF16)
    dq = jnp.einsum("hgqk,khd->qhgd", ds, k, preferred_element_type=F32) * HEAD_SIZE ** (-0.5)
    dk = jnp.einsum("hgqk,qhgd->khd", ds, q, preferred_element_type=F32) * HEAD_SIZE ** (-0.5)
    return jnp.concatenate(
        [dq.reshape(rows, -1), dk.reshape(rows, -1), dv.reshape(rows, -1)], axis=1
    ).astype(BF16)


def column_parts(n, j):
    qw, kw = QUERY_WIDTH // n, KV_WIDTH // n
    return (
        (j * qw, qw),
        (QUERY_WIDTH + j * kw, kw),
        (QUERY_WIDTH + KV_WIDTH + j * kw, kw),
    )


def plain_shards(
    edge_inputs, seq_lengths, routes, w_qkv, w_out, w_router, gain_attn, gain_moe, w_gate_up, w_down
):
    sec = lax.axis_index("section")
    owner = lax.axis_index("expert")
    shard_pos = lax.axis_index("shard")
    n_shard = lax.axis_size("shard")
    n_owner = lax.axis_size("expert")
    rows, width = edge_inputs.shape[2], edge_inputs.shape[3]
    experts = w_router.shape[2]
    group_rows = rows * n_shard
    half = width // n_shard
    heads, kv_heads = QUERY_HEADS // n_shard, KEY_VALUE_HEADS // n_shard

    def pick(array, index):
        return lax.dynamic_index_in_dim(array, index, 0, keepdims=False)

    own_edge, other_edge = pick(edge_inputs[0], sec), swap_cores(pick(edge_inputs[0], 1 - sec))
    x_in = jnp.where(sec == 0, own_edge, other_edge)
    dy = jnp.where(sec == 0, other_edge, own_edge)
    own_routes, other_routes = pick(routes[0], sec), swap_cores(pick(routes[0], 1 - sec))
    layer_routes = (
        jnp.where(sec == 0, own_routes, other_routes),
        jnp.where(sec == 0, other_routes, own_routes),
    )
    allowed = document_mask(pick(seq_lengths, sec)[0], group_rows)
    wq = both_layers(w_qkv[0])
    wo = both_layers(w_out[0])
    small = jnp.concatenate([w_router[0], gain_attn[0][:, None], gain_moe[0][:, None]], axis=1)
    small = lax.all_gather(both_layers(small), "shard", axis=1, tiled=True)
    wgu = both_layers(w_gate_up[0])
    wd = both_layers(w_down[0])
    columns = jnp.arange(experts, dtype=jnp.int32)
    route_masks = [
        jnp.any(r[:, :, None] == columns[None, None, :], axis=1).astype(BF16) for r in layer_routes
    ]
    plane_masks = [lax.all_gather(m, "expert", axis=0, tiled=True) for m in route_masks]

    def forward(layer, h):
        gain_a = small[layer, :, experts].astype(F32)[None, :]
        gain_m = small[layer, :, experts + 1].astype(F32)[None, :]
        router = small[layer, :, :experts]
        r1 = rms_scale(h)
        a = (h * r1 * gain_a).astype(BF16)
        a_half = lax.all_to_all(
            a.reshape(rows, n_shard, half), "shard", split_axis=1, concat_axis=0, tiled=True
        ).reshape(group_rows, half)
        blocks = []
        for j in range(n_shard):
            blocks.append(
                jnp.concatenate(
                    [
                        dot(a_half, wq[layer, :, at : at + size], ((1,), (0,)))
                        for at, size in column_parts(n_shard, j)
                    ],
                    axis=1,
                ).astype(BF16)
            )
        qkv = lax.psum_scatter(jnp.stack(blocks), "shard", scatter_dimension=0, tiled=False)
        o, p, heads_in = plain_attention(qkv, allowed, heads, kv_heads)
        part = dot(o, wo[layer], ((1,), (0,))).astype(BF16)
        h1 = h + lax.psum_scatter(part, "shard", scatter_dimension=0, tiled=True).astype(F32)
        r2 = rms_scale(h1)
        b = (h1 * r2 * gain_m).astype(BF16)
        b_all = lax.all_gather(b, "expert", axis=0, tiled=True)
        mask = plane_masks[layer].astype(F32) > 0
        logits = jnp.where(mask, dot(b_all, router, ((1,), (0,))), MASKED_SCORE)
        ex = jnp.where(mask, jnp.exp(logits - jnp.max(logits, axis=1, keepdims=True)), 0.0)
        gates = ex / jnp.sum(ex, axis=1, keepdims=True)
        own_gates = lax.dynamic_slice_in_dim(gates, owner * EXP_DEV, EXP_DEV, 1)
        kept, scaled = [], []
        for j in range(EXP_DEV):
            gu = dot(b_all, wgu[layer, j], ((1,), (0,)))
            g, u = gu[:, :FF], gu[:, FF:]
            scaled.append((g * jax.nn.sigmoid(g) * u * own_gates[:, j : j + 1]).astype(BF16))
            kept.append(gu.astype(BF16))
        scaled = jnp.concatenate(scaled, axis=1)
        moe_part = dot(scaled, wd[layer].reshape(EXP_DEV * FF, width), ((1,), (0,))).astype(BF16)
        moe = lax.psum_scatter(moe_part, "expert", scatter_dimension=0, tiled=True).astype(F32)
        state = (h, r1, a_half, p, heads_in, o, h1, r2, b_all, own_gates, kept, scaled, moe)
        return h1 + moe, state

    def backward(layer, dout, dout_low, state):
        h, r1, a_half, p, heads_in, o, h1, r2, b_all, own_gates, kept, scaled, moe = state
        gain_a = small[layer, :, experts].astype(F32)[None, :]
        gain_m = small[layer, :, experts + 1].astype(F32)[None, :]
        router = small[layer, :, :experts]
        own_router = lax.dynamic_slice_in_dim(router, owner * EXP_DEV, EXP_DEV, 1)
        total = lax.all_gather(jnp.sum(dout * moe, axis=1), "expert", axis=0, tiled=True)
        dout_all = lax.all_gather(dout_low, "expert", axis=0, tiled=True)
        dgus, dcs = [], []
        for j in range(EXP_DEV):
            gate = own_gates[:, j : j + 1]
            g, u = kept[j][:, :FF].astype(F32), kept[j][:, FF:].astype(F32)
            sig = jax.nn.sigmoid(g)
            silu = g * sig
            dz = dot(dout_all, wd[layer, j], ((1,), (1,)))
            dgate = jnp.sum(dz * silu * u, axis=1, keepdims=True)
            dcs.append(gate * (dgate - total[:, None]))
            dz = dz * gate
            dgus.append(
                jnp.concatenate(
                    [dz * u * sig * (1.0 + g * (1.0 - sig)), dz * silu], axis=1
                ).astype(BF16)
            )
        dc = jnp.concatenate(dcs, axis=1)
        db_part = sum(dot(dgus[j], wgu[layer, j], ((1,), (1,))) for j in range(EXP_DEV))
        for j in range(EXP_DEV):
            db_part = db_part + dc[:, j : j + 1] * own_router[:, j].astype(F32)[None, :]
        db = lax.psum_scatter(
            db_part.astype(BF16), "expert", scatter_dimension=0, tiled=True
        ).astype(F32)
        grad_down = dot(scaled, dout_all, ((0,), (0,))).reshape(EXP_DEV, FF, width)
        grad_gu = jnp.stack([dot(b_all, dgus[j], ((0,), (0,))) for j in range(EXP_DEV)])
        grad_router = lax.dot_general(
            dc, b_all.astype(F32), (((0,), (0,)), ((), ())), precision=lax.Precision.HIGHEST
        )
        normed = h1 * r2
        grad_gain_m = jnp.sum(db * normed, axis=0)
        scaled_db = db * gain_m
        dh1 = dout + r2 * (scaled_db - normed * jnp.mean(scaled_db * normed, axis=1, keepdims=True))
        dattn = lax.all_gather(dh1.astype(BF16), "shard", axis=0, tiled=True)
        do = dot(dattn, wo[layer], ((1,), (1,))).astype(BF16)
        grad_out = dot(o, dattn, ((0,), (0,)))
        dqkv = lax.all_gather(plain_attention_backward(do, p, heads_in), "shard", axis=0, tiled=False)
        da = 0.0
        grad_qkv = []
        for part in range(3):
            grad_qkv.append([])
        for j in range(n_shard):
            at_local = 0
            for part, (at, size) in enumerate(column_parts(n_shard, j)):
                piece = dqkv[j, :, at_local : at_local + size]
                at_local += size
                da = da + dot(piece, wq[layer, :, at : at + size], ((1,), (1,)))
                grad_qkv[part].append(dot(a_half, piece, ((0,), (0,))))
        grad_qkv = jnp.concatenate([x for part in grad_qkv for x in part], axis=1)
        da = lax.all_to_all(
            da.astype(BF16), "shard", split_axis=0, concat_axis=1, tiled=True
        ).astype(F32)
        normed = h * r1
        grad_gain_a = jnp.sum(da * normed, axis=0)
        scaled_da = da * gain_a
        dh = dh1 + r1 * (scaled_da - normed * jnp.mean(scaled_da * normed, axis=1, keepdims=True))
        return dh, (grad_qkv, grad_out, grad_router, grad_gain_a, grad_gain_m, grad_gu, grad_down)

    out0, state0 = forward(0, x_in.astype(F32))
    mid = out0.astype(BF16).astype(F32)
    final, state1 = forward(1, mid)
    dh_one, grads1 = backward(1, dy.astype(F32), dy, state1)
    low = dh_one.astype(BF16)
    dh_zero, grads0 = backward(0, low.astype(F32), low, state0)

    def half_sum(grad):
        low_grad = grad.astype(BF16)
        halves = low_grad.reshape((2, -1) + low_grad.shape[1:])
        got = swap_cores(pick(halves, 1 - sec))
        return (pick(halves, sec).astype(F32) + got.astype(F32)).astype(BF16)

    def to_owner(half0, half1):
        keep = jnp.where(sec == 0, half0, half1)
        got = swap_cores(jnp.where(sec == 0, half1, half0))
        first = jnp.where(sec == 0, keep, got)
        second = jnp.where(sec == 0, got, keep)
        return jnp.concatenate([first, second], axis=0).astype(F32)

    attn_halves, exp_halves = [], []
    for grads in (grads0, grads1):
        attn = half_sum(jnp.concatenate([grads[0], grads[1]], axis=1))
        attn_halves.append(lax.psum(attn, "expert"))
        exp_halves.append(tuple(lax.psum(half_sum(g), "shard") for g in (grads[5], grads[6])))
    attn = to_owner(*attn_halves)
    grad_qkv, grad_out = attn[:, : w_qkv.shape[2]], attn[:, w_qkv.shape[2] :]
    grad_gu = to_owner(exp_halves[0][0], exp_halves[1][0])
    grad_down = to_owner(exp_halves[0][1], exp_halves[1][1])

    tiny = []
    for grads in (grads0, grads1):
        hot = jnp.arange(experts)[:, None] == owner * EXP_DEV + jnp.arange(EXP_DEV)[None, :]
        router = sum(
            jnp.where(hot[:, j : j + 1], grads[2][j][None, :], 0.0) for j in range(EXP_DEV)
        )
        tiny.append(jnp.concatenate([router, grads[3][None, :], grads[4][None, :]], axis=0))
    tiny = lax.psum(jnp.stack(tiny), ("section", "expert", "shard"))
    tiny = lax.dynamic_slice_in_dim(pick(tiny, sec), shard_pos * half, half, 1)

    send = jnp.where(sec == 0, final, dh_zero)
    keep = jnp.where(sec == 0, dh_zero, final)
    got = swap_cores(send)
    edge = jnp.where(sec == 0, jnp.stack([keep, got]), jnp.stack([got, keep]))
    return (
        edge[None],
        grad_qkv[None],
        grad_out[None],
        tiny[:experts].T[None],
        tiny[experts][None],
        tiny[experts + 1][None],
        grad_gu[None],
        grad_down[None],
    )


def kernel_shards(
    edge_inputs, seq_lengths, routes, w_qkv, w_out, w_router, gain_attn, gain_moe, w_gate_up, w_down
):
    sec = lax.axis_index("section")
    owner = lax.axis_index("expert")
    shard_pos = lax.axis_index("shard")
    rows, width = edge_inputs.shape[2], edge_inputs.shape[3]
    experts = w_router.shape[2]
    half = width // 2
    attn_cols = w_qkv.shape[2] + w_out.shape[2]

    def pick(array, index):
        return lax.dynamic_index_in_dim(array, index, 0, keepdims=False)

    def swap_shards(value):
        return lax.ppermute(value, "shard", [(0, 1), (1, 0)])

    def by_core(own, other):
        return jnp.where(sec == 0, own, other), jnp.where(sec == 0, other, own)

    small = jnp.concatenate([w_router[0].T, gain_attn, gain_moe], axis=0)
    across = lax.ppermute(small, ("section", "shard"), [(0, 3), (1, 2), (2, 1), (3, 0)])

    def joined(mine, other):
        return jnp.where(
            shard_pos == 0,
            jnp.concatenate([mine, other], axis=1),
            jnp.concatenate([other, mine], axis=1),
        )

    layer_small = by_core(joined(small, swap_shards(small)), joined(swap_cores(small), across))
    x_in, dy = by_core(pick(edge_inputs[0], sec), swap_cores(pick(edge_inputs[0], 1 - sec)))
    layer_routes = by_core(pick(routes[0], sec), swap_cores(pick(routes[0], 1 - sec)))
    lens = pick(seq_lengths, sec)[0]
    attn_weights = (w_qkv[0], swap_cores(w_qkv[0]), w_out[0], swap_cores(w_out[0]))
    expert_weights = (
        w_gate_up[0], swap_cores(w_gate_up[0]), w_down[0], swap_cores(w_down[0])
    )
    def forward(layer, h):
        block, h1, *attn_state = attention_forward(
            layer, experts, lens, h, layer_small[layer], layer_routes[layer], attn_weights, 1 + layer
        )
        moe, out, *expert_state = moe_forward(
            layer, block, h1, expert_weights, experts, F32 if layer else BF16, 3 + layer
        )
        return out, (h, h1, moe, attn_state, expert_state)

    def backward(layer, dout, state, later, later_attn):
        h, h1, moe, attn_state, expert_state = state
        results = moe_backward(
            layer, dout, moe, layer_small[layer], expert_weights, expert_state, later, experts,
            5 + layer,
        )
        db, keep_gu, keep_down, send_gu, send_down, grad_router = results[:6]
        dh, columns, grad_attn, *piece = attention_backward(
            layer, experts, grad_router, db, dout, h1, h, layer_small[layer], *attn_state, attn_weights,
            later_attn + tuple(results[7:8]) if later else (), 7 + layer,
        )
        places = LINE * SIDE
        sub = half // (2 * places)
        grad_attn = grad_attn.reshape(places, 2, sub, attn_cols)
        columns = columns.reshape(2, places, 2, sub, LANES)
        return dh, grad_attn, columns, (keep_gu, keep_down, send_gu, send_down), results[6:8], piece

    out0, state0 = forward(0, x_in)
    final, state1 = forward(1, out0)
    dh_one, attn1, columns1, experts1, *_ = backward(1, dy, state1, (), ())
    dh_zero, attn0, columns0, experts0, sums1, (shares1, tail1) = backward(
        0, dh_one, state0, experts1, (attn1, columns1)
    )
    send = jnp.where(sec == 0, final, dh_zero)
    attn, gu_own, down_own, gu_got, down_got, down_one, gu_moved, down_moved, got = reduce_gradients(
        attn0, columns0, shares1, experts0, *sums1, tail1, send, 9
    )
    grad_qkv, grad_out, grad_gu, grad_down = finish_outputs(
        attn,
        (gu_own, gu_got, sums1[0], gu_moved),
        (down_own, down_got, down_one, down_moved),
        w_qkv.shape[2],
        w_out.shape[2],
    )
    tiny = attn[:, attn_cols : attn_cols + experts + 2].astype(F32)
    keep = jnp.where(sec == 0, dh_zero, final)
    edge = jnp.where(sec == 0, jnp.stack([keep, got]), jnp.stack([got, keep]))
    return (
        edge[None],
        grad_qkv[None],
        grad_out[None],
        tiny[:, :experts][None],
        tiny[:, experts][None],
        tiny[:, experts + 1][None],
        grad_gu[None],
        grad_down[None],
    )


def shards(*arrays):
    if lax.axis_size("expert") == LINE * SIDE and lax.axis_size("shard") == 2:
        return kernel_shards(*arrays)
    return plain_shards(*arrays)


def solution(mesh):
    in_specs = (
        P("section", None, ("expert", "shard"), None),
        P(None, "expert", None),
        P("section", None, ("expert", "shard"), None),
        P("section", "shard", None),
        P("section", "shard", None),
        P("section", "shard", None),
        P("section", "shard"),
        P("section", "shard"),
        P("section", "expert", None, None),
        P("section", "expert", None, None),
    )
    out_specs = (
        P("section", None, ("expert", "shard"), None),
        P("section", "shard", None),
        P("section", "shard", None),
        P("section", "shard", None),
        P("section", "shard"),
        P("section", "shard"),
        P("section", "expert", None, None),
        P("section", "expert", None, None),
    )
    return jax.shard_map(shards, mesh=mesh, in_specs=in_specs, out_specs=out_specs, check_vma=False)
```

```python
import functools

import jax
import jax.numpy as jnp
from jax import lax
from jax.experimental import pallas as pl
from jax.experimental.pallas import tpu as pltpu
from jax.sharding import PartitionSpec as P

QUERY_HEADS = 24
KEY_VALUE_HEADS = 8
HEAD_SIZE = 64
FF = 512
TOP = 8
EXP_DEV = 2
EPS = 1e-05
MASKED_SCORE = -1e30
QUERY_WIDTH = QUERY_HEADS * HEAD_SIZE
KV_WIDTH = KEY_VALUE_HEADS * HEAD_SIZE
F32 = jnp.float32
BF16 = jnp.bfloat16
MESH = pl.DeviceIdType.MESH
LINE = 4
SIDE = 2
LANES = 128
HALVES = 2
LATER_CROSS = 5
TILE = 256
VMEM_BYTES = 60 * 2**20
COST = pl.CostEstimate(flops=10**11, bytes_accessed=2**24, transcendentals=0)


def chunk_order(z, t):
    near = z + 1 - 2 * lax.rem(z, 2)
    third = jnp.where(z < 2, 2, 1)
    last = jnp.where(z < 2, 3, 0)
    return jnp.where(t == 0, z, jnp.where(t == 1, near, jnp.where(t == 2, third, last)))


def sum_order(z, i):
    first = jnp.where((z == 0) | (z == 2), 1, 2)
    second = jnp.where(z == 0, 2, jnp.where(z == 1, 3, jnp.where(z == 2, 0, 1)))
    third = jnp.where(z == 0, 3, jnp.where(z == 1, 0, jnp.where(z == 2, 3, 0)))
    return jnp.where(i == 0, first, jnp.where(i == 1, second, third))


class Plane:
    def __init__(self, rows, refs):
        (self.gathered, self.parts, self.from_side, self.from_low, self.from_high, self.sums,
         self.line_send, self.gather_recv, self.side_send, self.side_recv,
         self.sum_send, self.low_recv, self.high_recv) = refs
        self.sub = rows // HALVES
        self.both = SIDE * self.sub
        self.sec, self.owner, self.shard = (lax.axis_index(n) for n in ("section", "expert", "shard"))
        self.z, self.x = lax.div(self.owner, SIDE), lax.rem(self.owner, SIDE)
        self.inner = ((self.z > 0) & (self.z < LINE - 1)).astype(jnp.int32)

    def device(self, z, x):
        return (self.sec, z * SIDE + x, self.shard)

    def other_core(self):
        return (1 - self.sec, self.owner, self.shard)

    def other_shard(self):
        return (self.sec, self.owner, 1 - self.shard)

    def chunk(self, c, h):
        return pl.ds(pl.multiple_of((c * HALVES + h) * self.both, self.both), self.both)

    def block(self, c, h, x):
        return pl.ds(pl.multiple_of((c * HALVES + h) * self.both + x * self.sub, self.sub), self.sub)

    def barrier(self, *others):
        z, x = self.z, self.x
        sem = pltpu.get_barrier_semaphore()

        def greet(device):
            pl.semaphore_signal(sem, inc=1, device_id=device, device_id_type=MESH)

        for other in others:
            greet(other)
        greet(self.device(z, 1 - x))
        pl.when(z > 0)(lambda: greet(self.device(z - 1, x)))
        pl.when(z < LINE - 1)(lambda: greet(self.device(z + 1, x)))
        pl.semaphore_wait(sem, 2 + len(others) + self.inner)

    def place(self, block_ref):
        for h in range(HALVES):
            self.gathered[self.block(self.z, h, self.x)] = block_ref[pl.ds(h * self.sub, self.sub)]

    def gather_copy(self, way, c, h, x, device):
        ref = self.gathered.at[self.block(c, h, x)]
        q = c * HALVES + h
        return pltpu.make_async_remote_copy(
            src_ref=ref, dst_ref=ref, send_sem=self.line_send.at[way, q],
            recv_sem=self.gather_recv.at[q, x], device_id=device, device_id_type=MESH)

    def forward_up(self, c, h):
        return self.gather_copy(0, c, h, self.x, self.device(self.z + 1, self.x))

    def forward_down(self, c, h):
        return self.gather_copy(1, c, h, self.x, self.device(self.z - 1, self.x))

    def forward_side(self, c, h):
        return self.gather_copy(2, c, h, self.x, self.device(self.z, 1 - self.x))

    def start_gather(self):
        z = self.z
        for h in range(HALVES):
            pl.when(z < LINE - 1)(lambda h=h: self.forward_up(z, h).start())
            pl.when(z > 0)(lambda h=h: self.forward_down(z, h).start())
            self.forward_side(z, h).start()

    def relay(self, t, h):
        z = self.z

        @pl.when((t > 0) & (z - t >= 0))
        def _():
            c = z - t
            self.forward_side(c, h).wait_recv()
            pl.when(z < LINE - 1)(lambda: self.forward_up(c, h).start())
            self.forward_side(c, h).start()

        @pl.when((t > 0) & (z + t <= LINE - 1))
        def _():
            c = z + t
            self.forward_side(c, h).wait_recv()
            pl.when(z > 0)(lambda: self.forward_down(c, h).start())
            self.forward_side(c, h).start()

    def wait_side_block(self, c, h):
        self.gather_copy(2, c, h, 1 - self.x, self.device(self.z, 1 - self.x)).wait_recv()

    def side_copy(self, c, h):
        q = c * HALVES + h
        return pltpu.make_async_remote_copy(
            src_ref=self.parts.at[self.block(c, h, 1 - self.x)], dst_ref=self.from_side.at[q],
            send_sem=self.side_send.at[q], recv_sem=self.side_recv.at[q],
            device_id=self.device(self.z, 1 - self.x), device_id_type=MESH)

    def up_copy(self, c, h):
        q = c * HALVES + h
        return pltpu.make_async_remote_copy(
            src_ref=self.sums.at[q], dst_ref=self.from_low.at[q], send_sem=self.sum_send.at[q],
            recv_sem=self.low_recv.at[q],
            device_id=self.device(jnp.minimum(self.z + 1, LINE - 1), self.x), device_id_type=MESH)

    def down_copy(self, c, h):
        q = c * HALVES + h
        return pltpu.make_async_remote_copy(
            src_ref=self.sums.at[q], dst_ref=self.from_high.at[q], send_sem=self.sum_send.at[q],
            recv_sem=self.high_recv.at[q],
            device_id=self.device(jnp.maximum(self.z - 1, 0), self.x), device_id_type=MESH)

    def own_part(self, c, h, side=True):
        part = self.parts[self.block(c, h, self.x)].astype(F32)
        return part + self.from_side[c * HALVES + h].astype(F32) if side else part

    def pass_sum(self, t, h):
        i = t - 3 - self.inner
        pl.when((i >= 0) & (i < LINE - 1))(lambda: self.pass_chunk(sum_order(self.z, i), h))

    def pass_chunk(self, c, h, side=True, send=True):
        z = self.z
        q = c * HALVES + h
        if side:
            self.side_copy(c, h).wait_recv()

        @pl.when(c > z)
        def _():
            @pl.when(z > 0)
            def _():
                self.up_copy(c, h).wait_recv()
                self.sums[q] = (self.own_part(c, h, side) + self.from_low[q].astype(F32)).astype(BF16)

            @pl.when(z == 0)
            def _():
                self.sums[q] = self.own_part(c, h, side).astype(BF16)

        @pl.when(c < z)
        def _():
            @pl.when(z < LINE - 1)
            def _():
                self.down_copy(c, h).wait_recv()
                self.sums[q] = (self.own_part(c, h, side) + self.from_high[q].astype(F32)).astype(BF16)

            @pl.when(z == LINE - 1)
            def _():
                self.sums[q] = self.own_part(c, h, side).astype(BF16)

        if send:
            self.send_sum(c, h)

    def send_sum(self, c, h):
        pl.when(c > self.z)(lambda: self.up_copy(c, h).start())
        pl.when(c < self.z)(lambda: self.down_copy(c, h).start())

    def wait_sent_sum(self, c, h):
        pl.when(c > self.z)(lambda: self.up_copy(c, h).wait_send())
        pl.when(c < self.z)(lambda: self.down_copy(c, h).wait_send())

    def finish_sum(self, h, out_ref):
        z = self.z
        q = z * HALVES + h
        rows = pl.ds(pl.multiple_of(h * self.sub, self.sub), self.sub)
        self.side_copy(z, h).wait_recv()
        out_ref[rows] = self.own_part(z, h)

        @pl.when(z > 0)
        def _():
            self.up_copy(z, h).wait_recv()
            out_ref[rows] += self.from_low[q].astype(F32)

        @pl.when(z < LINE - 1)
        def _():
            self.down_copy(z, h).wait_recv()
            out_ref[rows] += self.from_high[q].astype(F32)

    def finish_piece(self, h, out_ref, side=True):
        z = self.z
        q = z * HALVES + h
        if side:
            self.side_copy(z, h).wait_recv()

        @pl.when(z == 0)
        def _():
            self.down_copy(z, h).wait_recv()
            out_ref[h] = (self.own_part(z, h, side) + self.from_high[q].astype(F32)).astype(BF16)

        @pl.when(z == LINE - 1)
        def _():
            self.up_copy(z, h).wait_recv()
            out_ref[h] = (self.own_part(z, h, side) + self.from_low[q].astype(F32)).astype(BF16)

        @pl.when((z > 0) & (z < LINE - 1))
        def _():
            self.up_copy(z, h).wait_recv()
            self.down_copy(z, h).wait_recv()
            total = self.own_part(z, h, side) + self.from_low[q].astype(F32)
            out_ref[h] = (total + self.from_high[q].astype(F32)).astype(BF16)

    def drain_gather(self):
        z = self.z

        def one(q, carry):
            c, h = lax.div(q, HALVES), lax.rem(q, HALVES)
            pl.when((z < LINE - 1) & (c <= z))(lambda: self.forward_up(c, h).wait_send())
            pl.when((z > 0) & (c >= z))(lambda: self.forward_down(c, h).wait_send())
            self.forward_side(c, h).wait_send()
            return carry

        lax.fori_loop(0, LINE * HALVES, one, 0)

    def drain(self):
        z = self.z

        def one(q, carry):
            c, h = lax.div(q, HALVES), lax.rem(q, HALVES)
            pl.when((z < LINE - 1) & (c <= z))(lambda: self.forward_up(c, h).wait_send())
            pl.when((z > 0) & (c >= z))(lambda: self.forward_down(c, h).wait_send())
            self.forward_side(c, h).wait_send()
            self.side_copy(c, h).wait_send()
            pl.when(c > z)(lambda: self.up_copy(c, h).wait_send())
            pl.when(c < z)(lambda: self.down_copy(c, h).wait_send())
            return carry

        lax.fori_loop(0, LINE * HALVES, one, 0)


def plane_scratch(rows, width, wide):
    count = LINE * HALVES
    block = pltpu.VMEM((count, rows // HALVES, width), BF16)
    return [
        pltpu.VMEM((LINE * SIDE * rows, wide), BF16),
        pltpu.VMEM((LINE * SIDE * rows, width), BF16),
        block, block, block, block,
        pltpu.SemaphoreType.DMA((3, count)),
        pltpu.SemaphoreType.DMA((count, SIDE)),
        pltpu.SemaphoreType.DMA((count,)),
        pltpu.SemaphoreType.DMA((count,)),
        pltpu.SemaphoreType.DMA((count,)),
        pltpu.SemaphoreType.DMA((count,)),
        pltpu.SemaphoreType.DMA((count,)),
    ]


def lane_tile(at, size=TILE):
    return pl.ds(pl.multiple_of(at * size, size), size)


def nn(a, b):
    return jnp.dot(a, b, preferred_element_type=F32)


def nt(a, b):
    return lax.dot_general(a, b, (((1,), (1,)), ((), ())), preferred_element_type=F32)


def tn(a, b):
    return lax.dot_general(a, b, (((0,), (0,)), ((), ())), preferred_element_type=F32)


def pick_lane(block, wanted):
    lane = lax.broadcasted_iota(jnp.int32, block.shape, 1)
    hot = lane == wanted[0]
    for other in wanted[1:]:
        hot = hot | (lane == other)
    return jnp.sum(jnp.where(hot, block, 0.0), axis=1, keepdims=True)


def own_gates(block, owner, experts):
    block = block.astype(F32)
    return [
        pick_lane(block, (owner * EXP_DEV + j, experts + owner * EXP_DEV + j)) for j in range(EXP_DEV)
    ]


def load_layer(layer, sec, own, other, dst, sem):
    copies = [pltpu.make_async_copy(own, dst, sem), pltpu.make_async_copy(other, dst, sem)]
    pl.when(sec == layer)(lambda: copies[0].start())
    pl.when(sec != layer)(lambda: copies[1].start())
    return copies[0]


def load_experts(layer, sec, gu, gu_other, down, down_other, gu_v, down_v, sems):
    loads = [load_layer(layer, sec, gu, gu_other, gu_v, sems.at[0])]
    for j in range(EXP_DEV):
        loads.append(load_layer(
            layer, sec, down.at[j], down_other.at[j], down_v.at[pl.ds(j * FF, FF)], sems.at[1 + j]))
    return loads


def moe_forward_kernel(layer, experts, rows, width, block_ref, h1_ref, gu_hbm, gu_other, down_hbm, down_other,
                       moe_ref, out_ref, rows_hbm, kept_hbm, scaled_hbm,
                       gu_v, down_v, kept, scaled, load_sem, store_sem, *plane_refs):
    plane = Plane(rows, plane_refs)
    gathered, parts = plane.gathered, plane.parts
    loads = load_experts(layer, plane.sec, gu_hbm, gu_other, down_hbm, down_other, gu_v, down_v, load_sem)
    plane.place(block_ref)
    plane.barrier()
    plane.start_gather()
    for load in loads:
        load.wait()

    def stores(c, h):
        q, at = c * HALVES + h, plane.chunk(c, h)
        return [
            pltpu.make_async_copy(gathered.at[at], rows_hbm.at[at], store_sem.at[0, q]),
            pltpu.make_async_copy(kept.at[at], kept_hbm.at[at], store_sem.at[1, q]),
            pltpu.make_async_copy(scaled.at[at], scaled_hbm.at[at], store_sem.at[2, q]),
        ]

    def step(k, carry):
        t, h = lax.div(k, HALVES), lax.rem(k, HALVES)
        plane.relay(t, h)
        plane.pass_sum(t, h)
        pl.when(t > 0)(lambda: work(chunk_order(plane.z, t - 1), h))
        return carry

    def work(c, h):
        at = plane.chunk(c, h)
        plane.wait_side_block(c, h)
        gates = own_gates(gathered[at, pl.ds(width, LANES)], plane.owner, experts)
        for j in range(EXP_DEV):
            for f in range(FF // TILE):
                data = gathered[at, pl.ds(0, width)]
                low, high = j * 2 * FF + f * TILE, j * 2 * FF + FF + f * TILE
                g = nn(data, gu_v[j, :, pl.ds(f * TILE, TILE)])
                u = nn(data, gu_v[j, :, pl.ds(FF + f * TILE, TILE)])
                z = g * jax.nn.sigmoid(g) * u * gates[j]
                scaled[at, pl.ds(j * FF + f * TILE, TILE)] = z.astype(BF16)
                kept[at, pl.ds(low, TILE)] = g.astype(BF16)
                kept[at, pl.ds(high, TILE)] = u.astype(BF16)
        for n in range(width // TILE):
            parts[at, pl.ds(n * TILE, TILE)] = nn(
                scaled[at, :], down_v[:, pl.ds(n * TILE, TILE)]).astype(BF16)
        plane.side_copy(c, h).start()
        for store in stores(c, h):
            store.start()

    lax.fori_loop(0, (LINE + 1) * HALVES, step, 0)

    def tail(k, carry):
        plane.pass_sum(lax.div(k, HALVES), lax.rem(k, HALVES))
        return carry

    lax.fori_loop((LINE + 1) * HALVES, (LINE + 3) * HALVES, tail, 0)

    def finish(h, carry):
        plane.finish_sum(h, moe_ref)
        return carry

    lax.fori_loop(0, HALVES, finish, 0)
    out_ref[...] = (h1_ref[...] + moe_ref[...]).astype(out_ref.dtype)
    plane.drain()

    def stored(q, carry):
        for store in stores(lax.div(q, HALVES), lax.rem(q, HALVES)):
            store.wait()
        return carry

    lax.fori_loop(0, LINE * HALVES, stored, 0)


def moe_forward(layer, block, h1, weights, experts, out_type, collective_id):
    rows, wide = block.shape
    width = wide - LANES
    total = LINE * SIDE * rows
    any_spec = pl.BlockSpec(memory_space=pl.ANY)
    vmem = pl.BlockSpec(memory_space=pltpu.VMEM)
    return pl.pallas_call(
        functools.partial(moe_forward_kernel, layer, experts, rows, width),
        name="moe_forward",
        out_shape=(
            jax.ShapeDtypeStruct((rows, width), F32),
            jax.ShapeDtypeStruct((rows, width), out_type),
            jax.ShapeDtypeStruct((total, wide), BF16),
            jax.ShapeDtypeStruct((total, EXP_DEV * 2 * FF), BF16),
            jax.ShapeDtypeStruct((total, EXP_DEV * FF), BF16),
        ),
        in_specs=[vmem] * 2 + [any_spec] * 4,
        out_specs=(vmem, vmem, any_spec, any_spec, any_spec),
        scratch_shapes=[
            pltpu.VMEM((EXP_DEV, width, 2 * FF), BF16),
            pltpu.VMEM((EXP_DEV * FF, width), BF16),
            pltpu.VMEM((total, EXP_DEV * 2 * FF), BF16),
            pltpu.VMEM((total, EXP_DEV * FF), BF16),
            pltpu.SemaphoreType.DMA((1 + EXP_DEV,)),
            pltpu.SemaphoreType.DMA((3, LINE * HALVES)),
        ] + plane_scratch(rows, width, wide),
        cost_estimate=COST,
        compiler_params=pltpu.CompilerParams(
            collective_id=collective_id, has_side_effects=True, vmem_limit_bytes=VMEM_BYTES),
    )(block, h1, *weights)


def moe_backward_kernel(layer, experts, rows, width, beside, dout_ref, moe_ref, s0, s1, s2, s3, gu_hbm, gu_other, down_hbm,
                        down_other, rows_hbm, kept_hbm, scaled_hbm, *refs):
    (later, refs) = (refs[:4], refs[4:]) if beside else ((), refs)
    (db_ref, keep_gu_hbm, keep_down_hbm, send_gu_hbm, send_down_hbm, grad_router_ref), refs = refs[:6], refs[6:]
    (later_out, refs) = (refs[:4], refs[4:]) if beside else ((), refs)
    (gu_v, down_v, fwd_rows, kept, scaled, dgu, send_gu, grad_gu, send_down, grad_down, router,
     load_sem, store_sem), refs = refs[:13], refs[13:]
    (later_v, refs) = (refs[:8], refs[8:]) if beside else ((), refs)
    plane_refs = refs
    plane = Plane(rows, plane_refs)
    gathered, parts = plane.gathered, plane.parts
    if beside:
        other_layer = LaterExperts(plane, *later, *later_out, *later_v)
        other_layer.start_loads()
    loads = load_experts(layer, plane.sec, gu_hbm, gu_other, down_hbm, down_other, gu_v, down_v, load_sem)
    loads.append(pltpu.make_async_copy(rows_hbm, fwd_rows, load_sem.at[3]))
    loads.append(pltpu.make_async_copy(kept_hbm, kept, load_sem.at[4]))
    loads.append(pltpu.make_async_copy(scaled_hbm, scaled, load_sem.at[5]))
    for load in loads[3:]:
        load.start()
    dout = dout_ref[...]
    outer = jnp.sum(dout.astype(F32) * moe_ref[...], axis=1, keepdims=True)
    top = outer.astype(BF16).astype(F32)
    lane = lax.broadcasted_iota(jnp.int32, (rows, LANES), 1)
    terms = (jnp.where(lane == 0, top, 0.0) + jnp.where(lane == 1, outer - top, 0.0)).astype(BF16)
    for h in range(HALVES):
        at, part = plane.block(plane.z, h, plane.x), slice(h * plane.sub, (h + 1) * plane.sub)
        gathered[at, pl.ds(0, width)] = dout[part]
        gathered[at, pl.ds(width, LANES)] = terms[part]
    for j, part in enumerate(layer_rows(layer, plane.sec, plane.shard, (s0, s1, s2, s3))):
        router[:, pl.ds(j * (width // 2), width // 2)] = part[:experts]
    plane.barrier(*([plane.other_core(), plane.other_shard()] if beside else []))
    plane.start_gather()
    if beside:
        other_layer.start_copies()
        other_layer.send()
    for load in loads:
        load.wait()
    total = plane.both
    up_at = EXP_DEV * 2 * FF

    def step(k, carry):
        t, h = lax.div(k, HALVES), lax.rem(k, HALVES)
        plane.relay(t, h)
        plane.pass_sum(t, h)
        pl.when(t > 0)(lambda: work(chunk_order(plane.z, t - 1), h))
        return carry

    def work(c, h):
        at = plane.chunk(c, h)
        plane.wait_side_block(c, h)
        gates = own_gates(fwd_rows[at, pl.ds(width, LANES)], plane.owner, experts)
        outer = jnp.sum(gathered[at, pl.ds(width, LANES)].astype(F32), axis=1, keepdims=True)
        dcs = []
        for j in range(EXP_DEV):
            dgate = jnp.zeros((total, 1), F32)
            for f in range(FF // TILE):
                low, high = pl.ds(j * 2 * FF + f * TILE, TILE), pl.ds(j * 2 * FF + FF + f * TILE, TILE)
                dz = nt(gathered[at, pl.ds(0, width)], down_v[pl.ds(j * FF + f * TILE, TILE), :])
                g = kept[at, low].astype(F32)
                u = kept[at, high].astype(F32)
                sig = jax.nn.sigmoid(g)
                silu = g * sig
                dgate = dgate + jnp.sum(dz * silu * u, axis=1, keepdims=True)
                dz = dz * gates[j]
                dgu[at, low] = (dz * u * sig * (1.0 + g * (1.0 - sig))).astype(BF16)
                dgu[at, high] = (dz * silu).astype(BF16)
            dcs.append(gates[j] * (dgate - outer))
        lane = lax.broadcasted_iota(jnp.int32, (total, LANES), 1)
        extra = jnp.zeros((total, LANES), F32)
        for j in range(EXP_DEV):
            top = dcs[j].astype(BF16).astype(F32)
            column = plane.owner * EXP_DEV + j
            extra = extra + jnp.where(lane == column, top, 0.0)
            extra = extra + jnp.where(lane == LANES // 2 + column, dcs[j] - top, 0.0)
        dgu[at, pl.ds(up_at, LANES)] = extra.astype(BF16)
        for n in range(width // TILE):
            cols = pl.ds(n * TILE, TILE)
            acc = nt(dgu[at, pl.ds(0, 2 * FF)], gu_v[0, cols, :])
            for j in range(1, EXP_DEV):
                acc = acc + nt(dgu[at, pl.ds(j * 2 * FF, 2 * FF)], gu_v[j, cols, :])
            for j in range(EXP_DEV):
                acc = acc + dcs[j] * router[pl.ds(plane.owner * EXP_DEV + j, 1), cols]
            parts[at, cols] = acc.astype(BF16)
        plane.side_copy(c, h).start()

    lax.fori_loop(0, (LINE + 1) * HALVES, step, 0)

    core = plane.sec
    gu_steps, down_steps = width // TILE, FF // TILE

    def stores_gu(n):
        at = lane_tile(n)
        return [pltpu.make_async_copy(send_gu.at[at], send_gu_hbm.at[at], store_sem.at[0, n]),
                pltpu.make_async_copy(grad_gu.at[at], keep_gu_hbm.at[at], store_sem.at[1, n])]

    def stores_down(n):
        at = lane_tile(n)
        return [pltpu.make_async_copy(send_down.at[at], send_down_hbm.at[at], store_sem.at[2, n]),
                pltpu.make_async_copy(grad_down.at[at], keep_down_hbm.at[at], store_sem.at[3, n])]

    def expert_cols(j, size):
        return pl.ds(pl.multiple_of(j * size, size), size)

    def grad_gu_rows(n):
        rows_t = fwd_rows[:, lane_tile(n)]
        send_gu[lane_tile(n), :] = tn(rows_t, dgu[:, expert_cols(1 - core, 2 * FF)]).astype(BF16)
        grad_gu[lane_tile(n), :] = tn(rows_t, dgu[:, expert_cols(core, 2 * FF)]).astype(BF16)
        grad_router_ref[lane_tile(n), :] = tn(rows_t, dgu[:, pl.ds(up_at, LANES)])
        for store in stores_gu(n):
            store.start()

    def grad_down_rows(n):
        def cols(j):
            return pl.ds(pl.multiple_of(j * FF + n * TILE, TILE), TILE)

        data = gathered[:, pl.ds(0, width)]
        send_down[lane_tile(n), :] = tn(scaled[:, cols(1 - core)], data).astype(BF16)
        grad_down[lane_tile(n), :] = tn(scaled[:, cols(core)], data).astype(BF16)
        for store in stores_down(n):
            store.start()

    slots = 2 * HALVES

    def tail(k, carry):
        pl.loop(lax.div(k * gu_steps, slots), lax.div((k + 1) * gu_steps, slots))(grad_gu_rows)
        plane.pass_sum(LINE + 1 + lax.div(k, HALVES), lax.rem(k, HALVES))
        return carry

    lax.fori_loop(0, slots, tail, 0)
    pl.loop(0, down_steps)(grad_down_rows)

    def finish(h, carry):
        plane.finish_sum(h, db_ref)
        return carry

    lax.fori_loop(0, HALVES, finish, 0)
    if beside:
        other_layer.finish()
    plane.drain()
    for n in range(gu_steps):
        for store in stores_gu(n):
            store.wait()
    for n in range(down_steps):
        for store in stores_down(n):
            store.wait()


def layer_rows(layer, sec, shard, refs):
    own, sideways, across, diagonal = (ref[...].astype(F32) for ref in refs)
    mine = jnp.where(sec == layer, own, across)
    others = jnp.where(sec == layer, sideways, diagonal)
    return jnp.where(shard == 0, mine, others), jnp.where(shard == 0, others, mine)


class LaterExperts:
    def __init__(self, plane, keep_gu, keep_down, send_gu, send_down, sum_gu_hbm, sum_down_hbm, land_gu, land_down,
                 gu_a, gu_b, down_a, down_b, load_sem, core_sem, send_sem, recv_sem):
        self.parts = []
        for keep, sent, out, land, a, b, count in (
            (keep_gu, send_gu, sum_gu_hbm, land_gu, gu_a, gu_b, 4),
            (keep_down, send_down, sum_down_hbm, land_down, down_a, down_b, 2),
        ):
            size = a.shape[0] // count
            for n in range(count):
                at, k = pl.ds(n * size, size), len(self.parts)
                shard_copy = land_copy = None
                if k < LATER_CROSS:
                    shard_copy = pltpu.make_async_remote_copy(
                        src_ref=a.at[at], dst_ref=land.at[at], send_sem=send_sem.at[k], recv_sem=recv_sem.at[k],
                        device_id=plane.other_shard(), device_id_type=MESH)
                    land_copy = pltpu.make_async_copy(land.at[at], b.at[at], load_sem.at[1, k])
                self.parts.append((
                    a.at[at], b.at[at],
                    pltpu.make_async_copy(keep.at[at], a.at[at], load_sem.at[0, k]),
                    pltpu.make_async_remote_copy(
                        src_ref=sent.at[at], dst_ref=b.at[at], send_sem=core_sem.at[0, k],
                        recv_sem=core_sem.at[1, k], device_id=plane.other_core(), device_id_type=MESH),
                    shard_copy, land_copy,
                    pltpu.make_async_copy(a.at[at], out.at[at], load_sem.at[2, k]),
                ))

    def start_loads(self):
        for _, _, load, *_ in self.parts:
            load.start()

    def start_copies(self):
        for _, _, _, core_copy, *_ in self.parts:
            core_copy.start()

    def send(self):
        for a, b, load, core_copy, shard_copy, _, store in self.parts:
            load.wait()
            core_copy.wait()
            a[...] = (a[...].astype(F32) + b[...].astype(F32)).astype(BF16)
            if shard_copy is not None:
                shard_copy.start()
            else:
                store.start()

    def finish(self):
        for _, _, _, _, shard_copy, land_copy, _ in self.parts:
            if shard_copy is not None:
                shard_copy.wait()
                land_copy.start()
        for a, b, _, _, shard_copy, land_copy, store in self.parts:
            if shard_copy is not None:
                land_copy.wait()
                a[...] = (a[...].astype(F32) + b[...].astype(F32)).astype(BF16)
                store.start()
        for *_, store in self.parts:
            store.wait()


def moe_backward(layer, dout, moe, small, weights, kept, later, experts, collective_id):
    rows, width = dout.shape
    wide = width + LANES
    total = LINE * SIDE * rows
    any_spec = pl.BlockSpec(memory_space=pl.ANY)
    vmem = pl.BlockSpec(memory_space=pltpu.VMEM)
    expert_gu, expert_down = pltpu.VMEM((width, 2 * FF), BF16), pltpu.VMEM((FF, width), BF16)
    gu_shape = jax.ShapeDtypeStruct((width, 2 * FF), BF16)
    down_shape = jax.ShapeDtypeStruct((FF, width), BF16)
    later_out, later_scratch = (), []
    if later:
        later_out = (gu_shape, down_shape) * 2
        later_scratch = [
            expert_gu, expert_gu, expert_down, expert_down,
            pltpu.SemaphoreType.DMA((3, 6)), pltpu.SemaphoreType.DMA((2, 6)),
            pltpu.SemaphoreType.DMA((LATER_CROSS,)), pltpu.SemaphoreType.DMA((LATER_CROSS,)),
        ]
    return pl.pallas_call(
        functools.partial(moe_backward_kernel, layer, experts, rows, width, bool(later)),
        name="moe_backward",
        out_shape=(
            jax.ShapeDtypeStruct((rows, width), F32),
            gu_shape, down_shape, gu_shape, down_shape,
            jax.ShapeDtypeStruct((width, LANES), F32),
        ) + later_out,
        in_specs=[vmem] * 6 + [any_spec] * (7 + len(later)),
        out_specs=(vmem,) + (any_spec,) * 4 + (vmem,) + (any_spec,) * len(later_out),
        scratch_shapes=[
            pltpu.VMEM((EXP_DEV, width, 2 * FF), BF16),
            pltpu.VMEM((EXP_DEV * FF, width), BF16),
            pltpu.VMEM((total, wide), BF16),
            pltpu.VMEM((total, EXP_DEV * 2 * FF), BF16),
            pltpu.VMEM((total, EXP_DEV * FF), BF16),
            pltpu.VMEM((total, EXP_DEV * 2 * FF + LANES), BF16),
            expert_gu, expert_gu, expert_down, expert_down,
            pltpu.VMEM((experts, width), F32),
            pltpu.SemaphoreType.DMA((6,)),
            pltpu.SemaphoreType.DMA((4, width // TILE)),
        ] + later_scratch + plane_scratch(rows, width, wide),
        cost_estimate=COST,
        compiler_params=pltpu.CompilerParams(
            collective_id=collective_id, has_side_effects=True, vmem_limit_bytes=VMEM_BYTES),
    )(dout, moe, *small, *weights, *kept, *later)


def split_terms(values):
    high = values.astype(BF16)
    return high, (values - high.astype(F32)).astype(BF16)


def with_lanes(block, columns):
    extra = jnp.concatenate(columns, axis=1)
    extra = jnp.pad(extra, ((0, 0), (0, LANES - extra.shape[1])))
    return jnp.concatenate([block, extra], axis=1)


def far_order(z, i):
    low = jnp.where(i == 0, 3, jnp.where(i == 1, jnp.where(z == 0, 2, 0), jnp.where(z == 0, 1, 2)))
    high = jnp.where(i == 0, 0, jnp.where(i == 1, jnp.where(z == 3, 1, 3), jnp.where(z == 3, 2, 1)))
    return jnp.where(z < 2, low, high)


def remote_copy(src, dst, send_sem, recv_sem, device):
    return pltpu.make_async_remote_copy(
        src_ref=src, dst_ref=dst, send_sem=send_sem, recv_sem=recv_sem, device_id=device, device_id_type=MESH)


class GradientSum:
    def __init__(self, plane, h, cols, grad, small, core_got, small_own, small_got, load_sem, core_sem, small_sem):
        self.plane, self.h, self.cols = plane, h, cols
        self.core_got, self.small_own, self.small_got = core_got, small_own, small_got
        core, shard = plane.sec, plane.shard
        places = [(c, side) for c in range(LINE) for side in range(SIDE)]
        self.loads = [
            pltpu.make_async_copy(
                grad.at[n, core], plane.parts.at[plane.block(c, h, side), pl.ds(0, cols)], load_sem.at[n])
            for n, (c, side) in enumerate(places)
        ]
        self.loads.append(pltpu.make_async_copy(small.at[shard, :, core], small_own, load_sem.at[len(places)]))
        self.copies = [
            remote_copy(grad.at[:, 1 - core], core_got, core_sem.at[0], core_sem.at[1], plane.other_core())
        ]
        for n, (there, half, device) in enumerate((
            (shard, 1 - core, plane.other_core()),
            (1 - shard, core, plane.other_shard()),
            (1 - shard, 1 - core, self.diagonal(plane)),
        )):
            self.copies.append(remote_copy(
                small.at[there, :, half], small_got.at[n], small_sem.at[0, n], small_sem.at[1, n], device))

    @staticmethod
    def diagonal(plane):
        return (1 - plane.sec, plane.owner, 1 - plane.shard)

    def start_loads(self):
        for load in self.loads:
            load.start()

    def start_copies(self):
        for copy in self.copies:
            copy.start()

    def wait_terms(self):
        for load in self.loads:
            load.wait()
        for copy in self.copies:
            copy.wait_recv()

    def prepare(self, first, last):
        plane, h, cols = self.plane, self.h, self.cols

        def one(k, carry):
            c = jnp.where(k < 2 * (LINE - 1), far_order(plane.z, lax.div(k, 2)), plane.z)
            side = jnp.where(lax.rem(k, 2) == 0, 1 - plane.x, plane.x)
            n = c * SIDE + side
            at = plane.block(c, h, side)
            plane.parts[at, pl.ds(0, cols)] = (
                plane.parts[at, pl.ds(0, cols)].astype(F32) + self.core_got[n].astype(F32)).astype(BF16)
            total = self.small_own[n].astype(F32)
            for other in range(3):
                total = total + self.small_got[other, n].astype(F32)
            plane.parts[at, pl.ds(cols, LANES)] = total.astype(BF16)
            pl.when(side != plane.x)(lambda: plane.side_copy(c, h).start())
            return carry

        lax.fori_loop(first, last, one, 0)

    def pass_on(self, i):
        self.plane.pass_chunk(far_order(self.plane.z, i), self.h)

    def hand_over(self, out_ref):
        plane, h = self.plane, self.h
        second, third = far_order(plane.z, 1), far_order(plane.z, 2)
        plane.pass_chunk(second, h, send=False)
        out_ref[0] = plane.sums[second * HALVES + h]
        for n, c in ((1, third), (2, plane.z)):
            plane.side_copy(c, h).wait_recv()
            out_ref[n] = plane.own_part(c, h).astype(BF16)

    def drain(self, chunks=LINE - 1):
        plane, h = self.plane, self.h
        for copy in self.copies:
            copy.wait_send()

        def one(c, carry):
            plane.side_copy(c, h).wait_send()
            return carry

        lax.fori_loop(0, LINE, one, 0)
        for i in range(chunks):
            plane.wait_sent_sum(far_order(plane.z, i), h)


def sum_scratch(places, sub, cols):
    plane = plane_scratch(HALVES * sub, cols + LANES, cols + LANES)
    own = [
        pltpu.VMEM((places, sub, cols), BF16),
        pltpu.VMEM((places, sub, LANES), BF16),
        pltpu.VMEM((3, places, sub, LANES), BF16),
        pltpu.SemaphoreType.DMA((places + 1,)),
        pltpu.SemaphoreType.DMA((2,)),
        pltpu.SemaphoreType.DMA((2, 3)),
    ]
    return own, plane


def reduce_kernel(sub, cols, g0, t0, shares1, gu_hbm, down_hbm, sent_gu_hbm, sent_down_hbm, gu1_hbm, down1_hbm, tail1_hbm, dh, final,
                  sum_hbm, own_gu_hbm, own_down_hbm, got_gu_hbm, got_down_hbm, own_down1_hbm, got_gu1_hbm,
                  got_down1_hbm, got_edge,
                  core_got, small_own, small_got, load_sem, core_sem, small_sem,
                  result, own_gu, core_gu, other_gu, own_down, core_down, other_down,
                  share_sem, expert_load_sem, expert_core_sem, edge_sem, move_sem, expert_sem,
                  core_expert_sem, store_sem, *plane_refs):
    plane = Plane(HALVES * sub, plane_refs)
    gathered = plane.gathered
    core, z, x = plane.sec, plane.z, plane.x
    remote = remote_copy
    sums = GradientSum(plane, 1, cols, g0, t0, core_got, small_own, small_got, load_sem, core_sem, small_sem)
    pieces, expert_loads = [], []
    for layer, hbm, sent, own, there, other, own_hbm, got_hbm, count, first in (
        (0, gu_hbm, sent_gu_hbm, own_gu, core_gu, other_gu, own_gu_hbm, got_gu_hbm, 4, 0),
        (0, down_hbm, sent_down_hbm, own_down, core_down, other_down, own_down_hbm, got_down_hbm, 2, 0),
    ):
        size = own.shape[0] // count
        for n in range(first, count):
            at, k = pl.ds(n * size, size), len(pieces)
            pieces.append((layer, own, there, other, own_hbm, got_hbm, at))
            expert_loads.append((
                pltpu.make_async_copy(hbm.at[at], own.at[at], expert_load_sem.at[k]),
                None if sent is None else remote(
                    sent.at[at], there.at[at], expert_core_sem.at[0, k], expert_core_sem.at[1, k],
                    plane.other_core()),
            ))
    count = LINE * SIDE * HALVES
    split = tail1_hbm.shape[0]
    low, high = pl.ds(0, split), pl.ds(split, split)
    ready_copies = [
        pltpu.make_async_copy(down1_hbm.at[low], own_down1_hbm.at[low], store_sem.at[count + 6]),
        pltpu.make_async_copy(tail1_hbm, own_down1_hbm.at[high], store_sem.at[count + 7]),
    ]
    second, third = far_order(z, 1), far_order(z, 2)
    load_shares = [
        pltpu.make_async_copy(shares1.at[0], plane.sums.at[second * HALVES], share_sem.at[0]),
        pltpu.make_async_copy(shares1.at[1], plane.parts.at[plane.block(third, 0, x)], share_sem.at[1]),
        pltpu.make_async_copy(shares1.at[2], plane.parts.at[plane.block(z, 0, x)], share_sem.at[2]),
    ]
    for load in load_shares:
        load.start()
    expert_loads[0][0].start()
    sums.start_loads()
    for load, _ in expert_loads[1:]:
        load.start()
    plane.barrier(plane.other_core(), plane.other_shard(), sums.diagonal(plane))
    expert_loads[0][1].start()
    sums.start_copies()
    for _, copy in expert_loads[1:]:
        copy.start()

    def move(h):
        return remote(
            result.at[h], gathered.at[plane.block(z, core, x)], move_sem.at[0], move_sem.at[1], plane.other_core())

    def send_block(h):
        pl.when(z < LINE - 1)(lambda: plane.forward_up(z, h).start())
        pl.when(z > 0)(lambda: plane.forward_down(z, h).start())
        plane.forward_side(z, h).start()

    def begin_gather(h):
        own_layer = core == 1 - h
        pl.when(jnp.logical_not(own_layer))(lambda: move(h).start())

        @pl.when(own_layer)
        def _():
            gathered[plane.block(z, core, x)] = result[h]
            send_block(core)
            arrived = remote(
                result.at[h], gathered.at[plane.block(z, 1 - core, x)], move_sem.at[0], move_sem.at[1],
                plane.other_core())
            arrived.wait_recv()
            send_block(1 - core)

    exchange = []

    def send_piece():
        n = len(exchange)
        layer, own, there, other, own_hbm, got_hbm, at = pieces[n]
        for load in expert_loads[n]:
            if load is not None:
                load.wait()
        if there is not None:
            own[at] = (own[at].astype(F32) + there[at].astype(F32)).astype(BF16)
        exchange.append(
            remote(own.at[at], other.at[at], expert_sem.at[0, n], expert_sem.at[1, n], plane.other_shard()))
        exchange[-1].start()

    send_piece()
    for load in load_shares:
        load.wait()
    plane.send_sum(second, 0)
    edges = remote(final, got_edge, edge_sem.at[0], edge_sem.at[1], plane.other_core())
    edge_back = remote(dh, got_edge, edge_sem.at[0], edge_sem.at[1], plane.other_core())
    pl.when(core == 0)(lambda: edges.start())
    pl.when(core == 1)(lambda: edge_back.start())
    later_copies = [
        remote(gu1_hbm, got_gu1_hbm, edge_sem.at[2], edge_sem.at[3], plane.other_core()),
        remote(down1_hbm.at[low], got_down1_hbm.at[low], edge_sem.at[4], edge_sem.at[5], plane.other_core()),
        remote(tail1_hbm, got_down1_hbm.at[high], edge_sem.at[6], edge_sem.at[7], plane.other_core()),
    ]
    for copy in later_copies:
        pl.when(core == 0)(lambda copy=copy: copy.start())
    for copy in ready_copies:
        copy.start()

    def out_copy(c, h, side):
        at = pl.multiple_of(((c * SIDE + side) * HALVES + h) * sub, sub)
        return pltpu.make_async_copy(
            gathered.at[plane.block(c, h, side)], sum_hbm.at[pl.ds(at, sub)],
            store_sem.at[(c * SIDE + side) * HALVES + h])

    def gather(t):
        for turn in range(HALVES):
            h = core if turn == 0 else 1 - core
            plane.relay(t, h)
            c = chunk_order(z, t - 1)
            plane.wait_side_block(c, h)
            out_copy(c, h, x).start()
            out_copy(c, h, 1 - x).start()

    def to_core(n):
        layer, own, there, other, own_hbm, got_hbm, at = pieces[n]
        return remote(
            own.at[at], got_hbm.at[at], core_expert_sem.at[0, n], core_expert_sem.at[1, n], plane.other_core())

    def keep(n):
        layer, own, there, other, own_hbm, got_hbm, at = pieces[n]
        return pltpu.make_async_copy(own.at[at], own_hbm.at[at], store_sem.at[count + n])

    def expert_piece(n):
        layer, own, there, other, own_hbm, got_hbm, at = pieces[n]
        exchange[n].wait()
        own[at] = (own[at].astype(F32) + other[at].astype(F32)).astype(BF16)
        pl.when(core != layer)(lambda: to_core(n).start())
        keep(n).start()

    sums.wait_terms()
    sums.prepare(0, LINE)
    plane.pass_chunk(third, 0, side=False)
    send_piece()
    sums.prepare(LINE, LINE * SIDE)
    sums.pass_on(0)
    send_piece()
    plane.finish_piece(0, result, side=False)
    begin_gather(0)
    for i in range(1, LINE - 1):
        sums.pass_on(i)
        send_piece()
        pl.when(core == 1)(lambda i=i: gather(i))
    while len(exchange) < len(pieces):
        send_piece()
    plane.finish_piece(1, result)
    begin_gather(1)
    for n in range(2):
        expert_piece(n)

    @pl.when(core == 1)
    def _():
        gather(LINE - 1)
        gather(LINE)

    @pl.when(core == 0)
    def _():
        def one(t, carry):
            gather(t)
            return carry

        lax.fori_loop(1, LINE + 1, one, 0)

    for n in range(2, len(pieces)):
        expert_piece(n)
    sums.drain()
    plane.wait_sent_sum(second, 0)
    plane.wait_sent_sum(third, 0)
    plane.drain_gather()
    move(0).wait_send()

    def stored(k, carry):
        out_copy(lax.div(k, SIDE * HALVES), lax.rem(k, HALVES), lax.rem(lax.div(k, HALVES), SIDE)).wait()
        return carry

    lax.fori_loop(0, count, stored, 0)
    for n in range(len(pieces)):
        keep(n).wait()
        pl.when(core != pieces[n][0])(lambda n=n: to_core(n).wait_send())
        pl.when(core == pieces[n][0])(lambda n=n: to_core(n).wait_recv())
    edges.wait()
    for copy in ready_copies:
        copy.wait()
    for copy in later_copies:
        pl.when(core == 0)(lambda copy=copy: copy.wait_send())
        pl.when(core == 1)(lambda copy=copy: copy.wait_recv())


def reduce_gradients(g0, t0, shares1, experts0, gu1, down1, tail1, dh, final, collective_id):
    places, halves, sub, cols = g0.shape
    grad_gu, grad_down = experts0[:2]
    any_spec = pl.BlockSpec(memory_space=pl.ANY)
    wide = cols + LANES
    gu, down = jax.ShapeDtypeStruct(grad_gu.shape, BF16), jax.ShapeDtypeStruct(grad_down.shape, BF16)
    gu_v, down_v = pltpu.VMEM(grad_gu.shape, BF16), pltpu.VMEM(grad_down.shape, BF16)
    own, plane = sum_scratch(places, sub, cols)
    return pl.pallas_call(
        functools.partial(reduce_kernel, sub, cols),
        name="reduce_gradients",
        out_shape=(
            jax.ShapeDtypeStruct((places * halves * sub, wide), BF16), gu, down, gu, down, down, gu, down,
            jax.ShapeDtypeStruct(dh.shape, dh.dtype),
        ),
        in_specs=[any_spec] * 12,
        out_specs=(any_spec,) * 9,
        scratch_shapes=own + [
            pltpu.VMEM((2, sub, wide), BF16),
            gu_v, gu_v, gu_v, down_v, down_v, down_v,
            pltpu.SemaphoreType.DMA((3,)),
            pltpu.SemaphoreType.DMA((6,)),
            pltpu.SemaphoreType.DMA((2, 6)),
            pltpu.SemaphoreType.DMA((8,)),
            pltpu.SemaphoreType.DMA((2,)),
            pltpu.SemaphoreType.DMA((2, 6)),
            pltpu.SemaphoreType.DMA((2, 6)),
            pltpu.SemaphoreType.DMA((places * halves + 8,)),
        ] + plane,
        compiler_params=pltpu.CompilerParams(
            collective_id=collective_id, has_side_effects=True, vmem_limit_bytes=VMEM_BYTES),
    )(g0, t0, shares1, *experts0, gu1, down1, tail1, dh, final)


def finish_kernel(qkv_cols, attn, gu_own, gu_got, gu_one, gu_moved, down_own, down_got, down_one, down_moved,
                  qkv_hbm, out_hbm, gu_hbm, down_hbm, attn_v, gu_v, down_v, qkv_f, out_f, gu_f, down_f,
                  load_sem, store_sem):
    core = lax.axis_index("section")
    steps = []

    def chunks(rows, count):
        return [pl.ds(n * (rows // count), rows // count) for n in range(count)]

    def choose(zero, one, dst, sem):
        copies = [pltpu.make_async_copy(zero, dst, sem), pltpu.make_async_copy(one, dst, sem)]
        pl.when(core == 0)(lambda: copies[0].start())
        pl.when(core == 1)(lambda: copies[1].start())
        return copies[0]

    def add(load, convert, stores):
        steps.append((load, convert, stores))

    def store(src, dst, n):
        return pltpu.make_async_copy(src, dst, store_sem.at[n])

    stored = 0
    for j, (zero, one) in enumerate(((gu_own, gu_moved), (gu_got, gu_one))):
        for at in chunks(gu_f.shape[1], 6):
            def convert(j=j, at=at):
                gu_f[j, at, :] = gu_v[j, at, :].astype(F32)

            load = choose(zero.at[at], one.at[at], gu_v.at[j, at], load_sem.at[len(steps)])
            add(load, convert, [store(gu_f.at[j, at], gu_hbm.at[j, at], stored)])
            stored += 1
    for j, (zero, one) in enumerate(((down_own, down_moved), (down_got, down_one))):
        for at in chunks(down_f.shape[1], 2):
            def convert(j=j, at=at):
                down_f[j, at, :] = down_v[j, at, :].astype(F32)

            load = choose(zero.at[at], one.at[at], down_v.at[j, at], load_sem.at[len(steps)])
            add(load, convert, [store(down_f.at[j, at], down_hbm.at[j, at], stored)])
            stored += 1
    for at in chunks(attn_v.shape[0], 8):
        def convert(at=at):
            qkv_f[at, :] = attn_v[at, pl.ds(0, qkv_cols)].astype(F32)
            out_f[at, :] = attn_v[at, pl.ds(qkv_cols, out_f.shape[1])].astype(F32)

        load = pltpu.make_async_copy(attn.at[at, pl.ds(0, attn_v.shape[1])], attn_v.at[at], load_sem.at[len(steps)])
        load.start()
        add(load, convert, [
            store(qkv_f.at[at], qkv_hbm.at[at], stored), store(out_f.at[at], out_hbm.at[at], stored + 1)])
        stored += 2
    for load, convert, stores in steps:
        load.wait()
        convert()
        for copy in stores:
            copy.start()
    for load, convert, stores in steps:
        for copy in stores:
            copy.wait()


def finish_outputs(attn, gus, downs, qkv_cols, out_cols):
    rows = attn.shape[0]
    gu, down = (EXP_DEV,) + gus[0].shape, (EXP_DEV,) + downs[0].shape
    any_spec = pl.BlockSpec(memory_space=pl.ANY)
    return pl.pallas_call(
        functools.partial(finish_kernel, qkv_cols),
        name="finish_outputs",
        out_shape=(
            jax.ShapeDtypeStruct((rows, qkv_cols), F32),
            jax.ShapeDtypeStruct((rows, out_cols), F32),
            jax.ShapeDtypeStruct(gu, F32),
            jax.ShapeDtypeStruct(down, F32),
        ),
        in_specs=[any_spec] * 9,
        out_specs=(any_spec,) * 4,
        scratch_shapes=[
            pltpu.VMEM((rows, qkv_cols + out_cols), BF16),
            pltpu.VMEM(gu, BF16),
            pltpu.VMEM(down, BF16),
            pltpu.VMEM((rows, qkv_cols), F32),
            pltpu.VMEM((rows, out_cols), F32),
            pltpu.VMEM(gu, F32),
            pltpu.VMEM(down, F32),
            pltpu.SemaphoreType.DMA((24,)),
            pltpu.SemaphoreType.DMA((32,)),
        ],
        compiler_params=pltpu.CompilerParams(vmem_limit_bytes=VMEM_BYTES),
    )(attn, *gus, *downs)


PAIRS = 2
GROUP = QUERY_HEADS // KEY_VALUE_HEADS
SCALE = HEAD_SIZE ** (-0.5)


class Pair:
    def __init__(self):
        self.sec, self.owner, self.me = (lax.axis_index(n) for n in ("section", "expert", "shard"))
        self.peer = 1 - self.me

    def barrier(self, with_core=False):
        sem = pltpu.get_barrier_semaphore()
        pl.semaphore_signal(
            sem, inc=1, device_id=(self.sec, self.owner, self.peer), device_id_type=MESH)
        if with_core:
            pl.semaphore_signal(
                sem, inc=1, device_id=(1 - self.sec, self.owner, self.me), device_id_type=MESH)
        pl.semaphore_wait(sem, 1 + with_core)

    def send(self, src, dst, send_sem, recv_sem):
        return pltpu.make_async_remote_copy(
            src_ref=src, dst_ref=dst, send_sem=send_sem, recv_sem=recv_sem,
            device_id=(self.sec, self.owner, self.peer), device_id_type=MESH)


def head_columns(shard):
    kv_pair = KEY_VALUE_HEADS // 2 // PAIRS * HEAD_SIZE
    q_pair = kv_pair * GROUP
    wide = q_pair + 2 * kv_pair
    spans = []
    for i in range(PAIRS):
        at = shard * PAIRS + i
        spans.append((at * q_pair, i * wide, q_pair))
        spans.append((QUERY_WIDTH + at * kv_pair, i * wide + q_pair, kv_pair))
        spans.append((QUERY_WIDTH + KV_WIDTH + at * kv_pair, i * wide + q_pair + kv_pair, kv_pair))
    return spans


def head_at(i, n, g):
    kv_pair = KEY_VALUE_HEADS // 2 // PAIRS * HEAD_SIZE
    q_pair = kv_pair * GROUP
    base = i * (q_pair + 2 * kv_pair)
    return (
        pl.ds(base + (n * GROUP + g) * HEAD_SIZE, HEAD_SIZE),
        pl.ds(base + q_pair + n * HEAD_SIZE, HEAD_SIZE),
        pl.ds(base + q_pair + kv_pair + n * HEAD_SIZE, HEAD_SIZE),
    )


KV_IN_PAIR = KEY_VALUE_HEADS // 2 // PAIRS


def load_attention(layer, sec, wq, wq_other, wo, wo_other, wq_v, wo_v, sems):
    loads = []
    for j in range(2):
        for at, local, size in head_columns(j):
            loads.append(load_layer(
                layer, sec, wq.at[:, pl.ds(at, size)], wq_other.at[:, pl.ds(at, size)],
                wq_v.at[j, :, pl.ds(local, size)], sems.at[len(loads)]))
    loads.append(load_layer(layer, sec, wo, wo_other, wo_v, sems.at[len(loads)]))
    return loads


LOADS = 2 * PAIRS * 3 + 1


def attention_forward_kernel(layer, experts, rows, width, lens_ref, h_ref, s0, s1, s2, s3, routes_own, routes_other, wq,
                             wq_other,
                             wo, wo_other, block_ref, h1_ref, a_ref, qkv_ref, p_ref, o_ref,
                             small_v, router_v, wq_v, wo_v, a_parts, a_half, part_send, got_part, out_send, got_out,
                             load_sem, send_sem, recv_sem, *turn):
    pair = Pair()
    me, peer = pair.me, pair.peer
    half = width // 2
    loads = load_attention(layer, pair.sec, wq, wq_other, wo, wo_other, wq_v, wo_v, load_sem)
    pair.barrier(bool(turn))

    def span(who):
        return pl.ds(pl.multiple_of(who * rows, rows), rows)

    h = h_ref[...].astype(F32)
    r1 = lax.rsqrt(jnp.mean(h * h, axis=1, keepdims=True) + EPS)
    for j, part in enumerate(layer_rows(layer, pair.sec, me, (s0, s1, s2, s3))):
        small_v[:, pl.ds(j * half, half)] = part
    gains = small_v[pl.ds(experts, 2)]
    a = (h * r1 * gains[0:1]).astype(BF16)
    for j in range(2):
        a_parts[j] = a[:, j * half : (j + 1) * half]
    a_half[span(me)] = a_parts[me]
    for load in loads[:-1]:
        load.wait()
    part_send[span(me)] = nn(a_parts[me], wq_v[peer]).astype(BF16)
    if turn:
        pl.when(pair.sec == 0)(lambda: pl.semaphore_wait(turn[0], 1))
    send_a = pair.send(a_parts.at[peer], a_half.at[span(me)], send_sem.at[0], recv_sem.at[0])
    send_a.start()
    send_own = pair.send(part_send.at[span(me)], got_part.at[span(me)], send_sem.at[1], recv_sem.at[1])
    send_own.start()
    send_a.wait_recv()
    part_send[span(peer)] = nn(a_half[span(peer)], wq_v[peer]).astype(BF16)
    send_other = pair.send(
        part_send.at[span(peer)], got_part.at[span(peer)], send_sem.at[2], recv_sem.at[2])
    send_other.start()
    mine = nn(a_half[...], wq_v[me])
    a_ref[...] = a_half[...]
    send_own.wait_recv()
    send_other.wait_recv()
    qkv_ref[...] = (mine + got_part[...].astype(F32)).astype(BF16)
    query = lax.broadcasted_iota(jnp.int32, (2 * rows, 2 * rows), 0)
    key = lax.broadcasted_iota(jnp.int32, (2 * rows, 2 * rows), 1)
    allowed = key <= query
    end = 0
    for n in range(lens_ref.shape[0]):
        end = end + lens_ref[n]
        allowed = allowed & ((query >= end) == (key >= end))
    for i in range(PAIRS):
        for n in range(KV_IN_PAIR):
            for g in range(GROUP):
                q_at, k_at, v_at = head_at(i, n, g)
                j = (i * KV_IN_PAIR + n) * GROUP + g
                s = nt(qkv_ref[:, q_at], qkv_ref[:, k_at]) * SCALE
                s = jnp.where(allowed, s, MASKED_SCORE)
                ex = jnp.exp(s - jnp.max(s, axis=1, keepdims=True))
                p = (ex / jnp.sum(ex, axis=1, keepdims=True)).astype(BF16)
                p_ref[j] = p
                o_ref[:, pl.ds(j * HEAD_SIZE, HEAD_SIZE)] = nn(p, qkv_ref[:, v_at]).astype(BF16)
    loads[-1].wait()
    out_send[...] = nn(o_ref[span(peer)], wo_v[...]).astype(BF16)
    send_out = pair.send(out_send, got_out, send_sem.at[3], recv_sem.at[3])
    send_out.start()
    own = nn(o_ref[span(me)], wo_v[...])
    send_out.wait_recv()
    if turn:
        @pl.when(pair.sec == 1)
        def _():
            pl.semaphore_signal(
                turn[0], inc=1, device_id=(1 - pair.sec, pair.owner, me), device_id_type=MESH)

    h1 = h + own + got_out[...].astype(F32)
    h1_ref[...] = h1
    r2 = lax.rsqrt(jnp.mean(h1 * h1, axis=1, keepdims=True) + EPS)
    b = (h1 * r2 * gains[1:2]).astype(BF16)
    block_ref[:, pl.ds(0, width)] = b
    router_v[...] = jnp.zeros_like(router_v)
    for copy in range(2):
        router_v[pl.ds(copy * experts, experts)] = small_v[pl.ds(0, experts)].astype(BF16)
    lane = lax.broadcasted_iota(jnp.int32, (rows, LANES), 1)
    column = jnp.where(lane < experts, lane, lane - experts)
    routes = jnp.where(pair.sec == layer, routes_own[...], routes_other[...])
    mask = routes[:, 0:1] == column
    for n in range(1, TOP):
        mask = mask | (routes[:, n : n + 1] == column)
    mask = mask & (lane < 2 * experts)
    logits = jnp.where(mask, nt(b, router_v[...]), MASKED_SCORE)
    ex = jnp.where(mask, jnp.exp(logits - jnp.max(logits, axis=1, keepdims=True)), 0.0)
    gates = ex / (0.5 * jnp.sum(ex, axis=1, keepdims=True))
    high = gates.astype(BF16).astype(F32)
    block_ref[:, pl.ds(width, LANES)] = jnp.where(lane >= experts, gates - high, high).astype(BF16)
    for send in (send_a, send_own, send_other, send_out):
        send.wait_send()


def attention_forward(layer, experts, lens, h, small, routes, weights, collective_id):
    rows, width = h.shape
    half, group = width // 2, 2 * rows
    qkv = (QUERY_WIDTH + 2 * KV_WIDTH) // 2
    heads = QUERY_HEADS // 2
    any_spec = pl.BlockSpec(memory_space=pl.ANY)
    vmem = pl.BlockSpec(memory_space=pltpu.VMEM)
    return pl.pallas_call(
        functools.partial(attention_forward_kernel, layer, experts, rows, width),
        name="attention_forward",
        out_shape=(
            jax.ShapeDtypeStruct((rows, width + LANES), BF16),
            jax.ShapeDtypeStruct((rows, width), F32),
            jax.ShapeDtypeStruct((group, half), BF16),
            jax.ShapeDtypeStruct((group, qkv), BF16),
            jax.ShapeDtypeStruct((heads, group, group), BF16),
            jax.ShapeDtypeStruct((group, QUERY_WIDTH // 2), BF16),
        ),
        in_specs=[pl.BlockSpec(memory_space=pltpu.SMEM)] + [vmem] * 7 + [any_spec] * 4,
        out_specs=(vmem,) * 6,
        scratch_shapes=[
            pltpu.VMEM((experts + 2, width), F32),
            pltpu.VMEM((LANES, width), BF16),
            pltpu.VMEM((2, half, qkv), BF16),
            pltpu.VMEM((QUERY_WIDTH // 2, width), BF16),
            pltpu.VMEM((2, rows, half), BF16),
            pltpu.VMEM((group, half), BF16),
            pltpu.VMEM((group, qkv), BF16),
            pltpu.VMEM((group, qkv), BF16),
            pltpu.VMEM((rows, width), BF16),
            pltpu.VMEM((rows, width), BF16),
            pltpu.SemaphoreType.DMA((LOADS,)),
            pltpu.SemaphoreType.DMA((4,)),
            pltpu.SemaphoreType.DMA((4,)),
        ] + ([pltpu.SemaphoreType.REGULAR] if layer == 0 else []),
        cost_estimate=COST,
        compiler_params=pltpu.CompilerParams(
            collective_id=collective_id, has_side_effects=True, vmem_limit_bytes=VMEM_BYTES),
    )(lens, h, *small, *routes, *weights)


ATTENTION_BACKWARD_REFS = 20


def attention_backward_kernel(layer, rows, width, experts, router_grad_ref, db_ref, dout_ref, h1_ref, h_ref, s0, s1, s2, s3, a_ref, qkv_ref,
                              p_ref, o_ref, wq, wq_other, wo, wo_other, *refs):
    beside = len(refs) > ATTENTION_BACKWARD_REFS
    (later, refs) = (refs[:3], refs[3:]) if beside else ((), refs)
    (dh_ref, columns_ref, grad_hbm), refs = refs[:3], refs[3:]
    (later_out, refs) = (refs[:2], refs[2:]) if beside else ((), refs)
    (wq_v, wo_v, d_all, do, dqkv, got_dqkv, da_send, got_da, dh1_v, grad_q, grad_o,
     gain_grads_ref, columns_v, load_sem, store_sem, send_sem, recv_sem), refs = refs[:17], refs[17:]
    pair = Pair()
    me, peer = pair.me, pair.peer
    half = width // 2
    qkv_cols = dqkv.shape[1]
    pair_cols = qkv_cols // PAIRS
    loads = load_attention(layer, pair.sec, wq, wq_other, wo, wo_other, wq_v, wo_v, load_sem)
    if beside:
        sub, cols_all = later[0].shape[2:]
        plane = Plane(HALVES * sub, (None,) + tuple(refs[10:]))
        sums = GradientSum(plane, 0, cols_all, *later[:2], *refs[:6])
        tail_own, tail_got, tail_load, tail_sem = refs[6:10]
        tail_rows = tail_own.shape[0]
        load_tail = pltpu.make_async_copy(later[2].at[pl.ds(tail_rows, tail_rows)], tail_own, tail_load)
        load_tail.start()
        sums.start_loads()
        plane.barrier(plane.other_core(), plane.other_shard(), sums.diagonal(plane))
        sums.start_copies()
        load_tail.wait()
        tail_copies = []
        for n in range(2):
            at = pl.ds(n * (tail_rows // 2), tail_rows // 2)
            tail_copies.append(pair.send(tail_own.at[at], tail_got.at[at], tail_sem.at[0, n], tail_sem.at[1, n]))
        tail_copies[0].start()
    else:
        pair.barrier()

    def span(who):
        return pl.ds(pl.multiple_of(who * rows, rows), rows)

    h1 = h1_ref[...]
    r2 = lax.rsqrt(jnp.mean(h1 * h1, axis=1, keepdims=True) + EPS)
    normed = h1 * r2
    db = db_ref[...]
    halves = layer_rows(layer, pair.sec, me, (s0, s1, s2, s3))
    gains = jnp.concatenate([part[experts : experts + 2] for part in halves], axis=1)
    scaled = db * gains[1:2]
    gain_grads_ref[...] = jnp.zeros_like(gain_grads_ref)
    gain_grads_ref[pl.ds(experts + 1, 1), :] = jnp.sum(db * normed, axis=0, keepdims=True)
    dh1 = dout_ref[...].astype(F32) + r2 * (
        scaled - normed * jnp.mean(scaled * normed, axis=1, keepdims=True))
    dh1_v[...] = dh1
    d_all[span(me)] = dh1.astype(BF16)
    send_d = pair.send(d_all.at[span(me)], d_all.at[span(me)], send_sem.at[0], recv_sem.at[0])
    send_d.start()
    router_terms = router_grad_ref[...]
    lane = lax.broadcasted_iota(jnp.int32, router_terms.shape, 1)
    router_terms = router_terms + pltpu.roll(router_terms, LANES // 2, 1)
    columns_v[...] = jnp.where(lane < experts, router_terms, 0.0)
    if beside:
        sums.wait_terms()
        sums.prepare(0, LINE)
    for load in loads:
        load.wait()
    do[span(me)] = nt(d_all[span(me)], wo_v[...]).astype(BF16)
    send_d.wait_recv()
    do[span(peer)] = nt(d_all[span(peer)], wo_v[...]).astype(BF16)
    sends = [send_d]
    if beside:
        tail_copies[1].start()
        pl.when(plane.inner == 0)(lambda: sums.pass_on(0))
        sums.prepare(LINE, LINE * SIDE)
    for i in range(PAIRS):
        cols = pl.ds(i * pair_cols, pair_cols)
        for n in range(KV_IN_PAIR):
            dk = dv = None
            for g in range(GROUP):
                q_at, k_at, v_at = head_at(i, n, g)
                j = (i * KV_IN_PAIR + n) * GROUP + g
                p_low = p_ref[j]
                p = p_low.astype(F32)
                d_head = do[:, pl.ds(j * HEAD_SIZE, HEAD_SIZE)]
                weighted = p * nt(d_head, qkv_ref[:, v_at])
                ds = (weighted - p * jnp.sum(weighted, axis=1, keepdims=True)).astype(BF16)
                dqkv[:, q_at] = (nn(ds, qkv_ref[:, k_at]) * SCALE).astype(BF16)
                dk_part, dv_part = tn(ds, qkv_ref[:, q_at]), tn(p_low, d_head)
                dk = dk_part if dk is None else dk + dk_part
                dv = dv_part if dv is None else dv + dv_part
            dqkv[:, k_at] = (dk * SCALE).astype(BF16)
            dqkv[:, v_at] = dv.astype(BF16)
        send = pair.send(dqkv.at[:, cols], got_dqkv.at[:, cols], send_sem.at[1 + i], recv_sem.at[1 + i])
        send.start()
        sends.append(send)
        if beside and i == 0:
            pl.when(plane.inner == 1)(lambda: sums.pass_on(0))
    da = nt(dqkv[...], wq_v[me])
    grad_q[me] = tn(a_ref[...], dqkv[...]).astype(BF16)
    grad_o[...] = tn(o_ref[...], d_all[...]).astype(BF16)
    store_o = pltpu.make_async_copy(
        grad_o, grad_hbm.at[:, pl.ds(QUERY_WIDTH + 2 * KV_WIDTH, width)], store_sem.at[LOADS - 1])
    store_o.start()
    for send in sends[1:]:
        send.wait_recv()
    da = da + nt(got_dqkv[...], wq_v[peer])
    da_send[...] = jnp.where(me == 0, da[rows:], da[:rows]).astype(BF16)
    send_da = pair.send(da_send, got_da, send_sem.at[1 + PAIRS], recv_sem.at[1 + PAIRS])
    send_da.start()
    own_da = jnp.where(me == 0, da[:rows], da[rows:])
    grad_q[peer] = tn(a_ref[...], got_dqkv[...]).astype(BF16)
    stores = [store_o]
    for j in range(2):
        for at, local, size in head_columns(j):
            store = pltpu.make_async_copy(
                grad_q.at[j, :, pl.ds(local, size)], grad_hbm.at[:, pl.ds(at, size)],
                store_sem.at[len(stores) - 1])
            store.start()
            stores.append(store)
    send_da.wait_recv()
    other_da = got_da[...].astype(F32)
    h = h_ref[...].astype(F32)
    r1 = lax.rsqrt(jnp.mean(h * h, axis=1, keepdims=True) + EPS)
    halves = []
    total = jnp.zeros((rows, 1), F32)
    for j in range(2):
        cols = pl.ds(j * half, half)
        da_j = jnp.where(me == j, own_da, other_da)
        normed = h[:, j * half : (j + 1) * half] * r1
        gain_grads_ref[pl.ds(experts, 1), cols] = jnp.sum(da_j * normed, axis=0, keepdims=True)
        scaled = da_j * gains[0:1, j * half : (j + 1) * half]
        total = total + jnp.sum(scaled * normed, axis=1, keepdims=True)
        halves.append((cols, scaled, normed))
    columns = columns_v[...] + jnp.transpose(gain_grads_ref[...])
    columns_ref[...] = columns.astype(BF16)
    for cols, scaled, normed in halves:
        dh_ref[:, cols] = (dh1_v[:, cols] + r1 * (scaled - normed * (total / width))).astype(dh_ref.dtype)
    if beside:
        sums.hand_over(later_out[0])
        for copy in tail_copies:
            copy.wait()
        later_out[1][...] = (tail_own[...].astype(F32) + tail_got[...].astype(F32)).astype(BF16)
        sums.drain(1)
    for send in sends + [send_da]:
        send.wait_send()
    for store in stores:
        store.wait()


def attention_backward(layer, experts, router_grad, db, dout, h1, h, small, a_half, qkv, p, o, weights, later,
                       collective_id):
    rows, width = db.shape
    half, group = width // 2, 2 * rows
    cols = (QUERY_WIDTH + 2 * KV_WIDTH) // 2
    any_spec = pl.BlockSpec(memory_space=pl.ANY)
    vmem = pl.BlockSpec(memory_space=pltpu.VMEM)
    later_out, later_scratch = (), []
    if later:
        places, _, sub, later_cols = later[0].shape
        own, plane = sum_scratch(places, sub, later_cols)
        tail_shape = (later[2].shape[0] // 2, later[2].shape[1])
        later_out = (
            jax.ShapeDtypeStruct((3, sub, later_cols + LANES), BF16),
            jax.ShapeDtypeStruct(tail_shape, BF16),
        )
        later_scratch = own + [
            pltpu.VMEM(tail_shape, BF16),
            pltpu.VMEM(tail_shape, BF16),
            pltpu.SemaphoreType.DMA,
            pltpu.SemaphoreType.DMA((2, 2)),
        ] + plane[1:]
    return pl.pallas_call(
        functools.partial(attention_backward_kernel, layer, rows, width, experts),
        name="attention_backward",
        out_shape=(
            jax.ShapeDtypeStruct((rows, width), F32 if layer == 0 else BF16),
            jax.ShapeDtypeStruct((width, LANES), BF16),
            jax.ShapeDtypeStruct((half, QUERY_WIDTH + 2 * KV_WIDTH + width), BF16),
        ) + later_out,
        in_specs=[vmem] * 13 + [any_spec] * (4 + len(later)),
        out_specs=(vmem, vmem, any_spec) + (vmem,) * len(later_out),
        scratch_shapes=[
            pltpu.VMEM((2, half, cols), BF16),
            pltpu.VMEM((QUERY_WIDTH // 2, width), BF16),
            pltpu.VMEM((group, width), BF16),
            pltpu.VMEM((group, QUERY_WIDTH // 2), BF16),
            pltpu.VMEM((group, cols), BF16),
            pltpu.VMEM((group, cols), BF16),
            pltpu.VMEM((rows, half), BF16),
            pltpu.VMEM((rows, half), BF16),
            pltpu.VMEM((rows, width), F32),
            pltpu.VMEM((2, half, cols), BF16),
            pltpu.VMEM((QUERY_WIDTH // 2, width), BF16),
            pltpu.VMEM((LANES, width), F32),
            pltpu.VMEM((width, LANES), F32),
            pltpu.SemaphoreType.DMA((LOADS,)),
            pltpu.SemaphoreType.DMA((LOADS,)),
            pltpu.SemaphoreType.DMA((2 + PAIRS,)),
            pltpu.SemaphoreType.DMA((2 + PAIRS,)),
        ] + later_scratch,
        cost_estimate=COST,
        compiler_params=pltpu.CompilerParams(
            collective_id=collective_id, has_side_effects=True, vmem_limit_bytes=VMEM_BYTES),
    )(router_grad, db, dout, h1, h, *small, a_half, qkv, p, o, *weights, *later)


def dot(a, b, dims):
    return lax.dot_general(a, b, (dims, ((), ())), preferred_element_type=F32)


def rms_scale(values):
    return lax.rsqrt(jnp.mean(values * values, axis=-1, keepdims=True) + EPS)


def swap_cores(value):
    return lax.ppermute(value, "section", [(0, 1), (1, 0)])


def both_layers(own):
    return lax.all_gather(own, "section", axis=0, tiled=False)


def document_mask(sequence_lengths, rows):
    pos = jnp.arange(rows, dtype=jnp.int32)
    ends = jnp.cumsum(sequence_lengths)
    doc = jnp.sum((pos[:, None] >= ends[None, :]).astype(jnp.int32), axis=1)
    return (doc[:, None] == doc[None, :]) & (pos[None, :] <= pos[:, None])


def plain_attention(qkv, allowed, heads, kv_heads):
    rows = qkv.shape[0]
    group = heads // kv_heads
    q = qkv[:, : heads * HEAD_SIZE].reshape(rows, kv_heads, group, HEAD_SIZE)
    k = qkv[:, heads * HEAD_SIZE : (heads + kv_heads) * HEAD_SIZE].reshape(rows, kv_heads, HEAD_SIZE)
    v = qkv[:, (heads + kv_heads) * HEAD_SIZE :].reshape(rows, kv_heads, HEAD_SIZE)
    s = jnp.einsum("qhgd,khd->hgqk", q, k, preferred_element_type=F32) * HEAD_SIZE ** (-0.5)
    s = jnp.where(allowed[None, None], s, MASKED_SCORE)
    ex = jnp.exp(s - jnp.max(s, axis=-1, keepdims=True))
    p = ex / jnp.sum(ex, axis=-1, keepdims=True)
    o = jnp.einsum("hgqk,khd->qhgd", p.astype(BF16), v, preferred_element_type=F32)
    return o.reshape(rows, heads * HEAD_SIZE).astype(BF16), p, (q, k, v)


def plain_attention_backward(do, p, heads_in):
    q, k, v = heads_in
    rows = q.shape[0]
    dh = do.reshape(q.shape)
    dv = jnp.einsum("hgqk,qhgd->khd", p.astype(BF16), dh, preferred_element_type=F32)
    dp = jnp.einsum("qhgd,khd->hgqk", dh, v, preferred_element_type=F32)
    ds = (p * (dp - jnp.sum(p * dp, axis=-1, keepdims=True))).astype(BF16)
    dq = jnp.einsum("hgqk,khd->qhgd", ds, k, preferred_element_type=F32) * HEAD_SIZE ** (-0.5)
    dk = jnp.einsum("hgqk,qhgd->khd", ds, q, preferred_element_type=F32) * HEAD_SIZE ** (-0.5)
    return jnp.concatenate(
        [dq.reshape(rows, -1), dk.reshape(rows, -1), dv.reshape(rows, -1)], axis=1
    ).astype(BF16)


def column_parts(n, j):
    qw, kw = QUERY_WIDTH // n, KV_WIDTH // n
    return (
        (j * qw, qw),
        (QUERY_WIDTH + j * kw, kw),
        (QUERY_WIDTH + KV_WIDTH + j * kw, kw),
    )


def plain_shards(
    edge_inputs, seq_lengths, routes, w_qkv, w_out, w_router, gain_attn, gain_moe, w_gate_up, w_down
):
    sec = lax.axis_index("section")
    owner = lax.axis_index("expert")
    shard_pos = lax.axis_index("shard")
    n_shard = lax.axis_size("shard")
    n_owner = lax.axis_size("expert")
    rows, width = edge_inputs.shape[2], edge_inputs.shape[3]
    experts = w_router.shape[2]
    group_rows = rows * n_shard
    half = width // n_shard
    heads, kv_heads = QUERY_HEADS // n_shard, KEY_VALUE_HEADS // n_shard

    def pick(array, index):
        return lax.dynamic_index_in_dim(array, index, 0, keepdims=False)

    own_edge, other_edge = pick(edge_inputs[0], sec), swap_cores(pick(edge_inputs[0], 1 - sec))
    x_in = jnp.where(sec == 0, own_edge, other_edge)
    dy = jnp.where(sec == 0, other_edge, own_edge)
    own_routes, other_routes = pick(routes[0], sec), swap_cores(pick(routes[0], 1 - sec))
    layer_routes = (
        jnp.where(sec == 0, own_routes, other_routes),
        jnp.where(sec == 0, other_routes, own_routes),
    )
    allowed = document_mask(pick(seq_lengths, sec)[0], group_rows)
    wq = both_layers(w_qkv[0])
    wo = both_layers(w_out[0])
    small = jnp.concatenate([w_router[0], gain_attn[0][:, None], gain_moe[0][:, None]], axis=1)
    small = lax.all_gather(both_layers(small), "shard", axis=1, tiled=True)
    wgu = both_layers(w_gate_up[0])
    wd = both_layers(w_down[0])
    columns = jnp.arange(experts, dtype=jnp.int32)
    route_masks = [
        jnp.any(r[:, :, None] == columns[None, None, :], axis=1).astype(BF16) for r in layer_routes
    ]
    plane_masks = [lax.all_gather(m, "expert", axis=0, tiled=True) for m in route_masks]

    def forward(layer, h):
        gain_a = small[layer, :, experts].astype(F32)[None, :]
        gain_m = small[layer, :, experts + 1].astype(F32)[None, :]
        router = small[layer, :, :experts]
        r1 = rms_scale(h)
        a = (h * r1 * gain_a).astype(BF16)
        a_half = lax.all_to_all(
            a.reshape(rows, n_shard, half), "shard", split_axis=1, concat_axis=0, tiled=True
        ).reshape(group_rows, half)
        blocks = []
        for j in range(n_shard):
            blocks.append(
                jnp.concatenate(
                    [
                        dot(a_half, wq[layer, :, at : at + size], ((1,), (0,)))
                        for at, size in column_parts(n_shard, j)
                    ],
                    axis=1,
                ).astype(BF16)
            )
        qkv = lax.psum_scatter(jnp.stack(blocks), "shard", scatter_dimension=0, tiled=False)
        o, p, heads_in = plain_attention(qkv, allowed, heads, kv_heads)
        part = dot(o, wo[layer], ((1,), (0,))).astype(BF16)
        h1 = h + lax.psum_scatter(part, "shard", scatter_dimension=0, tiled=True).astype(F32)
        r2 = rms_scale(h1)
        b = (h1 * r2 * gain_m).astype(BF16)
        b_all = lax.all_gather(b, "expert", axis=0, tiled=True)
        mask = plane_masks[layer].astype(F32) > 0
        logits = jnp.where(mask, dot(b_all, router, ((1,), (0,))), MASKED_SCORE)
        ex = jnp.where(mask, jnp.exp(logits - jnp.max(logits, axis=1, keepdims=True)), 0.0)
        gates = ex / jnp.sum(ex, axis=1, keepdims=True)
        own_gates = lax.dynamic_slice_in_dim(gates, owner * EXP_DEV, EXP_DEV, 1)
        kept, scaled = [], []
        for j in range(EXP_DEV):
            gu = dot(b_all, wgu[layer, j], ((1,), (0,)))
            g, u = gu[:, :FF], gu[:, FF:]
            scaled.append((g * jax.nn.sigmoid(g) * u * own_gates[:, j : j + 1]).astype(BF16))
            kept.append(gu.astype(BF16))
        scaled = jnp.concatenate(scaled, axis=1)
        moe_part = dot(scaled, wd[layer].reshape(EXP_DEV * FF, width), ((1,), (0,))).astype(BF16)
        moe = lax.psum_scatter(moe_part, "expert", scatter_dimension=0, tiled=True).astype(F32)
        state = (h, r1, a_half, p, heads_in, o, h1, r2, b_all, own_gates, kept, scaled, moe)
        return h1 + moe, state

    def backward(layer, dout, dout_low, state):
        h, r1, a_half, p, heads_in, o, h1, r2, b_all, own_gates, kept, scaled, moe = state
        gain_a = small[layer, :, experts].astype(F32)[None, :]
        gain_m = small[layer, :, experts + 1].astype(F32)[None, :]
        router = small[layer, :, :experts]
        own_router = lax.dynamic_slice_in_dim(router, owner * EXP_DEV, EXP_DEV, 1)
        total = lax.all_gather(jnp.sum(dout * moe, axis=1), "expert", axis=0, tiled=True)
        dout_all = lax.all_gather(dout_low, "expert", axis=0, tiled=True)
        dgus, dcs = [], []
        for j in range(EXP_DEV):
            gate = own_gates[:, j : j + 1]
            g, u = kept[j][:, :FF].astype(F32), kept[j][:, FF:].astype(F32)
            sig = jax.nn.sigmoid(g)
            silu = g * sig
            dz = dot(dout_all, wd[layer, j], ((1,), (1,)))
            dgate = jnp.sum(dz * silu * u, axis=1, keepdims=True)
            dcs.append(gate * (dgate - total[:, None]))
            dz = dz * gate
            dgus.append(
                jnp.concatenate(
                    [dz * u * sig * (1.0 + g * (1.0 - sig)), dz * silu], axis=1
                ).astype(BF16)
            )
        dc = jnp.concatenate(dcs, axis=1)
        db_part = sum(dot(dgus[j], wgu[layer, j], ((1,), (1,))) for j in range(EXP_DEV))
        for j in range(EXP_DEV):
            db_part = db_part + dc[:, j : j + 1] * own_router[:, j].astype(F32)[None, :]
        db = lax.psum_scatter(
            db_part.astype(BF16), "expert", scatter_dimension=0, tiled=True
        ).astype(F32)
        grad_down = dot(scaled, dout_all, ((0,), (0,))).reshape(EXP_DEV, FF, width)
        grad_gu = jnp.stack([dot(b_all, dgus[j], ((0,), (0,))) for j in range(EXP_DEV)])
        grad_router = lax.dot_general(
            dc, b_all.astype(F32), (((0,), (0,)), ((), ())), precision=lax.Precision.HIGHEST
        )
        normed = h1 * r2
        grad_gain_m = jnp.sum(db * normed, axis=0)
        scaled_db = db * gain_m
        dh1 = dout + r2 * (scaled_db - normed * jnp.mean(scaled_db * normed, axis=1, keepdims=True))
        dattn = lax.all_gather(dh1.astype(BF16), "shard", axis=0, tiled=True)
        do = dot(dattn, wo[layer], ((1,), (1,))).astype(BF16)
        grad_out = dot(o, dattn, ((0,), (0,)))
        dqkv = lax.all_gather(plain_attention_backward(do, p, heads_in), "shard", axis=0, tiled=False)
        da = 0.0
        grad_qkv = []
        for part in range(3):
            grad_qkv.append([])
        for j in range(n_shard):
            at_local = 0
            for part, (at, size) in enumerate(column_parts(n_shard, j)):
                piece = dqkv[j, :, at_local : at_local + size]
                at_local += size
                da = da + dot(piece, wq[layer, :, at : at + size], ((1,), (1,)))
                grad_qkv[part].append(dot(a_half, piece, ((0,), (0,))))
        grad_qkv = jnp.concatenate([x for part in grad_qkv for x in part], axis=1)
        da = lax.all_to_all(
            da.astype(BF16), "shard", split_axis=0, concat_axis=1, tiled=True
        ).astype(F32)
        normed = h * r1
        grad_gain_a = jnp.sum(da * normed, axis=0)
        scaled_da = da * gain_a
        dh = dh1 + r1 * (scaled_da - normed * jnp.mean(scaled_da * normed, axis=1, keepdims=True))
        return dh, (grad_qkv, grad_out, grad_router, grad_gain_a, grad_gain_m, grad_gu, grad_down)

    out0, state0 = forward(0, x_in.astype(F32))
    mid = out0.astype(BF16).astype(F32)
    final, state1 = forward(1, mid)
    dh_one, grads1 = backward(1, dy.astype(F32), dy, state1)
    low = dh_one.astype(BF16)
    dh_zero, grads0 = backward(0, low.astype(F32), low, state0)

    def half_sum(grad):
        low_grad = grad.astype(BF16)
        halves = low_grad.reshape((2, -1) + low_grad.shape[1:])
        got = swap_cores(pick(halves, 1 - sec))
        return (pick(halves, sec).astype(F32) + got.astype(F32)).astype(BF16)

    def to_owner(half0, half1):
        keep = jnp.where(sec == 0, half0, half1)
        got = swap_cores(jnp.where(sec == 0, half1, half0))
        first = jnp.where(sec == 0, keep, got)
        second = jnp.where(sec == 0, got, keep)
        return jnp.concatenate([first, second], axis=0).astype(F32)

    attn_halves, exp_halves = [], []
    for grads in (grads0, grads1):
        attn = half_sum(jnp.concatenate([grads[0], grads[1]], axis=1))
        attn_halves.append(lax.psum(attn, "expert"))
        exp_halves.append(tuple(lax.psum(half_sum(g), "shard") for g in (grads[5], grads[6])))
    attn = to_owner(*attn_halves)
    grad_qkv, grad_out = attn[:, : w_qkv.shape[2]], attn[:, w_qkv.shape[2] :]
    grad_gu = to_owner(exp_halves[0][0], exp_halves[1][0])
    grad_down = to_owner(exp_halves[0][1], exp_halves[1][1])

    tiny = []
    for grads in (grads0, grads1):
        hot = jnp.arange(experts)[:, None] == owner * EXP_DEV + jnp.arange(EXP_DEV)[None, :]
        router = sum(
            jnp.where(hot[:, j : j + 1], grads[2][j][None, :], 0.0) for j in range(EXP_DEV)
        )
        tiny.append(jnp.concatenate([router, grads[3][None, :], grads[4][None, :]], axis=0))
    tiny = lax.psum(jnp.stack(tiny), ("section", "expert", "shard"))
    tiny = lax.dynamic_slice_in_dim(pick(tiny, sec), shard_pos * half, half, 1)

    send = jnp.where(sec == 0, final, dh_zero)
    keep = jnp.where(sec == 0, dh_zero, final)
    got = swap_cores(send)
    edge = jnp.where(sec == 0, jnp.stack([keep, got]), jnp.stack([got, keep]))
    return (
        edge[None],
        grad_qkv[None],
        grad_out[None],
        tiny[:experts].T[None],
        tiny[experts][None],
        tiny[experts + 1][None],
        grad_gu[None],
        grad_down[None],
    )


def kernel_shards(
    edge_inputs, seq_lengths, routes, w_qkv, w_out, w_router, gain_attn, gain_moe, w_gate_up, w_down
):
    sec = lax.axis_index("section")
    owner = lax.axis_index("expert")
    shard_pos = lax.axis_index("shard")
    rows, width = edge_inputs.shape[2], edge_inputs.shape[3]
    experts = w_router.shape[2]
    half = width // 2
    attn_cols = w_qkv.shape[2] + w_out.shape[2]

    def pick(array, index):
        return lax.dynamic_index_in_dim(array, index, 0, keepdims=False)

    def swap_shards(value):
        return lax.ppermute(value, "shard", [(0, 1), (1, 0)])

    def by_core(own, other):
        return jnp.where(sec == 0, own, other), jnp.where(sec == 0, other, own)

    small = jnp.concatenate([w_router[0].T, gain_attn, gain_moe], axis=0)
    across = lax.ppermute(small, ("section", "shard"), [(0, 3), (1, 2), (2, 1), (3, 0)])

    smalls = (small, swap_shards(small), swap_cores(small), across)
    x_in, dy = by_core(pick(edge_inputs[0], sec), swap_cores(pick(edge_inputs[0], 1 - sec)))
    core_routes = (pick(routes[0], sec), swap_cores(pick(routes[0], 1 - sec)))
    lens = pick(seq_lengths, sec)[0]
    attn_weights = (w_qkv[0], swap_cores(w_qkv[0]), w_out[0], swap_cores(w_out[0]))
    expert_weights = (
        w_gate_up[0], swap_cores(w_gate_up[0]), w_down[0], swap_cores(w_down[0])
    )
    def forward(layer, h):
        block, h1, *attn_state = attention_forward(
            layer, experts, lens, h, smalls, core_routes, attn_weights, 1 + layer
        )
        moe, out, *expert_state = moe_forward(
            layer, block, h1, expert_weights, experts, F32 if layer else BF16, 3 + layer
        )
        return out, (h, h1, moe, attn_state, expert_state)

    def backward(layer, dout, state, later, later_attn):
        h, h1, moe, attn_state, expert_state = state
        results = moe_backward(
            layer, dout, moe, smalls, expert_weights, expert_state, later, experts,
            5 + layer,
        )
        db, keep_gu, keep_down, send_gu, send_down, grad_router = results[:6]
        dh, columns, grad_attn, *piece = attention_backward(
            layer, experts, grad_router, db, dout, h1, h, smalls, *attn_state, attn_weights,
            later_attn + tuple(results[7:8]) if later else (), 7 + layer,
        )
        places = LINE * SIDE
        sub = half // (2 * places)
        grad_attn = grad_attn.reshape(places, 2, sub, attn_cols)
        columns = columns.reshape(2, places, 2, sub, LANES)
        return dh, grad_attn, columns, (keep_gu, keep_down, send_gu, send_down), results[6:8], piece

    out0, state0 = forward(0, x_in)
    final, state1 = forward(1, out0)
    dh_one, attn1, columns1, experts1, *_ = backward(1, dy, state1, (), ())
    dh_zero, attn0, columns0, experts0, sums1, (shares1, tail1) = backward(
        0, dh_one, state0, experts1, (attn1, columns1)
    )
    attn, gu_own, down_own, gu_got, down_got, down_one, gu_moved, down_moved, got = reduce_gradients(
        attn0, columns0, shares1, experts0, *sums1, tail1, dh_zero, final, 9
    )
    grad_qkv, grad_out, grad_gu, grad_down = finish_outputs(
        attn,
        (gu_own, gu_got, sums1[0], gu_moved),
        (down_own, down_got, down_one, down_moved),
        w_qkv.shape[2],
        w_out.shape[2],
    )
    tiny = attn[:, attn_cols : attn_cols + experts + 2].astype(F32)
    keep = jnp.where(sec == 0, dh_zero, final)
    edge = jnp.where(sec == 0, jnp.stack([keep, got]), jnp.stack([got, keep]))
    return (
        edge[None],
        grad_qkv[None],
        grad_out[None],
        tiny[:, :experts][None],
        tiny[:, experts][None],
        tiny[:, experts + 1][None],
        grad_gu[None],
        grad_down[None],
    )


def shards(*arrays):
    if lax.axis_size("expert") == LINE * SIDE and lax.axis_size("shard") == 2:
        return kernel_shards(*arrays)
    return plain_shards(*arrays)


def solution(mesh):
    in_specs = (
        P("section", None, ("expert", "shard"), None),
        P(None, "expert", None),
        P("section", None, ("expert", "shard"), None),
        P("section", "shard", None),
        P("section", "shard", None),
        P("section", "shard", None),
        P("section", "shard"),
        P("section", "shard"),
        P("section", "expert", None, None),
        P("section", "expert", None, None),
    )
    out_specs = (
        P("section", None, ("expert", "shard"), None),
        P("section", "shard", None),
        P("section", "shard", None),
        P("section", "shard", None),
        P("section", "shard"),
        P("section", "shard"),
        P("section", "expert", None, None),
        P("section", "expert", None, None),
    )
    return jax.shard_map(shards, mesh=mesh, in_specs=in_specs, out_specs=out_specs, check_vma=False)
```
